32 devices in a mesh: store: 8 (over y, x, core), layer: 4 (over z).
Axes of the slice: x: 2, y: 2, z: 4, core: 2. Of those that a mesh axis runs over, the one named last changes fastest.
Arguments:
- query_grads: bfloat16 [64, 32768], P('store', 'layer'), may hold values from -6 to 6
- factor_out: float32 [8, 64, 64], P('layer'), may hold values from -0.75 to 0.75
- factor_in: float32 [8, 64, 64], P('layer'), may hold values from -0.75 to 0.75
- page_store: bfloat16 [2048, 32768], P('store', 'layer'), may hold values from -0.03125 to 0.03125
- page_home: int32 [2048], replicated, may hold values from 0 to 2047, as said below
- cand_lists: int32 [8, 256], P('store'), may hold values from 0 to 2047, as said below
- counts: int32 [8], P('store'), may hold values from 32 to 256, as said below
Outputs:
- influence: float32 [8, 256, 64], P('store', 'layer')
The draws below stay inside these ranges and needn't reach their ends.
Inputs may be any that keep to these rules, and one draw needn't show every extreme that they name: `page_home`: A permutation: every location holds one page id. The holder of location p is p // 256. `cand_lists`: among the first counts[b] slots of list b the ids are distinct, and at most 32 of them lie at one holder; in every list some holder has exactly 32. Slots from counts[b] on hold arbitrary ids. `counts`: some list uses all 256 slots.
All inputs are finite; a program needn't handle non-finite values.
Results may differ from the reference program's by a relative error of at most 0.0029.
Values may be sent and summed in bfloat16 or wider, within the bound.
No kernel may reach another device: no remote copies, remote signals or barrier semaphores. Data moves between devices by JAX's collectives and lax.ppermute only.
A program may use at most 128 MiB of HBM per device.

```python
import jax
import jax.numpy as jnp
from jax import lax

R = 64
K = 4096
L = 8
NQ = 64
PAGES_DEV = 256
PAGES = 2048
CAP = 32
LISTS = 8
CAND = 256


def shared_lists(key):
    location = jax.random.permutation(jax.random.fold_in(key, 11), PAGES).astype(jnp.int32)
    inverse = jnp.argsort(location).astype(jnp.int32)
    holders = PAGES // PAGES_DEV
    loads = jax.random.randint(jax.random.fold_in(key, 12), (LISTS, holders), 0, CAP + 1)
    forced = jax.random.randint(jax.random.fold_in(key, 13), (LISTS,), 0, holders)
    column = jnp.arange(holders)[None, :]
    loads = jnp.where(column == forced[:, None], CAP, loads)
    fullest = jax.random.randint(jax.random.fold_in(key, 14), (), 0, LISTS)
    loads = jnp.where(jnp.arange(LISTS)[:, None] == fullest, CAP, loads).astype(jnp.int32)
    ranking = jax.random.randint(jax.random.fold_in(key, 15), (LISTS, holders, PAGES_DEV), 0, 2 ** 18) * PAGES_DEV + jnp.arange(PAGES_DEV)
    picked = lax.top_k(ranking, CAP)[1].astype(jnp.int32)
    base = (jnp.arange(holders) * PAGES_DEV).astype(jnp.int32)[None, :, None]
    page_ids = inverse[base + picked].reshape(LISTS, CAND)
    usable = (jnp.arange(CAP)[None, None, :] < loads[:, :, None]).reshape(LISTS, CAND)
    order_key = jax.random.randint(jax.random.fold_in(key, 16), (LISTS, CAND), 0, 2 ** 18) * CAND + jnp.arange(CAND) + jnp.where(usable, 0, 2 ** 30)
    order = jnp.argsort(order_key, axis=1)
    page_ids = jnp.take_along_axis(page_ids, order, axis=1)
    totals = jnp.sum(loads, axis=1).astype(jnp.int32)
    filler = jax.random.randint(jax.random.fold_in(key, 17), (LISTS, CAND), 0, PAGES)
    page_ids = jnp.where(jnp.arange(CAND)[None, :] < totals[:, None], page_ids, filler).astype(jnp.int32)
    return (location, page_ids, totals)


def draw_page_home(key, part):
    location, page_ids, totals = shared_lists(key)
    return location


def draw_cand_lists(key, part):
    location, page_ids, totals = shared_lists(key)
    return page_ids


def draw_counts(key, part):
    location, page_ids, totals = shared_lists(key)
    return totals


def steps_of(rng, dims, pieces, smallest, largest):
    def one(axis_at, blocks):
        heights = jax.random.uniform(jax.random.fold_in(jax.random.fold_in(rng, 6), axis_at), (blocks,), jnp.float32, smallest / len(pieces), largest / len(pieces))
        return jnp.repeat(jnp.exp(heights), dims[axis_at] // blocks).reshape((-1,) + (1,) * (len(dims) - axis_at - 1))

    gain = one(*pieces[0])
    for cut in pieces[1:]:
        gain = gain * one(*cut)
    return gain


def normal_values(stream_key, dims, spread, most, pieces=(), held_as=jnp.bfloat16):
    result = jax.random.normal(stream_key, dims, jnp.float32) * spread
    if len(pieces) > 0:
        result = steps_of(stream_key, dims, pieces, -0.22, 0.18) * result
    return jnp.clip(result, min=-most, max=most).astype(held_as)


def setup_inputs(seed: int = 0) -> dict:
    streams_of = jax.random.split(jax.random.key(seed), 8)
    return {
        "query_grads": normal_values(streams_of[0], (NQ, L * K), 1.0, 6.0, ((0, 8), (1, 4))),
        "factor_out": normal_values(streams_of[1], (L, R, R), R ** -0.5, 0.75, ((0, 4),), jnp.float32),
        "factor_in": normal_values(streams_of[2], (L, R, R), R ** -0.5, 0.75, ((0, 4),), jnp.float32),
        "page_store": normal_values(streams_of[3], (PAGES, L * K), (L * K) ** -0.5, 0.03125, ((0, 8), (1, 4))),
        "page_home": draw_page_home(jax.random.fold_in(streams_of[7], 71), 0),
        "cand_lists": draw_cand_lists(jax.random.fold_in(streams_of[7], 71), 0),
        "counts": draw_counts(jax.random.fold_in(streams_of[7], 71), 0),
    }


def reference(query_grads, factor_out, factor_in, page_store, page_home, cand_lists, counts):
    total_queries = query_grads.shape[0]
    matrices = query_grads.astype(jnp.float32).reshape(total_queries, L, R, R)
    conditioned = jnp.einsum("lab,nlbc,lcd->nlad", factor_out.astype(jnp.float32), matrices, factor_in.astype(jnp.float32), precision=lax.Precision.HIGHEST)
    conditioned = conditioned.reshape(total_queries, L * R * R).astype(jnp.bfloat16)
    transposed = conditioned.T

    def score_list(item):
        wanted, count = item
        rows = page_store[page_home[wanted]]
        scores = jnp.dot(rows, transposed, preferred_element_type=jnp.float32)
        usable = jnp.arange(CAND) < count
        return jnp.where(usable[:, None], scores, jnp.zeros((), scores.dtype))

    return lax.map(score_list, (cand_lists, counts))
```

```python
import functools

import jax
import jax.numpy as jnp
from jax import lax
from jax.experimental import pallas as pl
from jax.experimental.pallas import tpu as pltpu
from jax.sharding import PartitionSpec as P

HIGHEST = lax.Precision.HIGHEST
VMEM = pl.BlockSpec(memory_space=pltpu.VMEM)
SMEM = pl.BlockSpec(memory_space=pltpu.SMEM)
ANY = pl.BlockSpec(memory_space=pl.ANY)
LANES = 128
CHUNKS = 4


def iota(shape, dimension):
    return lax.broadcasted_iota(jnp.int32, shape, dimension)


def condition_kernel(holders, per_holder, count_ref, query_ref, out_factor_ref, in_factor_ref, home_ref, cand_ref, packed_ref):
    rows, width = query_ref.shape
    layers, rank, _ = in_factor_ref.shape
    half = rank // 2
    query = query_ref[...].astype(jnp.float32)
    low = iota((half, LANES), 1) < rank
    zero = jnp.zeros((rank, rank), jnp.float32)
    for layer in range(layers):
        first = layer * half
        packed = jnp.concatenate(
            [query[:, (first + t) * LANES:(first + t + 1) * LANES] for t in range(half)], axis=0
        )
        factor = in_factor_ref[layer]
        doubled = jnp.concatenate(
            [jnp.concatenate([factor, zero], axis=1), jnp.concatenate([zero, factor], axis=1)], axis=0
        )
        right = jnp.dot(packed, doubled, precision=HIGHEST, preferred_element_type=jnp.float32)
        right = jnp.swapaxes(right.reshape(half, rows, LANES), 0, 1)
        wide = jnp.concatenate([right[q] for q in range(rows)], axis=1)
        left = jnp.dot(out_factor_ref[layer], wide, precision=HIGHEST, preferred_element_type=jnp.float32)
        done = []
        for q in range(rows):
            part = left[:, q * LANES:(q + 1) * LANES]
            ee, eo, oe, oo = (part[i * half:(i + 1) * half] for i in range(4))
            done.append(jnp.where(low, ee, oo) + pltpu.roll(jnp.where(low, oe, eo), rank, 1))
        done = jnp.swapaxes(jnp.stack(done), 0, 1)
        for t in range(half):
            packed_ref[:, (first + t) * LANES:(first + t + 1) * LANES] = done[t].astype(jnp.bfloat16)

    slots = cand_ref.shape[1]
    groups = home_ref.shape[0]
    wanted = cand_ref[...]
    onehot = (iota((LANES, slots), 0) == wanted % LANES).astype(jnp.float32).astype(jnp.bfloat16)
    home = home_ref[...]
    table = jnp.concatenate([home // per_holder, home % per_holder], axis=0).astype(jnp.float32).astype(jnp.bfloat16)
    found = jnp.dot(table, onehot, preferred_element_type=jnp.float32)
    mine = iota((groups, slots), 0) == wanted // LANES
    holder = jnp.sum(jnp.where(mine, found[:groups], 0.0), axis=0, keepdims=True)
    within = jnp.sum(jnp.where(mine, found[groups:], 0.0), axis=0, keepdims=True)
    holder = jnp.where(iota((1, slots), 1) < count_ref[0], holder, float(holders))
    rest = jnp.zeros((rows - 2, slots), jnp.float32)
    packed_ref[:, width:] = jnp.concatenate([holder, within, rest], axis=0).astype(jnp.bfloat16)


def score_kernel(holders, me_ref, *refs):
    packed_refs, pages_ref, out_refs = refs[:holders], refs[holders], refs[holders + 1:2 * holders + 1]
    held, total, arrived = refs[2 * holders + 1:]
    me = me_ref[0]
    count, width = pages_ref.shape
    rows = packed_refs[0].shape[0]
    slots = packed_refs[0].shape[1] - width
    step = width // CHUNKS
    copies = [
        pltpu.make_async_copy(
            pages_ref.at[:, pl.ds(i * step, step)], held.at[:, pl.ds(i * step, step)], arrived.at[i]
        )
        for i in range(CHUNKS)
    ]
    for copy in copies:
        copy.start()
    scores = jnp.zeros((holders * rows, count), jnp.float32)
    for i in range(CHUNKS):
        columns = slice(i * step, (i + 1) * step)
        queries = jnp.concatenate([ref[:, columns].astype(jnp.float32) for ref in packed_refs], axis=0)
        copies[i].wait()
        scores = scores + lax.dot_general(
            queries.astype(jnp.bfloat16), held[:, columns], (((1,), (1,)), ((), ())),
            preferred_element_type=jnp.float32,
        )
    for k in range(holders):
        start = pl.multiple_of((me ^ k) * rows, rows)
        total[pl.ds(start, rows), :] = scores[k * rows:(k + 1) * rows]
    ordered = total[...].astype(jnp.bfloat16)
    page = iota((count, slots), 0).astype(jnp.float32)
    here = me.astype(jnp.float32)
    for k in range(holders):
        notes = packed_refs[k][:, width:].astype(jnp.float32)
        chosen = jnp.where(notes[0:1] == here, notes[1:2], -1.0)
        onehot = (page == chosen).astype(jnp.float32).astype(jnp.bfloat16)
        out_refs[k][...] = jnp.dot(ordered, onehot, preferred_element_type=jnp.float32).astype(jnp.bfloat16)


def split_kernel(holders, groups, me_ref, *refs):
    me = me_ref[0]
    total = refs[0][...].astype(jnp.float32)
    for ref in refs[1:holders]:
        total = total + ref[...].astype(jnp.float32)
    share = total.shape[1] // groups
    parts = [total[:, g * share:(g + 1) * share] for g in range(groups)]
    for j in range(groups):
        part = parts[0]
        for g in range(1, groups):
            part = jnp.where((me ^ j) == g, parts[g], part)
        refs[holders + j][...] = part.astype(jnp.bfloat16)


def add_kernel(*refs):
    total = refs[0][...].astype(jnp.float32)
    for ref in refs[1:-1]:
        total = total + ref[...].astype(jnp.float32)
    refs[-1][0] = total.T


def swap(value, axis, distance):
    size = lax.axis_size(axis)
    return lax.ppermute(value, axis, [(i, i ^ distance) for i in range(size)])


def on_device(query_grads, factor_out, factor_in, page_store, page_home, cand_lists, counts):
    holders = lax.axis_size("store")
    groups = lax.axis_size("layer")
    rows, width = query_grads.shape
    layers, rank, _ = factor_out.shape
    per_holder = page_store.shape[0]
    slots = cand_lists.shape[1]
    bf16 = jnp.bfloat16
    store_at = lax.axis_index("store").astype(jnp.int32).reshape(1)
    layer_at = lax.axis_index("layer").astype(jnp.int32).reshape(1)

    out_factor = factor_out.reshape(layers, rank // 2, 2, rank // 2, 2)
    out_factor = out_factor.transpose(0, 2, 4, 1, 3).reshape(layers, 2 * rank, rank // 2)
    packed = pl.pallas_call(
        functools.partial(condition_kernel, holders, per_holder),
        out_shape=jax.ShapeDtypeStruct((rows, width + slots), bf16),
        in_specs=[SMEM] + [VMEM] * 5,
        out_specs=VMEM,
    )(counts, query_grads, out_factor, factor_in, page_home.reshape(-1, LANES), cand_lists)

    blocks = [None] * holders
    blocks[0] = packed
    blocks[1] = swap(packed, "store", 1)
    for k in range(2, holders, 2):
        blocks[k] = swap(packed, "store", k)
    for k in range(2, holders, 2):
        blocks[k + 1] = swap(blocks[k], "store", 1)

    total = holders * rows
    picked = pl.pallas_call(
        functools.partial(score_kernel, holders),
        out_shape=[jax.ShapeDtypeStruct((total, slots), bf16)] * holders,
        in_specs=[SMEM] + [VMEM] * holders + [ANY],
        out_specs=[VMEM] * holders,
        scratch_shapes=[
            pltpu.VMEM((per_holder, width), bf16),
            pltpu.VMEM((total, per_holder), jnp.float32),
            pltpu.SemaphoreType.DMA((CHUNKS,)),
        ],
        compiler_params=pltpu.CompilerParams(vmem_limit_bytes=56 * 2**20),
    )(store_at, *blocks, page_store)

    landed = [picked[0]] + [swap(picked[k], "store", k) for k in range(1, holders)]
    share = slots // groups
    parts = pl.pallas_call(
        functools.partial(split_kernel, holders, groups),
        out_shape=[jax.ShapeDtypeStruct((total, share), bf16)] * groups,
        in_specs=[SMEM] + [VMEM] * holders,
        out_specs=[VMEM] * groups,
        compiler_params=pltpu.CompilerParams(vmem_limit_bytes=56 * 2**20),
    )(layer_at, *landed)

    terms = [parts[0]] + [swap(parts[j], "layer", j) for j in range(1, groups)]
    return pl.pallas_call(
        add_kernel,
        out_shape=jax.ShapeDtypeStruct((1, share, total), jnp.float32),
        in_specs=[VMEM] * groups,
        out_specs=VMEM,
    )(*terms)


def solution(mesh):
    placed = (
        P("store", "layer"),
        P("layer", None, None),
        P("layer", None, None),
        P("store", "layer"),
        P(),
        P("store", None),
        P("store"),
    )
    return jax.shard_map(
        on_device, mesh=mesh, in_specs=placed, out_specs=P("store", "layer", None), check_vma=False
    )
```

```python
import functools

import jax
import jax.numpy as jnp
from jax import lax
from jax.experimental import pallas as pl
from jax.experimental.pallas import tpu as pltpu
from jax.sharding import PartitionSpec as P

HIGHEST = lax.Precision.HIGHEST
VMEM = pl.BlockSpec(memory_space=pltpu.VMEM)
SMEM = pl.BlockSpec(memory_space=pltpu.SMEM)
LANES = 128
CHUNKS = 4


def iota(shape, dimension):
    return lax.broadcasted_iota(jnp.int32, shape, dimension)


def bit_reversed(size):
    bits = size.bit_length() - 1
    return [sum(((p >> b) & 1) << (bits - 1 - b) for b in range(bits)) for p in range(size)]


def parts_of(value):
    parts = []
    for _ in range(3):
        part = value.astype(jnp.bfloat16)
        value = value - part.astype(jnp.float32)
        parts.append(part)
    return parts


def condition_kernel(
    holders, groups, per_holder, count_ref, at_ref, query_ref, out_factor_ref, in_factor_ref, home_ref, cand_ref, packed_ref
):
    rows, width = query_ref.shape
    layers, rank, _ = in_factor_ref.shape
    half = rank // 2
    query = query_ref[...].astype(jnp.float32)
    low = iota((half, LANES), 1) < rank
    zero = jnp.zeros((rank, rank), jnp.float32)
    source = iota((rank, rank), 0)
    place = iota((rank, rank), 1)
    split = (source == 2 * (place % half) + place // half).astype(jnp.float32)
    for layer in range(layers):
        first = layer * half
        packed = jnp.concatenate(
            [query[:, (first + t) * LANES:(first + t + 1) * LANES] for t in range(half)], axis=0
        ).astype(jnp.bfloat16)
        factor = in_factor_ref[layer]
        doubled = jnp.concatenate(
            [jnp.concatenate([factor, zero], axis=1), jnp.concatenate([zero, factor], axis=1)], axis=0
        )
        right = sum(jnp.dot(packed, part, preferred_element_type=jnp.float32) for part in parts_of(doubled)[::-1])
        right = jnp.swapaxes(right.reshape(half, rows, LANES), 0, 1)
        wide = jnp.concatenate([right[q] for q in range(rows)], axis=1)
        sorted_columns = jnp.dot(out_factor_ref[layer], split, precision=HIGHEST, preferred_element_type=jnp.float32)
        sorted_both = lax.dot_general(
            split, sorted_columns, (((0,), (0,)), ((), ())), precision=HIGHEST, preferred_element_type=jnp.float32
        )
        quarters = jnp.concatenate(
            [sorted_both[r * half:(r + 1) * half, c * half:(c + 1) * half] for r in range(2) for c in range(2)], axis=0
        )
        left = jnp.dot(quarters, wide, precision=HIGHEST, preferred_element_type=jnp.float32)
        done = []
        for q in range(rows):
            part = left[:, q * LANES:(q + 1) * LANES]
            ee, eo, oe, oo = (part[i * half:(i + 1) * half] for i in range(4))
            done.append(jnp.where(low, ee, oo) + pltpu.roll(jnp.where(low, oe, eo), rank, 1))
        done = jnp.swapaxes(jnp.stack(done), 0, 1)
        for t in range(half):
            packed_ref[:, (first + t) * LANES:(first + t + 1) * LANES] = done[t].astype(jnp.bfloat16)

    slots = cand_ref.shape[1]
    share = slots // groups
    home_rows = home_ref.shape[0]
    wanted = jnp.where(iota((1, slots), 1) < count_ref[0], cand_ref[...], -1)
    ranges = [wanted[:, g * share:(g + 1) * share] for g in range(groups)]
    ordered = []
    for j in bit_reversed(groups):
        chosen = ranges[0]
        for g in range(1, groups):
            chosen = jnp.where((at_ref[0] ^ j) == g, ranges[g], chosen)
        ordered.append(chosen)
    wanted = jnp.concatenate(ordered, axis=1)
    known = jnp.maximum(wanted, 0)
    onehot = (iota((LANES, slots), 0) == known % LANES).astype(jnp.float32).astype(jnp.bfloat16)
    home = home_ref[...]
    table = jnp.concatenate([home // per_holder, home % per_holder], axis=0).astype(jnp.float32).astype(jnp.bfloat16)
    found = jnp.dot(table, onehot, preferred_element_type=jnp.float32)
    mine = iota((home_rows, slots), 0) == known // LANES
    holder = jnp.sum(jnp.where(mine, found[:home_rows], 0.0), axis=0, keepdims=True)
    within = jnp.sum(jnp.where(mine, found[home_rows:], 0.0), axis=0, keepdims=True)
    holder = jnp.where(wanted >= 0, holder, float(holders))
    rest = jnp.zeros((rows - 2, slots), jnp.float32)
    packed_ref[:, width:] = jnp.concatenate([holder, within, rest], axis=0).astype(jnp.bfloat16)


def score_kernel(holders, me_ref, *refs):
    packed_refs, pages_ref = refs[:holders], refs[holders]
    keep_ref, send_ref, total = refs[holders + 1:]
    me = me_ref[0]
    count, width = pages_ref.shape
    rows = packed_refs[0].shape[0]
    slots = packed_refs[0].shape[1] - width
    step = width // CHUNKS
    scores = jnp.zeros((holders * rows, count), jnp.float32)
    for i in range(CHUNKS):
        columns = slice(i * step, (i + 1) * step)
        queries = jnp.concatenate([ref[:, columns].astype(jnp.float32) for ref in packed_refs], axis=0)
        scores = scores + lax.dot_general(
            queries.astype(jnp.bfloat16), pages_ref[:, columns], (((1,), (1,)), ((), ())),
            preferred_element_type=jnp.float32,
        )
    for k in range(holders):
        start = pl.multiple_of((me ^ k) * rows, rows)
        total[pl.ds(start, rows), :] = scores[k * rows:(k + 1) * rows]
    ordered = total[...].astype(jnp.bfloat16)
    page = iota((count, slots), 0).astype(jnp.float32)
    here = me.astype(jnp.float32)
    for place, k in enumerate(bit_reversed(holders)):
        notes = packed_refs[k][:, width:].astype(jnp.float32)
        chosen = jnp.where(notes[0:1] == here, notes[1:2], -1.0)
        onehot = (page == chosen).astype(jnp.float32).astype(jnp.bfloat16)
        picked = jnp.dot(ordered, onehot, preferred_element_type=jnp.float32).astype(jnp.bfloat16)
        target = (keep_ref, send_ref)[place // (holders // 2)]
        target[place % (holders // 2)] = picked


def add_kernel(one_ref, other_ref, out_ref):
    out_ref[0] = (one_ref[...] + other_ref[...]).T


def swap(value, axis, distance):
    size = lax.axis_size(axis)
    return lax.ppermute(value, axis, [(i, i ^ distance) for i in range(size)])


def on_device(query_grads, factor_out, factor_in, page_store, page_home, cand_lists, counts):
    holders = lax.axis_size("store")
    groups = lax.axis_size("layer")
    rows, width = query_grads.shape
    layers, rank, _ = factor_out.shape
    per_holder = page_store.shape[0]
    slots = cand_lists.shape[1]
    bf16 = jnp.bfloat16
    store_at = lax.axis_index("store").astype(jnp.int32).reshape(1)
    layer_at = lax.axis_index("layer").astype(jnp.int32).reshape(1)

    packed = pl.pallas_call(
        functools.partial(condition_kernel, holders, groups, per_holder),
        out_shape=jax.ShapeDtypeStruct((rows, width + slots), bf16),
        in_specs=[SMEM] * 2 + [VMEM] * 5,
        out_specs=VMEM,
        compiler_params=pltpu.CompilerParams(vmem_limit_bytes=8 * 2**20),
    )(counts, layer_at, query_grads, factor_out, factor_in, page_home.reshape(-1, LANES), cand_lists)

    blocks = [None] * holders
    blocks[0] = packed
    blocks[1] = swap(packed, "store", 1)
    for k in range(2, holders, 2):
        blocks[k] = swap(packed, "store", k)
    for k in range(2, holders, 2):
        blocks[k + 1] = swap(blocks[k], "store", 1)

    total = holders * rows
    bytes_out = 2 * holders * total * slots
    bytes_in = 2 * holders * rows * (width + slots) + 2 * per_holder * width
    keep, send = pl.pallas_call(
        functools.partial(score_kernel, holders),
        out_shape=[jax.ShapeDtypeStruct((holders // 2, total, slots), bf16)] * 2,
        in_specs=[SMEM] + [VMEM] * (holders + 1),
        out_specs=[VMEM] * 2,
        scratch_shapes=[pltpu.VMEM((total, per_holder), jnp.float32)],
        compiler_params=pltpu.CompilerParams(vmem_limit_bytes=8 * 2**20 + bytes_in + bytes_out),
    )(store_at, *blocks, page_store)

    distance = 1
    while True:
        landed = swap(send, "store", distance)
        distance *= 2
        if distance == holders:
            break
        cut = keep.shape[0] // 2
        keep, send = keep[:cut] + landed[:cut], keep[cut:] + landed[cut:]
    scores = (keep + landed)[0]

    distance = 1
    while distance < groups:
        cut = scores.shape[1] // 2
        landed = swap(scores[:, cut:], "layer", distance).astype(jnp.float32)
        keep = scores[:, :cut].astype(jnp.float32)
        distance *= 2
        if distance < groups:
            scores = keep + landed
    return pl.pallas_call(
        add_kernel,
        out_shape=jax.ShapeDtypeStruct((1, slots // groups, total), jnp.float32),
        in_specs=[VMEM] * 2,
        out_specs=VMEM,
        compiler_params=pltpu.CompilerParams(vmem_limit_bytes=2 * 2**20),
    )(keep, landed)


def solution(mesh):
    placed = (
        P("store", "layer"),
        P("layer", None, None),
        P("layer", None, None),
        P("store", "layer"),
        P(),
        P("store", None),
        P("store"),
    )
    return jax.shard_map(
        on_device, mesh=mesh, in_specs=placed, out_specs=P("store", "layer", None), check_vma=False
    )
```

```python
import functools

import jax
import jax.numpy as jnp
from jax import lax
from jax.experimental import pallas as pl
from jax.experimental.pallas import tpu as pltpu
from jax.sharding import PartitionSpec as P

HIGHEST = lax.Precision.HIGHEST
VMEM = pl.BlockSpec(memory_space=pltpu.VMEM)
SMEM = pl.BlockSpec(memory_space=pltpu.SMEM)
HBM = pl.BlockSpec(memory_space=pltpu.HBM)
LANES = 128
CHUNKS = 4


def iota(shape, dimension):
    return lax.broadcasted_iota(jnp.int32, shape, dimension)


def bit_reversed(size):
    bits = size.bit_length() - 1
    return [sum(((p >> b) & 1) << (bits - 1 - b) for b in range(bits)) for p in range(size)]


def parts_of(value):
    parts = []
    for _ in range(3):
        part = value.astype(jnp.bfloat16)
        value = value - part.astype(jnp.float32)
        parts.append(part)
    return parts


def condition_kernel(holders, groups, count_ref, at_ref, *refs):
    sources, packed_ref, pages_ref, landing, arrived = refs[:6], refs[6], refs[7], refs[8:13], refs[13]
    copies = [
        pltpu.make_async_copy(source, target, arrived.at[i])
        for i, (source, target) in enumerate(zip(sources, landing + (pages_ref,)))
    ]
    for copy in copies:
        copy.start()
    for copy in copies[:-1]:
        copy.wait()
    query_ref, in_factor_ref, out_factor_ref, home_ref, cand_ref = landing
    per_holder = pages_ref.shape[0]
    rows, width = query_ref.shape
    layers, rank, _ = in_factor_ref.shape
    half = rank // 2
    query = query_ref[...].astype(jnp.float32)
    low = iota((half, LANES), 1) < rank
    zero = jnp.zeros((rank, rank), jnp.float32)
    source = iota((rank, rank), 0)
    place = iota((rank, rank), 1)
    split = (source == 2 * (place % half) + place // half).astype(jnp.float32)
    for layer in range(layers):
        first = layer * half
        packed = jnp.concatenate(
            [query[:, (first + t) * LANES:(first + t + 1) * LANES] for t in range(half)], axis=0
        ).astype(jnp.bfloat16)
        factor = in_factor_ref[layer]
        doubled = jnp.concatenate(
            [jnp.concatenate([factor, zero], axis=1), jnp.concatenate([zero, factor], axis=1)], axis=0
        )
        right = sum(jnp.dot(packed, part, preferred_element_type=jnp.float32) for part in parts_of(doubled)[::-1])
        right = jnp.swapaxes(right.reshape(half, rows, LANES), 0, 1)
        wide = jnp.concatenate([right[q] for q in range(rows)], axis=1)
        sorted_columns = jnp.dot(out_factor_ref[layer], split, precision=HIGHEST, preferred_element_type=jnp.float32)
        sorted_both = lax.dot_general(
            split, sorted_columns, (((0,), (0,)), ((), ())), precision=HIGHEST, preferred_element_type=jnp.float32
        )
        quarters = jnp.concatenate(
            [sorted_both[r * half:(r + 1) * half, c * half:(c + 1) * half] for r in range(2) for c in range(2)], axis=0
        )
        left = jnp.dot(quarters, wide, precision=HIGHEST, preferred_element_type=jnp.float32)
        done = []
        for q in range(rows):
            part = left[:, q * LANES:(q + 1) * LANES]
            ee, eo, oe, oo = (part[i * half:(i + 1) * half] for i in range(4))
            done.append(jnp.where(low, ee, oo) + pltpu.roll(jnp.where(low, oe, eo), rank, 1))
        done = jnp.swapaxes(jnp.stack(done), 0, 1)
        for t in range(half):
            packed_ref[:, (first + t) * LANES:(first + t + 1) * LANES] = done[t].astype(jnp.bfloat16)

    slots = cand_ref.shape[1]
    share = slots // groups
    home_rows = home_ref.shape[0]
    wanted = jnp.where(iota((1, slots), 1) < count_ref[0], cand_ref[...], -1)
    ranges = [wanted[:, g * share:(g + 1) * share] for g in range(groups)]
    ordered = []
    for j in bit_reversed(groups):
        chosen = ranges[0]
        for g in range(1, groups):
            chosen = jnp.where((at_ref[0] ^ j) == g, ranges[g], chosen)
        ordered.append(chosen)
    wanted = jnp.concatenate(ordered, axis=1)
    known = jnp.maximum(wanted, 0)
    onehot = (iota((LANES, slots), 0) == known % LANES).astype(jnp.float32).astype(jnp.bfloat16)
    home = home_ref[...]
    table = jnp.concatenate([home // per_holder, home % per_holder], axis=0).astype(jnp.float32).astype(jnp.bfloat16)
    found = jnp.dot(table, onehot, preferred_element_type=jnp.float32)
    mine = iota((home_rows, slots), 0) == known // LANES
    holder = jnp.sum(jnp.where(mine, found[:home_rows], 0.0), axis=0, keepdims=True)
    within = jnp.sum(jnp.where(mine, found[home_rows:], 0.0), axis=0, keepdims=True)
    holder = jnp.where(wanted >= 0, holder, float(holders))
    rest = jnp.zeros((rows - 2, slots), jnp.float32)
    packed_ref[:, width:] = jnp.concatenate([holder, within, rest], axis=0).astype(jnp.bfloat16)
    copies[-1].wait()


def score_kernel(holders, me_ref, *refs):
    packed_refs, pages_ref = refs[:holders], refs[holders]
    keep_ref, send_ref, total = refs[holders + 1:]
    me = me_ref[0]
    count, width = pages_ref.shape
    rows = packed_refs[0].shape[0]
    slots = packed_refs[0].shape[1] - width
    step = width // CHUNKS
    scores = jnp.zeros((holders * rows, count), jnp.float32)
    for i in range(CHUNKS):
        columns = slice(i * step, (i + 1) * step)
        queries = jnp.concatenate([ref[:, columns].astype(jnp.float32) for ref in packed_refs], axis=0)
        scores = scores + lax.dot_general(
            queries.astype(jnp.bfloat16), pages_ref[:, columns], (((1,), (1,)), ((), ())),
            preferred_element_type=jnp.float32,
        )
    for k in range(holders):
        start = pl.multiple_of((me ^ k) * rows, rows)
        total[pl.ds(start, rows), :] = scores[k * rows:(k + 1) * rows]
    ordered = total[...].astype(jnp.bfloat16)
    page = iota((count, slots), 0).astype(jnp.float32)
    here = me.astype(jnp.float32)
    for place, k in enumerate(bit_reversed(holders)):
        notes = packed_refs[k][:, width:].astype(jnp.float32)
        chosen = jnp.where(notes[0:1] == here, notes[1:2], -1.0)
        onehot = (page == chosen).astype(jnp.float32).astype(jnp.bfloat16)
        picked = jnp.dot(ordered, onehot, preferred_element_type=jnp.float32).astype(jnp.bfloat16)
        target = (keep_ref, send_ref)[place // (holders // 2)]
        target[place % (holders // 2)] = picked


def finish_kernel(me_ref, one_ref, other_ref, handed_ref, out_ref):
    out_ref[0] = jnp.where(me_ref[0] % 2 == 1, one_ref[...] + other_ref[...], handed_ref[...]).T


def swap(value, axis, distance):
    return lax.ppermute(value, axis, [(i, i ^ distance) for i in range(lax.axis_size(axis))])


def swap_seconds(value, distance):
    return lax.ppermute(value, "store", [(i, i ^ distance) for i in range(1, lax.axis_size("store"), 2)])


def on_device(query_grads, factor_out, factor_in, page_store, page_home, cand_lists, counts):
    holders = lax.axis_size("store")
    groups = lax.axis_size("layer")
    rows, width = query_grads.shape
    layers, rank, _ = factor_out.shape
    per_holder = page_store.shape[0]
    slots = cand_lists.shape[1]
    bf16 = jnp.bfloat16
    store_at = lax.axis_index("store").astype(jnp.int32).reshape(1)
    layer_at = lax.axis_index("layer").astype(jnp.int32).reshape(1)

    home = page_home.reshape(-1, LANES)
    sources = [
        pltpu.with_memory_space_constraint(source, pltpu.HBM)
        for source in (query_grads, factor_in, factor_out, home, cand_lists, page_store)
    ]
    packed, pages = pl.pallas_call(
        functools.partial(condition_kernel, holders, groups),
        out_shape=[
            jax.ShapeDtypeStruct((rows, width + slots), bf16), jax.ShapeDtypeStruct(page_store.shape, bf16)
        ],
        in_specs=[SMEM] * 2 + [HBM] * len(sources),
        out_specs=[VMEM] * 2,
        scratch_shapes=[pltpu.VMEM(source.shape, source.dtype) for source in sources[:-1]]
        + [pltpu.SemaphoreType.DMA((len(sources),))],
        compiler_params=pltpu.CompilerParams(vmem_limit_bytes=14 * 2**20),
    )(counts, layer_at, *sources)

    blocks = [None] * holders
    blocks[0] = packed
    blocks[1] = swap(packed, "store", 1)
    for k in range(2, holders, 2):
        blocks[k] = swap(packed, "store", k)
    for k in range(2, holders, 2):
        blocks[k + 1] = swap(blocks[k], "store", 1)

    total = holders * rows
    bytes_out = 2 * holders * total * slots
    bytes_in = 2 * holders * rows * (width + slots) + 2 * per_holder * width
    keep, send = pl.pallas_call(
        functools.partial(score_kernel, holders),
        out_shape=[jax.ShapeDtypeStruct((holders // 2, total, slots), bf16)] * 2,
        in_specs=[SMEM] + [VMEM] * (holders + 1),
        out_specs=[VMEM] * 2,
        scratch_shapes=[pltpu.VMEM((total, per_holder), jnp.float32)],
        compiler_params=pltpu.CompilerParams(vmem_limit_bytes=8 * 2**20 + bytes_in + bytes_out),
    )(store_at, *blocks, pages)

    even, odd = keep, send
    first_to_second = [(i, i + 1) for i in range(0, holders, 2)]
    odd, even = (
        odd + lax.ppermute(even, "store", first_to_second), even + lax.ppermute(odd, "store", first_to_second)
    )
    both = jnp.stack([even, odd])
    distance = 2
    while distance < holders:
        cut = both.shape[1] // 2
        both = both[:, :cut] + swap_seconds(both[:, cut:], distance)
        distance *= 2
    both = both[:, 0]

    distance = 1
    while distance < groups:
        cut = both.shape[2] // 2
        moving = both[:, :, cut:]
        landed = lax.ppermute(
            moving, ("store", "layer"),
            [(s * groups + g, s * groups + (g ^ distance)) for s in range(1, holders, 2) for g in range(groups)],
        ).astype(jnp.float32)
        keep = both[:, :, :cut].astype(jnp.float32)
        distance *= 2
        if distance < groups:
            both = keep + landed
    handed = lax.ppermute(keep[1] + landed[1], "store", [(i + 1, i) for i in range(0, holders, 2)])
    return pl.pallas_call(
        finish_kernel,
        out_shape=jax.ShapeDtypeStruct((1, slots // groups, total), jnp.float32),
        in_specs=[SMEM] + [VMEM] * 3,
        out_specs=VMEM,
        compiler_params=pltpu.CompilerParams(vmem_limit_bytes=2 * 2**20),
    )(store_at, keep[0], landed[0], handed)


def solution(mesh):
    placed = (
        P("store", "layer"),
        P("layer", None, None),
        P("layer", None, None),
        P("store", "layer"),
        P(),
        P("store", None),
        P("store"),
    )
    return jax.shard_map(
        on_device, mesh=mesh, in_specs=placed, out_specs=P("store", "layer", None), check_vma=False
    )
```

```python
import functools

import jax
import jax.numpy as jnp
from jax import lax
from jax.experimental import pallas as pl
from jax.experimental.pallas import tpu as pltpu
from jax.sharding import PartitionSpec as P

HIGHEST = lax.Precision.HIGHEST
VMEM = pl.BlockSpec(memory_space=pltpu.VMEM)
SMEM = pl.BlockSpec(memory_space=pltpu.SMEM)
HBM = pl.BlockSpec(memory_space=pltpu.HBM)
LANES = 128
CHUNKS = 4


def iota(shape, dimension):
    return lax.broadcasted_iota(jnp.int32, shape, dimension)


def store_steps(holders):
    return [1] + [(1 << b) | 1 for b in range(1, holders.bit_length() - 1)]


def layer_steps(groups):
    return [1 << b for b in range(groups.bit_length() - 1)]


def halving_order(steps):
    order = [0]
    for step in reversed(steps):
        order = order + [k ^ step for k in order]
    return order


def parts_of(value):
    parts = []
    for _ in range(3):
        part = value.astype(jnp.bfloat16)
        value = value - part.astype(jnp.float32)
        parts.append(part)
    return parts


def condition_kernel(holders, groups, count_ref, at_ref, *refs):
    sources, packed_ref, pages_ref, landing, arrived = refs[:6], refs[6], refs[7], refs[8:13], refs[13]
    copies = [
        pltpu.make_async_copy(source, target, arrived.at[i])
        for i, (source, target) in enumerate(zip(sources, landing + (pages_ref,)))
    ]
    for copy in copies:
        copy.start()
    for copy in copies[:-1]:
        copy.wait()
    query_ref, in_factor_ref, out_factor_ref, home_ref, cand_ref = landing
    per_holder = pages_ref.shape[0]
    rows, width = query_ref.shape
    layers, rank, _ = in_factor_ref.shape
    half = rank // 2
    query = query_ref[...].astype(jnp.float32)
    low = iota((half, LANES), 1) < rank
    zero = jnp.zeros((rank, rank), jnp.float32)
    source = iota((rank, rank), 0)
    place = iota((rank, rank), 1)
    split = (source == 2 * (place % half) + place // half).astype(jnp.float32)
    for layer in range(layers):
        first = layer * half
        packed = jnp.concatenate(
            [query[:, (first + t) * LANES:(first + t + 1) * LANES] for t in range(half)], axis=0
        ).astype(jnp.bfloat16)
        factor = in_factor_ref[layer]
        doubled = jnp.concatenate(
            [jnp.concatenate([factor, zero], axis=1), jnp.concatenate([zero, factor], axis=1)], axis=0
        )
        right = sum(jnp.dot(packed, part, preferred_element_type=jnp.float32) for part in parts_of(doubled)[::-1])
        right = jnp.swapaxes(right.reshape(half, rows, LANES), 0, 1)
        wide = jnp.concatenate([right[q] for q in range(rows)], axis=1)
        sorted_columns = jnp.dot(out_factor_ref[layer], split, precision=HIGHEST, preferred_element_type=jnp.float32)
        sorted_both = lax.dot_general(
            split, sorted_columns, (((0,), (0,)), ((), ())), precision=HIGHEST, preferred_element_type=jnp.float32
        )
        quarters = jnp.concatenate(
            [sorted_both[r * half:(r + 1) * half, c * half:(c + 1) * half] for r in range(2) for c in range(2)], axis=0
        )
        left = jnp.dot(quarters, wide, precision=HIGHEST, preferred_element_type=jnp.float32)
        done = []
        for q in range(rows):
            part = left[:, q * LANES:(q + 1) * LANES]
            ee, eo, oe, oo = (part[i * half:(i + 1) * half] for i in range(4))
            done.append(jnp.where(low, ee, oo) + pltpu.roll(jnp.where(low, oe, eo), rank, 1))
        done = jnp.swapaxes(jnp.stack(done), 0, 1)
        for t in range(half):
            packed_ref[:, (first + t) * LANES:(first + t + 1) * LANES] = done[t].astype(jnp.bfloat16)

    slots = cand_ref.shape[1]
    share = slots // groups
    home_rows = home_ref.shape[0]
    wanted = jnp.where(iota((1, slots), 1) < count_ref[0], cand_ref[...], -1)
    ranges = [wanted[:, g * share:(g + 1) * share] for g in range(groups)]
    ordered = []
    for j in halving_order(layer_steps(groups)):
        chosen = ranges[0]
        for g in range(1, groups):
            chosen = jnp.where((at_ref[0] ^ j) == g, ranges[g], chosen)
        ordered.append(chosen)
    wanted = jnp.concatenate(ordered, axis=1)
    known = jnp.maximum(wanted, 0)
    onehot = (iota((LANES, slots), 0) == known % LANES).astype(jnp.float32).astype(jnp.bfloat16)
    home = home_ref[...]
    table = jnp.concatenate([home // per_holder, home % per_holder], axis=0).astype(jnp.float32).astype(jnp.bfloat16)
    found = jnp.dot(table, onehot, preferred_element_type=jnp.float32)
    mine = iota((home_rows, slots), 0) == known // LANES
    holder = jnp.sum(jnp.where(mine, found[:home_rows], 0.0), axis=0, keepdims=True)
    within = jnp.sum(jnp.where(mine, found[home_rows:], 0.0), axis=0, keepdims=True)
    holder = jnp.where(wanted >= 0, holder, float(holders))
    rest = jnp.zeros((rows - 2, slots), jnp.float32)
    packed_ref[:, width:] = jnp.concatenate([holder, within, rest], axis=0).astype(jnp.bfloat16)
    copies[-1].wait()


def score_kernel(holders, me_ref, *refs):
    packed_refs, pages_ref = refs[:holders], refs[holders]
    keep_ref, send_ref, total = refs[holders + 1:]
    me = me_ref[0]
    count, width = pages_ref.shape
    rows = packed_refs[0].shape[0]
    slots = packed_refs[0].shape[1] - width
    step = width // CHUNKS
    scores = jnp.zeros((holders * rows, count), jnp.float32)
    for i in range(CHUNKS):
        columns = slice(i * step, (i + 1) * step)
        queries = jnp.concatenate([ref[:, columns].astype(jnp.float32) for ref in packed_refs], axis=0)
        scores = scores + lax.dot_general(
            queries.astype(jnp.bfloat16), pages_ref[:, columns], (((1,), (1,)), ((), ())),
            preferred_element_type=jnp.float32,
        )
    for k in range(holders):
        start = pl.multiple_of((me ^ k) * rows, rows)
        total[pl.ds(start, rows), :] = scores[k * rows:(k + 1) * rows]
    ordered = total[...].astype(jnp.bfloat16)
    page = iota((count, slots), 0).astype(jnp.float32)
    here = me.astype(jnp.float32)
    for place, k in enumerate(halving_order(store_steps(holders))):
        notes = packed_refs[k][:, width:].astype(jnp.float32)
        chosen = jnp.where(notes[0:1] == here, notes[1:2], -1.0)
        onehot = (page == chosen).astype(jnp.float32).astype(jnp.bfloat16)
        picked = jnp.dot(ordered, onehot, preferred_element_type=jnp.float32).astype(jnp.bfloat16)
        target = (keep_ref, send_ref)[place // (holders // 2)]
        target[place % (holders // 2)] = picked


def add_kernel(one_ref, other_ref, out_ref):
    out_ref[0] = (one_ref[...] + other_ref[...]).T


def swap(value, axis, distance):
    return lax.ppermute(value, axis, [(i, i ^ distance) for i in range(lax.axis_size(axis))])


def on_device(query_grads, factor_out, factor_in, page_store, page_home, cand_lists, counts):
    holders = lax.axis_size("store")
    groups = lax.axis_size("layer")
    rows, width = query_grads.shape
    layers, rank, _ = factor_out.shape
    per_holder = page_store.shape[0]
    slots = cand_lists.shape[1]
    bf16 = jnp.bfloat16
    store_at = lax.axis_index("store").astype(jnp.int32).reshape(1)
    layer_at = lax.axis_index("layer").astype(jnp.int32).reshape(1)

    home = page_home.reshape(-1, LANES)
    sources = [
        pltpu.with_memory_space_constraint(source, pltpu.HBM)
        for source in (query_grads, factor_in, factor_out, home, cand_lists, page_store)
    ]
    packed, pages = pl.pallas_call(
        functools.partial(condition_kernel, holders, groups),
        out_shape=[
            jax.ShapeDtypeStruct((rows, width + slots), bf16), pltpu.VMEM(page_store.shape, bf16)
        ],
        in_specs=[SMEM] * 2 + [HBM] * len(sources),
        out_specs=[VMEM] * 2,
        scratch_shapes=[pltpu.VMEM(source.shape, source.dtype) for source in sources[:-1]]
        + [pltpu.SemaphoreType.DMA((len(sources),))],
        compiler_params=pltpu.CompilerParams(vmem_limit_bytes=14 * 2**20),
    )(counts, layer_at, *sources)

    blocks = [None] * holders
    blocks[0] = packed
    blocks[1] = swap(packed, "store", 1)
    for k in range(2, holders, 2):
        blocks[k] = swap(packed, "store", k)
    for k in range(2, holders, 2):
        blocks[k + 1] = swap(blocks[k], "store", 1)

    total = holders * rows
    bytes_out = 2 * holders * total * slots
    bytes_in = 2 * holders * rows * (width + slots) + 2 * per_holder * width
    keep, send = pl.pallas_call(
        functools.partial(score_kernel, holders),
        out_shape=[jax.ShapeDtypeStruct((holders // 2, total, slots), bf16)] * 2,
        in_specs=[SMEM] + [VMEM] * (holders + 1),
        out_specs=[VMEM] * 2,
        scratch_shapes=[pltpu.VMEM((total, per_holder), jnp.float32)],
        compiler_params=pltpu.CompilerParams(vmem_limit_bytes=8 * 2**20 + bytes_in + bytes_out),
    )(store_at, *blocks, pltpu.with_memory_space_constraint(pages, pltpu.VMEM))

    for step in store_steps(holders):
        landed = swap(send, "store", step)
        cut = keep.shape[0] // 2
        if cut:
            keep, send = keep[:cut] + landed[:cut], keep[cut:] + landed[cut:]
    scores = (keep + landed)[0]

    for step in layer_steps(groups):
        cut = scores.shape[1] // 2
        landed = swap(scores[:, cut:], "layer", step).astype(jnp.float32)
        keep = scores[:, :cut].astype(jnp.float32)
        if step < groups // 2:
            scores = keep + landed
    return pl.pallas_call(
        add_kernel,
        out_shape=jax.ShapeDtypeStruct((1, slots // groups, total), jnp.float32),
        in_specs=[VMEM] * 2,
        out_specs=VMEM,
        compiler_params=pltpu.CompilerParams(vmem_limit_bytes=2 * 2**20),
    )(keep, landed)


def solution(mesh):
    placed = (
        P("store", "layer"),
        P("layer", None, None),
        P("layer", None, None),
        P("store", "layer"),
        P(),
        P("store", None),
        P("store"),
    )
    return jax.shard_map(
        on_device, mesh=mesh, in_specs=placed, out_specs=P("store", "layer", None), check_vma=False
    )
```

```python
import functools

import jax
import jax.numpy as jnp
from jax import lax
from jax.experimental import pallas as pl
from jax.experimental.pallas import tpu as pltpu
from jax.sharding import PartitionSpec as P

HIGHEST = lax.Precision.HIGHEST
VMEM = pl.BlockSpec(memory_space=pltpu.VMEM)
SMEM = pl.BlockSpec(memory_space=pltpu.SMEM)
HBM = pl.BlockSpec(memory_space=pltpu.HBM)
LANES = 128
CHUNKS = 4


def iota(shape, dimension):
    return lax.broadcasted_iota(jnp.int32, shape, dimension)


def store_steps(holders):
    return [1] + [(1 << b) | 1 for b in range(1, holders.bit_length() - 1)]


def layer_steps(groups):
    return [1 << b for b in range(groups.bit_length() - 1)]


def halving_order(steps):
    order = [0]
    for step in reversed(steps):
        order = order + [k ^ step for k in order]
    return order


def parts_of(value):
    parts = []
    for _ in range(3):
        part = value.astype(jnp.bfloat16)
        value = value - part.astype(jnp.float32)
        parts.append(part)
    return parts


def condition_kernel(holders, groups, count_ref, *refs):
    sources, packed_ref, pages_ref, landing, arrived = refs[:6], refs[6], refs[7], refs[8:13], refs[13]
    copies = [
        pltpu.make_async_copy(source, target, arrived.at[i])
        for i, (source, target) in enumerate(zip(sources, landing + (pages_ref,)))
    ]
    for copy in copies:
        copy.start()
    for copy in copies[:-1]:
        copy.wait()
    query_ref, in_factor_ref, out_factor_ref, home_ref, cand_ref = landing
    per_holder = pages_ref.shape[0]
    at = lax.axis_index("layer")
    rows, width = query_ref.shape
    layers, rank, _ = in_factor_ref.shape
    half = rank // 2
    query = query_ref[...].astype(jnp.float32)
    low = iota((half, LANES), 1) < rank
    zero = jnp.zeros((rank, rank), jnp.float32)
    source = iota((rank, rank), 0)
    place = iota((rank, rank), 1)
    split = (source == 2 * (place % half) + place // half).astype(jnp.float32)
    for layer in range(layers):
        first = layer * half
        packed = jnp.concatenate(
            [query[:, (first + t) * LANES:(first + t + 1) * LANES] for t in range(half)], axis=0
        ).astype(jnp.bfloat16)
        factor = in_factor_ref[layer]
        doubled = jnp.concatenate(
            [jnp.concatenate([factor, zero], axis=1), jnp.concatenate([zero, factor], axis=1)], axis=0
        )
        right = sum(jnp.dot(packed, part, preferred_element_type=jnp.float32) for part in parts_of(doubled)[::-1])
        right = jnp.swapaxes(right.reshape(half, rows, LANES), 0, 1)
        wide = jnp.concatenate([right[q] for q in range(rows)], axis=1)
        sorted_columns = jnp.dot(out_factor_ref[layer], split, precision=HIGHEST, preferred_element_type=jnp.float32)
        sorted_both = lax.dot_general(
            split, sorted_columns, (((0,), (0,)), ((), ())), precision=HIGHEST, preferred_element_type=jnp.float32
        )
        quarters = jnp.concatenate(
            [sorted_both[r * half:(r + 1) * half, c * half:(c + 1) * half] for r in range(2) for c in range(2)], axis=0
        )
        left = jnp.dot(quarters, wide, precision=HIGHEST, preferred_element_type=jnp.float32)
        done = []
        for q in range(rows):
            part = left[:, q * LANES:(q + 1) * LANES]
            ee, eo, oe, oo = (part[i * half:(i + 1) * half] for i in range(4))
            done.append(jnp.where(low, ee, oo) + pltpu.roll(jnp.where(low, oe, eo), rank, 1))
        done = jnp.swapaxes(jnp.stack(done), 0, 1)
        for t in range(half):
            packed_ref[:, (first + t) * LANES:(first + t + 1) * LANES] = done[t].astype(jnp.bfloat16)

    slots = cand_ref.shape[1]
    share = slots // groups
    home_rows = home_ref.shape[0]
    wanted = jnp.where(iota((1, slots), 1) < count_ref[0], cand_ref[...], -1)
    ranges = [wanted[:, g * share:(g + 1) * share] for g in range(groups)]
    ordered = []
    for j in halving_order(layer_steps(groups)):
        chosen = ranges[0]
        for g in range(1, groups):
            chosen = jnp.where((at ^ j) == g, ranges[g], chosen)
        ordered.append(chosen)
    wanted = jnp.concatenate(ordered, axis=1)
    known = jnp.maximum(wanted, 0)
    onehot = (iota((LANES, slots), 0) == known % LANES).astype(jnp.float32).astype(jnp.bfloat16)
    home = home_ref[...]
    table = jnp.concatenate([home // per_holder, home % per_holder], axis=0).astype(jnp.float32).astype(jnp.bfloat16)
    found = jnp.dot(table, onehot, preferred_element_type=jnp.float32)
    mine = iota((home_rows, slots), 0) == known // LANES
    holder = jnp.sum(jnp.where(mine, found[:home_rows], 0.0), axis=0, keepdims=True)
    within = jnp.sum(jnp.where(mine, found[home_rows:], 0.0), axis=0, keepdims=True)
    holder = jnp.where(wanted >= 0, holder, float(holders))
    rest = jnp.zeros((rows - 2, slots), jnp.float32)
    packed_ref[:, width:] = jnp.concatenate([holder, within, rest], axis=0).astype(jnp.bfloat16)
    copies[-1].wait()


def score_kernel(holders, *refs):
    packed_refs, pages_ref = refs[:holders], refs[holders]
    keep_ref, send_ref, total = refs[holders + 1:]
    me = lax.axis_index("store")
    count, width = pages_ref.shape
    rows = packed_refs[0].shape[0]
    slots = packed_refs[0].shape[1] - width
    step = width // CHUNKS
    scores = jnp.zeros((holders * rows, count), jnp.float32)
    for i in range(CHUNKS):
        columns = slice(i * step, (i + 1) * step)
        queries = jnp.concatenate([ref[:, columns].astype(jnp.float32) for ref in packed_refs], axis=0)
        scores = scores + lax.dot_general(
            queries.astype(jnp.bfloat16), pages_ref[:, columns], (((1,), (1,)), ((), ())),
            preferred_element_type=jnp.float32,
        )
    for k in range(holders):
        start = pl.multiple_of((me ^ k) * rows, rows)
        total[pl.ds(start, rows), :] = scores[k * rows:(k + 1) * rows]
    ordered = total[...].astype(jnp.bfloat16)
    page = iota((count, slots), 0).astype(jnp.float32)
    here = me.astype(jnp.float32)
    for place, k in enumerate(halving_order(store_steps(holders))):
        notes = packed_refs[k][:, width:].astype(jnp.float32)
        chosen = jnp.where(notes[0:1] == here, notes[1:2], -1.0)
        onehot = (page == chosen).astype(jnp.float32).astype(jnp.bfloat16)
        picked = jnp.dot(ordered, onehot, preferred_element_type=jnp.float32).astype(jnp.bfloat16)
        target = (keep_ref, send_ref)[place // (holders // 2)]
        target[place % (holders // 2)] = picked


def add_kernel(one_ref, other_ref, out_ref):
    out_ref[0] = (one_ref[...] + other_ref[...]).T


def swap(value, axis, distance):
    return lax.ppermute(value, axis, [(i, i ^ distance) for i in range(lax.axis_size(axis))])


def on_device(query_grads, factor_out, factor_in, page_store, page_home, cand_lists, counts):
    holders = lax.axis_size("store")
    groups = lax.axis_size("layer")
    rows, width = query_grads.shape
    layers, rank, _ = factor_out.shape
    per_holder = page_store.shape[0]
    slots = cand_lists.shape[1]
    bf16 = jnp.bfloat16

    home = page_home.reshape(-1, LANES)
    sources = [
        pltpu.with_memory_space_constraint(source, pltpu.HBM)
        for source in (query_grads, factor_in, factor_out, home, cand_lists, page_store)
    ]
    packed, pages = pl.pallas_call(
        functools.partial(condition_kernel, holders, groups),
        out_shape=[
            jax.ShapeDtypeStruct((rows, width + slots), bf16), pltpu.VMEM(page_store.shape, bf16)
        ],
        in_specs=[SMEM] + [HBM] * len(sources),
        out_specs=[VMEM] * 2,
        scratch_shapes=[pltpu.VMEM(source.shape, source.dtype) for source in sources[:-1]]
        + [pltpu.SemaphoreType.DMA((len(sources),))],
        compiler_params=pltpu.CompilerParams(vmem_limit_bytes=14 * 2**20),
    )(counts, *sources)

    blocks = [None] * holders
    blocks[0] = packed
    blocks[1] = swap(packed, "store", 1)
    for k in range(2, holders, 2):
        blocks[k] = swap(packed, "store", k)
    for k in range(2, holders, 2):
        blocks[k + 1] = swap(blocks[k], "store", 1)

    total = holders * rows
    bytes_out = 2 * holders * total * slots
    bytes_in = 2 * holders * rows * (width + slots) + 2 * per_holder * width
    keep, send = pl.pallas_call(
        functools.partial(score_kernel, holders),
        out_shape=[jax.ShapeDtypeStruct((holders // 2, total, slots), bf16)] * 2,
        in_specs=[VMEM] * (holders + 1),
        out_specs=[VMEM] * 2,
        scratch_shapes=[pltpu.VMEM((total, per_holder), jnp.float32)],
        compiler_params=pltpu.CompilerParams(vmem_limit_bytes=8 * 2**20 + bytes_in + bytes_out),
    )(*blocks, pltpu.with_memory_space_constraint(pages, pltpu.VMEM))

    for step in store_steps(holders):
        landed = swap(send, "store", step)
        cut = keep.shape[0] // 2
        if cut:
            keep, send = keep[:cut] + landed[:cut], keep[cut:] + landed[cut:]
    scores = (keep + landed)[0]

    for step in layer_steps(groups):
        cut = scores.shape[1] // 2
        landed = swap(scores[:, cut:], "layer", step).astype(jnp.float32)
        keep = scores[:, :cut].astype(jnp.float32)
        if step < groups // 2:
            scores = keep + landed
    return pl.pallas_call(
        add_kernel,
        out_shape=jax.ShapeDtypeStruct((1, slots // groups, total), jnp.float32),
        in_specs=[VMEM] * 2,
        out_specs=VMEM,
        compiler_params=pltpu.CompilerParams(vmem_limit_bytes=2 * 2**20),
    )(keep, landed)


def solution(mesh):
    placed = (
        P("store", "layer"),
        P("layer", None, None),
        P("layer", None, None),
        P("store", "layer"),
        P(),
        P("store", None),
        P("store"),
    )
    return jax.shard_map(
        on_device, mesh=mesh, in_specs=placed, out_specs=P("store", "layer", None), check_vma=False
    )
```

```python
import functools

import jax
import jax.numpy as jnp
from jax import lax
from jax.experimental import pallas as pl
from jax.experimental.pallas import tpu as pltpu
from jax.sharding import PartitionSpec as P

HIGHEST = lax.Precision.HIGHEST
VMEM = pl.BlockSpec(memory_space=pltpu.VMEM)
SMEM = pl.BlockSpec(memory_space=pltpu.SMEM)
HBM = pl.BlockSpec(memory_space=pltpu.HBM)
LANES = 128
CHUNKS = 4


def iota(shape, dimension):
    return lax.broadcasted_iota(jnp.int32, shape, dimension)


def layer_steps(groups):
    return [1 << b for b in range(groups.bit_length() - 1)]


def halving_order(steps):
    order = [0]
    for step in reversed(steps):
        order = order + [k ^ step for k in order]
    return order


def parts_of(value):
    parts = []
    for _ in range(3):
        part = value.astype(jnp.bfloat16)
        value = value - part.astype(jnp.float32)
        parts.append(part)
    return parts


def exact_bf16(value):
    return value.astype(jnp.float32).astype(jnp.bfloat16)


def condition_kernel(holders, groups, capacity, count_ref, *refs):
    sources, packed_ref, pages_ref, found_ref, landing, arrived = refs[:6], refs[6], refs[7], refs[8], refs[9:14], refs[14]
    copies = [
        pltpu.make_async_copy(source, target, arrived.at[i])
        for i, (source, target) in enumerate(zip(sources, landing + (pages_ref,)))
    ]
    for copy in copies:
        copy.start()
    for copy in copies[:-1]:
        copy.wait()
    query_ref, in_factor_ref, out_factor_ref, home_ref, cand_ref = landing
    per_holder = pages_ref.shape[0]
    at = lax.axis_index("layer")
    rows, width = query_ref.shape
    layers, rank, _ = in_factor_ref.shape
    half = rank // 2
    query = query_ref[...].astype(jnp.float32)
    low = iota((half, LANES), 1) < rank
    zero = jnp.zeros((rank, rank), jnp.float32)
    source = iota((rank, rank), 0)
    place = iota((rank, rank), 1)
    split = (source == 2 * (place % half) + place // half).astype(jnp.float32)
    for layer in range(layers):
        first = layer * half
        packed = jnp.concatenate(
            [query[:, (first + t) * LANES:(first + t + 1) * LANES] for t in range(half)], axis=0
        ).astype(jnp.bfloat16)
        factor = in_factor_ref[layer]
        doubled = jnp.concatenate(
            [jnp.concatenate([factor, zero], axis=1), jnp.concatenate([zero, factor], axis=1)], axis=0
        )
        right = sum(jnp.dot(packed, part, preferred_element_type=jnp.float32) for part in parts_of(doubled)[::-1])
        right = jnp.swapaxes(right.reshape(half, rows, LANES), 0, 1)
        wide = jnp.concatenate([right[q] for q in range(rows)], axis=1)
        sorted_columns = jnp.dot(out_factor_ref[layer], split, precision=HIGHEST, preferred_element_type=jnp.float32)
        sorted_both = lax.dot_general(
            split, sorted_columns, (((0,), (0,)), ((), ())), precision=HIGHEST, preferred_element_type=jnp.float32
        )
        quarters = jnp.concatenate(
            [sorted_both[r * half:(r + 1) * half, c * half:(c + 1) * half] for r in range(2) for c in range(2)], axis=0
        )
        left = jnp.dot(quarters, wide, precision=HIGHEST, preferred_element_type=jnp.float32)
        done = []
        for q in range(rows):
            part = left[:, q * LANES:(q + 1) * LANES]
            ee, eo, oe, oo = (part[i * half:(i + 1) * half] for i in range(4))
            done.append(jnp.where(low, ee, oo) + pltpu.roll(jnp.where(low, oe, eo), rank, 1))
        done = jnp.swapaxes(jnp.stack(done), 0, 1)
        for t in range(half):
            packed_ref[:, (first + t) * LANES:(first + t + 1) * LANES] = done[t].astype(jnp.bfloat16)

    slots = cand_ref.shape[1]
    share = slots // groups
    home_rows = home_ref.shape[0]
    wanted = jnp.where(iota((1, slots), 1) < count_ref[0], cand_ref[...], -1)
    ranges = [wanted[:, g * share:(g + 1) * share] for g in range(groups)]
    ordered = []
    for j in halving_order(layer_steps(groups)):
        chosen = ranges[0]
        for g in range(1, groups):
            chosen = jnp.where((at ^ j) == g, ranges[g], chosen)
        ordered.append(chosen)
    wanted = jnp.concatenate(ordered, axis=1)
    known = jnp.maximum(wanted, 0)
    onehot = (iota((LANES, slots), 0) == known % LANES).astype(jnp.float32).astype(jnp.bfloat16)
    home = home_ref[...]
    table = jnp.concatenate([home // per_holder, home % per_holder], axis=0).astype(jnp.float32).astype(jnp.bfloat16)
    found = jnp.dot(table, onehot, preferred_element_type=jnp.float32)
    mine = iota((home_rows, slots), 0) == known // LANES
    holder = jnp.sum(jnp.where(mine, found[:home_rows], 0.0), axis=0, keepdims=True)
    within = jnp.sum(jnp.where(mine, found[home_rows:], 0.0), axis=0, keepdims=True)
    holder = jnp.where(wanted >= 0, holder, float(holders))
    at_holder = iota((holders, slots), 0).astype(jnp.float32) == holder
    earlier = exact_bf16(iota((slots, slots), 0) < iota((slots, slots), 1))
    before = jnp.dot(exact_bf16(at_holder), earlier, preferred_element_type=jnp.float32)
    rank_there = jnp.sum(jnp.where(at_holder, before, 0.0), axis=0, keepdims=True)
    ranked = exact_bf16(iota((capacity, slots), 0).astype(jnp.float32) == rank_there)
    asked = lax.dot_general(
        exact_bf16(jnp.where(at_holder, within + 1.0, 0.0)), ranked, (((1,), (1,)), ((), ())),
        preferred_element_type=jnp.float32,
    )
    blocks = [asked[h:h + rows] for h in range(0, holders, rows)]
    spare = packed_ref.shape[1] - width - capacity * len(blocks)
    if spare:
        blocks.append(jnp.zeros((rows, spare), jnp.float32))
    packed_ref[:, width:] = jnp.concatenate(blocks, axis=1).astype(jnp.bfloat16)
    found_ref[...] = jnp.concatenate([holder, rank_there, jnp.zeros((6, slots), jnp.float32)], axis=0)
    copies[-1].wait()


def score_kernel(holders, capacity, *refs):
    packed_refs, pages_ref, out_ref, total = refs[:holders], refs[holders], refs[holders + 1], refs[holders + 2]
    me = lax.axis_index("store")
    count, width = pages_ref.shape
    rows = packed_refs[0].shape[0]
    half = capacity // 2
    step = width // CHUNKS
    scores = jnp.zeros((holders * rows, count), jnp.float32)
    for i in range(CHUNKS):
        columns = slice(i * step, (i + 1) * step)
        queries = jnp.concatenate([ref[:, columns].astype(jnp.float32) for ref in packed_refs], axis=0)
        scores = scores + lax.dot_general(
            queries.astype(jnp.bfloat16), pages_ref[:, columns], (((1,), (1,)), ((), ())),
            preferred_element_type=jnp.float32,
        )
    for k in range(holders):
        start = pl.multiple_of((me ^ k) * rows, rows)
        total[pl.ds(start, rows), :] = scores[k * rows:(k + 1) * rows]
    asked = []
    for k in range(holders):
        notes = packed_refs[k][:, width:].astype(jnp.float32)
        notes = jnp.sum(jnp.where(iota(notes.shape, 0) == me % rows, notes, 0.0), axis=0, keepdims=True)
        mine = notes[:, :capacity]
        for block in range(1, holders // rows):
            mine = jnp.where(me // rows == block, notes[:, block * capacity:(block + 1) * capacity], mine)
        asked.append(mine)
    page = iota((count, holders * half), 0).astype(jnp.float32) + 1.0
    picked = jnp.zeros((holders * half, 2 * holders * rows), jnp.float32)
    parts = parts_of(total[...])[::-1]
    nothing = jnp.zeros_like(parts[0])
    for side in range(2):
        chosen = exact_bf16(page == jnp.concatenate([row[:, side * half:(side + 1) * half] for row in asked], axis=1))
        for part in parts:
            wide = jnp.concatenate([nothing, part] if side else [part, nothing], axis=0)
            picked = picked + lax.dot_general(
                chosen, wide, (((0,), (1,)), ((), ())), preferred_element_type=jnp.float32
            )
    for k in range(holders):
        out_ref[me ^ k] = picked[k * half:(k + 1) * half]


def spread_kernel(holders, found_ref, landed_ref, keep_ref, send_ref):
    half = landed_ref.shape[1]
    slots = found_ref.shape[1]
    total = landed_ref.shape[2] // 2
    cut = slots // 2
    holder, rank_there = found_ref[0:1], found_ref[1:2]
    place = iota((holders * half, slots), 0).astype(jnp.float32)
    parts = parts_of(jnp.concatenate([landed_ref[h] for h in range(holders)], axis=0))[::-1]
    result = jnp.zeros((total, slots), jnp.float32)
    for side in range(2):
        on_side = (rank_there >= half) if side else (rank_there < half)
        target = jnp.where(on_side, holder * half + rank_there - side * half, -1.0)
        chosen = exact_bf16(place == target)
        for part in parts:
            spread = lax.dot_general(part, chosen, (((0,), (0,)), ((), ())), preferred_element_type=jnp.float32)
            result = result + spread[side * total:(side + 1) * total]
    keep_ref[...] = result[:, :cut]
    send_ref[...] = result[:, cut:]


def add_kernel(one_ref, other_ref, out_ref):
    out_ref[0] = (one_ref[...] + other_ref[...]).T


def swap(value, axis, distance):
    return lax.ppermute(value, axis, [(i, i ^ distance) for i in range(lax.axis_size(axis))])


def on_device(query_grads, factor_out, factor_in, page_store, page_home, cand_lists, counts):
    holders = lax.axis_size("store")
    groups = lax.axis_size("layer")
    rows, width = query_grads.shape
    layers, rank, _ = factor_out.shape
    per_holder = page_store.shape[0]
    slots = cand_lists.shape[1]
    bf16 = jnp.bfloat16

    capacity = slots // holders
    home = page_home.reshape(-1, LANES)
    sources = [
        pltpu.with_memory_space_constraint(source, pltpu.HBM)
        for source in (query_grads, factor_in, factor_out, home, cand_lists, page_store)
    ]
    notes = max(LANES, holders // rows * capacity)
    packed, pages, found = pl.pallas_call(
        functools.partial(condition_kernel, holders, groups, capacity),
        out_shape=[
            jax.ShapeDtypeStruct((rows, width + notes), bf16),
            pltpu.VMEM(page_store.shape, bf16),
            jax.ShapeDtypeStruct((8, slots), jnp.float32),
        ],
        in_specs=[SMEM] + [HBM] * len(sources),
        out_specs=[VMEM] * 3,
        scratch_shapes=[pltpu.VMEM(source.shape, source.dtype) for source in sources[:-1]]
        + [pltpu.SemaphoreType.DMA((len(sources),))],
        compiler_params=pltpu.CompilerParams(vmem_limit_bytes=10 * 2**20 + 24 * slots * slots),
    )(counts, *sources)

    blocks = [None] * holders
    blocks[0] = packed
    blocks[1] = swap(packed, "store", 1)
    for k in range(2, holders, 2):
        blocks[k] = swap(packed, "store", k)
    for k in range(2, holders, 2):
        blocks[k + 1] = swap(blocks[k], "store", 1)

    total = holders * rows
    bytes_in = 2 * holders * rows * (width + notes) + 2 * per_holder * width
    asked = pl.pallas_call(
        functools.partial(score_kernel, holders, capacity),
        out_shape=jax.ShapeDtypeStruct((holders, capacity // 2, 2 * total), jnp.float32),
        in_specs=[VMEM] * (holders + 1),
        out_specs=VMEM,
        scratch_shapes=[pltpu.VMEM((total, per_holder), jnp.float32)],
        compiler_params=pltpu.CompilerParams(vmem_limit_bytes=8 * 2**20 + bytes_in + 48 * total * slots),
    )(*blocks, pltpu.with_memory_space_constraint(pages, pltpu.VMEM))

    landed = lax.all_to_all(asked, "store", split_axis=0, concat_axis=0, tiled=True)
    keep, send = pl.pallas_call(
        functools.partial(spread_kernel, holders),
        out_shape=[jax.ShapeDtypeStruct((total, slots // 2), jnp.float32)] * 2,
        in_specs=[VMEM] * 2,
        out_specs=[VMEM] * 2,
        compiler_params=pltpu.CompilerParams(vmem_limit_bytes=4 * 2**20 + 64 * total * slots),
    )(found, landed)

    for step in layer_steps(groups):
        landed = swap(send, "layer", step)
        if step < groups // 2:
            scores = keep + landed
            cut = scores.shape[1] // 2
            keep, send = scores[:, :cut], scores[:, cut:]
    return pl.pallas_call(
        add_kernel,
        out_shape=jax.ShapeDtypeStruct((1, slots // groups, total), jnp.float32),
        in_specs=[VMEM] * 2,
        out_specs=VMEM,
        compiler_params=pltpu.CompilerParams(vmem_limit_bytes=2 * 2**20),
    )(keep, landed)


def solution(mesh):
    placed = (
        P("store", "layer"),
        P("layer", None, None),
        P("layer", None, None),
        P("store", "layer"),
        P(),
        P("store", None),
        P("store"),
    )
    return jax.shard_map(
        on_device, mesh=mesh, in_specs=placed, out_specs=P("store", "layer", None), check_vma=False
    )
```

```python
import functools

import jax
import jax.numpy as jnp
from jax import lax
from jax.experimental import pallas as pl
from jax.experimental.pallas import tpu as pltpu
from jax.sharding import PartitionSpec as P

HIGHEST = lax.Precision.HIGHEST
VMEM = pl.BlockSpec(memory_space=pltpu.VMEM)
SMEM = pl.BlockSpec(memory_space=pltpu.SMEM)
HBM = pl.BlockSpec(memory_space=pltpu.HBM)
LANES = 128
CHUNKS = 4


def iota(shape, dimension):
    return lax.broadcasted_iota(jnp.int32, shape, dimension)


def parts_of(value):
    parts = []
    for _ in range(3):
        part = value.astype(jnp.bfloat16)
        value = value - part.astype(jnp.float32)
        parts.append(part)
    return parts


def exact_bf16(value):
    return value.astype(jnp.float32).astype(jnp.bfloat16)


def condition_kernel(holders, capacity, count_ref, *refs):
    sources, packed_ref, pages_ref, found_ref, landing, arrived = refs[:6], refs[6], refs[7], refs[8], refs[9:14], refs[14]
    copies = [
        pltpu.make_async_copy(source, target, arrived.at[i])
        for i, (source, target) in enumerate(zip(sources, landing + (pages_ref,)))
    ]
    for copy in copies:
        copy.start()
    for copy in copies[:-1]:
        copy.wait()
    query_ref, in_factor_ref, out_factor_ref, home_ref, cand_ref = landing
    per_holder = pages_ref.shape[0]
    rows, width = query_ref.shape
    layers, rank, _ = in_factor_ref.shape
    half = rank // 2
    query = query_ref[...].astype(jnp.float32)
    low = iota((half, LANES), 1) < rank
    zero = jnp.zeros((rank, rank), jnp.float32)
    source = iota((rank, rank), 0)
    place = iota((rank, rank), 1)
    split = (source == 2 * (place % half) + place // half).astype(jnp.float32)
    for layer in range(layers):
        first = layer * half
        packed = jnp.concatenate(
            [query[:, (first + t) * LANES:(first + t + 1) * LANES] for t in range(half)], axis=0
        ).astype(jnp.bfloat16)
        factor = in_factor_ref[layer]
        doubled = jnp.concatenate(
            [jnp.concatenate([factor, zero], axis=1), jnp.concatenate([zero, factor], axis=1)], axis=0
        )
        right = sum(jnp.dot(packed, part, preferred_element_type=jnp.float32) for part in parts_of(doubled)[::-1])
        right = jnp.swapaxes(right.reshape(half, rows, LANES), 0, 1)
        wide = jnp.concatenate([right[q] for q in range(rows)], axis=1)
        sorted_columns = jnp.dot(out_factor_ref[layer], split, precision=HIGHEST, preferred_element_type=jnp.float32)
        sorted_both = lax.dot_general(
            split, sorted_columns, (((0,), (0,)), ((), ())), precision=HIGHEST, preferred_element_type=jnp.float32
        )
        quarters = jnp.concatenate(
            [sorted_both[r * half:(r + 1) * half, c * half:(c + 1) * half] for r in range(2) for c in range(2)], axis=0
        )
        left = jnp.dot(quarters, wide, precision=HIGHEST, preferred_element_type=jnp.float32)
        done = []
        for q in range(rows):
            part = left[:, q * LANES:(q + 1) * LANES]
            ee, eo, oe, oo = (part[i * half:(i + 1) * half] for i in range(4))
            done.append(jnp.where(low, ee, oo) + pltpu.roll(jnp.where(low, oe, eo), rank, 1))
        done = jnp.swapaxes(jnp.stack(done), 0, 1)
        for t in range(half):
            packed_ref[:, (first + t) * LANES:(first + t + 1) * LANES] = done[t].astype(jnp.bfloat16)

    slots = cand_ref.shape[1]
    home_rows = home_ref.shape[0]
    wanted = jnp.where(iota((1, slots), 1) < count_ref[0], cand_ref[...], -1)
    known = jnp.maximum(wanted, 0)
    onehot = (iota((LANES, slots), 0) == known % LANES).astype(jnp.float32).astype(jnp.bfloat16)
    home = home_ref[...]
    table = jnp.concatenate([home // per_holder, home % per_holder], axis=0).astype(jnp.float32).astype(jnp.bfloat16)
    found = jnp.dot(table, onehot, preferred_element_type=jnp.float32)
    mine = iota((home_rows, slots), 0) == known // LANES
    holder = jnp.sum(jnp.where(mine, found[:home_rows], 0.0), axis=0, keepdims=True)
    within = jnp.sum(jnp.where(mine, found[home_rows:], 0.0), axis=0, keepdims=True)
    holder = jnp.where(wanted >= 0, holder, float(holders))
    at_holder = iota((holders, slots), 0).astype(jnp.float32) == holder
    earlier = exact_bf16(iota((slots, slots), 0) < iota((slots, slots), 1))
    before = jnp.dot(exact_bf16(at_holder), earlier, preferred_element_type=jnp.float32)
    rank_there = jnp.sum(jnp.where(at_holder, before, 0.0), axis=0, keepdims=True)
    ranked = exact_bf16(iota((capacity, slots), 0).astype(jnp.float32) == rank_there)
    asked = lax.dot_general(
        exact_bf16(jnp.where(at_holder, within + 1.0, 0.0)), ranked, (((1,), (1,)), ((), ())),
        preferred_element_type=jnp.float32,
    )
    blocks = [asked[h:h + rows] for h in range(0, holders, rows)]
    spare = packed_ref.shape[1] - width - capacity * len(blocks)
    if spare:
        blocks.append(jnp.zeros((rows, spare), jnp.float32))
    packed_ref[:, width:] = jnp.concatenate(blocks, axis=1).astype(jnp.bfloat16)
    found_ref[...] = jnp.concatenate([holder, rank_there, jnp.zeros((6, slots), jnp.float32)], axis=0)
    copies[-1].wait()


def score_kernel(holders, capacity, *refs):
    packed_refs, pages_ref, out_ref, total = refs[:holders], refs[holders], refs[holders + 1], refs[holders + 2]
    me = lax.axis_index("store")
    count, width = pages_ref.shape
    rows = packed_refs[0].shape[0]
    half = capacity // 2
    step = width // CHUNKS
    scores = jnp.zeros((holders * rows, count), jnp.float32)
    for i in range(CHUNKS):
        columns = slice(i * step, (i + 1) * step)
        queries = jnp.concatenate([ref[:, columns].astype(jnp.float32) for ref in packed_refs], axis=0)
        scores = scores + lax.dot_general(
            queries.astype(jnp.bfloat16), pages_ref[:, columns], (((1,), (1,)), ((), ())),
            preferred_element_type=jnp.float32,
        )
    for k in range(holders):
        start = pl.multiple_of((me ^ k) * rows, rows)
        total[pl.ds(start, rows), :] = scores[k * rows:(k + 1) * rows]
    asked = []
    for k in range(holders):
        notes = packed_refs[k][:, width:].astype(jnp.float32)
        notes = jnp.sum(jnp.where(iota(notes.shape, 0) == me % rows, notes, 0.0), axis=0, keepdims=True)
        mine = notes[:, :capacity]
        for block in range(1, holders // rows):
            mine = jnp.where(me // rows == block, notes[:, block * capacity:(block + 1) * capacity], mine)
        asked.append(mine)
    page = iota((count, holders * half), 0).astype(jnp.float32) + 1.0
    picked = jnp.zeros((holders * half, 2 * holders * rows), jnp.float32)
    parts = parts_of(total[...])[::-1]
    nothing = jnp.zeros_like(parts[0])
    for side in range(2):
        chosen = exact_bf16(page == jnp.concatenate([row[:, side * half:(side + 1) * half] for row in asked], axis=1))
        for part in parts:
            wide = jnp.concatenate([nothing, part] if side else [part, nothing], axis=0)
            picked = picked + lax.dot_general(
                chosen, wide, (((0,), (1,)), ((), ())), preferred_element_type=jnp.float32
            )
    for k in range(holders):
        out_ref[me ^ k] = picked[k * half:(k + 1) * half]


def spread_kernel(holders, found_ref, landed_ref, out_ref):
    half = landed_ref.shape[1]
    slots = found_ref.shape[1]
    total = landed_ref.shape[2] // 2
    groups = out_ref.shape[0]
    share = slots // groups
    holder, rank_there = found_ref[0:1], found_ref[1:2]
    place = iota((holders * half, slots), 0).astype(jnp.float32)
    parts = parts_of(jnp.concatenate([landed_ref[h] for h in range(holders)], axis=0))[::-1]
    result = jnp.zeros((total, slots), jnp.float32)
    for side in range(2):
        on_side = (rank_there >= half) if side else (rank_there < half)
        target = jnp.where(on_side, holder * half + rank_there - side * half, -1.0)
        chosen = exact_bf16(place == target)
        for part in parts:
            spread = lax.dot_general(part, chosen, (((0,), (0,)), ((), ())), preferred_element_type=jnp.float32)
            result = result + spread[side * total:(side + 1) * total]
    for g in range(groups):
        block = result[:, g * share:(g + 1) * share]
        out_ref[g] = jnp.concatenate([block[:total // 2], block[total // 2:]], axis=1)


def add_kernel(terms_ref, out_ref):
    total = terms_ref[0]
    for g in range(1, terms_ref.shape[0]):
        total = total + terms_ref[g]
    share = total.shape[1] // 2
    out_ref[0] = jnp.concatenate([total[:, :share], total[:, share:]], axis=0).T


def swap(value, axis, distance):
    return lax.ppermute(value, axis, [(i, i ^ distance) for i in range(lax.axis_size(axis))])


def on_device(query_grads, factor_out, factor_in, page_store, page_home, cand_lists, counts):
    holders = lax.axis_size("store")
    groups = lax.axis_size("layer")
    rows, width = query_grads.shape
    layers, rank, _ = factor_out.shape
    per_holder = page_store.shape[0]
    slots = cand_lists.shape[1]
    bf16 = jnp.bfloat16

    capacity = slots // holders
    home = page_home.reshape(-1, LANES)
    sources = [
        pltpu.with_memory_space_constraint(source, pltpu.HBM)
        for source in (query_grads, factor_in, factor_out, home, cand_lists, page_store)
    ]
    notes = max(LANES, holders // rows * capacity)
    packed, pages, found = pl.pallas_call(
        functools.partial(condition_kernel, holders, capacity),
        out_shape=[
            jax.ShapeDtypeStruct((rows, width + notes), bf16),
            pltpu.VMEM(page_store.shape, bf16),
            jax.ShapeDtypeStruct((8, slots), jnp.float32),
        ],
        in_specs=[SMEM] + [HBM] * len(sources),
        out_specs=[VMEM] * 3,
        scratch_shapes=[pltpu.VMEM(source.shape, source.dtype) for source in sources[:-1]]
        + [pltpu.SemaphoreType.DMA((len(sources),))],
        compiler_params=pltpu.CompilerParams(vmem_limit_bytes=10 * 2**20 + 24 * slots * slots),
    )(counts, *sources)

    blocks = [None] * holders
    blocks[0] = packed
    blocks[1] = swap(packed, "store", 1)
    for k in range(2, holders, 2):
        blocks[k] = swap(packed, "store", k)
    for k in range(2, holders, 2):
        blocks[k + 1] = swap(blocks[k], "store", 1)

    total = holders * rows
    bytes_in = 2 * holders * rows * (width + notes) + 2 * per_holder * width
    asked = pl.pallas_call(
        functools.partial(score_kernel, holders, capacity),
        out_shape=jax.ShapeDtypeStruct((holders, capacity // 2, 2 * total), jnp.float32),
        in_specs=[VMEM] * (holders + 1),
        out_specs=VMEM,
        scratch_shapes=[pltpu.VMEM((total, per_holder), jnp.float32)],
        compiler_params=pltpu.CompilerParams(vmem_limit_bytes=8 * 2**20 + bytes_in + 48 * total * slots),
    )(*blocks, pltpu.with_memory_space_constraint(pages, pltpu.VMEM))

    landed = lax.all_to_all(asked, "store", split_axis=0, concat_axis=0, tiled=True)
    share = slots // groups
    terms = pl.pallas_call(
        functools.partial(spread_kernel, holders),
        out_shape=jax.ShapeDtypeStruct((groups, total // 2, 2 * share), jnp.float32),
        in_specs=[VMEM] * 2,
        out_specs=VMEM,
        compiler_params=pltpu.CompilerParams(vmem_limit_bytes=4 * 2**20 + 64 * total * slots),
    )(found, landed)
    terms = lax.all_to_all(terms, "layer", split_axis=0, concat_axis=0, tiled=True)
    return pl.pallas_call(
        add_kernel,
        out_shape=jax.ShapeDtypeStruct((1, share, total), jnp.float32),
        in_specs=[VMEM],
        out_specs=VMEM,
        compiler_params=pltpu.CompilerParams(vmem_limit_bytes=4 * 2**20),
    )(terms)


def solution(mesh):
    placed = (
        P("store", "layer"),
        P("layer", None, None),
        P("layer", None, None),
        P("store", "layer"),
        P(),
        P("store", None),
        P("store"),
    )
    return jax.shard_map(
        on_device, mesh=mesh, in_specs=placed, out_specs=P("store", "layer", None), check_vma=False
    )
```

```python
import functools

import jax
import jax.numpy as jnp
from jax import lax
from jax.experimental import pallas as pl
from jax.experimental.pallas import tpu as pltpu
from jax.sharding import PartitionSpec as P

HIGHEST = lax.Precision.HIGHEST
VMEM = pl.BlockSpec(memory_space=pltpu.VMEM)
SMEM = pl.BlockSpec(memory_space=pltpu.SMEM)
HBM = pl.BlockSpec(memory_space=pltpu.HBM)
LANES = 128
CHUNKS = 4


def iota(shape, dimension):
    return lax.broadcasted_iota(jnp.int32, shape, dimension)


def gather_plan(holders):
    if holders == 8:
        across = [((2, 4), None), ((4, 2), None), ((4, 2), 0)]
    else:
        across = [((k, k), None) for k in range(2, holders, 2)]
    plan, owners = [], []
    for pairs, source in across:
        before = owners[source] if source is not None else (0, 0)
        owners.append((before[0] ^ pairs[0], before[1] ^ pairs[1]))
        plan.append((source, pairs, owners[-1]))
    plan.append((None, (1, 1), (1, 1)))
    for place in range(len(across)):
        plan.append((place, (1, 1), (owners[place][1] ^ 1, owners[place][0] ^ 1)))
    return plan


def layer_steps(groups):
    return [1 << b for b in range(groups.bit_length() - 1)]


def halving_order(steps):
    order = [0]
    for step in reversed(steps):
        order = order + [k ^ step for k in order]
    return order


def parts_of(value):
    parts = []
    for _ in range(3):
        part = value.astype(jnp.bfloat16)
        value = value - part.astype(jnp.float32)
        parts.append(part)
    return parts


def exact_bf16(value):
    return value.astype(jnp.float32).astype(jnp.bfloat16)


def condition_kernel(holders, groups, capacity, count_ref, *refs):
    sources, packed_ref, pages_ref, found_ref, landing, arrived = refs[:6], refs[6], refs[7], refs[8], refs[9:14], refs[14]
    copies = [
        pltpu.make_async_copy(source, target, arrived.at[i])
        for i, (source, target) in enumerate(zip(sources, landing + (pages_ref,)))
    ]
    for copy in copies:
        copy.start()
    for copy in copies[:-1]:
        copy.wait()
    query_ref, in_factor_ref, out_factor_ref, home_ref, cand_ref = landing
    per_holder = pages_ref.shape[0]
    at = lax.axis_index("layer")
    rows, width = query_ref.shape
    layers, rank, _ = in_factor_ref.shape
    half = rank // 2
    query = query_ref[...].astype(jnp.float32)
    low = iota((half, LANES), 1) < rank
    zero = jnp.zeros((rank, rank), jnp.float32)
    source = iota((rank, rank), 0)
    place = iota((rank, rank), 1)
    split = (source == 2 * (place % half) + place // half).astype(jnp.float32)
    for layer in range(layers):
        first = layer * half
        packed = jnp.concatenate(
            [query[:, (first + t) * LANES:(first + t + 1) * LANES] for t in range(half)], axis=0
        ).astype(jnp.bfloat16)
        factor = in_factor_ref[layer]
        doubled = jnp.concatenate(
            [jnp.concatenate([factor, zero], axis=1), jnp.concatenate([zero, factor], axis=1)], axis=0
        )
        right = sum(jnp.dot(packed, part, preferred_element_type=jnp.float32) for part in parts_of(doubled)[::-1])
        right = jnp.swapaxes(right.reshape(half, rows, LANES), 0, 1)
        wide = jnp.concatenate([right[q] for q in range(rows)], axis=1)
        sorted_columns = jnp.dot(out_factor_ref[layer], split, precision=HIGHEST, preferred_element_type=jnp.float32)
        sorted_both = lax.dot_general(
            split, sorted_columns, (((0,), (0,)), ((), ())), precision=HIGHEST, preferred_element_type=jnp.float32
        )
        quarters = jnp.concatenate(
            [sorted_both[r * half:(r + 1) * half, c * half:(c + 1) * half] for r in range(2) for c in range(2)], axis=0
        )
        left = jnp.dot(quarters, wide, precision=HIGHEST, preferred_element_type=jnp.float32)
        done = []
        for q in range(rows):
            part = left[:, q * LANES:(q + 1) * LANES]
            ee, eo, oe, oo = (part[i * half:(i + 1) * half] for i in range(4))
            done.append(jnp.where(low, ee, oo) + pltpu.roll(jnp.where(low, oe, eo), rank, 1))
        done = jnp.swapaxes(jnp.stack(done), 0, 1)
        for t in range(half):
            packed_ref[:, (first + t) * LANES:(first + t + 1) * LANES] = done[t].astype(jnp.bfloat16)

    slots = cand_ref.shape[1]
    share = slots // groups
    home_rows = home_ref.shape[0]
    wanted = jnp.where(iota((1, slots), 1) < count_ref[0], cand_ref[...], -1)
    ranges = [wanted[:, g * share:(g + 1) * share] for g in range(groups)]
    ordered = []
    for j in halving_order(layer_steps(groups)):
        chosen = ranges[0]
        for g in range(1, groups):
            chosen = jnp.where((at ^ j) == g, ranges[g], chosen)
        ordered.append(chosen)
    wanted = jnp.concatenate(ordered, axis=1)
    known = jnp.maximum(wanted, 0)
    onehot = (iota((LANES, slots), 0) == known % LANES).astype(jnp.float32).astype(jnp.bfloat16)
    home = home_ref[...]
    table = jnp.concatenate([home // per_holder, home % per_holder], axis=0).astype(jnp.float32).astype(jnp.bfloat16)
    found = jnp.dot(table, onehot, preferred_element_type=jnp.float32)
    mine = iota((home_rows, slots), 0) == known // LANES
    holder = jnp.sum(jnp.where(mine, found[:home_rows], 0.0), axis=0, keepdims=True)
    within = jnp.sum(jnp.where(mine, found[home_rows:], 0.0), axis=0, keepdims=True)
    holder = jnp.where(wanted >= 0, holder, float(holders))
    at_holder = iota((holders, slots), 0).astype(jnp.float32) == holder
    earlier = exact_bf16(iota((slots, slots), 0) < iota((slots, slots), 1))
    before = jnp.dot(exact_bf16(at_holder), earlier, preferred_element_type=jnp.float32)
    rank_there = jnp.sum(jnp.where(at_holder, before, 0.0), axis=0, keepdims=True)
    ranked = exact_bf16(iota((capacity, slots), 0).astype(jnp.float32) == rank_there)
    asked = lax.dot_general(
        exact_bf16(jnp.where(at_holder, within + 1.0, 0.0)), ranked, (((1,), (1,)), ((), ())),
        preferred_element_type=jnp.float32,
    )
    blocks = [asked[h:h + rows] for h in range(0, holders, rows)]
    spare = packed_ref.shape[1] - width - capacity * len(blocks)
    if spare:
        blocks.append(jnp.zeros((rows, spare), jnp.float32))
    packed_ref[:, width:] = jnp.concatenate(blocks, axis=1).astype(jnp.bfloat16)
    found_ref[...] = jnp.concatenate([holder, rank_there, jnp.zeros((6, slots), jnp.float32)], axis=0)
    copies[-1].wait()


def score_kernel(holders, capacity, *refs):
    packed_refs, pages_ref, out_ref, total = refs[:holders], refs[holders], refs[holders + 1], refs[holders + 2]
    me = lax.axis_index("store")
    owners = [me] + [me ^ jnp.where(me % 2 == 1, second, first) for _, _, (first, second) in gather_plan(holders)]
    count, width = pages_ref.shape
    rows = packed_refs[0].shape[0]
    half = capacity // 2
    step = width // CHUNKS
    scores = jnp.zeros((holders * rows, count), jnp.float32)
    for i in range(CHUNKS):
        columns = slice(i * step, (i + 1) * step)
        queries = jnp.concatenate([ref[:, columns].astype(jnp.float32) for ref in packed_refs], axis=0)
        scores = scores + lax.dot_general(
            queries.astype(jnp.bfloat16), pages_ref[:, columns], (((1,), (1,)), ((), ())),
            preferred_element_type=jnp.float32,
        )
    for k in range(holders):
        start = pl.multiple_of(owners[k] * rows, rows)
        total[pl.ds(start, rows), :] = scores[k * rows:(k + 1) * rows]
    asked = []
    for k in range(holders):
        notes = packed_refs[k][:, width:].astype(jnp.float32)
        notes = jnp.sum(jnp.where(iota(notes.shape, 0) == me % rows, notes, 0.0), axis=0, keepdims=True)
        mine = notes[:, :capacity]
        for block in range(1, holders // rows):
            mine = jnp.where(me // rows == block, notes[:, block * capacity:(block + 1) * capacity], mine)
        asked.append(mine)
    page = iota((count, holders * half), 0).astype(jnp.float32) + 1.0
    picked = jnp.zeros((holders * half, 2 * holders * rows), jnp.float32)
    parts = parts_of(total[...])[::-1]
    nothing = jnp.zeros_like(parts[0])
    for side in range(2):
        chosen = exact_bf16(page == jnp.concatenate([row[:, side * half:(side + 1) * half] for row in asked], axis=1))
        for part in parts:
            wide = jnp.concatenate([nothing, part] if side else [part, nothing], axis=0)
            picked = picked + lax.dot_general(
                chosen, wide, (((0,), (1,)), ((), ())), preferred_element_type=jnp.float32
            )
    for k in range(holders):
        out_ref[owners[k]] = picked[k * half:(k + 1) * half]


def spread_kernel(holders, found_ref, landed_ref, keep_ref, send_ref):
    half = landed_ref.shape[1]
    slots = found_ref.shape[1]
    total = landed_ref.shape[2] // 2
    cut = slots // 2
    holder, rank_there = found_ref[0:1], found_ref[1:2]
    place = iota((holders * half, slots), 0).astype(jnp.float32)
    parts = parts_of(jnp.concatenate([landed_ref[h] for h in range(holders)], axis=0))[::-1]
    result = jnp.zeros((total, slots), jnp.float32)
    for side in range(2):
        on_side = (rank_there >= half) if side else (rank_there < half)
        target = jnp.where(on_side, holder * half + rank_there - side * half, -1.0)
        chosen = exact_bf16(place == target)
        for part in parts:
            spread = lax.dot_general(part, chosen, (((0,), (0,)), ((), ())), preferred_element_type=jnp.float32)
            result = result + spread[side * total:(side + 1) * total]
    keep_ref[...] = result[:, :cut]
    send_ref[...] = result[:, cut:]


def add_kernel(one_ref, other_ref, out_ref):
    out_ref[0] = (one_ref[...] + other_ref[...]).T


def swap(value, axis, distance):
    return lax.ppermute(value, axis, [(i, i ^ distance) for i in range(lax.axis_size(axis))])


def on_device(query_grads, factor_out, factor_in, page_store, page_home, cand_lists, counts):
    holders = lax.axis_size("store")
    groups = lax.axis_size("layer")
    rows, width = query_grads.shape
    layers, rank, _ = factor_out.shape
    per_holder = page_store.shape[0]
    slots = cand_lists.shape[1]
    bf16 = jnp.bfloat16

    capacity = slots // holders
    home = page_home.reshape(-1, LANES)
    sources = [
        pltpu.with_memory_space_constraint(source, pltpu.HBM)
        for source in (query_grads, factor_in, factor_out, home, cand_lists, page_store)
    ]
    notes = max(LANES, holders // rows * capacity)
    packed, pages, found = pl.pallas_call(
        functools.partial(condition_kernel, holders, groups, capacity),
        out_shape=[
            jax.ShapeDtypeStruct((rows, width + notes), bf16),
            pltpu.VMEM(page_store.shape, bf16),
            jax.ShapeDtypeStruct((8, slots), jnp.float32),
        ],
        in_specs=[SMEM] + [HBM] * len(sources),
        out_specs=[VMEM] * 3,
        scratch_shapes=[pltpu.VMEM(source.shape, source.dtype) for source in sources[:-1]]
        + [pltpu.SemaphoreType.DMA((len(sources),))],
        compiler_params=pltpu.CompilerParams(vmem_limit_bytes=10 * 2**20 + 24 * slots * slots),
    )(counts, *sources)

    blocks = []
    for source, pairs, _ in gather_plan(holders):
        moving = packed if source is None else blocks[source]
        blocks.append(lax.ppermute(moving, "store", [(i, i ^ pairs[i % 2]) for i in range(holders)]))
    blocks = [packed] + blocks

    total = holders * rows
    bytes_in = 2 * holders * rows * (width + notes) + 2 * per_holder * width
    asked = pl.pallas_call(
        functools.partial(score_kernel, holders, capacity),
        out_shape=jax.ShapeDtypeStruct((holders, capacity // 2, 2 * total), jnp.float32),
        in_specs=[VMEM] * (holders + 1),
        out_specs=VMEM,
        scratch_shapes=[pltpu.VMEM((total, per_holder), jnp.float32)],
        compiler_params=pltpu.CompilerParams(vmem_limit_bytes=8 * 2**20 + bytes_in + 48 * total * slots),
    )(*blocks, pltpu.with_memory_space_constraint(pages, pltpu.VMEM))

    landed = lax.all_to_all(asked, "store", split_axis=0, concat_axis=0, tiled=True)
    keep, send = pl.pallas_call(
        functools.partial(spread_kernel, holders),
        out_shape=[jax.ShapeDtypeStruct((total, slots // 2), jnp.float32)] * 2,
        in_specs=[VMEM] * 2,
        out_specs=[VMEM] * 2,
        compiler_params=pltpu.CompilerParams(vmem_limit_bytes=4 * 2**20 + 64 * total * slots),
    )(found, landed)

    for step in layer_steps(groups):
        landed = swap(send, "layer", step)
        if step < groups // 2:
            scores = keep + landed
            cut = scores.shape[1] // 2
            keep, send = scores[:, :cut], scores[:, cut:]
    return pl.pallas_call(
        add_kernel,
        out_shape=jax.ShapeDtypeStruct((1, slots // groups, total), jnp.float32),
        in_specs=[VMEM] * 2,
        out_specs=VMEM,
        compiler_params=pltpu.CompilerParams(vmem_limit_bytes=2 * 2**20),
    )(keep, landed)


def solution(mesh):
    placed = (
        P("store", "layer"),
        P("layer", None, None),
        P("layer", None, None),
        P("store", "layer"),
        P(),
        P("store", None),
        P("store"),
    )
    return jax.shard_map(
        on_device, mesh=mesh, in_specs=placed, out_specs=P("store", "layer", None), check_vma=False
    )
```

```python
import functools

import jax
import jax.numpy as jnp
from jax import lax
from jax.experimental import pallas as pl
from jax.experimental.pallas import tpu as pltpu
from jax.sharding import PartitionSpec as P

HIGHEST = lax.Precision.HIGHEST
VMEM = pl.BlockSpec(memory_space=pltpu.VMEM)
SMEM = pl.BlockSpec(memory_space=pltpu.SMEM)
HBM = pl.BlockSpec(memory_space=pltpu.HBM)
LANES = 128
CHUNKS = 4


def iota(shape, dimension):
    return lax.broadcasted_iota(jnp.int32, shape, dimension)


def parts_of(value):
    parts = []
    for _ in range(3):
        part = value.astype(jnp.bfloat16)
        value = value - part.astype(jnp.float32)
        parts.append(part)
    return parts


def exact_bf16(value):
    return value.astype(jnp.float32).astype(jnp.bfloat16)


def condition_kernel(holders, groups, capacity, count_ref, *refs):
    sources, packed_ref, pages_ref, found_ref, landing, arrived = refs[:6], refs[6], refs[7], refs[8], refs[9:14], refs[14]
    copies = [
        pltpu.make_async_copy(source, target, arrived.at[i])
        for i, (source, target) in enumerate(zip(sources, landing + (pages_ref,)))
    ]
    for copy in copies:
        copy.start()
    for copy in copies[:-1]:
        copy.wait()
    query_ref, in_factor_ref, out_factor_ref, home_ref, cand_ref = landing
    per_holder = pages_ref.shape[0]
    rows, width = query_ref.shape
    layers, rank, _ = in_factor_ref.shape
    half = rank // 2
    query = query_ref[...].astype(jnp.float32)
    low = iota((half, LANES), 1) < rank
    zero = jnp.zeros((rank, rank), jnp.float32)
    source = iota((rank, rank), 0)
    place = iota((rank, rank), 1)
    split = (source == 2 * (place % half) + place // half).astype(jnp.float32)
    for layer in range(layers):
        first = layer * half
        packed = jnp.concatenate(
            [query[:, (first + t) * LANES:(first + t + 1) * LANES] for t in range(half)], axis=0
        ).astype(jnp.bfloat16)
        factor = in_factor_ref[layer]
        doubled = jnp.concatenate(
            [jnp.concatenate([factor, zero], axis=1), jnp.concatenate([zero, factor], axis=1)], axis=0
        )
        right = sum(jnp.dot(packed, part, preferred_element_type=jnp.float32) for part in parts_of(doubled)[::-1])
        right = jnp.swapaxes(right.reshape(half, rows, LANES), 0, 1)
        wide = jnp.concatenate([right[q] for q in range(rows)], axis=1)
        sorted_columns = jnp.dot(out_factor_ref[layer], split, precision=HIGHEST, preferred_element_type=jnp.float32)
        sorted_both = lax.dot_general(
            split, sorted_columns, (((0,), (0,)), ((), ())), precision=HIGHEST, preferred_element_type=jnp.float32
        )
        quarters = jnp.concatenate(
            [sorted_both[r * half:(r + 1) * half, c * half:(c + 1) * half] for r in range(2) for c in range(2)], axis=0
        )
        left = jnp.dot(quarters, wide, precision=HIGHEST, preferred_element_type=jnp.float32)
        done = []
        for q in range(rows):
            part = left[:, q * LANES:(q + 1) * LANES]
            ee, eo, oe, oo = (part[i * half:(i + 1) * half] for i in range(4))
            done.append(jnp.where(low, ee, oo) + pltpu.roll(jnp.where(low, oe, eo), rank, 1))
        done = jnp.swapaxes(jnp.stack(done), 0, 1)
        for t in range(half):
            packed_ref[:, (first + t) * LANES:(first + t + 1) * LANES] = done[t].astype(jnp.bfloat16)

    slots = cand_ref.shape[1]
    home_rows = home_ref.shape[0]
    share = slots // groups
    at = lax.axis_index("layer")
    wanted = jnp.where(iota((1, slots), 1) < count_ref[0], cand_ref[...], -1)
    ranges = [wanted[:, g * share:(g + 1) * share] for g in range(groups)]
    ordered = []
    for j in range(groups):
        chosen = ranges[0]
        for g in range(1, groups):
            chosen = jnp.where((at ^ j) == g, ranges[g], chosen)
        ordered.append(chosen)
    wanted = jnp.concatenate(ordered, axis=1)
    known = jnp.maximum(wanted, 0)
    onehot = (iota((LANES, slots), 0) == known % LANES).astype(jnp.float32).astype(jnp.bfloat16)
    home = home_ref[...]
    table = jnp.concatenate([home // per_holder, home % per_holder], axis=0).astype(jnp.float32).astype(jnp.bfloat16)
    found = jnp.dot(table, onehot, preferred_element_type=jnp.float32)
    mine = iota((home_rows, slots), 0) == known // LANES
    holder = jnp.sum(jnp.where(mine, found[:home_rows], 0.0), axis=0, keepdims=True)
    within = jnp.sum(jnp.where(mine, found[home_rows:], 0.0), axis=0, keepdims=True)
    holder = jnp.where(wanted >= 0, holder, float(holders))
    at_holder = iota((holders, slots), 0).astype(jnp.float32) == holder
    earlier = exact_bf16(iota((slots, slots), 0) < iota((slots, slots), 1))
    before = jnp.dot(exact_bf16(at_holder), earlier, preferred_element_type=jnp.float32)
    rank_there = jnp.sum(jnp.where(at_holder, before, 0.0), axis=0, keepdims=True)
    ranked = exact_bf16(iota((capacity, slots), 0).astype(jnp.float32) == rank_there)
    asked = lax.dot_general(
        exact_bf16(jnp.where(at_holder, within + 1.0, 0.0)), ranked, (((1,), (1,)), ((), ())),
        preferred_element_type=jnp.float32,
    )
    blocks = [asked[h:h + rows] for h in range(0, holders, rows)]
    spare = packed_ref.shape[1] - width - capacity * len(blocks)
    if spare:
        blocks.append(jnp.zeros((rows, spare), jnp.float32))
    packed_ref[:, width:] = jnp.concatenate(blocks, axis=1).astype(jnp.bfloat16)
    found_ref[...] = jnp.concatenate([holder, rank_there, jnp.zeros((6, slots), jnp.float32)], axis=0)
    copies[-1].wait()


def score_kernel(holders, capacity, *refs):
    packed_refs, pages_ref, out_ref, total = refs[:holders], refs[holders], refs[holders + 1], refs[holders + 2]
    me = lax.axis_index("store")
    count, width = pages_ref.shape
    rows = packed_refs[0].shape[0]
    half = capacity // 2
    step = width // CHUNKS
    scores = jnp.zeros((holders * rows, count), jnp.float32)
    for i in range(CHUNKS):
        columns = slice(i * step, (i + 1) * step)
        queries = jnp.concatenate([ref[:, columns].astype(jnp.float32) for ref in packed_refs], axis=0)
        scores = scores + lax.dot_general(
            queries.astype(jnp.bfloat16), pages_ref[:, columns], (((1,), (1,)), ((), ())),
            preferred_element_type=jnp.float32,
        )
    for k in range(holders):
        start = pl.multiple_of((me ^ k) * rows, rows)
        total[pl.ds(start, rows), :] = scores[k * rows:(k + 1) * rows]
    asked = []
    for k in range(holders):
        notes = packed_refs[k][:, width:].astype(jnp.float32)
        notes = jnp.sum(jnp.where(iota(notes.shape, 0) == me % rows, notes, 0.0), axis=0, keepdims=True)
        mine = notes[:, :capacity]
        for block in range(1, holders // rows):
            mine = jnp.where(me // rows == block, notes[:, block * capacity:(block + 1) * capacity], mine)
        asked.append(mine)
    page = iota((count, holders * half), 0).astype(jnp.float32) + 1.0
    picked = jnp.zeros((holders * half, 2 * holders * rows), jnp.float32)
    parts = parts_of(total[...])[::-1]
    nothing = jnp.zeros_like(parts[0])
    for side in range(2):
        chosen = exact_bf16(page == jnp.concatenate([row[:, side * half:(side + 1) * half] for row in asked], axis=1))
        for part in parts:
            wide = jnp.concatenate([nothing, part] if side else [part, nothing], axis=0)
            picked = picked + lax.dot_general(
                chosen, wide, (((0,), (1,)), ((), ())), preferred_element_type=jnp.float32
            )
    for k in range(holders):
        out_ref[me ^ k] = picked[k * half:(k + 1) * half]


def spread_kernel(holders, found_ref, landed_ref, *out_refs):
    half = landed_ref.shape[1]
    slots = found_ref.shape[1]
    total = landed_ref.shape[2] // 2
    groups = len(out_refs)
    share = slots // groups
    holder, rank_there = found_ref[0:1], found_ref[1:2]
    place = iota((holders * half, slots), 0).astype(jnp.float32)
    parts = parts_of(jnp.concatenate([landed_ref[h] for h in range(holders)], axis=0))[::-1]
    result = jnp.zeros((total, slots), jnp.float32)
    for side in range(2):
        on_side = (rank_there >= half) if side else (rank_there < half)
        target = jnp.where(on_side, holder * half + rank_there - side * half, -1.0)
        chosen = exact_bf16(place == target)
        for part in parts:
            spread = lax.dot_general(part, chosen, (((0,), (0,)), ((), ())), preferred_element_type=jnp.float32)
            result = result + spread[side * total:(side + 1) * total]
    for g in range(groups):
        block = result[:, g * share:(g + 1) * share]
        out_refs[g][...] = jnp.concatenate([block[:total // 2], block[total // 2:]], axis=1)


def add_kernel(*refs):
    out_ref = refs[-1]
    total = refs[0][...]
    for ref in refs[1:-1]:
        total = total + ref[...]
    share = total.shape[1] // 2
    out_ref[0] = jnp.concatenate([total[:, :share], total[:, share:]], axis=0).T


def swap(value, axis, distance):
    return lax.ppermute(value, axis, [(i, i ^ distance) for i in range(lax.axis_size(axis))])


def on_device(query_grads, factor_out, factor_in, page_store, page_home, cand_lists, counts):
    holders = lax.axis_size("store")
    groups = lax.axis_size("layer")
    rows, width = query_grads.shape
    layers, rank, _ = factor_out.shape
    per_holder = page_store.shape[0]
    slots = cand_lists.shape[1]
    bf16 = jnp.bfloat16

    capacity = slots // holders
    home = page_home.reshape(-1, LANES)
    sources = [
        pltpu.with_memory_space_constraint(source, pltpu.HBM)
        for source in (query_grads, factor_in, factor_out, home, cand_lists, page_store)
    ]
    notes = max(LANES, holders // rows * capacity)
    packed, pages, found = pl.pallas_call(
        functools.partial(condition_kernel, holders, groups, capacity),
        out_shape=[
            jax.ShapeDtypeStruct((rows, width + notes), bf16),
            pltpu.VMEM(page_store.shape, bf16),
            jax.ShapeDtypeStruct((8, slots), jnp.float32),
        ],
        in_specs=[SMEM] + [HBM] * len(sources),
        out_specs=[VMEM] * 3,
        scratch_shapes=[pltpu.VMEM(source.shape, source.dtype) for source in sources[:-1]]
        + [pltpu.SemaphoreType.DMA((len(sources),))],
        compiler_params=pltpu.CompilerParams(vmem_limit_bytes=10 * 2**20 + 24 * slots * slots),
    )(counts, *sources)

    blocks = [None] * holders
    blocks[0] = packed
    blocks[1] = swap(packed, "store", 1)
    for k in range(2, holders, 2):
        blocks[k] = swap(packed, "store", k)
    for k in range(2, holders, 2):
        blocks[k + 1] = swap(blocks[k], "store", 1)

    total = holders * rows
    bytes_in = 2 * holders * rows * (width + notes) + 2 * per_holder * width
    asked = pl.pallas_call(
        functools.partial(score_kernel, holders, capacity),
        out_shape=jax.ShapeDtypeStruct((holders, capacity // 2, 2 * total), jnp.float32),
        in_specs=[VMEM] * (holders + 1),
        out_specs=VMEM,
        scratch_shapes=[pltpu.VMEM((total, per_holder), jnp.float32)],
        compiler_params=pltpu.CompilerParams(vmem_limit_bytes=8 * 2**20 + bytes_in + 48 * total * slots),
    )(*blocks, pltpu.with_memory_space_constraint(pages, pltpu.VMEM))

    landed = lax.all_to_all(asked, "store", split_axis=0, concat_axis=0, tiled=True)
    share = slots // groups
    terms = pl.pallas_call(
        functools.partial(spread_kernel, holders),
        out_shape=[jax.ShapeDtypeStruct((total // 2, 2 * share), jnp.float32)] * groups,
        in_specs=[VMEM] * 2,
        out_specs=[VMEM] * groups,
        compiler_params=pltpu.CompilerParams(vmem_limit_bytes=4 * 2**20 + 64 * total * slots),
    )(found, landed)
    terms = [terms[0]] + [swap(terms[j], "layer", j) for j in reversed(range(1, groups))]
    return pl.pallas_call(
        add_kernel,
        out_shape=jax.ShapeDtypeStruct((1, share, total), jnp.float32),
        in_specs=[VMEM] * groups,
        out_specs=VMEM,
        compiler_params=pltpu.CompilerParams(vmem_limit_bytes=4 * 2**20),
    )(*terms)


def solution(mesh):
    placed = (
        P("store", "layer"),
        P("layer", None, None),
        P("layer", None, None),
        P("store", "layer"),
        P(),
        P("store", None),
        P("store"),
    )
    return jax.shard_map(
        on_device, mesh=mesh, in_specs=placed, out_specs=P("store", "layer", None), check_vma=False
    )
```

```python
import functools

import jax
import jax.numpy as jnp
from jax import lax
from jax.experimental import pallas as pl
from jax.experimental.pallas import tpu as pltpu
from jax.sharding import PartitionSpec as P

HIGHEST = lax.Precision.HIGHEST
VMEM = pl.BlockSpec(memory_space=pltpu.VMEM)
SMEM = pl.BlockSpec(memory_space=pltpu.SMEM)
HBM = pl.BlockSpec(memory_space=pltpu.HBM)
LANES = 128
CHUNKS = 4


def iota(shape, dimension):
    return lax.broadcasted_iota(jnp.int32, shape, dimension)


def parts_of(value):
    parts = []
    for _ in range(3):
        part = value.astype(jnp.bfloat16)
        value = value - part.astype(jnp.float32)
        parts.append(part)
    return parts


def exact_bf16(value):
    return value.astype(jnp.float32).astype(jnp.bfloat16)


def condition_kernel(holders, groups, capacity, count_ref, *refs):
    sources, packed_ref, pages_ref, found_ref, landing, arrived = refs[:6], refs[6], refs[7], refs[8], refs[9:14], refs[14]
    copies = [
        pltpu.make_async_copy(source, target, arrived.at[i])
        for i, (source, target) in enumerate(zip(sources, landing + (pages_ref,)))
    ]
    for copy in copies:
        copy.start()
    for copy in copies[:-1]:
        copy.wait()
    query_ref, in_factor_ref, out_factor_ref, home_ref, cand_ref = landing
    per_holder = pages_ref.shape[0]
    rows, width = query_ref.shape
    layers, rank, _ = in_factor_ref.shape
    half = rank // 2
    query = query_ref[...].astype(jnp.float32)
    low = iota((half, LANES), 1) < rank
    zero = jnp.zeros((rank, rank), jnp.float32)
    source = iota((rank, rank), 0)
    place = iota((rank, rank), 1)
    split = (source == 2 * (place % half) + place // half).astype(jnp.float32)
    for layer in range(layers):
        first = layer * half
        packed = jnp.concatenate(
            [query[:, (first + t) * LANES:(first + t + 1) * LANES] for t in range(half)], axis=0
        ).astype(jnp.bfloat16)
        factor = in_factor_ref[layer]
        doubled = jnp.concatenate(
            [jnp.concatenate([factor, zero], axis=1), jnp.concatenate([zero, factor], axis=1)], axis=0
        )
        right = sum(jnp.dot(packed, part, preferred_element_type=jnp.float32) for part in parts_of(doubled)[::-1])
        right = jnp.swapaxes(right.reshape(half, rows, LANES), 0, 1)
        wide = jnp.concatenate([right[q] for q in range(rows)], axis=1)
        sorted_columns = jnp.dot(out_factor_ref[layer], split, precision=HIGHEST, preferred_element_type=jnp.float32)
        sorted_both = lax.dot_general(
            split, sorted_columns, (((0,), (0,)), ((), ())), precision=HIGHEST, preferred_element_type=jnp.float32
        )
        quarters = jnp.concatenate(
            [sorted_both[r * half:(r + 1) * half, c * half:(c + 1) * half] for r in range(2) for c in range(2)], axis=0
        )
        left = jnp.dot(quarters, wide, precision=HIGHEST, preferred_element_type=jnp.float32)
        done = []
        for q in range(rows):
            part = left[:, q * LANES:(q + 1) * LANES]
            ee, eo, oe, oo = (part[i * half:(i + 1) * half] for i in range(4))
            done.append(jnp.where(low, ee, oo) + pltpu.roll(jnp.where(low, oe, eo), rank, 1))
        done = jnp.swapaxes(jnp.stack(done), 0, 1)
        for t in range(half):
            packed_ref[:, (first + t) * LANES:(first + t + 1) * LANES] = done[t].astype(jnp.bfloat16)

    slots = cand_ref.shape[1]
    home_rows = home_ref.shape[0]
    share = slots // groups
    at = lax.axis_index("layer")
    wanted = jnp.where(iota((1, slots), 1) < count_ref[0], cand_ref[...], -1)
    ranges = [wanted[:, g * share:(g + 1) * share] for g in range(groups)]
    ordered = []
    for j in range(groups):
        chosen = ranges[0]
        for g in range(1, groups):
            chosen = jnp.where((at + j) % groups == g, ranges[g], chosen)
        ordered.append(chosen)
    wanted = jnp.concatenate(ordered, axis=1)
    known = jnp.maximum(wanted, 0)
    onehot = (iota((LANES, slots), 0) == known % LANES).astype(jnp.float32).astype(jnp.bfloat16)
    home = home_ref[...]
    table = jnp.concatenate([home // per_holder, home % per_holder], axis=0).astype(jnp.float32).astype(jnp.bfloat16)
    found = jnp.dot(table, onehot, preferred_element_type=jnp.float32)
    mine = iota((home_rows, slots), 0) == known // LANES
    holder = jnp.sum(jnp.where(mine, found[:home_rows], 0.0), axis=0, keepdims=True)
    within = jnp.sum(jnp.where(mine, found[home_rows:], 0.0), axis=0, keepdims=True)
    holder = jnp.where(wanted >= 0, holder, float(holders))
    at_holder = iota((holders, slots), 0).astype(jnp.float32) == holder
    earlier = exact_bf16(iota((slots, slots), 0) < iota((slots, slots), 1))
    before = jnp.dot(exact_bf16(at_holder), earlier, preferred_element_type=jnp.float32)
    rank_there = jnp.sum(jnp.where(at_holder, before, 0.0), axis=0, keepdims=True)
    ranked = exact_bf16(iota((capacity, slots), 0).astype(jnp.float32) == rank_there)
    asked = lax.dot_general(
        exact_bf16(jnp.where(at_holder, within + 1.0, 0.0)), ranked, (((1,), (1,)), ((), ())),
        preferred_element_type=jnp.float32,
    )
    blocks = [asked[h:h + rows] for h in range(0, holders, rows)]
    spare = packed_ref.shape[1] - width - capacity * len(blocks)
    if spare:
        blocks.append(jnp.zeros((rows, spare), jnp.float32))
    packed_ref[:, width:] = jnp.concatenate(blocks, axis=1).astype(jnp.bfloat16)
    found_ref[...] = jnp.concatenate([holder, rank_there, jnp.zeros((6, slots), jnp.float32)], axis=0)
    copies[-1].wait()


def score_kernel(holders, capacity, *refs):
    packed_refs, pages_ref, out_ref, total = refs[:holders], refs[holders], refs[holders + 1], refs[holders + 2]
    me = lax.axis_index("store")
    count, width = pages_ref.shape
    rows = packed_refs[0].shape[0]
    half = capacity // 2
    step = width // CHUNKS
    scores = jnp.zeros((holders * rows, count), jnp.float32)
    for i in range(CHUNKS):
        columns = slice(i * step, (i + 1) * step)
        queries = jnp.concatenate([ref[:, columns].astype(jnp.float32) for ref in packed_refs], axis=0)
        scores = scores + lax.dot_general(
            queries.astype(jnp.bfloat16), pages_ref[:, columns], (((1,), (1,)), ((), ())),
            preferred_element_type=jnp.float32,
        )
    for k in range(holders):
        start = pl.multiple_of((me ^ k) * rows, rows)
        total[pl.ds(start, rows), :] = scores[k * rows:(k + 1) * rows]
    asked = []
    for k in range(holders):
        notes = packed_refs[k][:, width:].astype(jnp.float32)
        notes = jnp.sum(jnp.where(iota(notes.shape, 0) == me % rows, notes, 0.0), axis=0, keepdims=True)
        mine = notes[:, :capacity]
        for block in range(1, holders // rows):
            mine = jnp.where(me // rows == block, notes[:, block * capacity:(block + 1) * capacity], mine)
        asked.append(mine)
    page = iota((count, holders * half), 0).astype(jnp.float32) + 1.0
    picked = jnp.zeros((holders * half, 2 * holders * rows), jnp.float32)
    parts = parts_of(total[...])[::-1]
    nothing = jnp.zeros_like(parts[0])
    for side in range(2):
        chosen = exact_bf16(page == jnp.concatenate([row[:, side * half:(side + 1) * half] for row in asked], axis=1))
        for part in parts:
            wide = jnp.concatenate([nothing, part] if side else [part, nothing], axis=0)
            picked = picked + lax.dot_general(
                chosen, wide, (((0,), (1,)), ((), ())), preferred_element_type=jnp.float32
            )
    for k in range(holders):
        out_ref[me ^ k] = picked[k * half:(k + 1) * half]


def spread_kernel(holders, found_ref, landed_ref, *out_refs):
    half = landed_ref.shape[1]
    slots = found_ref.shape[1]
    total = landed_ref.shape[2] // 2
    groups = len(out_refs)
    share = slots // groups
    holder, rank_there = found_ref[0:1], found_ref[1:2]
    place = iota((holders * half, slots), 0).astype(jnp.float32)
    parts = parts_of(jnp.concatenate([landed_ref[h] for h in range(holders)], axis=0))[::-1]
    result = jnp.zeros((total, slots), jnp.float32)
    for side in range(2):
        on_side = (rank_there >= half) if side else (rank_there < half)
        target = jnp.where(on_side, holder * half + rank_there - side * half, -1.0)
        chosen = exact_bf16(place == target)
        for part in parts:
            spread = lax.dot_general(part, chosen, (((0,), (0,)), ((), ())), preferred_element_type=jnp.float32)
            result = result + spread[side * total:(side + 1) * total]
    for g in range(groups):
        block = result[:, g * share:(g + 1) * share]
        out_refs[g][...] = jnp.concatenate([block[:total // 2], block[total // 2:]], axis=1)


def add_kernel(*refs):
    out_ref = refs[-1]
    total = refs[0][...]
    for ref in refs[1:-1]:
        total = total + ref[...]
    share = total.shape[1] // 2
    out_ref[0] = jnp.concatenate([total[:, :share], total[:, share:]], axis=0).T


def swap(value, axis, distance):
    return lax.ppermute(value, axis, [(i, i ^ distance) for i in range(lax.axis_size(axis))])


def on_device(query_grads, factor_out, factor_in, page_store, page_home, cand_lists, counts):
    holders = lax.axis_size("store")
    groups = lax.axis_size("layer")
    rows, width = query_grads.shape
    layers, rank, _ = factor_out.shape
    per_holder = page_store.shape[0]
    slots = cand_lists.shape[1]
    bf16 = jnp.bfloat16

    capacity = slots // holders
    home = page_home.reshape(-1, LANES)
    sources = [
        pltpu.with_memory_space_constraint(source, pltpu.HBM)
        for source in (query_grads, factor_in, factor_out, home, cand_lists, page_store)
    ]
    notes = max(LANES, holders // rows * capacity)
    packed, pages, found = pl.pallas_call(
        functools.partial(condition_kernel, holders, groups, capacity),
        out_shape=[
            jax.ShapeDtypeStruct((rows, width + notes), bf16),
            pltpu.VMEM(page_store.shape, bf16),
            jax.ShapeDtypeStruct((8, slots), jnp.float32),
        ],
        in_specs=[SMEM] + [HBM] * len(sources),
        out_specs=[VMEM] * 3,
        scratch_shapes=[pltpu.VMEM(source.shape, source.dtype) for source in sources[:-1]]
        + [pltpu.SemaphoreType.DMA((len(sources),))],
        compiler_params=pltpu.CompilerParams(vmem_limit_bytes=10 * 2**20 + 24 * slots * slots),
    )(counts, *sources)

    blocks = [None] * holders
    blocks[0] = packed
    blocks[1] = swap(packed, "store", 1)
    for k in range(2, holders, 2):
        blocks[k] = swap(packed, "store", k)
    for k in range(2, holders, 2):
        blocks[k + 1] = swap(blocks[k], "store", 1)

    total = holders * rows
    bytes_in = 2 * holders * rows * (width + notes) + 2 * per_holder * width
    asked = pl.pallas_call(
        functools.partial(score_kernel, holders, capacity),
        out_shape=jax.ShapeDtypeStruct((holders, capacity // 2, 2 * total), jnp.float32),
        in_specs=[VMEM] * (holders + 1),
        out_specs=VMEM,
        scratch_shapes=[pltpu.VMEM((total, per_holder), jnp.float32)],
        compiler_params=pltpu.CompilerParams(vmem_limit_bytes=8 * 2**20 + bytes_in + 48 * total * slots),
    )(*blocks, pltpu.with_memory_space_constraint(pages, pltpu.VMEM))

    landed = lax.all_to_all(asked, "store", split_axis=0, concat_axis=0, tiled=True)
    share = slots // groups
    terms = pl.pallas_call(
        functools.partial(spread_kernel, holders),
        out_shape=[jax.ShapeDtypeStruct((total // 2, 2 * share), jnp.float32)] * groups,
        in_specs=[VMEM] * 2,
        out_specs=[VMEM] * groups,
        compiler_params=pltpu.CompilerParams(vmem_limit_bytes=4 * 2**20 + 64 * total * slots),
    )(found, landed)
    terms = [terms[0]] + [
        lax.ppermute(terms[j], "layer", [(g, (g + j) % groups) for g in range(groups)]) for j in range(1, groups)
    ]
    return pl.pallas_call(
        add_kernel,
        out_shape=jax.ShapeDtypeStruct((1, share, total), jnp.float32),
        in_specs=[VMEM] * groups,
        out_specs=VMEM,
        compiler_params=pltpu.CompilerParams(vmem_limit_bytes=4 * 2**20),
    )(*terms)


def solution(mesh):
    placed = (
        P("store", "layer"),
        P("layer", None, None),
        P("layer", None, None),
        P("store", "layer"),
        P(),
        P("store", None),
        P("store"),
    )
    return jax.shard_map(
        on_device, mesh=mesh, in_specs=placed, out_specs=P("store", "layer", None), check_vma=False
    )
```

```python
import functools

import jax
import jax.numpy as jnp
from jax import lax
from jax.experimental import pallas as pl
from jax.experimental.pallas import tpu as pltpu
from jax.sharding import PartitionSpec as P

VMEM = pl.BlockSpec(memory_space=pltpu.VMEM)
SMEM = pl.BlockSpec(memory_space=pltpu.SMEM)
HBM = pl.BlockSpec(memory_space=pltpu.HBM)
LANES = 128
CHUNKS = 4


def iota(shape, dimension):
    return lax.broadcasted_iota(jnp.int32, shape, dimension)


def parts_of(value):
    parts = []
    for _ in range(3):
        part = value.astype(jnp.bfloat16)
        value = value - part.astype(jnp.float32)
        parts.append(part)
    return parts


def exact_bf16(value):
    return value.astype(jnp.float32).astype(jnp.bfloat16)


def condition_kernel(holders, groups, capacity, count_ref, *refs):
    sources, packed_ref, pages_ref, found_ref, landing, arrived = refs[:6], refs[6], refs[7], refs[8], refs[9:14], refs[14]
    turned_ref = refs[15]
    copies = [
        pltpu.make_async_copy(source, target, arrived.at[i])
        for i, (source, target) in enumerate(zip(sources, landing + (pages_ref,)))
    ]
    for copy in copies:
        copy.start()
    for copy in copies[:-1]:
        copy.wait()
    query_ref, in_factor_ref, out_factor_ref, home_ref, cand_ref = landing
    per_holder = pages_ref.shape[0]
    rows, width = query_ref.shape
    layers, rank, _ = in_factor_ref.shape
    half = rank // 2
    query = query_ref[...].astype(jnp.float32)
    low = iota((half, LANES), 1) < rank
    zero = jnp.zeros((rank, rank), jnp.float32)
    terms = [(0, 0), (0, 1), (0, 2), (1, 0), (1, 1), (2, 0)]
    group = 2 * LANES
    source, place = iota((rank, 2 * group), 0), iota((rank, 2 * group), 1)
    inside = place % group
    column_found = (source == 2 * (inside % half) + place // group)
    chosen_part = sum((inside >= half * start).astype(jnp.int32) for start in (3, 5, 6))
    pickers = [exact_bf16(column_found & (chosen_part == i)) for i in range(3)]
    for layer in range(layers):
        first = layer * half
        packed = jnp.concatenate(
            [query[:, (first + t) * LANES:(first + t + 1) * LANES] for t in range(half)], axis=0
        ).astype(jnp.bfloat16)
        factor = in_factor_ref[layer]
        doubled = parts_of(
            jnp.concatenate(
                [jnp.concatenate([factor, zero], axis=1), jnp.concatenate([zero, factor], axis=1)], axis=0
            )
        )
        small = jnp.dot(
            jnp.concatenate([packed, packed], axis=1), jnp.concatenate(doubled[1:], axis=0),
            preferred_element_type=jnp.float32,
        )
        turned_ref[layer] = small + jnp.dot(packed, doubled[0], preferred_element_type=jnp.float32)
        wide = jnp.concatenate([turned_ref[layer, pl.ds(q, half, stride=rows), :] for q in range(rows)], axis=1)
        wide = parts_of(wide)
        stacked = jnp.concatenate([wide[j] for _, j in terms], axis=0)
        by_row = jnp.concatenate(
            [out_factor_ref[layer, pl.ds(parity, half, stride=2), :] for parity in range(2)], axis=0
        )
        sorted_columns = sum(
            jnp.dot(part, picker, preferred_element_type=jnp.float32) for part, picker in zip(parts_of(by_row), pickers)
        )
        quarters = jnp.concatenate(
            [
                sorted_columns[r * half:(r + 1) * half, c * group:c * group + len(terms) * half]
                for r in range(2) for c in range(2)
            ],
            axis=0,
        ).astype(jnp.bfloat16)
        left = jnp.dot(quarters, stacked, preferred_element_type=jnp.float32)
        for q in range(rows):
            part = left[:, q * LANES:(q + 1) * LANES]
            ee, eo, oe, oo = (part[i * half:(i + 1) * half] for i in range(4))
            done = jnp.where(low, ee, oo) + pltpu.roll(jnp.where(low, oe, eo), rank, 1)
            turned_ref[layer, pl.ds(q, half, stride=rows), :] = done
        for t in range(half):
            packed_ref[:, (first + t) * LANES:(first + t + 1) * LANES] = (
                turned_ref[layer, t * rows:(t + 1) * rows, :].astype(jnp.bfloat16)
            )

    slots = cand_ref.shape[1]
    home_rows = home_ref.shape[0]
    share = slots // groups
    at = lax.axis_index("layer")
    wanted = jnp.where(iota((1, slots), 1) < count_ref[0], cand_ref[...], -1)
    ranges = [wanted[:, g * share:(g + 1) * share] for g in range(groups)]
    ordered = []
    for j in range(groups):
        chosen = ranges[0]
        for g in range(1, groups):
            chosen = jnp.where((at + j) % groups == g, ranges[g], chosen)
        ordered.append(chosen)
    wanted = jnp.concatenate(ordered, axis=1)
    known = jnp.maximum(wanted, 0)
    onehot = (iota((LANES, slots), 0) == known % LANES).astype(jnp.float32).astype(jnp.bfloat16)
    home = home_ref[...]
    table = jnp.concatenate([home // per_holder, home % per_holder], axis=0).astype(jnp.float32).astype(jnp.bfloat16)
    found = jnp.dot(table, onehot, preferred_element_type=jnp.float32)
    mine = iota((home_rows, slots), 0) == known // LANES
    holder = jnp.sum(jnp.where(mine, found[:home_rows], 0.0), axis=0, keepdims=True)
    within = jnp.sum(jnp.where(mine, found[home_rows:], 0.0), axis=0, keepdims=True)
    holder = jnp.where(wanted >= 0, holder, float(holders))
    at_holder = iota((holders, slots), 0).astype(jnp.float32) == holder
    earlier = exact_bf16(iota((slots, slots), 0) < iota((slots, slots), 1))
    before = jnp.dot(exact_bf16(at_holder), earlier, preferred_element_type=jnp.float32)
    rank_there = jnp.sum(jnp.where(at_holder, before, 0.0), axis=0, keepdims=True)
    ranked = exact_bf16(iota((capacity, slots), 0).astype(jnp.float32) == rank_there)
    asked = lax.dot_general(
        exact_bf16(jnp.where(at_holder, within + 1.0, 0.0)), ranked, (((1,), (1,)), ((), ())),
        preferred_element_type=jnp.float32,
    )
    blocks = [asked[h:h + rows] for h in range(0, holders, rows)]
    spare = packed_ref.shape[1] - width - capacity * len(blocks)
    if spare:
        blocks.append(jnp.zeros((rows, spare), jnp.float32))
    packed_ref[:, width:] = jnp.concatenate(blocks, axis=1).astype(jnp.bfloat16)
    found_ref[...] = jnp.concatenate([holder, rank_there, jnp.zeros((6, slots), jnp.float32)], axis=0)
    copies[-1].wait()


def score_kernel(holders, capacity, *refs):
    packed_refs, pages_ref, out_ref, total, queries = refs[:holders], *refs[holders:]
    me = lax.axis_index("store")
    count, width = pages_ref.shape
    rows = packed_refs[0].shape[0]
    half = capacity // 2
    step = width // CHUNKS
    scores = jnp.zeros((holders * rows, count), jnp.float32)
    for i in range(CHUNKS):
        columns = slice(i * step, (i + 1) * step)
        for k in range(holders):
            queries[k * rows:(k + 1) * rows, columns] = packed_refs[k][:, columns]
        scores = scores + lax.dot_general(
            queries[:, columns], pages_ref[:, columns], (((1,), (1,)), ((), ())), preferred_element_type=jnp.float32
        )
    for k in range(holders):
        start = pl.multiple_of((me ^ k) * rows, rows)
        total[pl.ds(start, rows), :] = scores[k * rows:(k + 1) * rows]
    asked = []
    for k in range(holders):
        notes = packed_refs[k][:, width:].astype(jnp.float32)
        notes = jnp.sum(jnp.where(iota(notes.shape, 0) == me % rows, notes, 0.0), axis=0, keepdims=True)
        mine = notes[:, :capacity]
        for block in range(1, holders // rows):
            mine = jnp.where(me // rows == block, notes[:, block * capacity:(block + 1) * capacity], mine)
        asked.append(mine)
    page = iota((count, holders * half), 0).astype(jnp.float32) + 1.0
    picked = jnp.zeros((holders * half, 2 * holders * rows), jnp.float32)
    parts = parts_of(total[...])[::-1]
    nothing = jnp.zeros_like(parts[0])
    for side in range(2):
        chosen = exact_bf16(page == jnp.concatenate([row[:, side * half:(side + 1) * half] for row in asked], axis=1))
        for part in parts:
            wide = jnp.concatenate([nothing, part] if side else [part, nothing], axis=0)
            picked = picked + lax.dot_general(
                chosen, wide, (((0,), (1,)), ((), ())), preferred_element_type=jnp.float32
            )
    for k in range(holders):
        out_ref[me ^ k] = picked[k * half:(k + 1) * half]


def spread_kernel(holders, found_ref, landed_ref, *out_refs):
    half = landed_ref.shape[1]
    slots = found_ref.shape[1]
    total = landed_ref.shape[2] // 2
    groups = len(out_refs)
    share = slots // groups
    holder, rank_there = found_ref[0:1], found_ref[1:2]
    place = iota((holders * half, slots), 0).astype(jnp.float32)
    parts = parts_of(jnp.concatenate([landed_ref[h] for h in range(holders)], axis=0))[::-1]
    result = jnp.zeros((total, slots), jnp.float32)
    for side in range(2):
        on_side = (rank_there >= half) if side else (rank_there < half)
        target = jnp.where(on_side, holder * half + rank_there - side * half, -1.0)
        chosen = exact_bf16(place == target)
        for part in parts:
            spread = lax.dot_general(part, chosen, (((0,), (0,)), ((), ())), preferred_element_type=jnp.float32)
            result = result + spread[side * total:(side + 1) * total]
    for g in range(groups):
        block = result[:, g * share:(g + 1) * share]
        out_refs[g][...] = jnp.concatenate([block[:total // 2], block[total // 2:]], axis=1)


def add_kernel(*refs):
    out_ref = refs[-1]
    total = refs[0][...]
    for ref in refs[1:-1]:
        total = total + ref[...]
    share = total.shape[1] // 2
    out_ref[0] = jnp.concatenate([total[:, :share], total[:, share:]], axis=0).T


def swap(value, axis, distance):
    return lax.ppermute(value, axis, [(i, i ^ distance) for i in range(lax.axis_size(axis))])


def on_device(query_grads, factor_out, factor_in, page_store, page_home, cand_lists, counts):
    holders = lax.axis_size("store")
    groups = lax.axis_size("layer")
    rows, width = query_grads.shape
    layers, rank, _ = factor_out.shape
    per_holder = page_store.shape[0]
    slots = cand_lists.shape[1]
    bf16 = jnp.bfloat16

    capacity = slots // holders
    home = page_home.reshape(-1, LANES)
    sources = [
        pltpu.with_memory_space_constraint(source, pltpu.HBM)
        for source in (query_grads, factor_in, factor_out, home, cand_lists, page_store)
    ]
    notes = max(LANES, holders // rows * capacity)
    packed, pages, found = pl.pallas_call(
        functools.partial(condition_kernel, holders, groups, capacity),
        out_shape=[
            jax.ShapeDtypeStruct((rows, width + notes), bf16),
            pltpu.VMEM(page_store.shape, bf16),
            jax.ShapeDtypeStruct((8, slots), jnp.float32),
        ],
        in_specs=[SMEM] + [HBM] * len(sources),
        out_specs=[VMEM] * 3,
        scratch_shapes=[pltpu.VMEM(source.shape, source.dtype) for source in sources[:-1]]
        + [pltpu.SemaphoreType.DMA((len(sources),)), pltpu.VMEM((layers, rows * rank // 2, LANES), jnp.float32)],
        compiler_params=pltpu.CompilerParams(vmem_limit_bytes=10 * 2**20 + 24 * slots * slots),
    )(counts, *sources)

    blocks = [None] * holders
    blocks[0] = packed
    blocks[1] = swap(packed, "store", 1)
    for k in range(2, holders, 2):
        blocks[k] = swap(packed, "store", k)
    for k in range(2, holders, 2):
        blocks[k + 1] = swap(blocks[k], "store", 1)

    total = holders * rows
    bytes_in = 2 * holders * rows * (width + notes) + 2 * per_holder * width
    asked = pl.pallas_call(
        functools.partial(score_kernel, holders, capacity),
        out_shape=jax.ShapeDtypeStruct((holders, capacity // 2, 2 * total), jnp.float32),
        in_specs=[VMEM] * (holders + 1),
        out_specs=VMEM,
        scratch_shapes=[pltpu.VMEM((total, per_holder), jnp.float32), pltpu.VMEM((total, width), bf16)],
        compiler_params=pltpu.CompilerParams(vmem_limit_bytes=8 * 2**20 + 2 * bytes_in + 48 * total * slots),
    )(*blocks, pltpu.with_memory_space_constraint(pages, pltpu.VMEM))

    landed = lax.all_to_all(asked, "store", split_axis=0, concat_axis=0, tiled=True)
    share = slots // groups
    terms = pl.pallas_call(
        functools.partial(spread_kernel, holders),
        out_shape=[jax.ShapeDtypeStruct((total // 2, 2 * share), jnp.float32)] * groups,
        in_specs=[VMEM] * 2,
        out_specs=[VMEM] * groups,
        compiler_params=pltpu.CompilerParams(vmem_limit_bytes=4 * 2**20 + 64 * total * slots),
    )(found, landed)
    terms = [terms[0]] + [
        lax.ppermute(terms[j], "layer", [(g, (g + j) % groups) for g in range(groups)]) for j in range(1, groups)
    ]
    return pl.pallas_call(
        add_kernel,
        out_shape=jax.ShapeDtypeStruct((1, share, total), jnp.float32),
        in_specs=[VMEM] * groups,
        out_specs=VMEM,
        compiler_params=pltpu.CompilerParams(vmem_limit_bytes=4 * 2**20),
    )(*terms)


def solution(mesh):
    placed = (
        P("store", "layer"),
        P("layer", None, None),
        P("layer", None, None),
        P("store", "layer"),
        P(),
        P("store", None),
        P("store"),
    )
    return jax.shard_map(
        on_device, mesh=mesh, in_specs=placed, out_specs=P("store", "layer", None), check_vma=False
    )
```

```python
import functools

import jax
import jax.numpy as jnp
from jax import lax
from jax.experimental import pallas as pl
from jax.experimental.pallas import tpu as pltpu
from jax.sharding import PartitionSpec as P

VMEM = pl.BlockSpec(memory_space=pltpu.VMEM)
SMEM = pl.BlockSpec(memory_space=pltpu.SMEM)
HBM = pl.BlockSpec(memory_space=pltpu.HBM)
LANES = 128
CHUNKS = 4


def iota(shape, dimension):
    return lax.broadcasted_iota(jnp.int32, shape, dimension)


def parts_of(value):
    parts = []
    for _ in range(3):
        part = value.astype(jnp.bfloat16)
        value = value - part.astype(jnp.float32)
        parts.append(part)
    return parts


def exact_bf16(value):
    return value.astype(jnp.float32).astype(jnp.bfloat16)


def condition_kernel(holders, groups, capacity, per_holder, count_ref, *refs):
    sources, packed_ref, again_ref, found_ref, landing, arrived, turned_ref = refs[:5], *refs[5:8], refs[8:13], *refs[13:]
    copies = [
        pltpu.make_async_copy(source, target, arrived.at[i])
        for i, (source, target) in enumerate(zip(sources, landing))
    ]
    for copy in copies:
        copy.start()
    for copy in copies:
        copy.wait()
    query_ref, in_factor_ref, out_factor_ref, home_ref, cand_ref = landing
    rows, width = query_ref.shape
    layers, rank, _ = in_factor_ref.shape
    half = rank // 2
    query = query_ref[...].astype(jnp.float32)
    low = iota((half, LANES), 1) < rank
    zero = jnp.zeros((rank, rank), jnp.float32)
    terms = [(0, 0), (0, 1), (0, 2), (1, 0), (1, 1), (2, 0)]
    group = 2 * LANES
    source, place = iota((rank, 2 * group), 0), iota((rank, 2 * group), 1)
    inside = place % group
    column_found = (source == 2 * (inside % half) + place // group)
    chosen_part = sum((inside >= half * start).astype(jnp.int32) for start in (3, 5, 6))
    pickers = [exact_bf16(column_found & (chosen_part == i)) for i in range(3)]
    for layer in range(layers):
        first = layer * half
        packed = jnp.concatenate(
            [query[:, (first + t) * LANES:(first + t + 1) * LANES] for t in range(half)], axis=0
        ).astype(jnp.bfloat16)
        factor = in_factor_ref[layer]
        doubled = parts_of(
            jnp.concatenate(
                [jnp.concatenate([factor, zero], axis=1), jnp.concatenate([zero, factor], axis=1)], axis=0
            )
        )
        small = jnp.dot(
            jnp.concatenate([packed, packed], axis=1), jnp.concatenate(doubled[1:], axis=0),
            preferred_element_type=jnp.float32,
        )
        turned_ref[layer] = small + jnp.dot(packed, doubled[0], preferred_element_type=jnp.float32)
        wide = jnp.concatenate([turned_ref[layer, pl.ds(q, half, stride=rows), :] for q in range(rows)], axis=1)
        wide = parts_of(wide)
        stacked = jnp.concatenate([wide[j] for _, j in terms], axis=0)
        by_row = jnp.concatenate(
            [out_factor_ref[layer, pl.ds(parity, half, stride=2), :] for parity in range(2)], axis=0
        )
        sorted_columns = sum(
            jnp.dot(part, picker, preferred_element_type=jnp.float32) for part, picker in zip(parts_of(by_row), pickers)
        )
        quarters = jnp.concatenate(
            [
                sorted_columns[r * half:(r + 1) * half, c * group:c * group + len(terms) * half]
                for r in range(2) for c in range(2)
            ],
            axis=0,
        ).astype(jnp.bfloat16)
        left = jnp.dot(quarters, stacked, preferred_element_type=jnp.float32)
        for q in range(rows):
            part = left[:, q * LANES:(q + 1) * LANES]
            ee, eo, oe, oo = (part[i * half:(i + 1) * half] for i in range(4))
            done = jnp.where(low, ee, oo) + pltpu.roll(jnp.where(low, oe, eo), rank, 1)
            turned_ref[layer, pl.ds(q, half, stride=rows), :] = done
        for t in range(half):
            packed_ref[:, (first + t) * LANES:(first + t + 1) * LANES] = (
                turned_ref[layer, t * rows:(t + 1) * rows, :].astype(jnp.bfloat16)
            )

    slots = cand_ref.shape[1]
    home_rows = home_ref.shape[0]
    share = slots // groups
    at = lax.axis_index("layer")
    wanted = jnp.where(iota((1, slots), 1) < count_ref[0], cand_ref[...], -1)
    ranges = [wanted[:, g * share:(g + 1) * share] for g in range(groups)]
    ordered = []
    for j in range(groups):
        chosen = ranges[0]
        for g in range(1, groups):
            chosen = jnp.where((at + j) % groups == g, ranges[g], chosen)
        ordered.append(chosen)
    wanted = jnp.concatenate(ordered, axis=1)
    known = jnp.maximum(wanted, 0)
    onehot = (iota((LANES, slots), 0) == known % LANES).astype(jnp.float32).astype(jnp.bfloat16)
    home = home_ref[...]
    table = jnp.concatenate([home // per_holder, home % per_holder], axis=0).astype(jnp.float32).astype(jnp.bfloat16)
    found = jnp.dot(table, onehot, preferred_element_type=jnp.float32)
    mine = iota((home_rows, slots), 0) == known // LANES
    holder = jnp.sum(jnp.where(mine, found[:home_rows], 0.0), axis=0, keepdims=True)
    within = jnp.sum(jnp.where(mine, found[home_rows:], 0.0), axis=0, keepdims=True)
    holder = jnp.where(wanted >= 0, holder, float(holders))
    at_holder = iota((holders, slots), 0).astype(jnp.float32) == holder
    earlier = exact_bf16(iota((slots, slots), 0) < iota((slots, slots), 1))
    before = jnp.dot(exact_bf16(at_holder), earlier, preferred_element_type=jnp.float32)
    rank_there = jnp.sum(jnp.where(at_holder, before, 0.0), axis=0, keepdims=True)
    ranked = exact_bf16(iota((capacity, slots), 0).astype(jnp.float32) == rank_there)
    asked = lax.dot_general(
        exact_bf16(jnp.where(at_holder, within + 1.0, 0.0)), ranked, (((1,), (1,)), ((), ())),
        preferred_element_type=jnp.float32,
    )
    blocks = [asked[h:h + rows] for h in range(0, holders, rows)]
    spare = packed_ref.shape[1] - width - capacity * len(blocks)
    if spare:
        blocks.append(jnp.zeros((rows, spare), jnp.float32))
    packed_ref[:, width:] = jnp.concatenate(blocks, axis=1).astype(jnp.bfloat16)
    again_ref[...] = packed_ref[...]
    found_ref[...] = jnp.concatenate([holder, rank_there, jnp.zeros((6, slots), jnp.float32)], axis=0)


def load_kernel(block_ref, source_ref, same_block_ref, target_ref, arrived):
    copy = pltpu.make_async_copy(source_ref, target_ref, arrived)
    copy.start()
    copy.wait()


def score_kernel(holders, capacity, *refs):
    packed_refs, pages_ref, out_ref, queries = refs[:holders], *refs[holders:]
    me = lax.axis_index("store")
    count, width = pages_ref.shape
    rows = packed_refs[0].shape[0]
    total = holders * rows
    half = capacity // 2
    step = width // CHUNKS
    scores = jnp.zeros((count, total), jnp.float32)
    for i in range(CHUNKS):
        columns = slice(i * step, (i + 1) * step)
        for k in range(holders):
            queries[k * rows:(k + 1) * rows, columns] = packed_refs[k][:, columns]
        scores = scores + lax.dot_general(
            pages_ref[:, columns], queries[:, columns], (((1,), (1,)), ((), ())), preferred_element_type=jnp.float32
        )
    asked = []
    for k in range(holders):
        notes = packed_refs[k][:, width:].astype(jnp.float32)
        notes = jnp.sum(jnp.where(iota(notes.shape, 0) == me % rows, notes, 0.0), axis=0, keepdims=True)
        mine = notes[:, :capacity]
        for block in range(1, holders // rows):
            mine = jnp.where(me // rows == block, notes[:, block * capacity:(block + 1) * capacity], mine)
        asked.append(mine)
    page = iota((holders * half, count), 1).astype(jnp.float32) + 1.0
    came, goes = iota((total, 2 * total), 0), iota((total, 2 * total), 1)
    own_place = (me ^ (came // rows)) * rows + came % rows
    picked = jnp.zeros((holders * half, 2 * total), jnp.float32)
    parts = parts_of(scores)[::-1]
    for side in range(2):
        row = jnp.concatenate([row[:, side * half:(side + 1) * half] for row in asked], axis=1)
        chosen = exact_bf16(page == jnp.broadcast_to(row, (8, holders * half)).T[:, :1])
        placing = exact_bf16(goes == own_place + side * total)
        for part in parts:
            placed = jnp.dot(part, placing, preferred_element_type=jnp.float32).astype(jnp.bfloat16)
            picked = picked + jnp.dot(chosen, placed, preferred_element_type=jnp.float32)
    for k in range(holders):
        out_ref[me ^ k] = picked[k * half:(k + 1) * half]


def spread_kernel(holders, found_ref, landed_ref, *out_refs):
    half = landed_ref.shape[1]
    slots = found_ref.shape[1]
    total = landed_ref.shape[2] // 2
    groups = len(out_refs)
    share = slots // groups
    holder, rank_there = found_ref[0:1], found_ref[1:2]
    place = iota((holders * half, slots), 0).astype(jnp.float32)
    parts = parts_of(jnp.concatenate([landed_ref[h] for h in range(holders)], axis=0))[::-1]
    result = jnp.zeros((total, slots), jnp.float32)
    for side in range(2):
        on_side = (rank_there >= half) if side else (rank_there < half)
        target = jnp.where(on_side, holder * half + rank_there - side * half, -1.0)
        chosen = exact_bf16(place == target)
        for part in parts:
            spread = lax.dot_general(part, chosen, (((0,), (0,)), ((), ())), preferred_element_type=jnp.float32)
            result = result + spread[side * total:(side + 1) * total]
    for g in range(groups):
        block = result[:, g * share:(g + 1) * share]
        out_refs[g][...] = jnp.concatenate([block[:total // 2], block[total // 2:]], axis=1)


def add_kernel(*refs):
    out_ref = refs[-1]
    total = refs[0][...]
    for ref in refs[1:-1]:
        total = total + ref[...]
    share = total.shape[1] // 2
    out_ref[0] = jnp.concatenate([total[:, :share], total[:, share:]], axis=0).T


def swap(value, axis, distance):
    return lax.ppermute(value, axis, [(i, i ^ distance) for i in range(lax.axis_size(axis))])


def on_device(query_grads, factor_out, factor_in, page_store, page_home, cand_lists, counts):
    holders = lax.axis_size("store")
    groups = lax.axis_size("layer")
    rows, width = query_grads.shape
    layers, rank, _ = factor_out.shape
    per_holder = page_store.shape[0]
    slots = cand_lists.shape[1]
    bf16 = jnp.bfloat16

    capacity = slots // holders
    home = page_home.reshape(-1, LANES)
    sources = [
        pltpu.with_memory_space_constraint(source, pltpu.HBM)
        for source in (query_grads, factor_in, factor_out, home, cand_lists)
    ]
    notes = max(LANES, holders // rows * capacity)
    packed, again, found = pl.pallas_call(
        functools.partial(condition_kernel, holders, groups, capacity, per_holder),
        out_shape=[
            jax.ShapeDtypeStruct((rows, width + notes), bf16),
            jax.ShapeDtypeStruct((rows, width + notes), bf16),
            jax.ShapeDtypeStruct((8, slots), jnp.float32),
        ],
        in_specs=[SMEM] + [HBM] * len(sources),
        out_specs=[VMEM] * 3,
        scratch_shapes=[pltpu.VMEM(source.shape, source.dtype) for source in sources]
        + [pltpu.SemaphoreType.DMA((len(sources),)), pltpu.VMEM((layers, rows * rank // 2, LANES), jnp.float32)],
        compiler_params=pltpu.CompilerParams(vmem_limit_bytes=10 * 2**20 + 24 * slots * slots),
    )(counts, *sources)

    again, pages = pl.pallas_call(
        load_kernel,
        out_shape=[jax.ShapeDtypeStruct(again.shape, bf16), pltpu.VMEM(page_store.shape, bf16)],
        in_specs=[VMEM, HBM],
        out_specs=[VMEM] * 2,
        input_output_aliases={0: 0},
        scratch_shapes=[pltpu.SemaphoreType.DMA(())],
        compiler_params=pltpu.CompilerParams(vmem_limit_bytes=2 * 2**20),
        cost_estimate=pl.CostEstimate(flops=0, bytes_accessed=2 * page_store.size, transcendentals=0),
    )(again, pltpu.with_memory_space_constraint(page_store, pltpu.HBM))

    blocks = [None] * holders
    blocks[0] = packed
    blocks[1] = swap(again, "store", 1)
    for k in range(2, holders, 2):
        blocks[k] = swap(packed, "store", k)
    for k in range(2, holders, 2):
        blocks[k + 1] = swap(blocks[k], "store", 1)

    total = holders * rows
    bytes_in = 2 * holders * rows * (width + notes) + 2 * per_holder * width
    asked = pl.pallas_call(
        functools.partial(score_kernel, holders, capacity),
        out_shape=jax.ShapeDtypeStruct((holders, capacity // 2, 2 * total), jnp.float32),
        in_specs=[VMEM] * (holders + 1),
        out_specs=VMEM,
        scratch_shapes=[pltpu.VMEM((total, width), bf16)],
        compiler_params=pltpu.CompilerParams(vmem_limit_bytes=8 * 2**20 + 2 * bytes_in + 48 * total * slots),
    )(*blocks, pltpu.with_memory_space_constraint(pages, pltpu.VMEM))

    landed = lax.all_to_all(asked, "store", split_axis=0, concat_axis=0, tiled=True)
    share = slots // groups
    terms = pl.pallas_call(
        functools.partial(spread_kernel, holders),
        out_shape=[jax.ShapeDtypeStruct((total // 2, 2 * share), jnp.float32)] * groups,
        in_specs=[VMEM] * 2,
        out_specs=[VMEM] * groups,
        compiler_params=pltpu.CompilerParams(vmem_limit_bytes=4 * 2**20 + 64 * total * slots),
    )(found, landed)
    terms = [terms[0]] + [
        lax.ppermute(terms[j], "layer", [(g, (g + j) % groups) for g in range(groups)]) for j in range(1, groups)
    ]
    return pl.pallas_call(
        add_kernel,
        out_shape=jax.ShapeDtypeStruct((1, share, total), jnp.float32),
        in_specs=[VMEM] * groups,
        out_specs=VMEM,
        compiler_params=pltpu.CompilerParams(vmem_limit_bytes=4 * 2**20),
    )(*terms)


def solution(mesh):
    placed = (
        P("store", "layer"),
        P("layer", None, None),
        P("layer", None, None),
        P("store", "layer"),
        P(),
        P("store", None),
        P("store"),
    )
    return jax.shard_map(
        on_device, mesh=mesh, in_specs=placed, out_specs=P("store", "layer", None), check_vma=False
    )
```

```python
import functools

import jax
import jax.numpy as jnp
from jax import lax
from jax.experimental import pallas as pl
from jax.experimental.pallas import tpu as pltpu
from jax.sharding import PartitionSpec as P

VMEM = pl.BlockSpec(memory_space=pltpu.VMEM)
SMEM = pl.BlockSpec(memory_space=pltpu.SMEM)
HBM = pl.BlockSpec(memory_space=pltpu.HBM)
LANES = 128
CHUNKS = 4


def iota(shape, dimension):
    return lax.broadcasted_iota(jnp.int32, shape, dimension)


def layer_plan(groups):
    if groups == 4:
        return [[1, 2, 0, 3], [2, 0, 1, 3], [3, 1, 2, 0], [0, 3, 2, 1], [0, 1, 3, 2]]
    return [[(g + step) % groups for g in range(groups)] for step in range(1, groups)]


def entry(values, index):
    return sum(jnp.where(index == i, value, 0) for i, value in enumerate(values))


def parts_of(value):
    parts = []
    for _ in range(3):
        part = value.astype(jnp.bfloat16)
        value = value - part.astype(jnp.float32)
        parts.append(part)
    return parts


def exact_bf16(value):
    return value.astype(jnp.float32).astype(jnp.bfloat16)


def condition_kernel(holders, capacity, count_ref, *refs):
    sources, packed_ref, pages_ref, found_ref, landing, arrived = refs[:6], refs[6], refs[7], refs[8], refs[9:14], refs[14]
    turned_ref = refs[15]
    copies = [
        pltpu.make_async_copy(source, target, arrived.at[i])
        for i, (source, target) in enumerate(zip(sources, landing + (pages_ref,)))
    ]
    for copy in copies:
        copy.start()
    for copy in copies[:-1]:
        copy.wait()
    query_ref, in_factor_ref, out_factor_ref, home_ref, cand_ref = landing
    per_holder = pages_ref.shape[0]
    rows, width = query_ref.shape
    layers, rank, _ = in_factor_ref.shape
    half = rank // 2
    query = query_ref[...].astype(jnp.float32)
    low = iota((half, LANES), 1) < rank
    zero = jnp.zeros((rank, rank), jnp.float32)
    terms = [(0, 0), (0, 1), (0, 2), (1, 0), (1, 1), (2, 0)]
    group = 2 * LANES
    source, place = iota((rank, 2 * group), 0), iota((rank, 2 * group), 1)
    inside = place % group
    column_found = (source == 2 * (inside % half) + place // group)
    chosen_part = sum((inside >= half * start).astype(jnp.int32) for start in (3, 5, 6))
    pickers = [exact_bf16(column_found & (chosen_part == i)) for i in range(3)]
    for layer in range(layers):
        first = layer * half
        packed = jnp.concatenate(
            [query[:, (first + t) * LANES:(first + t + 1) * LANES] for t in range(half)], axis=0
        ).astype(jnp.bfloat16)
        factor = in_factor_ref[layer]
        doubled = parts_of(
            jnp.concatenate(
                [jnp.concatenate([factor, zero], axis=1), jnp.concatenate([zero, factor], axis=1)], axis=0
            )
        )
        small = jnp.dot(
            jnp.concatenate([packed, packed], axis=1), jnp.concatenate(doubled[1:], axis=0),
            preferred_element_type=jnp.float32,
        )
        turned_ref[layer] = small + jnp.dot(packed, doubled[0], preferred_element_type=jnp.float32)
        wide = jnp.concatenate([turned_ref[layer, pl.ds(q, half, stride=rows), :] for q in range(rows)], axis=1)
        wide = parts_of(wide)
        stacked = jnp.concatenate([wide[j] for _, j in terms], axis=0)
        by_row = jnp.concatenate(
            [out_factor_ref[layer, pl.ds(parity, half, stride=2), :] for parity in range(2)], axis=0
        )
        sorted_columns = sum(
            jnp.dot(part, picker, preferred_element_type=jnp.float32) for part, picker in zip(parts_of(by_row), pickers)
        )
        quarters = jnp.concatenate(
            [
                sorted_columns[r * half:(r + 1) * half, c * group:c * group + len(terms) * half]
                for r in range(2) for c in range(2)
            ],
            axis=0,
        ).astype(jnp.bfloat16)
        left = jnp.dot(quarters, stacked, preferred_element_type=jnp.float32)
        for q in range(rows):
            part = left[:, q * LANES:(q + 1) * LANES]
            ee, eo, oe, oo = (part[i * half:(i + 1) * half] for i in range(4))
            done = jnp.where(low, ee, oo) + pltpu.roll(jnp.where(low, oe, eo), rank, 1)
            turned_ref[layer, pl.ds(q, half, stride=rows), :] = done
        for t in range(half):
            packed_ref[:, (first + t) * LANES:(first + t + 1) * LANES] = (
                turned_ref[layer, t * rows:(t + 1) * rows, :].astype(jnp.bfloat16)
            )

    slots = cand_ref.shape[1]
    home_rows = home_ref.shape[0]
    wanted = jnp.where(iota((1, slots), 1) < count_ref[0], cand_ref[...], -1)
    known = jnp.maximum(wanted, 0)
    onehot = (iota((LANES, slots), 0) == known % LANES).astype(jnp.float32).astype(jnp.bfloat16)
    home = home_ref[...]
    table = jnp.concatenate([home // per_holder, home % per_holder], axis=0).astype(jnp.float32).astype(jnp.bfloat16)
    found = jnp.dot(table, onehot, preferred_element_type=jnp.float32)
    mine = iota((home_rows, slots), 0) == known // LANES
    holder = jnp.sum(jnp.where(mine, found[:home_rows], 0.0), axis=0, keepdims=True)
    within = jnp.sum(jnp.where(mine, found[home_rows:], 0.0), axis=0, keepdims=True)
    holder = jnp.where(wanted >= 0, holder, float(holders))
    at_holder = iota((holders, slots), 0).astype(jnp.float32) == holder
    earlier = exact_bf16(iota((slots, slots), 0) < iota((slots, slots), 1))
    before = jnp.dot(exact_bf16(at_holder), earlier, preferred_element_type=jnp.float32)
    rank_there = jnp.sum(jnp.where(at_holder, before, 0.0), axis=0, keepdims=True)
    ranked = exact_bf16(iota((capacity, slots), 0).astype(jnp.float32) == rank_there)
    asked = lax.dot_general(
        exact_bf16(jnp.where(at_holder, within + 1.0, 0.0)), ranked, (((1,), (1,)), ((), ())),
        preferred_element_type=jnp.float32,
    )
    blocks = [asked[h:h + rows] for h in range(0, holders, rows)]
    spare = packed_ref.shape[1] - width - capacity * len(blocks)
    if spare:
        blocks.append(jnp.zeros((rows, spare), jnp.float32))
    packed_ref[:, width:] = jnp.concatenate(blocks, axis=1).astype(jnp.bfloat16)
    found_ref[...] = jnp.concatenate([holder, rank_there, jnp.zeros((6, slots), jnp.float32)], axis=0)
    copies[-1].wait()


def score_kernel(holders, capacity, *refs):
    packed_refs, pages_ref, out_ref, total, queries = refs[:holders], *refs[holders:]
    me = lax.axis_index("store")
    count, width = pages_ref.shape
    rows = packed_refs[0].shape[0]
    half = capacity // 2
    step = width // CHUNKS
    scores = jnp.zeros((holders * rows, count), jnp.float32)
    for i in range(CHUNKS):
        columns = slice(i * step, (i + 1) * step)
        for k in range(holders):
            queries[k * rows:(k + 1) * rows, columns] = packed_refs[k][:, columns]
        scores = scores + lax.dot_general(
            queries[:, columns], pages_ref[:, columns], (((1,), (1,)), ((), ())), preferred_element_type=jnp.float32
        )
    for k in range(holders):
        start = pl.multiple_of((me ^ k) * rows, rows)
        total[pl.ds(start, rows), :] = scores[k * rows:(k + 1) * rows]
    asked = []
    for k in range(holders):
        notes = packed_refs[k][:, width:].astype(jnp.float32)
        notes = jnp.sum(jnp.where(iota(notes.shape, 0) == me % rows, notes, 0.0), axis=0, keepdims=True)
        mine = notes[:, :capacity]
        for block in range(1, holders // rows):
            mine = jnp.where(me // rows == block, notes[:, block * capacity:(block + 1) * capacity], mine)
        asked.append(mine)
    page = iota((count, holders * half), 0).astype(jnp.float32) + 1.0
    parts = parts_of(total[...])[::-1]
    picked = []
    for side in range(2):
        row = jnp.concatenate([row[:, side * half:(side + 1) * half] for row in asked], axis=1)
        chosen = exact_bf16(page == row)
        picked.append(sum(jnp.dot(part, chosen, preferred_element_type=jnp.float32) for part in parts))
    picked = jnp.concatenate(picked, axis=0).T
    for k in range(holders):
        out_ref[me ^ k] = picked[k * half:(k + 1) * half]


def spread_kernel(holders, groups, found_ref, landed_ref, *out_refs):
    half = landed_ref.shape[1]
    slots = found_ref.shape[1]
    total = landed_ref.shape[2] // 2
    plan = layer_plan(groups)
    at = lax.axis_index("layer")
    share = slots // groups
    holder, rank_there = found_ref[0:1], found_ref[1:2]
    place = iota((holders * half, slots), 0).astype(jnp.float32)
    parts = parts_of(jnp.concatenate([landed_ref[h] for h in range(holders)], axis=0))[::-1]
    result = jnp.zeros((total, slots), jnp.float32)
    for side in range(2):
        on_side = (rank_there >= half) if side else (rank_there < half)
        target = jnp.where(on_side, holder * half + rank_there - side * half, -1.0)
        chosen = exact_bf16(place == target)
        for part in parts:
            spread = lax.dot_general(part, chosen, (((0,), (0,)), ((), ())), preferred_element_type=jnp.float32)
            result = result + spread[side * total:(side + 1) * total]
    blocks = []
    for g in range(groups):
        block = result[:, g * share:(g + 1) * share]
        blocks.append(jnp.concatenate([block[:total // 2], block[total // 2:]], axis=1))
    for out_ref, targets in zip(out_refs, [list(range(groups))] + plan):
        chosen = blocks[0]
        for g in range(1, groups):
            chosen = jnp.where(entry(targets, at) == g, blocks[g], chosen)
        out_ref[...] = chosen


def add_kernel(groups, *refs):
    at = lax.axis_index("layer")
    out_ref = refs[-1]
    total = refs[0][...]
    for ref, targets in zip(refs[1:], layer_plan(groups)):
        total = total + jnp.where(entry(targets, at) == at, 0.0, ref[...])
    share = total.shape[1] // 2
    out_ref[0] = jnp.concatenate([total[:, :share], total[:, share:]], axis=0).T


def swap(value, axis, distance):
    return lax.ppermute(value, axis, [(i, i ^ distance) for i in range(lax.axis_size(axis))])


def on_device(query_grads, factor_out, factor_in, page_store, page_home, cand_lists, counts):
    holders = lax.axis_size("store")
    groups = lax.axis_size("layer")
    rows, width = query_grads.shape
    layers, rank, _ = factor_out.shape
    per_holder = page_store.shape[0]
    slots = cand_lists.shape[1]
    bf16 = jnp.bfloat16

    capacity = slots // holders
    home = page_home.reshape(-1, LANES)
    sources = [
        pltpu.with_memory_space_constraint(source, pltpu.HBM)
        for source in (query_grads, factor_in, factor_out, home, cand_lists, page_store)
    ]
    notes = max(LANES, holders // rows * capacity)
    packed, pages, found = pl.pallas_call(
        functools.partial(condition_kernel, holders, capacity),
        out_shape=[
            jax.ShapeDtypeStruct((rows, width + notes), bf16),
            pltpu.VMEM(page_store.shape, bf16),
            jax.ShapeDtypeStruct((8, slots), jnp.float32),
        ],
        in_specs=[SMEM] + [HBM] * len(sources),
        out_specs=[VMEM] * 3,
        scratch_shapes=[pltpu.VMEM(source.shape, source.dtype) for source in sources[:-1]]
        + [pltpu.SemaphoreType.DMA((len(sources),)), pltpu.VMEM((layers, rows * rank // 2, LANES), jnp.float32)],
        compiler_params=pltpu.CompilerParams(vmem_limit_bytes=10 * 2**20 + 24 * slots * slots),
    )(counts, *sources)

    blocks = [None] * holders
    blocks[0] = packed
    blocks[1] = swap(packed, "store", 1)
    for k in range(2, holders, 2):
        blocks[k] = swap(packed, "store", k)
    for k in range(2, holders, 2):
        blocks[k + 1] = swap(blocks[k], "store", 1)

    total = holders * rows
    bytes_in = 2 * holders * rows * (width + notes) + 2 * per_holder * width
    asked = pl.pallas_call(
        functools.partial(score_kernel, holders, capacity),
        out_shape=jax.ShapeDtypeStruct((holders, capacity // 2, 2 * total), jnp.float32),
        in_specs=[VMEM] * (holders + 1),
        out_specs=VMEM,
        scratch_shapes=[pltpu.VMEM((total, per_holder), jnp.float32), pltpu.VMEM((total, width), bf16)],
        compiler_params=pltpu.CompilerParams(vmem_limit_bytes=8 * 2**20 + 2 * bytes_in + 48 * total * slots),
    )(*blocks, pltpu.with_memory_space_constraint(pages, pltpu.VMEM))

    landed = lax.all_to_all(asked, "store", split_axis=0, concat_axis=0, tiled=True)
    share = slots // groups
    plan = layer_plan(groups)
    terms = pl.pallas_call(
        functools.partial(spread_kernel, holders, groups),
        out_shape=[jax.ShapeDtypeStruct((total // 2, 2 * share), jnp.float32)] * (1 + len(plan)),
        in_specs=[VMEM] * 2,
        out_specs=[VMEM] * (1 + len(plan)),
        compiler_params=pltpu.CompilerParams(vmem_limit_bytes=4 * 2**20 + 64 * total * slots),
    )(found, landed)
    terms = [terms[0]] + [
        lax.ppermute(term, "layer", list(enumerate(targets))) for term, targets in zip(terms[1:], plan)
    ]
    return pl.pallas_call(
        functools.partial(add_kernel, groups),
        out_shape=jax.ShapeDtypeStruct((1, share, total), jnp.float32),
        in_specs=[VMEM] * len(terms),
        out_specs=VMEM,
        compiler_params=pltpu.CompilerParams(vmem_limit_bytes=4 * 2**20),
    )(*terms)


def solution(mesh):
    placed = (
        P("store", "layer"),
        P("layer", None, None),
        P("layer", None, None),
        P("store", "layer"),
        P(),
        P("store", None),
        P("store"),
    )
    return jax.shard_map(
        on_device, mesh=mesh, in_specs=placed, out_specs=P("store", "layer", None), check_vma=False
    )
```

```python
import functools

import jax
import jax.numpy as jnp
from jax import lax
from jax.experimental import pallas as pl
from jax.experimental.pallas import tpu as pltpu
from jax.sharding import PartitionSpec as P

VMEM = pl.BlockSpec(memory_space=pltpu.VMEM)
SMEM = pl.BlockSpec(memory_space=pltpu.SMEM)
HBM = pl.BlockSpec(memory_space=pltpu.HBM)
LANES = 128
CHUNKS = 4


def iota(shape, dimension):
    return lax.broadcasted_iota(jnp.int32, shape, dimension)


def parts_of(value):
    parts = []
    for _ in range(3):
        part = value.astype(jnp.bfloat16)
        value = value - part.astype(jnp.float32)
        parts.append(part)
    return parts


def exact_bf16(value):
    return value.astype(jnp.float32).astype(jnp.bfloat16)


def condition_kernel(holders, capacity, *refs):
    sources, packed_ref, pages_ref, found_ref, landing, arrived, turned_ref = refs[:6], *refs[6:9], refs[9:14], *refs[14:]
    copies = [
        pltpu.make_async_copy(source, target, arrived.at[i])
        for i, (source, target) in enumerate(zip(sources, landing + (pages_ref,)))
    ]
    for copy in copies:
        copy.start()
    for copy in copies[:-1]:
        copy.wait()
    query_ref, in_factor_ref, out_factor_ref, home_ref, cand_ref = landing
    per_holder = pages_ref.shape[0]
    rows, width = query_ref.shape
    layers, rank, _ = in_factor_ref.shape
    half = rank // 2
    query = query_ref[...].astype(jnp.float32)
    low = iota((half, LANES), 1) < rank
    zero = jnp.zeros((rank, rank), jnp.float32)
    terms = [(0, 0), (0, 1), (0, 2), (1, 0), (1, 1), (2, 0)]
    group = 2 * LANES
    source, place = iota((rank, 2 * group), 0), iota((rank, 2 * group), 1)
    inside = place % group
    column_found = (source == 2 * (inside % half) + place // group)
    chosen_part = sum((inside >= half * start).astype(jnp.int32) for start in (3, 5, 6))
    pickers = [exact_bf16(column_found & (chosen_part == i)) for i in range(3)]
    for layer in range(layers):
        first = layer * half
        packed = jnp.concatenate(
            [query[:, (first + t) * LANES:(first + t + 1) * LANES] for t in range(half)], axis=0
        ).astype(jnp.bfloat16)
        factor = in_factor_ref[layer]
        doubled = parts_of(
            jnp.concatenate(
                [jnp.concatenate([factor, zero], axis=1), jnp.concatenate([zero, factor], axis=1)], axis=0
            )
        )
        small = jnp.dot(
            jnp.concatenate([packed, packed], axis=1), jnp.concatenate(doubled[1:], axis=0),
            preferred_element_type=jnp.float32,
        )
        turned_ref[layer] = small + jnp.dot(packed, doubled[0], preferred_element_type=jnp.float32)
        wide = jnp.concatenate([turned_ref[layer, pl.ds(q, half, stride=rows), :] for q in range(rows)], axis=1)
        wide = parts_of(wide)
        stacked = jnp.concatenate([wide[j] for _, j in terms], axis=0)
        by_row = jnp.concatenate(
            [out_factor_ref[layer, pl.ds(parity, half, stride=2), :] for parity in range(2)], axis=0
        )
        sorted_columns = sum(
            jnp.dot(part, picker, preferred_element_type=jnp.float32) for part, picker in zip(parts_of(by_row), pickers)
        )
        quarters = jnp.concatenate(
            [
                sorted_columns[r * half:(r + 1) * half, c * group:c * group + len(terms) * half]
                for r in range(2) for c in range(2)
            ],
            axis=0,
        ).astype(jnp.bfloat16)
        left = jnp.dot(quarters, stacked, preferred_element_type=jnp.float32)
        for q in range(rows):
            part = left[:, q * LANES:(q + 1) * LANES]
            ee, eo, oe, oo = (part[i * half:(i + 1) * half] for i in range(4))
            done = jnp.where(low, ee, oo) + pltpu.roll(jnp.where(low, oe, eo), rank, 1)
            turned_ref[layer, pl.ds(q, half, stride=rows), :] = done
        for t in range(half):
            packed_ref[:, (first + t) * LANES:(first + t + 1) * LANES] = (
                turned_ref[layer, t * rows:(t + 1) * rows, :].astype(jnp.bfloat16)
            )

    slots = cand_ref.shape[1]
    home_rows = home_ref.shape[0]
    wanted = cand_ref[...]
    onehot = (iota((LANES, slots), 0) == wanted % LANES).astype(jnp.float32).astype(jnp.bfloat16)
    home = home_ref[...]
    table = jnp.concatenate([home // per_holder, home % per_holder], axis=0).astype(jnp.float32).astype(jnp.bfloat16)
    found = jnp.dot(table, onehot, preferred_element_type=jnp.float32)
    mine = iota((home_rows, slots), 0) == wanted // LANES
    holder = jnp.sum(jnp.where(mine, found[:home_rows], 0.0), axis=0, keepdims=True)
    within = jnp.sum(jnp.where(mine, found[home_rows:], 0.0), axis=0, keepdims=True)
    at_holder = iota((holders, slots), 0).astype(jnp.float32) == holder
    earlier = exact_bf16(iota((slots, slots), 0) < iota((slots, slots), 1))
    before = jnp.dot(exact_bf16(at_holder), earlier, preferred_element_type=jnp.float32)
    rank_there = jnp.sum(jnp.where(at_holder, before, 0.0), axis=0, keepdims=True)
    ranked = exact_bf16(iota((capacity, slots), 0).astype(jnp.float32) == rank_there)
    asked = lax.dot_general(
        exact_bf16(jnp.where(at_holder, within + 1.0, 0.0)), ranked, (((1,), (1,)), ((), ())),
        preferred_element_type=jnp.float32,
    )
    blocks = [asked[h:h + rows] for h in range(0, holders, rows)]
    spare = packed_ref.shape[1] - width - capacity * len(blocks)
    if spare:
        blocks.append(jnp.zeros((rows, spare), jnp.float32))
    packed_ref[:, width:] = jnp.concatenate(blocks, axis=1).astype(jnp.bfloat16)
    found_ref[...] = jnp.concatenate([holder, rank_there, jnp.zeros((6, slots), jnp.float32)], axis=0)
    copies[-1].wait()


def score_kernel(holders, capacity, *refs):
    packed_refs, pages_ref, out_ref, total, queries = refs[:holders], *refs[holders:]
    me = lax.axis_index("store")
    count, width = pages_ref.shape
    rows = packed_refs[0].shape[0]
    half = capacity // 2
    step = width // CHUNKS
    scores = jnp.zeros((holders * rows, count), jnp.float32)
    for i in range(CHUNKS):
        columns = slice(i * step, (i + 1) * step)
        for k in range(holders):
            queries[k * rows:(k + 1) * rows, columns] = packed_refs[k][:, columns]
        scores = scores + lax.dot_general(
            queries[:, columns], pages_ref[:, columns], (((1,), (1,)), ((), ())), preferred_element_type=jnp.float32
        )
    for k in range(holders):
        start = pl.multiple_of((me ^ k) * rows, rows)
        total[pl.ds(start, rows), :] = scores[k * rows:(k + 1) * rows]
    asked = []
    for k in range(holders):
        notes = packed_refs[k][:, width:].astype(jnp.float32)
        notes = jnp.sum(jnp.where(iota(notes.shape, 0) == me % rows, notes, 0.0), axis=0, keepdims=True)
        mine = notes[:, :capacity]
        for block in range(1, holders // rows):
            mine = jnp.where(me // rows == block, notes[:, block * capacity:(block + 1) * capacity], mine)
        asked.append(mine)
    page = iota((count, holders * half), 0).astype(jnp.float32) + 1.0
    parts = parts_of(total[...])[::-1]
    picked = []
    for side in range(2):
        row = jnp.concatenate([row[:, side * half:(side + 1) * half] for row in asked], axis=1)
        chosen = exact_bf16(page == row)
        picked.append(sum(jnp.dot(part, chosen, preferred_element_type=jnp.float32) for part in parts))
    picked = jnp.concatenate(picked, axis=0).T
    for k in range(holders):
        out_ref[me ^ k] = picked[k * half:(k + 1) * half]


def spread_kernel(holders, groups, count_ref, found_ref, landed_ref, *out_refs):
    half = landed_ref.shape[1]
    slots = found_ref.shape[1]
    total = landed_ref.shape[2] // 2
    at = lax.axis_index("layer")
    share = slots // groups
    used = iota((1, slots), 1) < count_ref[0]
    holder, rank_there = jnp.where(used, found_ref[0:1], float(holders)), found_ref[1:2]
    place = iota((holders * half, slots), 0).astype(jnp.float32)
    parts = parts_of(jnp.concatenate([landed_ref[h] for h in range(holders)], axis=0))[::-1]
    result = jnp.zeros((total, slots), jnp.float32)
    for side in range(2):
        on_side = (rank_there >= half) if side else (rank_there < half)
        target = jnp.where(on_side, holder * half + rank_there - side * half, -1.0)
        chosen = exact_bf16(place == target)
        for part in parts:
            spread = lax.dot_general(part, chosen, (((0,), (0,)), ((), ())), preferred_element_type=jnp.float32)
            result = result + spread[side * total:(side + 1) * total]
    result = result.T
    blocks = []
    for g in range(groups):
        block = result[g * share:(g + 1) * share]
        blocks.append(jnp.concatenate([block[:share // 2], block[share // 2:]], axis=1))
    for step, out_ref in enumerate(out_refs):
        chosen = blocks[0]
        for g in range(1, groups):
            chosen = jnp.where((at + step) % groups == g, blocks[g], chosen)
        out_ref[...] = chosen


def swap(value, axis, distance):
    return lax.ppermute(value, axis, [(i, i ^ distance) for i in range(lax.axis_size(axis))])


def on_device(query_grads, factor_out, factor_in, page_store, page_home, cand_lists, counts):
    holders = lax.axis_size("store")
    groups = lax.axis_size("layer")
    rows, width = query_grads.shape
    layers, rank, _ = factor_out.shape
    per_holder = page_store.shape[0]
    slots = cand_lists.shape[1]
    bf16 = jnp.bfloat16

    capacity = slots // holders
    home = page_home.reshape(-1, LANES)
    sources = [
        pltpu.with_memory_space_constraint(source, pltpu.HBM)
        for source in (query_grads, factor_in, factor_out, home, cand_lists, page_store)
    ]
    notes = max(LANES, holders // rows * capacity)
    packed, pages, found = pl.pallas_call(
        functools.partial(condition_kernel, holders, capacity),
        out_shape=[
            jax.ShapeDtypeStruct((rows, width + notes), bf16),
            pltpu.VMEM(page_store.shape, bf16),
            jax.ShapeDtypeStruct((8, slots), jnp.float32),
        ],
        in_specs=[HBM] * len(sources),
        out_specs=[VMEM] * 3,
        scratch_shapes=[pltpu.VMEM(source.shape, source.dtype) for source in sources[:-1]]
        + [pltpu.SemaphoreType.DMA((len(sources),)), pltpu.VMEM((layers, rows * rank // 2, LANES), jnp.float32)],
        compiler_params=pltpu.CompilerParams(vmem_limit_bytes=10 * 2**20 + 24 * slots * slots),
    )(*sources)

    blocks = [None] * holders
    blocks[0] = packed
    blocks[1] = swap(packed, "store", 1)
    for k in range(2, holders, 2):
        blocks[k] = swap(packed, "store", k)
    for k in range(2, holders, 2):
        blocks[k + 1] = swap(blocks[k], "store", 1)

    total = holders * rows
    bytes_in = 2 * holders * rows * (width + notes) + 2 * per_holder * width
    asked = pl.pallas_call(
        functools.partial(score_kernel, holders, capacity),
        out_shape=jax.ShapeDtypeStruct((holders, capacity // 2, 2 * total), jnp.float32),
        in_specs=[VMEM] * (holders + 1),
        out_specs=VMEM,
        scratch_shapes=[pltpu.VMEM((total, per_holder), jnp.float32), pltpu.VMEM((total, width), bf16)],
        compiler_params=pltpu.CompilerParams(vmem_limit_bytes=8 * 2**20 + 2 * bytes_in + 48 * total * slots),
    )(*blocks, pltpu.with_memory_space_constraint(pages, pltpu.VMEM))

    landed = lax.all_to_all(asked, "store", split_axis=0, concat_axis=0, tiled=True)
    share = slots // groups
    terms = pl.pallas_call(
        functools.partial(spread_kernel, holders, groups),
        out_shape=[jax.ShapeDtypeStruct((share // 2, 2 * total), jnp.float32)] * groups,
        in_specs=[SMEM] + [VMEM] * 2,
        out_specs=[VMEM] * groups,
        compiler_params=pltpu.CompilerParams(vmem_limit_bytes=4 * 2**20 + 64 * total * slots),
    )(counts, found, landed)
    summed = terms[0]
    for step in range(1, groups):
        summed = summed + lax.ppermute(terms[step], "layer", [(g, (g + step) % groups) for g in range(groups)])
    return jnp.concatenate([summed[:, :total], summed[:, total:]], axis=0)[None]


def solution(mesh):
    placed = (
        P("store", "layer"),
        P("layer", None, None),
        P("layer", None, None),
        P("store", "layer"),
        P(),
        P("store", None),
        P("store"),
    )
    return jax.shard_map(
        on_device, mesh=mesh, in_specs=placed, out_specs=P("store", "layer", None), check_vma=False
    )
```

```python
import functools

import jax
import jax.numpy as jnp
from jax import lax
from jax.experimental import pallas as pl
from jax.experimental.pallas import tpu as pltpu
from jax.sharding import PartitionSpec as P

VMEM = pl.BlockSpec(memory_space=pltpu.VMEM)
SMEM = pl.BlockSpec(memory_space=pltpu.SMEM)
HBM = pl.BlockSpec(memory_space=pltpu.HBM)
LANES = 128
CHUNKS = 4


def iota(shape, dimension):
    return lax.broadcasted_iota(jnp.int32, shape, dimension)


def parts_of(value):
    parts = []
    for _ in range(3):
        part = value.astype(jnp.bfloat16)
        value = value - part.astype(jnp.float32)
        parts.append(part)
    return parts


def exact_bf16(value):
    return value.astype(jnp.float32).astype(jnp.bfloat16)


def condition_kernel(holders, capacity, *refs):
    sources, packed_ref, pages_ref, found_ref, landing, arrived, turned_ref = refs[:6], *refs[6:9], refs[9:14], *refs[14:]
    copies = [
        pltpu.make_async_copy(source, target, arrived.at[i])
        for i, (source, target) in enumerate(zip(sources, landing + (pages_ref,)))
    ]
    for copy in copies:
        copy.start()
    for copy in copies[:-1]:
        copy.wait()
    query_ref, in_factor_ref, out_factor_ref, home_ref, cand_ref = landing
    per_holder = pages_ref.shape[0]
    rows, width = query_ref.shape
    layers, rank, _ = in_factor_ref.shape
    half = rank // 2
    query = query_ref[...].astype(jnp.float32)
    low = iota((half, LANES), 1) < rank
    zero = jnp.zeros((rank, rank), jnp.float32)
    terms = [(0, 0), (0, 1), (0, 2), (1, 0), (1, 1), (2, 0)]
    group = 2 * LANES
    source, place = iota((rank, 2 * group), 0), iota((rank, 2 * group), 1)
    inside = place % group
    column_found = (source == 2 * (inside % half) + place // group)
    chosen_part = sum((inside >= half * start).astype(jnp.int32) for start in (3, 5, 6))
    pickers = [exact_bf16(column_found & (chosen_part == i)) for i in range(3)]
    for layer in range(layers):
        first = layer * half
        packed = jnp.concatenate(
            [query[:, (first + t) * LANES:(first + t + 1) * LANES] for t in range(half)], axis=0
        ).astype(jnp.bfloat16)
        factor = in_factor_ref[layer]
        doubled = parts_of(
            jnp.concatenate(
                [jnp.concatenate([factor, zero], axis=1), jnp.concatenate([zero, factor], axis=1)], axis=0
            )
        )
        small = jnp.dot(
            jnp.concatenate([packed, packed], axis=1), jnp.concatenate(doubled[1:], axis=0),
            preferred_element_type=jnp.float32,
        )
        turned_ref[layer] = small + jnp.dot(packed, doubled[0], preferred_element_type=jnp.float32)
        wide = jnp.concatenate([turned_ref[layer, pl.ds(q, half, stride=rows), :] for q in range(rows)], axis=1)
        wide = parts_of(wide)
        stacked = jnp.concatenate([wide[j] for _, j in terms], axis=0)
        by_row = jnp.concatenate(
            [out_factor_ref[layer, pl.ds(parity, half, stride=2), :] for parity in range(2)], axis=0
        )
        sorted_columns = sum(
            jnp.dot(part, picker, preferred_element_type=jnp.float32) for part, picker in zip(parts_of(by_row), pickers)
        )
        quarters = jnp.concatenate(
            [
                sorted_columns[r * half:(r + 1) * half, c * group:c * group + len(terms) * half]
                for r in range(2) for c in range(2)
            ],
            axis=0,
        ).astype(jnp.bfloat16)
        left = jnp.dot(quarters, stacked, preferred_element_type=jnp.float32)
        for q in range(rows):
            part = left[:, q * LANES:(q + 1) * LANES]
            ee, eo, oe, oo = (part[i * half:(i + 1) * half] for i in range(4))
            done = jnp.where(low, ee, oo) + pltpu.roll(jnp.where(low, oe, eo), rank, 1)
            turned_ref[layer, pl.ds(q, half, stride=rows), :] = done
        for t in range(half):
            packed_ref[:, (first + t) * LANES:(first + t + 1) * LANES] = (
                turned_ref[layer, t * rows:(t + 1) * rows, :].astype(jnp.bfloat16)
            )

    slots = cand_ref.shape[1]
    home_rows = home_ref.shape[0]
    wanted = cand_ref[...]
    onehot = (iota((LANES, slots), 0) == wanted % LANES).astype(jnp.float32).astype(jnp.bfloat16)
    home = home_ref[...]
    table = jnp.concatenate([home // per_holder, home % per_holder], axis=0).astype(jnp.float32).astype(jnp.bfloat16)
    found = jnp.dot(table, onehot, preferred_element_type=jnp.float32)
    mine = iota((home_rows, slots), 0) == wanted // LANES
    holder = jnp.sum(jnp.where(mine, found[:home_rows], 0.0), axis=0, keepdims=True)
    within = jnp.sum(jnp.where(mine, found[home_rows:], 0.0), axis=0, keepdims=True)
    at_holder = iota((holders, slots), 0).astype(jnp.float32) == holder
    earlier = exact_bf16(iota((slots, slots), 0) < iota((slots, slots), 1))
    before = jnp.dot(exact_bf16(at_holder), earlier, preferred_element_type=jnp.float32)
    rank_there = jnp.sum(jnp.where(at_holder, before, 0.0), axis=0, keepdims=True)
    ranked = exact_bf16(iota((capacity, slots), 0).astype(jnp.float32) == rank_there)
    asked = lax.dot_general(
        exact_bf16(jnp.where(at_holder, within + 1.0, 0.0)), ranked, (((1,), (1,)), ((), ())),
        preferred_element_type=jnp.float32,
    )
    blocks = [asked[h:h + rows] for h in range(0, holders, rows)]
    spare = packed_ref.shape[1] - width - capacity * len(blocks)
    if spare:
        blocks.append(jnp.zeros((rows, spare), jnp.float32))
    packed_ref[:, width:] = jnp.concatenate(blocks, axis=1).astype(jnp.bfloat16)
    found_ref[...] = jnp.concatenate([holder, rank_there, jnp.zeros((6, slots), jnp.float32)], axis=0)
    copies[-1].wait()


def score_kernel(holders, capacity, *refs):
    count_ref, found_ref, packed_refs = *refs[:2], refs[2:2 + holders]
    pages_ref, out_ref, used_ref, total, queries = refs[2 + holders:]
    me = lax.axis_index("store")
    count, width = pages_ref.shape
    rows = packed_refs[0].shape[0]
    half = capacity // 2
    step = width // CHUNKS
    scores = jnp.zeros((holders * rows, count), jnp.float32)
    for i in range(CHUNKS):
        columns = slice(i * step, (i + 1) * step)
        for k in range(holders):
            queries[k * rows:(k + 1) * rows, columns] = packed_refs[k][:, columns]
        scores = scores + lax.dot_general(
            queries[:, columns], pages_ref[:, columns], (((1,), (1,)), ((), ())), preferred_element_type=jnp.float32
        )
    for k in range(holders):
        start = pl.multiple_of((me ^ k) * rows, rows)
        total[pl.ds(start, rows), :] = scores[k * rows:(k + 1) * rows]
    asked = []
    for k in range(holders):
        notes = packed_refs[k][:, width:].astype(jnp.float32)
        notes = jnp.sum(jnp.where(iota(notes.shape, 0) == me % rows, notes, 0.0), axis=0, keepdims=True)
        mine = notes[:, :capacity]
        for block in range(1, holders // rows):
            mine = jnp.where(me // rows == block, notes[:, block * capacity:(block + 1) * capacity], mine)
        asked.append(mine)
    page = iota((count, holders * half), 0).astype(jnp.float32) + 1.0
    parts = parts_of(total[...])[::-1]
    picked = []
    for side in range(2):
        row = jnp.concatenate([row[:, side * half:(side + 1) * half] for row in asked], axis=1)
        chosen = exact_bf16(page == row)
        picked.append(sum(jnp.dot(part, chosen, preferred_element_type=jnp.float32) for part in parts))
    used_ref[...] = found_ref[...]
    own_slots = found_ref.shape[1]
    used_ref[0:1] = jnp.where(iota((1, own_slots), 1) < count_ref[0], found_ref[0:1], float(holders))
    picked = jnp.concatenate(picked, axis=0).T
    for k in range(holders):
        out_ref[me ^ k] = picked[k * half:(k + 1) * half]


def spread_kernel(holders, groups, found_ref, landed_ref, *out_refs):
    half = landed_ref.shape[1]
    slots = found_ref.shape[1]
    total = landed_ref.shape[2] // 2
    at = lax.axis_index("layer")
    share = slots // groups
    holder, rank_there = found_ref[0:1], found_ref[1:2]
    place = iota((holders * half, slots), 0).astype(jnp.float32)
    parts = parts_of(jnp.concatenate([landed_ref[h] for h in range(holders)], axis=0))[::-1]
    result = jnp.zeros((total, slots), jnp.float32)
    for side in range(2):
        on_side = (rank_there >= half) if side else (rank_there < half)
        target = jnp.where(on_side, holder * half + rank_there - side * half, -1.0)
        chosen = exact_bf16(place == target)
        for part in parts:
            spread = lax.dot_general(part, chosen, (((0,), (0,)), ((), ())), preferred_element_type=jnp.float32)
            result = result + spread[side * total:(side + 1) * total]
    result = result.T
    blocks = []
    for g in range(groups):
        block = result[g * share:(g + 1) * share]
        blocks.append(jnp.concatenate([block[:share // 2], block[share // 2:]], axis=1))
    for step, out_ref in enumerate(out_refs):
        chosen = blocks[0]
        for g in range(1, groups):
            chosen = jnp.where((at + step) % groups == g, blocks[g], chosen)
        out_ref[...] = chosen


def swap(value, axis, distance):
    return lax.ppermute(value, axis, [(i, i ^ distance) for i in range(lax.axis_size(axis))])


def on_device(query_grads, factor_out, factor_in, page_store, page_home, cand_lists, counts):
    holders = lax.axis_size("store")
    groups = lax.axis_size("layer")
    rows, width = query_grads.shape
    layers, rank, _ = factor_out.shape
    per_holder = page_store.shape[0]
    slots = cand_lists.shape[1]
    bf16 = jnp.bfloat16

    capacity = slots // holders
    home = page_home.reshape(-1, LANES)
    sources = [
        pltpu.with_memory_space_constraint(source, pltpu.HBM)
        for source in (query_grads, factor_in, factor_out, home, cand_lists, page_store)
    ]
    notes = max(LANES, holders // rows * capacity)
    packed, pages, found = pl.pallas_call(
        functools.partial(condition_kernel, holders, capacity),
        out_shape=[
            jax.ShapeDtypeStruct((rows, width + notes), bf16),
            pltpu.VMEM(page_store.shape, bf16),
            jax.ShapeDtypeStruct((8, slots), jnp.float32),
        ],
        in_specs=[HBM] * len(sources),
        out_specs=[VMEM] * 3,
        scratch_shapes=[pltpu.VMEM(source.shape, source.dtype) for source in sources[:-1]]
        + [pltpu.SemaphoreType.DMA((len(sources),)), pltpu.VMEM((layers, rows * rank // 2, LANES), jnp.float32)],
        compiler_params=pltpu.CompilerParams(vmem_limit_bytes=10 * 2**20 + 24 * slots * slots),
    )(*sources)

    blocks = [None] * holders
    blocks[0] = packed
    for k in reversed(range(2, holders, 2)):
        blocks[k] = swap(packed, "store", k)
    blocks[1] = swap(packed, "store", 1)
    for k in reversed(range(2, holders, 2)):
        blocks[k + 1] = swap(blocks[k], "store", 1)

    total = holders * rows
    bytes_in = 2 * holders * rows * (width + notes) + 2 * per_holder * width
    asked, used = pl.pallas_call(
        functools.partial(score_kernel, holders, capacity),
        out_shape=[
            jax.ShapeDtypeStruct((holders, capacity // 2, 2 * total), jnp.float32),
            jax.ShapeDtypeStruct(found.shape, jnp.float32),
        ],
        in_specs=[SMEM] + [VMEM] * (holders + 2),
        out_specs=[VMEM] * 2,
        scratch_shapes=[pltpu.VMEM((total, per_holder), jnp.float32), pltpu.VMEM((total, width), bf16)],
        compiler_params=pltpu.CompilerParams(vmem_limit_bytes=8 * 2**20 + 2 * bytes_in + 48 * total * slots),
    )(counts, found, *blocks, pltpu.with_memory_space_constraint(pages, pltpu.VMEM))

    landed = lax.all_to_all(asked, "store", split_axis=0, concat_axis=0, tiled=True)
    share = slots // groups
    terms = pl.pallas_call(
        functools.partial(spread_kernel, holders, groups),
        out_shape=[jax.ShapeDtypeStruct((share // 2, 2 * total), jnp.float32)] * groups,
        in_specs=[VMEM] * 2,
        out_specs=[VMEM] * groups,
        compiler_params=pltpu.CompilerParams(vmem_limit_bytes=4 * 2**20 + 64 * total * slots),
    )(used, landed)
    summed = terms[0]
    for step in range(1, groups):
        summed = summed + lax.ppermute(terms[step], "layer", [(g, (g + step) % groups) for g in range(groups)])
    return jnp.concatenate([summed[:, :total], summed[:, total:]], axis=0)[None]


def solution(mesh):
    placed = (
        P("store", "layer"),
        P("layer", None, None),
        P("layer", None, None),
        P("store", "layer"),
        P(),
        P("store", None),
        P("store"),
    )
    return jax.shard_map(
        on_device, mesh=mesh, in_specs=placed, out_specs=P("store", "layer", None), check_vma=False
    )
```

```python
import functools

import jax
import jax.numpy as jnp
from jax import lax
from jax.experimental import pallas as pl
from jax.experimental.pallas import tpu as pltpu
from jax.sharding import PartitionSpec as P

VMEM = pl.BlockSpec(memory_space=pltpu.VMEM)
SMEM = pl.BlockSpec(memory_space=pltpu.SMEM)
HBM = pl.BlockSpec(memory_space=pltpu.HBM)
LANES = 128
CHUNKS = 2


def iota(shape, dimension):
    return lax.broadcasted_iota(jnp.int32, shape, dimension)


def parts_of(value):
    parts = []
    for _ in range(3):
        part = value.astype(jnp.bfloat16)
        value = value - part.astype(jnp.float32)
        parts.append(part)
    return parts


def exact_bf16(value):
    return value.astype(jnp.float32).astype(jnp.bfloat16)


def condition_kernel(holders, capacity, *refs):
    sources, packed_refs, pages_ref, found_ref, landing, arrived, turned_ref = (
        refs[:6], refs[6:8], *refs[8:10], refs[10:15], *refs[15:]
    )
    copies = [
        pltpu.make_async_copy(source, target, arrived.at[i])
        for i, (source, target) in enumerate(zip(sources, landing + (pages_ref,)))
    ]
    for copy in copies:
        copy.start()
    for copy in copies[:-1]:
        copy.wait()
    query_ref, in_factor_ref, out_factor_ref, home_ref, cand_ref = landing
    per_holder = pages_ref.shape[0]
    rows, width = query_ref.shape
    layers, rank, _ = in_factor_ref.shape
    half = rank // 2
    query = query_ref[...].astype(jnp.float32)
    low = iota((half, LANES), 1) < rank
    zero = jnp.zeros((rank, rank), jnp.float32)
    terms = [(0, 0), (0, 1), (0, 2), (1, 0), (1, 1), (2, 0)]
    group = 2 * LANES
    source, place = iota((rank, 2 * group), 0), iota((rank, 2 * group), 1)
    inside = place % group
    column_found = (source == 2 * (inside % half) + place // group)
    chosen_part = sum((inside >= half * start).astype(jnp.int32) for start in (3, 5, 6))
    pickers = [exact_bf16(column_found & (chosen_part == i)) for i in range(3)]
    for layer in range(layers):
        first = layer * half
        packed = jnp.concatenate(
            [query[:, (first + t) * LANES:(first + t + 1) * LANES] for t in range(half)], axis=0
        ).astype(jnp.bfloat16)
        factor = in_factor_ref[layer]
        doubled = parts_of(
            jnp.concatenate(
                [jnp.concatenate([factor, zero], axis=1), jnp.concatenate([zero, factor], axis=1)], axis=0
            )
        )
        small = jnp.dot(
            jnp.concatenate([packed, packed], axis=1), jnp.concatenate(doubled[1:], axis=0),
            preferred_element_type=jnp.float32,
        )
        turned_ref[layer] = small + jnp.dot(packed, doubled[0], preferred_element_type=jnp.float32)
        wide = jnp.concatenate([turned_ref[layer, pl.ds(q, half, stride=rows), :] for q in range(rows)], axis=1)
        wide = parts_of(wide)
        stacked = jnp.concatenate([wide[j] for _, j in terms], axis=0)
        by_row = jnp.concatenate(
            [out_factor_ref[layer, pl.ds(parity, half, stride=2), :] for parity in range(2)], axis=0
        )
        sorted_columns = sum(
            jnp.dot(part, picker, preferred_element_type=jnp.float32) for part, picker in zip(parts_of(by_row), pickers)
        )
        quarters = jnp.concatenate(
            [
                sorted_columns[r * half:(r + 1) * half, c * group:c * group + len(terms) * half]
                for r in range(2) for c in range(2)
            ],
            axis=0,
        ).astype(jnp.bfloat16)
        left = jnp.dot(quarters, stacked, preferred_element_type=jnp.float32)
        for q in range(rows):
            part = left[:, q * LANES:(q + 1) * LANES]
            ee, eo, oe, oo = (part[i * half:(i + 1) * half] for i in range(4))
            done = jnp.where(low, ee, oo) + pltpu.roll(jnp.where(low, oe, eo), rank, 1)
            turned_ref[layer, pl.ds(q, half, stride=rows), :] = done
        for t in range(half):
            packed_ref, column = packed_refs[2 * layer // layers], (first + t) * LANES % (width // 2)
            packed_ref[:, column:column + LANES] = turned_ref[layer, t * rows:(t + 1) * rows, :].astype(jnp.bfloat16)

    slots = cand_ref.shape[1]
    home_rows = home_ref.shape[0]
    wanted = cand_ref[...]
    onehot = (iota((LANES, slots), 0) == wanted % LANES).astype(jnp.float32).astype(jnp.bfloat16)
    home = home_ref[...]
    table = jnp.concatenate([home // per_holder, home % per_holder], axis=0).astype(jnp.float32).astype(jnp.bfloat16)
    found = jnp.dot(table, onehot, preferred_element_type=jnp.float32)
    mine = iota((home_rows, slots), 0) == wanted // LANES
    holder = jnp.sum(jnp.where(mine, found[:home_rows], 0.0), axis=0, keepdims=True)
    within = jnp.sum(jnp.where(mine, found[home_rows:], 0.0), axis=0, keepdims=True)
    at_holder = iota((holders, slots), 0).astype(jnp.float32) == holder
    earlier = exact_bf16(iota((slots, slots), 0) < iota((slots, slots), 1))
    before = jnp.dot(exact_bf16(at_holder), earlier, preferred_element_type=jnp.float32)
    rank_there = jnp.sum(jnp.where(at_holder, before, 0.0), axis=0, keepdims=True)
    ranked = exact_bf16(iota((capacity, slots), 0).astype(jnp.float32) == rank_there)
    asked = lax.dot_general(
        exact_bf16(jnp.where(at_holder, within + 1.0, 0.0)), ranked, (((1,), (1,)), ((), ())),
        preferred_element_type=jnp.float32,
    )
    blocks = [asked[h:h + rows] for h in range(0, holders, rows)]
    spare = packed_refs[1].shape[1] - width // 2 - capacity * len(blocks)
    if spare:
        blocks.append(jnp.zeros((rows, spare), jnp.float32))
    packed_refs[1][:, width // 2:] = jnp.concatenate(blocks, axis=1).astype(jnp.bfloat16)
    found_ref[...] = jnp.concatenate([holder, rank_there, jnp.zeros((6, slots), jnp.float32)], axis=0)
    copies[-1].wait()


def scores_of(packed_refs, pages_ref, queries, first):
    width = queries.shape[1]
    rows = packed_refs[0].shape[0]
    scores = jnp.zeros((queries.shape[0], pages_ref.shape[0]), jnp.float32)
    step = width // CHUNKS
    for i in range(CHUNKS):
        columns = slice(i * step, (i + 1) * step)
        for k, ref in enumerate(packed_refs):
            queries[k * rows:(k + 1) * rows, columns] = ref[:, columns]
        scores = scores + lax.dot_general(
            queries[:, columns], pages_ref[:, first + i * step:first + (i + 1) * step], (((1,), (1,)), ((), ())),
            preferred_element_type=jnp.float32,
        )
    return scores


def first_kernel(holders, *refs):
    packed_refs, pages_ref, scores_ref, queries = refs[:holders], *refs[holders:]
    scores_ref[...] = scores_of(packed_refs, pages_ref, queries, 0)


def score_kernel(holders, capacity, *refs):
    count_ref, found_ref, begun_ref, packed_refs = *refs[:3], refs[3:3 + holders]
    pages_ref, out_ref, used_ref, total, queries = refs[3 + holders:]
    me = lax.axis_index("store")
    count = pages_ref.shape[0]
    width = queries.shape[1]
    rows = packed_refs[0].shape[0]
    half = capacity // 2
    scores = begun_ref[...] + scores_of(packed_refs, pages_ref, queries, width)
    for k in range(holders):
        start = pl.multiple_of((me ^ k) * rows, rows)
        total[pl.ds(start, rows), :] = scores[k * rows:(k + 1) * rows]
    asked = []
    for k in range(holders):
        notes = packed_refs[k][:, width:].astype(jnp.float32)
        notes = jnp.sum(jnp.where(iota(notes.shape, 0) == me % rows, notes, 0.0), axis=0, keepdims=True)
        mine = notes[:, :capacity]
        for block in range(1, holders // rows):
            mine = jnp.where(me // rows == block, notes[:, block * capacity:(block + 1) * capacity], mine)
        asked.append(mine)
    page = iota((count, holders * half), 0).astype(jnp.float32) + 1.0
    parts = parts_of(total[...])[::-1]
    picked = []
    for side in range(2):
        row = jnp.concatenate([row[:, side * half:(side + 1) * half] for row in asked], axis=1)
        chosen = exact_bf16(page == row)
        picked.append(sum(jnp.dot(part, chosen, preferred_element_type=jnp.float32) for part in parts))
    used_ref[...] = found_ref[...]
    own_slots = found_ref.shape[1]
    used_ref[0:1] = jnp.where(iota((1, own_slots), 1) < count_ref[0], found_ref[0:1], float(holders))
    picked = jnp.concatenate(picked, axis=0).T
    for k in range(holders):
        out_ref[me ^ k] = picked[k * half:(k + 1) * half]


def spread_kernel(holders, groups, found_ref, landed_ref, *out_refs):
    half = landed_ref.shape[1]
    slots = found_ref.shape[1]
    total = landed_ref.shape[2] // 2
    at = lax.axis_index("layer")
    share = slots // groups
    holder, rank_there = found_ref[0:1], found_ref[1:2]
    place = iota((holders * half, slots), 0).astype(jnp.float32)
    parts = parts_of(jnp.concatenate([landed_ref[h] for h in range(holders)], axis=0))[::-1]
    result = jnp.zeros((total, slots), jnp.float32)
    for side in range(2):
        on_side = (rank_there >= half) if side else (rank_there < half)
        target = jnp.where(on_side, holder * half + rank_there - side * half, -1.0)
        chosen = exact_bf16(place == target)
        for part in parts:
            spread = lax.dot_general(part, chosen, (((0,), (0,)), ((), ())), preferred_element_type=jnp.float32)
            result = result + spread[side * total:(side + 1) * total]
    result = result.T
    blocks = []
    for g in range(groups):
        block = result[g * share:(g + 1) * share]
        blocks.append(jnp.concatenate([block[:share // 2], block[share // 2:]], axis=1))
    for step, out_ref in enumerate(out_refs):
        chosen = blocks[0]
        for g in range(1, groups):
            chosen = jnp.where((at + step) % groups == g, blocks[g], chosen)
        out_ref[...] = chosen


def swap(value, axis, distance):
    return lax.ppermute(value, axis, [(i, i ^ distance) for i in range(lax.axis_size(axis))])


def on_device(query_grads, factor_out, factor_in, page_store, page_home, cand_lists, counts):
    holders = lax.axis_size("store")
    groups = lax.axis_size("layer")
    rows, width = query_grads.shape
    layers, rank, _ = factor_out.shape
    per_holder = page_store.shape[0]
    slots = cand_lists.shape[1]
    bf16 = jnp.bfloat16

    capacity = slots // holders
    home = page_home.reshape(-1, LANES)
    sources = [
        pltpu.with_memory_space_constraint(source, pltpu.HBM)
        for source in (query_grads, factor_in, factor_out, home, cand_lists, page_store)
    ]
    notes = max(LANES, holders // rows * capacity)
    *packed, pages, found = pl.pallas_call(
        functools.partial(condition_kernel, holders, capacity),
        out_shape=[
            jax.ShapeDtypeStruct((rows, width // 2), bf16),
            jax.ShapeDtypeStruct((rows, width // 2 + notes), bf16),
            pltpu.VMEM(page_store.shape, bf16),
            jax.ShapeDtypeStruct((8, slots), jnp.float32),
        ],
        in_specs=[HBM] * len(sources),
        out_specs=[VMEM] * 4,
        scratch_shapes=[pltpu.VMEM(source.shape, source.dtype) for source in sources[:-1]]
        + [pltpu.SemaphoreType.DMA((len(sources),)), pltpu.VMEM((layers, rows * rank // 2, LANES), jnp.float32)],
        compiler_params=pltpu.CompilerParams(vmem_limit_bytes=10 * 2**20 + 24 * slots * slots),
    )(*sources)

    across = list(reversed(range(2, holders, 2)))
    blocks = [[part] + [None] * (holders - 1) for part in packed]
    for part in range(2):
        for k in across:
            blocks[part][k] = swap(packed[part], "store", k)
    for part in range(2):
        blocks[part][1] = swap(packed[part], "store", 1)
        for k in across:
            blocks[part][k + 1] = swap(blocks[part][k], "store", 1)

    total = holders * rows
    bytes_in = 2 * holders * rows * (width + notes) + 2 * per_holder * width
    pages = pltpu.with_memory_space_constraint(pages, pltpu.VMEM)
    begun = pl.pallas_call(
        functools.partial(first_kernel, holders),
        out_shape=jax.ShapeDtypeStruct((total, per_holder), jnp.float32),
        in_specs=[VMEM] * (holders + 1),
        out_specs=VMEM,
        scratch_shapes=[pltpu.VMEM((total, width // 2), bf16)],
        compiler_params=pltpu.CompilerParams(vmem_limit_bytes=8 * 2**20 + 2 * bytes_in),
        cost_estimate=pl.CostEstimate(
            flops=total * per_holder * width, bytes_accessed=per_holder * width, transcendentals=0
        ),
    )(*blocks[0], pages)
    asked, used = pl.pallas_call(
        functools.partial(score_kernel, holders, capacity),
        out_shape=[
            jax.ShapeDtypeStruct((holders, capacity // 2, 2 * total), jnp.float32),
            jax.ShapeDtypeStruct(found.shape, jnp.float32),
        ],
        in_specs=[SMEM] + [VMEM] * (holders + 3),
        out_specs=[VMEM] * 2,
        scratch_shapes=[pltpu.VMEM((total, per_holder), jnp.float32), pltpu.VMEM((total, width // 2), bf16)],
        compiler_params=pltpu.CompilerParams(vmem_limit_bytes=8 * 2**20 + 2 * bytes_in + 48 * total * slots),
    )(counts, found, begun, *blocks[1], pages)

    landed = lax.all_to_all(asked, "store", split_axis=0, concat_axis=0, tiled=True)
    share = slots // groups
    terms = pl.pallas_call(
        functools.partial(spread_kernel, holders, groups),
        out_shape=[jax.ShapeDtypeStruct((share // 2, 2 * total), jnp.float32)] * groups,
        in_specs=[VMEM] * 2,
        out_specs=[VMEM] * groups,
        compiler_params=pltpu.CompilerParams(vmem_limit_bytes=4 * 2**20 + 64 * total * slots),
    )(used, landed)
    summed = terms[0]
    for step in range(1, groups):
        summed = summed + lax.ppermute(terms[step], "layer", [(g, (g + step) % groups) for g in range(groups)])
    return jnp.concatenate([summed[:, :total], summed[:, total:]], axis=0)[None]


def solution(mesh):
    placed = (
        P("store", "layer"),
        P("layer", None, None),
        P("layer", None, None),
        P("store", "layer"),
        P(),
        P("store", None),
        P("store"),
    )
    return jax.shard_map(
        on_device, mesh=mesh, in_specs=placed, out_specs=P("store", "layer", None), check_vma=False
    )
```

```python
import functools

import jax
import jax.numpy as jnp
from jax import lax
from jax.experimental import pallas as pl
from jax.experimental.pallas import tpu as pltpu
from jax.sharding import PartitionSpec as P

VMEM = pl.BlockSpec(memory_space=pltpu.VMEM)
SMEM = pl.BlockSpec(memory_space=pltpu.SMEM)
HBM = pl.BlockSpec(memory_space=pltpu.HBM)
LANES = 128
CHUNKS = 4


def iota(shape, dimension):
    return lax.broadcasted_iota(jnp.int32, shape, dimension)


def kept_distances(holders):
    return [0] + [k + 1 for k in range(2, holders, 2)]


def parts_of(value):
    parts = []
    for _ in range(3):
        part = value.astype(jnp.bfloat16)
        value = value - part.astype(jnp.float32)
        parts.append(part)
    return parts


def exact_bf16(value):
    return value.astype(jnp.float32).astype(jnp.bfloat16)


def condition_kernel(holders, capacity, per_holder, *refs):
    sources, packed_ref, again_ref, found_ref, landing, arrived, turned_ref = refs[:5], *refs[5:8], refs[8:13], *refs[13:]
    copies = [
        pltpu.make_async_copy(source, target, arrived.at[i])
        for i, (source, target) in enumerate(zip(sources, landing))
    ]
    for copy in copies:
        copy.start()
    for copy in copies:
        copy.wait()
    query_ref, in_factor_ref, out_factor_ref, home_ref, cand_ref = landing
    rows, width = query_ref.shape
    layers, rank, _ = in_factor_ref.shape
    half = rank // 2
    query = query_ref[...].astype(jnp.float32)
    low = iota((half, LANES), 1) < rank
    zero = jnp.zeros((rank, rank), jnp.float32)
    terms = [(0, 0), (0, 1), (0, 2), (1, 0), (1, 1), (2, 0)]
    group = 2 * LANES
    source, place = iota((rank, 2 * group), 0), iota((rank, 2 * group), 1)
    inside = place % group
    column_found = (source == 2 * (inside % half) + place // group)
    chosen_part = sum((inside >= half * start).astype(jnp.int32) for start in (3, 5, 6))
    pickers = [exact_bf16(column_found & (chosen_part == i)) for i in range(3)]
    for layer in range(layers):
        first = layer * half
        packed = jnp.concatenate(
            [query[:, (first + t) * LANES:(first + t + 1) * LANES] for t in range(half)], axis=0
        ).astype(jnp.bfloat16)
        factor = in_factor_ref[layer]
        doubled = parts_of(
            jnp.concatenate(
                [jnp.concatenate([factor, zero], axis=1), jnp.concatenate([zero, factor], axis=1)], axis=0
            )
        )
        small = jnp.dot(
            jnp.concatenate([packed, packed], axis=1), jnp.concatenate(doubled[1:], axis=0),
            preferred_element_type=jnp.float32,
        )
        turned_ref[layer] = small + jnp.dot(packed, doubled[0], preferred_element_type=jnp.float32)
        wide = jnp.concatenate([turned_ref[layer, pl.ds(q, half, stride=rows), :] for q in range(rows)], axis=1)
        wide = parts_of(wide)
        stacked = jnp.concatenate([wide[j] for _, j in terms], axis=0)
        by_row = jnp.concatenate(
            [out_factor_ref[layer, pl.ds(parity, half, stride=2), :] for parity in range(2)], axis=0
        )
        sorted_columns = sum(
            jnp.dot(part, picker, preferred_element_type=jnp.float32) for part, picker in zip(parts_of(by_row), pickers)
        )
        quarters = jnp.concatenate(
            [
                sorted_columns[r * half:(r + 1) * half, c * group:c * group + len(terms) * half]
                for r in range(2) for c in range(2)
            ],
            axis=0,
        ).astype(jnp.bfloat16)
        left = jnp.dot(quarters, stacked, preferred_element_type=jnp.float32)
        for q in range(rows):
            part = left[:, q * LANES:(q + 1) * LANES]
            ee, eo, oe, oo = (part[i * half:(i + 1) * half] for i in range(4))
            done = jnp.where(low, ee, oo) + pltpu.roll(jnp.where(low, oe, eo), rank, 1)
            turned_ref[layer, pl.ds(q, half, stride=rows), :] = done
        for t in range(half):
            packed_ref[:, (first + t) * LANES:(first + t + 1) * LANES] = (
                turned_ref[layer, t * rows:(t + 1) * rows, :].astype(jnp.bfloat16)
            )

    slots = cand_ref.shape[1]
    home_rows = home_ref.shape[0]
    wanted = cand_ref[...]
    onehot = (iota((LANES, slots), 0) == wanted % LANES).astype(jnp.float32).astype(jnp.bfloat16)
    home = home_ref[...]
    table = jnp.concatenate([home // per_holder, home % per_holder], axis=0).astype(jnp.float32).astype(jnp.bfloat16)
    found = jnp.dot(table, onehot, preferred_element_type=jnp.float32)
    mine = iota((home_rows, slots), 0) == wanted // LANES
    holder = jnp.sum(jnp.where(mine, found[:home_rows], 0.0), axis=0, keepdims=True)
    within = jnp.sum(jnp.where(mine, found[home_rows:], 0.0), axis=0, keepdims=True)
    at_holder = iota((holders, slots), 0).astype(jnp.float32) == holder
    earlier = exact_bf16(iota((slots, slots), 0) < iota((slots, slots), 1))
    before = jnp.dot(exact_bf16(at_holder), earlier, preferred_element_type=jnp.float32)
    rank_there = jnp.sum(jnp.where(at_holder, before, 0.0), axis=0, keepdims=True)
    ranked = exact_bf16(iota((capacity, slots), 0).astype(jnp.float32) == rank_there)
    asked = lax.dot_general(
        exact_bf16(jnp.where(at_holder, within + 1.0, 0.0)), ranked, (((1,), (1,)), ((), ())),
        preferred_element_type=jnp.float32,
    )
    blocks = [asked[h:h + rows] for h in range(0, holders, rows)]
    spare = packed_ref.shape[1] - width - capacity * len(blocks)
    if spare:
        blocks.append(jnp.zeros((rows, spare), jnp.float32))
    packed_ref[:, width:] = jnp.concatenate(blocks, axis=1).astype(jnp.bfloat16)
    again_ref[...] = packed_ref[...]
    found_ref[...] = jnp.concatenate([holder, rank_there, jnp.zeros((6, slots), jnp.float32)], axis=0)


def load_kernel(block_ref, source_ref, same_block_ref, target_ref, arrived):
    copy = pltpu.make_async_copy(source_ref, target_ref, arrived)
    copy.start()
    copy.wait()


def score_kernel(holders, capacity, *refs):
    count_ref, found_ref, packed_refs = *refs[:2], refs[2:2 + holders][::-1]
    pages_ref, keep_ref, send_ref, used_ref, total, queries = refs[2 + holders:]
    me = lax.axis_index("store")
    count, width = pages_ref.shape
    rows = packed_refs[0].shape[0]
    half = capacity // 2
    step = width // CHUNKS
    scores = jnp.zeros((holders * rows, count), jnp.float32)
    for i in range(CHUNKS):
        columns = slice(i * step, (i + 1) * step)
        for k in range(holders):
            queries[k * rows:(k + 1) * rows, columns] = packed_refs[k][:, columns]
        scores = scores + lax.dot_general(
            queries[:, columns], pages_ref[:, columns], (((1,), (1,)), ((), ())), preferred_element_type=jnp.float32
        )
    for k in range(holders):
        start = pl.multiple_of((me ^ k) * rows, rows)
        total[pl.ds(start, rows), :] = scores[k * rows:(k + 1) * rows]
    asked = []
    for k in range(holders):
        notes = packed_refs[k][:, width:].astype(jnp.float32)
        notes = jnp.sum(jnp.where(iota(notes.shape, 0) == me % rows, notes, 0.0), axis=0, keepdims=True)
        mine = notes[:, :capacity]
        for block in range(1, holders // rows):
            mine = jnp.where(me // rows == block, notes[:, block * capacity:(block + 1) * capacity], mine)
        asked.append(mine)
    page = iota((count, holders * half), 0).astype(jnp.float32) + 1.0
    parts = parts_of(total[...])[::-1]
    picked = []
    for side in range(2):
        row = jnp.concatenate([row[:, side * half:(side + 1) * half] for row in asked], axis=1)
        chosen = exact_bf16(page == row)
        picked.append(sum(jnp.dot(part, chosen, preferred_element_type=jnp.float32) for part in parts))
    used_ref[...] = found_ref[...]
    own_slots = found_ref.shape[1]
    used_ref[0:1] = jnp.where(iota((1, own_slots), 1) < count_ref[0], found_ref[0:1], float(holders))
    picked = jnp.concatenate(picked, axis=0).T
    for place, k in enumerate(kept_distances(holders)):
        keep_ref[place] = picked[k * half:(k + 1) * half]
        send_ref[place] = picked[(k ^ 1) * half:((k ^ 1) + 1) * half]


def spread_kernel(holders, groups, found_ref, *refs):
    landed_refs, out_refs = refs[:holders // 2], refs[holders // 2:]
    half = landed_refs[0].shape[1]
    slots = found_ref.shape[1]
    total = landed_refs[0].shape[2] // 2
    at = lax.axis_index("layer")
    share = slots // groups
    distance = found_ref[0:1].astype(jnp.int32) ^ lax.axis_index("store")
    order = [k ^ core for k in kept_distances(holders) for core in range(2)]
    begins = sum(jnp.where(distance == k, place * half + 1, 0) for place, k in enumerate(order)).astype(jnp.float32) - 1.0
    rank_there = found_ref[1:2]
    place = iota((holders * half, slots), 0).astype(jnp.float32)
    parts = parts_of(jnp.concatenate([ref[core] for ref in landed_refs for core in range(2)], axis=0))[::-1]
    result = jnp.zeros((total, slots), jnp.float32)
    for side in range(2):
        on_side = (rank_there >= half) if side else (rank_there < half)
        target = jnp.where(on_side & (begins >= 0.0), begins + rank_there - side * half, -1.0)
        chosen = exact_bf16(place == target)
        for part in parts:
            spread = lax.dot_general(part, chosen, (((0,), (0,)), ((), ())), preferred_element_type=jnp.float32)
            result = result + spread[side * total:(side + 1) * total]
    result = result.T
    blocks = []
    for g in range(groups):
        block = result[g * share:(g + 1) * share]
        blocks.append(jnp.concatenate([block[:share // 2], block[share // 2:]], axis=1))
    for step, out_ref in enumerate(out_refs):
        chosen = blocks[0]
        for g in range(1, groups):
            chosen = jnp.where((at + step) % groups == g, blocks[g], chosen)
        out_ref[...] = chosen


def swap(value, axis, distance):
    return lax.ppermute(value, axis, [(i, i ^ distance) for i in range(lax.axis_size(axis))])


def on_device(query_grads, factor_out, factor_in, page_store, page_home, cand_lists, counts):
    holders = lax.axis_size("store")
    groups = lax.axis_size("layer")
    rows, width = query_grads.shape
    layers, rank, _ = factor_out.shape
    per_holder = page_store.shape[0]
    slots = cand_lists.shape[1]
    bf16 = jnp.bfloat16

    capacity = slots // holders
    home = page_home.reshape(-1, LANES)
    sources = [
        pltpu.with_memory_space_constraint(source, pltpu.HBM)
        for source in (query_grads, factor_in, factor_out, home, cand_lists)
    ]
    notes = max(LANES, holders // rows * capacity)
    packed, again, found = pl.pallas_call(
        functools.partial(condition_kernel, holders, capacity, per_holder),
        out_shape=[
            jax.ShapeDtypeStruct((rows, width + notes), bf16),
            jax.ShapeDtypeStruct((rows, width + notes), bf16),
            jax.ShapeDtypeStruct((8, slots), jnp.float32),
        ],
        in_specs=[HBM] * len(sources),
        out_specs=[VMEM] * 3,
        scratch_shapes=[pltpu.VMEM(source.shape, source.dtype) for source in sources]
        + [pltpu.SemaphoreType.DMA((len(sources),)), pltpu.VMEM((layers, rows * rank // 2, LANES), jnp.float32)],
        compiler_params=pltpu.CompilerParams(vmem_limit_bytes=10 * 2**20 + 24 * slots * slots),
    )(*sources)

    again, pages = pl.pallas_call(
        load_kernel,
        out_shape=[jax.ShapeDtypeStruct(again.shape, bf16), pltpu.VMEM(page_store.shape, bf16)],
        in_specs=[VMEM, HBM],
        out_specs=[VMEM] * 2,
        input_output_aliases={0: 0},
        scratch_shapes=[pltpu.SemaphoreType.DMA(())],
        compiler_params=pltpu.CompilerParams(vmem_limit_bytes=2 * 2**20),
        cost_estimate=pl.CostEstimate(flops=0, bytes_accessed=2 * page_store.size, transcendentals=0),
    )(again, pltpu.with_memory_space_constraint(page_store, pltpu.HBM))

    blocks = [None] * holders
    blocks[0] = packed
    for k in range(2, holders, 2):
        blocks[k] = swap(packed, "store", k)
    blocks[1] = swap(again, "store", 1)
    for k in range(2, holders, 2):
        blocks[k + 1] = swap(blocks[k], "store", 1)

    total = holders * rows
    bytes_in = 2 * holders * rows * (width + notes) + 2 * per_holder * width
    keep, send, used = pl.pallas_call(
        functools.partial(score_kernel, holders, capacity),
        out_shape=[
            jax.ShapeDtypeStruct((holders // 2, capacity // 2, 2 * total), jnp.float32),
            jax.ShapeDtypeStruct((holders // 2, capacity // 2, 2 * total), jnp.float32),
            jax.ShapeDtypeStruct(found.shape, jnp.float32),
        ],
        in_specs=[SMEM] + [VMEM] * (holders + 2),
        out_specs=[VMEM] * 3,
        scratch_shapes=[pltpu.VMEM((total, per_holder), jnp.float32), pltpu.VMEM((total, width), bf16)],
        compiler_params=pltpu.CompilerParams(vmem_limit_bytes=8 * 2**20 + 2 * bytes_in + 48 * total * slots),
    )(counts, found, *blocks[::-1], pltpu.with_memory_space_constraint(pages, pltpu.VMEM))

    handed = swap(send, "store", 1)
    landed = []
    for place, k in enumerate(kept_distances(holders)):
        pair = jnp.stack([keep[place], handed[place]])
        landed.append(swap(pair, "store", k) if k else pair)
    share = slots // groups
    terms = pl.pallas_call(
        functools.partial(spread_kernel, holders, groups),
        out_shape=[jax.ShapeDtypeStruct((share // 2, 2 * total), jnp.float32)] * groups,
        in_specs=[VMEM] * (1 + len(landed)),
        out_specs=[VMEM] * groups,
        compiler_params=pltpu.CompilerParams(vmem_limit_bytes=4 * 2**20 + 64 * total * slots),
    )(used, *landed)
    summed = terms[0]
    for step in range(1, groups):
        summed = summed + lax.ppermute(terms[step], "layer", [(g, (g + step) % groups) for g in range(groups)])
    return jnp.concatenate([summed[:, :total], summed[:, total:]], axis=0)[None]


def solution(mesh):
    placed = (
        P("store", "layer"),
        P("layer", None, None),
        P("layer", None, None),
        P("store", "layer"),
        P(),
        P("store", None),
        P("store"),
    )
    return jax.shard_map(
        on_device, mesh=mesh, in_specs=placed, out_specs=P("store", "layer", None), check_vma=False
    )
```

```python
import functools

import jax
import jax.numpy as jnp
from jax import lax
from jax.experimental import pallas as pl
from jax.experimental.pallas import tpu as pltpu
from jax.sharding import PartitionSpec as P

VMEM = pl.BlockSpec(memory_space=pltpu.VMEM)
SMEM = pl.BlockSpec(memory_space=pltpu.SMEM)
HBM = pl.BlockSpec(memory_space=pltpu.HBM)
LANES = 128
CHUNKS = 4


def iota(shape, dimension):
    return lax.broadcasted_iota(jnp.int32, shape, dimension)


def gather_steps(holders):
    if holders == 8:
        return [(2, 4), (6, 6), (4, 2)]
    return [(k, k) for k in range(2, holders, 2)]


def block_owners(holders):
    across = gather_steps(holders)
    return [(0, 0), (1, 1)] + across + [(second ^ 1, first ^ 1) for first, second in across]


def kept_distances(holders):
    return [0] + [k + 1 for k in range(2, holders, 2)]


def parts_of(value):
    parts = []
    for _ in range(3):
        part = value.astype(jnp.bfloat16)
        value = value - part.astype(jnp.float32)
        parts.append(part)
    return parts


def exact_bf16(value):
    return value.astype(jnp.float32).astype(jnp.bfloat16)


def condition_kernel(holders, capacity, per_holder, *refs):
    sources, packed_ref, again_ref, found_ref, landing, arrived, turned_ref = refs[:5], *refs[5:8], refs[8:13], *refs[13:]
    copies = [
        pltpu.make_async_copy(source, target, arrived.at[i])
        for i, (source, target) in enumerate(zip(sources, landing))
    ]
    for copy in copies:
        copy.start()
    for copy in copies:
        copy.wait()
    query_ref, in_factor_ref, out_factor_ref, home_ref, cand_ref = landing
    rows, width = query_ref.shape
    layers, rank, _ = in_factor_ref.shape
    half = rank // 2
    query = query_ref[...].astype(jnp.float32)
    low = iota((half, LANES), 1) < rank
    zero = jnp.zeros((rank, rank), jnp.float32)
    terms = [(0, 0), (0, 1), (0, 2), (1, 0), (1, 1), (2, 0)]
    group = 2 * LANES
    source, place = iota((rank, 2 * group), 0), iota((rank, 2 * group), 1)
    inside = place % group
    column_found = (source == 2 * (inside % half) + place // group)
    chosen_part = sum((inside >= half * start).astype(jnp.int32) for start in (3, 5, 6))
    pickers = [exact_bf16(column_found & (chosen_part == i)) for i in range(3)]
    for layer in range(layers):
        first = layer * half
        packed = jnp.concatenate(
            [query[:, (first + t) * LANES:(first + t + 1) * LANES] for t in range(half)], axis=0
        ).astype(jnp.bfloat16)
        factor = in_factor_ref[layer]
        doubled = parts_of(
            jnp.concatenate(
                [jnp.concatenate([factor, zero], axis=1), jnp.concatenate([zero, factor], axis=1)], axis=0
            )
        )
        small = jnp.dot(
            jnp.concatenate([packed, packed], axis=1), jnp.concatenate(doubled[1:], axis=0),
            preferred_element_type=jnp.float32,
        )
        turned_ref[layer] = small + jnp.dot(packed, doubled[0], preferred_element_type=jnp.float32)
        wide = jnp.concatenate([turned_ref[layer, pl.ds(q, half, stride=rows), :] for q in range(rows)], axis=1)
        wide = parts_of(wide)
        stacked = jnp.concatenate([wide[j] for _, j in terms], axis=0)
        by_row = jnp.concatenate(
            [out_factor_ref[layer, pl.ds(parity, half, stride=2), :] for parity in range(2)], axis=0
        )
        sorted_columns = sum(
            jnp.dot(part, picker, preferred_element_type=jnp.float32) for part, picker in zip(parts_of(by_row), pickers)
        )
        quarters = jnp.concatenate(
            [
                sorted_columns[r * half:(r + 1) * half, c * group:c * group + len(terms) * half]
                for r in range(2) for c in range(2)
            ],
            axis=0,
        ).astype(jnp.bfloat16)
        left = jnp.dot(quarters, stacked, preferred_element_type=jnp.float32)
        for q in range(rows):
            part = left[:, q * LANES:(q + 1) * LANES]
            ee, eo, oe, oo = (part[i * half:(i + 1) * half] for i in range(4))
            done = jnp.where(low, ee, oo) + pltpu.roll(jnp.where(low, oe, eo), rank, 1)
            turned_ref[layer, pl.ds(q, half, stride=rows), :] = done
        for t in range(half):
            packed_ref[:, (first + t) * LANES:(first + t + 1) * LANES] = (
                turned_ref[layer, t * rows:(t + 1) * rows, :].astype(jnp.bfloat16)
            )

    slots = cand_ref.shape[1]
    home_rows = home_ref.shape[0]
    wanted = cand_ref[...]
    onehot = (iota((LANES, slots), 0) == wanted % LANES).astype(jnp.float32).astype(jnp.bfloat16)
    home = home_ref[...]
    table = jnp.concatenate([home // per_holder, home % per_holder], axis=0).astype(jnp.float32).astype(jnp.bfloat16)
    found = jnp.dot(table, onehot, preferred_element_type=jnp.float32)
    mine = iota((home_rows, slots), 0) == wanted // LANES
    holder = jnp.sum(jnp.where(mine, found[:home_rows], 0.0), axis=0, keepdims=True)
    within = jnp.sum(jnp.where(mine, found[home_rows:], 0.0), axis=0, keepdims=True)
    at_holder = iota((holders, slots), 0).astype(jnp.float32) == holder
    earlier = exact_bf16(iota((slots, slots), 0) < iota((slots, slots), 1))
    before = jnp.dot(exact_bf16(at_holder), earlier, preferred_element_type=jnp.float32)
    rank_there = jnp.sum(jnp.where(at_holder, before, 0.0), axis=0, keepdims=True)
    ranked = exact_bf16(iota((capacity, slots), 0).astype(jnp.float32) == rank_there)
    asked = lax.dot_general(
        exact_bf16(jnp.where(at_holder, within + 1.0, 0.0)), ranked, (((1,), (1,)), ((), ())),
        preferred_element_type=jnp.float32,
    )
    blocks = [asked[h:h + rows] for h in range(0, holders, rows)]
    spare = packed_ref.shape[1] - width - capacity * len(blocks)
    if spare:
        blocks.append(jnp.zeros((rows, spare), jnp.float32))
    packed_ref[:, width:] = jnp.concatenate(blocks, axis=1).astype(jnp.bfloat16)
    again_ref[...] = packed_ref[...]
    found_ref[...] = jnp.concatenate([holder, rank_there, jnp.zeros((6, slots), jnp.float32)], axis=0)


def load_kernel(block_ref, source_ref, same_block_ref, target_ref, arrived):
    copy = pltpu.make_async_copy(source_ref, target_ref, arrived)
    copy.start()
    copy.wait()


def score_kernel(holders, capacity, *refs):
    count_ref, found_ref, packed_refs = *refs[:2], refs[2:2 + holders][::-1]
    pages_ref, keep_ref, send_ref, used_ref, total, queries = refs[2 + holders:]
    me = lax.axis_index("store")
    count, width = pages_ref.shape
    rows = packed_refs[0].shape[0]
    half = capacity // 2
    step = width // CHUNKS
    scores = jnp.zeros((holders * rows, count), jnp.float32)
    for i in range(CHUNKS):
        columns = slice(i * step, (i + 1) * step)
        for k in range(holders):
            queries[k * rows:(k + 1) * rows, columns] = packed_refs[k][:, columns]
        scores = scores + lax.dot_general(
            queries[:, columns], pages_ref[:, columns], (((1,), (1,)), ((), ())), preferred_element_type=jnp.float32
        )
    second_core = me % 2 == 1
    owners = block_owners(holders)
    for k, (first, second) in enumerate(owners):
        start = pl.multiple_of((me ^ jnp.where(second_core, second, first)) * rows, rows)
        total[pl.ds(start, rows), :] = scores[k * rows:(k + 1) * rows]
    asked = []
    for k in range(holders):
        notes = packed_refs[k][:, width:].astype(jnp.float32)
        notes = jnp.sum(jnp.where(iota(notes.shape, 0) == me % rows, notes, 0.0), axis=0, keepdims=True)
        mine = notes[:, :capacity]
        for block in range(1, holders // rows):
            mine = jnp.where(me // rows == block, notes[:, block * capacity:(block + 1) * capacity], mine)
        asked.append(mine)
    places = [[pair[core] for pair in owners] for core in range(2)]
    asked = [
        jnp.where(second_core, asked[places[1].index(k)], asked[places[0].index(k)]) for k in range(holders)
    ]
    page = iota((count, holders * half), 0).astype(jnp.float32) + 1.0
    parts = parts_of(total[...])[::-1]
    picked = []
    for side in range(2):
        row = jnp.concatenate([row[:, side * half:(side + 1) * half] for row in asked], axis=1)
        chosen = exact_bf16(page == row)
        picked.append(sum(jnp.dot(part, chosen, preferred_element_type=jnp.float32) for part in parts))
    used_ref[...] = found_ref[...]
    own_slots = found_ref.shape[1]
    used_ref[0:1] = jnp.where(iota((1, own_slots), 1) < count_ref[0], found_ref[0:1], float(holders))
    picked = jnp.concatenate(picked, axis=0).T
    for place, k in enumerate(kept_distances(holders)):
        keep_ref[place] = picked[k * half:(k + 1) * half]
        send_ref[place] = picked[(k ^ 1) * half:((k ^ 1) + 1) * half]


def spread_kernel(holders, groups, found_ref, *refs):
    landed_refs, out_refs = refs[:holders // 2], refs[holders // 2:]
    half = landed_refs[0].shape[1]
    slots = found_ref.shape[1]
    total = landed_refs[0].shape[2] // 2
    at = lax.axis_index("layer")
    share = slots // groups
    distance = found_ref[0:1].astype(jnp.int32) ^ lax.axis_index("store")
    order = [k ^ core for k in kept_distances(holders) for core in range(2)]
    begins = sum(jnp.where(distance == k, place * half + 1, 0) for place, k in enumerate(order)).astype(jnp.float32) - 1.0
    rank_there = found_ref[1:2]
    place = iota((holders * half, slots), 0).astype(jnp.float32)
    parts = parts_of(jnp.concatenate([ref[core] for ref in landed_refs for core in range(2)], axis=0))[::-1]
    result = jnp.zeros((total, slots), jnp.float32)
    for side in range(2):
        on_side = (rank_there >= half) if side else (rank_there < half)
        target = jnp.where(on_side & (begins >= 0.0), begins + rank_there - side * half, -1.0)
        chosen = exact_bf16(place == target)
        for part in parts:
            spread = lax.dot_general(part, chosen, (((0,), (0,)), ((), ())), preferred_element_type=jnp.float32)
            result = result + spread[side * total:(side + 1) * total]
    result = result.T
    blocks = []
    for g in range(groups):
        block = result[g * share:(g + 1) * share]
        blocks.append(jnp.concatenate([block[:share // 2], block[share // 2:]], axis=1))
    for step, out_ref in enumerate(out_refs):
        chosen = blocks[0]
        for g in range(1, groups):
            chosen = jnp.where((at + step) % groups == g, blocks[g], chosen)
        out_ref[...] = chosen


def swap(value, axis, distance):
    return lax.ppermute(value, axis, [(i, i ^ distance) for i in range(lax.axis_size(axis))])


def on_device(query_grads, factor_out, factor_in, page_store, page_home, cand_lists, counts):
    holders = lax.axis_size("store")
    groups = lax.axis_size("layer")
    rows, width = query_grads.shape
    layers, rank, _ = factor_out.shape
    per_holder = page_store.shape[0]
    slots = cand_lists.shape[1]
    bf16 = jnp.bfloat16

    capacity = slots // holders
    home = page_home.reshape(-1, LANES)
    sources = [
        pltpu.with_memory_space_constraint(source, pltpu.HBM)
        for source in (query_grads, factor_in, factor_out, home, cand_lists)
    ]
    notes = max(LANES, holders // rows * capacity)
    packed, again, found = pl.pallas_call(
        functools.partial(condition_kernel, holders, capacity, per_holder),
        out_shape=[
            jax.ShapeDtypeStruct((rows, width + notes), bf16),
            jax.ShapeDtypeStruct((rows, width + notes), bf16),
            jax.ShapeDtypeStruct((8, slots), jnp.float32),
        ],
        in_specs=[HBM] * len(sources),
        out_specs=[VMEM] * 3,
        scratch_shapes=[pltpu.VMEM(source.shape, source.dtype) for source in sources]
        + [pltpu.SemaphoreType.DMA((len(sources),)), pltpu.VMEM((layers, rows * rank // 2, LANES), jnp.float32)],
        compiler_params=pltpu.CompilerParams(vmem_limit_bytes=10 * 2**20 + 24 * slots * slots),
    )(*sources)

    again, pages = pl.pallas_call(
        load_kernel,
        out_shape=[jax.ShapeDtypeStruct(again.shape, bf16), pltpu.VMEM(page_store.shape, bf16)],
        in_specs=[VMEM, HBM],
        out_specs=[VMEM] * 2,
        input_output_aliases={0: 0},
        scratch_shapes=[pltpu.SemaphoreType.DMA(())],
        compiler_params=pltpu.CompilerParams(vmem_limit_bytes=2 * 2**20),
        cost_estimate=pl.CostEstimate(flops=0, bytes_accessed=2 * page_store.size, transcendentals=0),
    )(again, pltpu.with_memory_space_constraint(page_store, pltpu.HBM))

    across = [
        lax.ppermute(packed, "store", [(i, i ^ step[i % 2]) for i in range(holders)]) for step in gather_steps(holders)
    ]
    blocks = [packed, swap(again, "store", 1)] + across + [swap(block, "store", 1) for block in across]

    total = holders * rows
    bytes_in = 2 * holders * rows * (width + notes) + 2 * per_holder * width
    keep, send, used = pl.pallas_call(
        functools.partial(score_kernel, holders, capacity),
        out_shape=[
            jax.ShapeDtypeStruct((holders // 2, capacity // 2, 2 * total), jnp.float32),
            jax.ShapeDtypeStruct((holders // 2, capacity // 2, 2 * total), jnp.float32),
            jax.ShapeDtypeStruct(found.shape, jnp.float32),
        ],
        in_specs=[SMEM] + [VMEM] * (holders + 2),
        out_specs=[VMEM] * 3,
        scratch_shapes=[pltpu.VMEM((total, per_holder), jnp.float32), pltpu.VMEM((total, width), bf16)],
        compiler_params=pltpu.CompilerParams(vmem_limit_bytes=8 * 2**20 + 2 * bytes_in + 48 * total * slots),
    )(counts, found, *blocks[::-1], pltpu.with_memory_space_constraint(pages, pltpu.VMEM))

    handed = swap(send, "store", 1)
    landed = []
    for place, k in enumerate(kept_distances(holders)):
        pair = jnp.stack([keep[place], handed[place]])
        landed.append(swap(pair, "store", k) if k else pair)
    share = slots // groups
    terms = pl.pallas_call(
        functools.partial(spread_kernel, holders, groups),
        out_shape=[jax.ShapeDtypeStruct((share // 2, 2 * total), jnp.float32)] * groups,
        in_specs=[VMEM] * (1 + len(landed)),
        out_specs=[VMEM] * groups,
        compiler_params=pltpu.CompilerParams(vmem_limit_bytes=4 * 2**20 + 64 * total * slots),
    )(used, *landed)
    summed = terms[0]
    for step in range(1, groups):
        summed = summed + lax.ppermute(terms[step], "layer", [(g, (g + step) % groups) for g in range(groups)])
    return jnp.concatenate([summed[:, :total], summed[:, total:]], axis=0)[None]


def solution(mesh):
    placed = (
        P("store", "layer"),
        P("layer", None, None),
        P("layer", None, None),
        P("store", "layer"),
        P(),
        P("store", None),
        P("store"),
    )
    return jax.shard_map(
        on_device, mesh=mesh, in_specs=placed, out_specs=P("store", "layer", None), check_vma=False
    )
```

```python
import functools

import jax
import jax.numpy as jnp
from jax import lax
from jax.experimental import pallas as pl
from jax.experimental.pallas import tpu as pltpu
from jax.sharding import PartitionSpec as P

VMEM = pl.BlockSpec(memory_space=pltpu.VMEM)
SMEM = pl.BlockSpec(memory_space=pltpu.SMEM)
HBM = pl.BlockSpec(memory_space=pltpu.HBM)
LANES = 128
CHUNKS = 4
LOADS = 8


def iota(shape, dimension):
    return lax.broadcasted_iota(jnp.int32, shape, dimension)


def kept_distances(holders):
    return [0] + [k + 1 for k in range(2, holders, 2)]


def parts_of(value):
    parts = []
    for _ in range(3):
        part = value.astype(jnp.bfloat16)
        value = value - part.astype(jnp.float32)
        parts.append(part)
    return parts


def exact_bf16(value):
    return value.astype(jnp.float32).astype(jnp.bfloat16)


def condition_kernel(holders, capacity, per_holder, *refs):
    sources, packed_ref, again_ref, found_ref, landing, arrived, turned_ref = refs[:5], *refs[5:8], refs[8:13], *refs[13:]
    copies = [
        pltpu.make_async_copy(source, target, arrived.at[i])
        for i, (source, target) in enumerate(zip(sources, landing))
    ]
    for copy in copies:
        copy.start()
    for copy in copies:
        copy.wait()
    query_ref, in_factor_ref, out_factor_ref, home_ref, cand_ref = landing
    rows, width = query_ref.shape
    layers, rank, _ = in_factor_ref.shape
    half = rank // 2
    query = query_ref[...].astype(jnp.float32)
    low = iota((half, LANES), 1) < rank
    zero = jnp.zeros((rank, rank), jnp.float32)
    terms = [(0, 0), (0, 1), (0, 2), (1, 0), (1, 1), (2, 0)]
    group = 2 * LANES
    source, place = iota((rank, 2 * group), 0), iota((rank, 2 * group), 1)
    inside = place % group
    column_found = (source == 2 * (inside % half) + place // group)
    chosen_part = sum((inside >= half * start).astype(jnp.int32) for start in (3, 5, 6))
    pickers = [exact_bf16(column_found & (chosen_part == i)) for i in range(3)]
    for layer in range(layers):
        first = layer * half
        packed = jnp.concatenate(
            [query[:, (first + t) * LANES:(first + t + 1) * LANES] for t in range(half)], axis=0
        ).astype(jnp.bfloat16)
        factor = in_factor_ref[layer]
        doubled = parts_of(
            jnp.concatenate(
                [jnp.concatenate([factor, zero], axis=1), jnp.concatenate([zero, factor], axis=1)], axis=0
            )
        )
        small = jnp.dot(
            jnp.concatenate([packed, packed], axis=1), jnp.concatenate(doubled[1:], axis=0),
            preferred_element_type=jnp.float32,
        )
        turned_ref[layer] = small + jnp.dot(packed, doubled[0], preferred_element_type=jnp.float32)
        wide = jnp.concatenate([turned_ref[layer, pl.ds(q, half, stride=rows), :] for q in range(rows)], axis=1)
        wide = parts_of(wide)
        stacked = jnp.concatenate([wide[j] for _, j in terms], axis=0)
        by_row = jnp.concatenate(
            [out_factor_ref[layer, pl.ds(parity, half, stride=2), :] for parity in range(2)], axis=0
        )
        sorted_columns = sum(
            jnp.dot(part, picker, preferred_element_type=jnp.float32) for part, picker in zip(parts_of(by_row), pickers)
        )
        quarters = jnp.concatenate(
            [
                sorted_columns[r * half:(r + 1) * half, c * group:c * group + len(terms) * half]
                for r in range(2) for c in range(2)
            ],
            axis=0,
        ).astype(jnp.bfloat16)
        left = jnp.dot(quarters, stacked, preferred_element_type=jnp.float32)
        for q in range(rows):
            part = left[:, q * LANES:(q + 1) * LANES]
            ee, eo, oe, oo = (part[i * half:(i + 1) * half] for i in range(4))
            done = jnp.where(low, ee, oo) + pltpu.roll(jnp.where(low, oe, eo), rank, 1)
            turned_ref[layer, pl.ds(q, half, stride=rows), :] = done
        for t in range(half):
            packed_ref[:, (first + t) * LANES:(first + t + 1) * LANES] = (
                turned_ref[layer, t * rows:(t + 1) * rows, :].astype(jnp.bfloat16)
            )

    slots = cand_ref.shape[1]
    home_rows = home_ref.shape[0]
    wanted = cand_ref[...]
    onehot = (iota((LANES, slots), 0) == wanted % LANES).astype(jnp.float32).astype(jnp.bfloat16)
    home = home_ref[...]
    table = jnp.concatenate([home // per_holder, home % per_holder], axis=0).astype(jnp.float32).astype(jnp.bfloat16)
    found = jnp.dot(table, onehot, preferred_element_type=jnp.float32)
    mine = iota((home_rows, slots), 0) == wanted // LANES
    holder = jnp.sum(jnp.where(mine, found[:home_rows], 0.0), axis=0, keepdims=True)
    within = jnp.sum(jnp.where(mine, found[home_rows:], 0.0), axis=0, keepdims=True)
    at_holder = iota((holders, slots), 0).astype(jnp.float32) == holder
    earlier = exact_bf16(iota((slots, slots), 0) < iota((slots, slots), 1))
    before = jnp.dot(exact_bf16(at_holder), earlier, preferred_element_type=jnp.float32)
    rank_there = jnp.sum(jnp.where(at_holder, before, 0.0), axis=0, keepdims=True)
    ranked = exact_bf16(iota((capacity, slots), 0).astype(jnp.float32) == rank_there)
    asked = lax.dot_general(
        exact_bf16(jnp.where(at_holder, within + 1.0, 0.0)), ranked, (((1,), (1,)), ((), ())),
        preferred_element_type=jnp.float32,
    )
    blocks = [asked[h:h + rows] for h in range(0, holders, rows)]
    spare = packed_ref.shape[1] - width - capacity * len(blocks)
    if spare:
        blocks.append(jnp.zeros((rows, spare), jnp.float32))
    packed_ref[:, width:] = jnp.concatenate(blocks, axis=1).astype(jnp.bfloat16)
    again_ref[...] = packed_ref[...]
    found_ref[...] = jnp.concatenate([holder, rank_there, jnp.zeros((6, slots), jnp.float32)], axis=0)


def load_kernel(block_ref, source_ref, same_block_ref, target_ref, landing, arrived):
    step = landing.shape[1] // LOADS
    copies = [
        pltpu.make_async_copy(
            source_ref.at[:, pl.ds(i * step, step)], landing.at[:, pl.ds(i * step, step)], arrived.at[i]
        )
        for i in range(LOADS)
    ]
    for copy in copies:
        copy.start()
    for i, copy in enumerate(copies):
        copy.wait()
        target_ref[i * step:(i + 1) * step, :] = landing[:, i * step:(i + 1) * step].T


def score_kernel(holders, capacity, *refs):
    count_ref, found_ref, packed_refs = *refs[:2], refs[2:2 + holders][::-1]
    pages_ref, keep_ref, send_ref, used_ref, total, queries = refs[2 + holders:]
    me = lax.axis_index("store")
    width, count = pages_ref.shape
    rows = packed_refs[0].shape[0]
    half = capacity // 2
    step = width // CHUNKS
    scores = jnp.zeros((holders * rows, count), jnp.float32)
    for i in range(CHUNKS):
        columns = slice(i * step, (i + 1) * step)
        for k in range(holders):
            queries[k * rows:(k + 1) * rows, columns] = packed_refs[k][:, columns]
        scores = scores + jnp.dot(queries[:, columns], pages_ref[columns], preferred_element_type=jnp.float32)
    for k in range(holders):
        start = pl.multiple_of((me ^ k) * rows, rows)
        total[pl.ds(start, rows), :] = scores[k * rows:(k + 1) * rows]
    asked = []
    for k in range(holders):
        notes = packed_refs[k][:, width:].astype(jnp.float32)
        notes = jnp.sum(jnp.where(iota(notes.shape, 0) == me % rows, notes, 0.0), axis=0, keepdims=True)
        mine = notes[:, :capacity]
        for block in range(1, holders // rows):
            mine = jnp.where(me // rows == block, notes[:, block * capacity:(block + 1) * capacity], mine)
        asked.append(mine)
    page = iota((count, holders * half), 0).astype(jnp.float32) + 1.0
    parts = parts_of(total[...])[::-1]
    picked = []
    for side in range(2):
        row = jnp.concatenate([row[:, side * half:(side + 1) * half] for row in asked], axis=1)
        chosen = exact_bf16(page == row)
        picked.append(sum(jnp.dot(part, chosen, preferred_element_type=jnp.float32) for part in parts))
    used_ref[...] = found_ref[...]
    own_slots = found_ref.shape[1]
    used_ref[0:1] = jnp.where(iota((1, own_slots), 1) < count_ref[0], found_ref[0:1], float(holders))
    picked = jnp.concatenate(picked, axis=0).T
    for place, k in enumerate(kept_distances(holders)):
        keep_ref[place] = picked[k * half:(k + 1) * half]
        send_ref[place] = picked[(k ^ 1) * half:((k ^ 1) + 1) * half]


def spread_kernel(holders, groups, found_ref, *refs):
    landed_refs, out_refs = refs[:holders // 2], refs[holders // 2:]
    half = landed_refs[0].shape[1]
    slots = found_ref.shape[1]
    total = landed_refs[0].shape[2] // 2
    at = lax.axis_index("layer")
    share = slots // groups
    distance = found_ref[0:1].astype(jnp.int32) ^ lax.axis_index("store")
    order = [k ^ core for k in kept_distances(holders) for core in range(2)]
    begins = sum(jnp.where(distance == k, place * half + 1, 0) for place, k in enumerate(order)).astype(jnp.float32) - 1.0
    rank_there = found_ref[1:2]
    place = iota((holders * half, slots), 0).astype(jnp.float32)
    parts = parts_of(jnp.concatenate([ref[core] for ref in landed_refs for core in range(2)], axis=0))[::-1]
    result = jnp.zeros((total, slots), jnp.float32)
    for side in range(2):
        on_side = (rank_there >= half) if side else (rank_there < half)
        target = jnp.where(on_side & (begins >= 0.0), begins + rank_there - side * half, -1.0)
        chosen = exact_bf16(place == target)
        for part in parts:
            spread = lax.dot_general(part, chosen, (((0,), (0,)), ((), ())), preferred_element_type=jnp.float32)
            result = result + spread[side * total:(side + 1) * total]
    result = result.T
    blocks = []
    for g in range(groups):
        block = result[g * share:(g + 1) * share]
        blocks.append(jnp.concatenate([block[:share // 2], block[share // 2:]], axis=1))
    for step, out_ref in enumerate(out_refs):
        chosen = blocks[0]
        for g in range(1, groups):
            chosen = jnp.where((at + step) % groups == g, blocks[g], chosen)
        out_ref[...] = chosen


def swap(value, axis, distance):
    return lax.ppermute(value, axis, [(i, i ^ distance) for i in range(lax.axis_size(axis))])


def on_device(query_grads, factor_out, factor_in, page_store, page_home, cand_lists, counts):
    holders = lax.axis_size("store")
    groups = lax.axis_size("layer")
    rows, width = query_grads.shape
    layers, rank, _ = factor_out.shape
    per_holder = page_store.shape[0]
    slots = cand_lists.shape[1]
    bf16 = jnp.bfloat16

    capacity = slots // holders
    home = page_home.reshape(-1, LANES)
    sources = [
        pltpu.with_memory_space_constraint(source, pltpu.HBM)
        for source in (query_grads, factor_in, factor_out, home, cand_lists)
    ]
    notes = max(LANES, holders // rows * capacity)
    packed, again, found = pl.pallas_call(
        functools.partial(condition_kernel, holders, capacity, per_holder),
        out_shape=[
            jax.ShapeDtypeStruct((rows, width + notes), bf16),
            jax.ShapeDtypeStruct((rows, width + notes), bf16),
            jax.ShapeDtypeStruct((8, slots), jnp.float32),
        ],
        in_specs=[HBM] * len(sources),
        out_specs=[VMEM] * 3,
        scratch_shapes=[pltpu.VMEM(source.shape, source.dtype) for source in sources]
        + [pltpu.SemaphoreType.DMA((len(sources),)), pltpu.VMEM((layers, rows * rank // 2, LANES), jnp.float32)],
        compiler_params=pltpu.CompilerParams(vmem_limit_bytes=10 * 2**20 + 24 * slots * slots),
    )(*sources)

    again, pages = pl.pallas_call(
        load_kernel,
        out_shape=[jax.ShapeDtypeStruct(again.shape, bf16), pltpu.VMEM((width, per_holder), bf16)],
        in_specs=[VMEM, HBM],
        out_specs=[VMEM] * 2,
        input_output_aliases={0: 0},
        scratch_shapes=[pltpu.VMEM(page_store.shape, bf16), pltpu.SemaphoreType.DMA((LOADS,))],
        compiler_params=pltpu.CompilerParams(vmem_limit_bytes=4 * 2**20 + 4 * per_holder * width),
        cost_estimate=pl.CostEstimate(flops=0, bytes_accessed=2 * page_store.size, transcendentals=0),
    )(again, pltpu.with_memory_space_constraint(page_store, pltpu.HBM))

    blocks = [None] * holders
    blocks[0] = packed
    for k in range(2, holders, 2):
        blocks[k] = swap(packed, "store", k)
    blocks[1] = swap(again, "store", 1)
    for k in range(2, holders, 2):
        blocks[k + 1] = swap(blocks[k], "store", 1)

    total = holders * rows
    bytes_in = 2 * holders * rows * (width + notes) + 2 * per_holder * width
    keep, send, used = pl.pallas_call(
        functools.partial(score_kernel, holders, capacity),
        out_shape=[
            jax.ShapeDtypeStruct((holders // 2, capacity // 2, 2 * total), jnp.float32),
            jax.ShapeDtypeStruct((holders // 2, capacity // 2, 2 * total), jnp.float32),
            jax.ShapeDtypeStruct(found.shape, jnp.float32),
        ],
        in_specs=[SMEM] + [VMEM] * (holders + 2),
        out_specs=[VMEM] * 3,
        scratch_shapes=[pltpu.VMEM((total, per_holder), jnp.float32), pltpu.VMEM((total, width), bf16)],
        compiler_params=pltpu.CompilerParams(vmem_limit_bytes=8 * 2**20 + 2 * bytes_in + 48 * total * slots),
    )(counts, found, *blocks[::-1], pltpu.with_memory_space_constraint(pages, pltpu.VMEM))

    handed = swap(send, "store", 1)
    landed = []
    for place, k in enumerate(kept_distances(holders)):
        pair = jnp.stack([keep[place], handed[place]])
        landed.append(swap(pair, "store", k) if k else pair)
    share = slots // groups
    terms = pl.pallas_call(
        functools.partial(spread_kernel, holders, groups),
        out_shape=[jax.ShapeDtypeStruct((share // 2, 2 * total), jnp.float32)] * groups,
        in_specs=[VMEM] * (1 + len(landed)),
        out_specs=[VMEM] * groups,
        compiler_params=pltpu.CompilerParams(vmem_limit_bytes=4 * 2**20 + 64 * total * slots),
    )(used, *landed)
    summed = terms[0]
    for step in range(1, groups):
        summed = summed + lax.ppermute(terms[step], "layer", [(g, (g + step) % groups) for g in range(groups)])
    return jnp.concatenate([summed[:, :total], summed[:, total:]], axis=0)[None]


def solution(mesh):
    placed = (
        P("store", "layer"),
        P("layer", None, None),
        P("layer", None, None),
        P("store", "layer"),
        P(),
        P("store", None),
        P("store"),
    )
    return jax.shard_map(
        on_device, mesh=mesh, in_specs=placed, out_specs=P("store", "layer", None), check_vma=False
    )
```

```python
import functools

import jax
import jax.numpy as jnp
from jax import lax
from jax.experimental import pallas as pl
from jax.experimental.pallas import tpu as pltpu
from jax.sharding import PartitionSpec as P

VMEM = pl.BlockSpec(memory_space=pltpu.VMEM)
SMEM = pl.BlockSpec(memory_space=pltpu.SMEM)
HBM = pl.BlockSpec(memory_space=pltpu.HBM)
LANES = 128
CHUNKS = 4
LOADS = 8


def iota(shape, dimension):
    return lax.broadcasted_iota(jnp.int32, shape, dimension)


def kept_distances(holders):
    return [0] + [k + 1 for k in range(2, holders, 2)]


def parts_of(value):
    parts = []
    for _ in range(3):
        part = value.astype(jnp.bfloat16)
        value = value - part.astype(jnp.float32)
        parts.append(part)
    return parts


def exact_product(value, chosen):
    rows = value.shape[0]
    product = jnp.dot(jnp.concatenate(parts_of(value), axis=0), chosen, preferred_element_type=jnp.float32)
    return product[2 * rows:] + product[rows:2 * rows] + product[:rows]


def exact_bf16(value):
    return value.astype(jnp.float32).astype(jnp.bfloat16)


def condition_kernel(holders, capacity, per_holder, *refs):
    sources, packed_ref, again_ref, found_ref, landing, arrived, turned_ref = refs[:5], *refs[5:8], refs[8:13], *refs[13:]
    copies = [
        pltpu.make_async_copy(source, target, arrived.at[i])
        for i, (source, target) in enumerate(zip(sources, landing))
    ]
    for copy in copies:
        copy.start()
    for copy in copies:
        copy.wait()
    query_ref, in_factor_ref, out_factor_ref, home_ref, cand_ref = landing
    rows, width = query_ref.shape
    layers, rank, _ = in_factor_ref.shape
    half = rank // 2
    query = query_ref[...].astype(jnp.float32)
    low = iota((half, LANES), 1) < rank
    zero = jnp.zeros((rank, rank), jnp.float32)
    terms = [(0, 0), (0, 1), (0, 2), (1, 0), (1, 1), (2, 0)]
    group = 2 * LANES
    source, place = iota((rank, 2 * group), 0), iota((rank, 2 * group), 1)
    inside = place % group
    column_found = (source == 2 * (inside % half) + place // group)
    chosen_part = sum((inside >= half * start).astype(jnp.int32) for start in (3, 5, 6))
    pickers = [exact_bf16(column_found & (chosen_part == i)) for i in range(3)]
    for layer in range(layers):
        first = layer * half
        packed = jnp.concatenate(
            [query[:, (first + t) * LANES:(first + t + 1) * LANES] for t in range(half)], axis=0
        ).astype(jnp.bfloat16)
        factor = in_factor_ref[layer]
        doubled = parts_of(
            jnp.concatenate(
                [jnp.concatenate([factor, zero], axis=1), jnp.concatenate([zero, factor], axis=1)], axis=0
            )
        )
        small = jnp.dot(
            jnp.concatenate([packed, packed], axis=1), jnp.concatenate(doubled[1:], axis=0),
            preferred_element_type=jnp.float32,
        )
        turned_ref[layer] = small + jnp.dot(packed, doubled[0], preferred_element_type=jnp.float32)
        wide = jnp.concatenate([turned_ref[layer, pl.ds(q, half, stride=rows), :] for q in range(rows)], axis=1)
        wide = parts_of(wide)
        stacked = jnp.concatenate([wide[j] for _, j in terms], axis=0)
        by_row = jnp.concatenate(
            [out_factor_ref[layer, pl.ds(parity, half, stride=2), :] for parity in range(2)], axis=0
        )
        sorted_columns = sum(
            jnp.dot(part, picker, preferred_element_type=jnp.float32) for part, picker in zip(parts_of(by_row), pickers)
        )
        quarters = jnp.concatenate(
            [
                sorted_columns[r * half:(r + 1) * half, c * group:c * group + len(terms) * half]
                for r in range(2) for c in range(2)
            ],
            axis=0,
        ).astype(jnp.bfloat16)
        left = jnp.dot(quarters, stacked, preferred_element_type=jnp.float32)
        for q in range(rows):
            part = left[:, q * LANES:(q + 1) * LANES]
            ee, eo, oe, oo = (part[i * half:(i + 1) * half] for i in range(4))
            done = jnp.where(low, ee, oo) + pltpu.roll(jnp.where(low, oe, eo), rank, 1)
            turned_ref[layer, pl.ds(q, half, stride=rows), :] = done
        for t in range(half):
            tile = turned_ref[layer, t * rows:(t + 1) * rows, :].astype(jnp.bfloat16)
            for target_ref in (packed_ref, again_ref):
                target_ref[:, (first + t) * LANES:(first + t + 1) * LANES] = tile

    slots = cand_ref.shape[1]
    home_rows = home_ref.shape[0]
    wanted = cand_ref[...]
    onehot = (iota((LANES, slots), 0) == wanted % LANES).astype(jnp.float32).astype(jnp.bfloat16)
    home = home_ref[...]
    table = jnp.concatenate([home // per_holder, home % per_holder], axis=0).astype(jnp.float32).astype(jnp.bfloat16)
    found = jnp.dot(table, onehot, preferred_element_type=jnp.float32)
    mine = iota((home_rows, slots), 0) == wanted // LANES
    holder = jnp.sum(jnp.where(mine, found[:home_rows], 0.0), axis=0, keepdims=True)
    within = jnp.sum(jnp.where(mine, found[home_rows:], 0.0), axis=0, keepdims=True)
    at_holder = iota((holders, slots), 0).astype(jnp.float32) == holder
    earlier = exact_bf16(iota((slots, slots), 0) < iota((slots, slots), 1))
    before = jnp.dot(exact_bf16(at_holder), earlier, preferred_element_type=jnp.float32)
    rank_there = jnp.sum(jnp.where(at_holder, before, 0.0), axis=0, keepdims=True)
    ranked = exact_bf16(iota((capacity, slots), 0).astype(jnp.float32) == rank_there)
    asked = lax.dot_general(
        exact_bf16(jnp.where(at_holder, within + 1.0, 0.0)), ranked, (((1,), (1,)), ((), ())),
        preferred_element_type=jnp.float32,
    )
    blocks = [asked[h:h + rows] for h in range(0, holders, rows)]
    spare = packed_ref.shape[1] - width - capacity * len(blocks)
    if spare:
        blocks.append(jnp.zeros((rows, spare), jnp.float32))
    for target_ref in (packed_ref, again_ref):
        target_ref[:, width:] = jnp.concatenate(blocks, axis=1).astype(jnp.bfloat16)
    found_ref[...] = jnp.concatenate([holder, rank_there, jnp.zeros((6, slots), jnp.float32)], axis=0)


def load_kernel(block_ref, source_ref, same_block_ref, target_ref, landing, arrived):
    step = landing.shape[1] // LOADS
    copies = [
        pltpu.make_async_copy(
            source_ref.at[:, pl.ds(i * step, step)], landing.at[:, pl.ds(i * step, step)], arrived.at[i]
        )
        for i in range(LOADS)
    ]
    for copy in copies:
        copy.start()
    for i, copy in enumerate(copies):
        copy.wait()
        target_ref[i * step:(i + 1) * step, :] = landing[:, i * step:(i + 1) * step].T


def score_kernel(holders, capacity, *refs):
    count_ref, found_ref, packed_refs = *refs[:2], refs[2:2 + holders][::-1]
    pages_ref, keep_ref, send_ref, used_ref, total, queries = refs[2 + holders:]
    me = lax.axis_index("store")
    width, count = pages_ref.shape
    rows = packed_refs[0].shape[0]
    half = capacity // 2
    step = width // CHUNKS
    scores = jnp.zeros((holders * rows, count), jnp.float32)
    for i in range(CHUNKS):
        columns = slice(i * step, (i + 1) * step)
        for k in range(holders):
            queries[k * rows:(k + 1) * rows, columns] = packed_refs[k][:, columns]
        scores = scores + jnp.dot(queries[:, columns], pages_ref[columns], preferred_element_type=jnp.float32)
    for k in range(holders):
        start = pl.multiple_of((me ^ k) * rows, rows)
        total[pl.ds(start, rows), :] = scores[k * rows:(k + 1) * rows]
    asked = []
    for k in range(holders):
        notes = packed_refs[k][:, width:].astype(jnp.float32)
        notes = jnp.sum(jnp.where(iota(notes.shape, 0) == me % rows, notes, 0.0), axis=0, keepdims=True)
        mine = notes[:, :capacity]
        for block in range(1, holders // rows):
            mine = jnp.where(me // rows == block, notes[:, block * capacity:(block + 1) * capacity], mine)
        asked.append(mine)
    wanted = jnp.concatenate(
        [row[:, side * half:(side + 1) * half] for side in range(2) for row in asked], axis=1
    )
    chosen = exact_bf16(iota((count, 2 * holders * half), 0).astype(jnp.float32) + 1.0 == wanted)
    picked = exact_product(total[...], chosen)
    used_ref[...] = found_ref[...]
    own_slots = found_ref.shape[1]
    used_ref[0:1] = jnp.where(iota((1, own_slots), 1) < count_ref[0], found_ref[0:1], float(holders))
    picked = jnp.concatenate([picked[:, :holders * half], picked[:, holders * half:]], axis=0).T
    for place, k in enumerate(kept_distances(holders)):
        keep_ref[place] = picked[k * half:(k + 1) * half]
        send_ref[place] = picked[(k ^ 1) * half:((k ^ 1) + 1) * half]


def spread_kernel(holders, groups, found_ref, *refs):
    landed_refs, out_refs = refs[:holders // 2], refs[holders // 2:]
    half = landed_refs[0].shape[1]
    slots = found_ref.shape[1]
    total = landed_refs[0].shape[2] // 2
    at = lax.axis_index("layer")
    share = slots // groups
    distance = found_ref[0:1].astype(jnp.int32) ^ lax.axis_index("store")
    order = [k ^ core for k in kept_distances(holders) for core in range(2)]
    begins = sum(jnp.where(distance == k, place * half + 1, 0) for place, k in enumerate(order)).astype(jnp.float32) - 1.0
    rank_there = found_ref[1:2]
    place = iota((2 * holders * half, slots), 0).astype(jnp.float32)
    upper = rank_there >= half
    target = begins + rank_there + jnp.where(upper, float(holders * half - half), 0.0)
    chosen = exact_bf16(place == jnp.where(begins >= 0.0, target, -1.0))
    landed = jnp.concatenate([ref[core] for ref in landed_refs for core in range(2)], axis=0).T
    result = exact_product(jnp.concatenate([landed[:total], landed[total:]], axis=1), chosen)
    result = result.T
    blocks = []
    for g in range(groups):
        block = result[g * share:(g + 1) * share]
        blocks.append(jnp.concatenate([block[:share // 2], block[share // 2:]], axis=1))
    for step, out_ref in enumerate(out_refs):
        chosen = blocks[0]
        for g in range(1, groups):
            chosen = jnp.where((at + step) % groups == g, blocks[g], chosen)
        out_ref[...] = chosen


def swap(value, axis, distance):
    return lax.ppermute(value, axis, [(i, i ^ distance) for i in range(lax.axis_size(axis))])


def on_device(query_grads, factor_out, factor_in, page_store, page_home, cand_lists, counts):
    holders = lax.axis_size("store")
    groups = lax.axis_size("layer")
    rows, width = query_grads.shape
    layers, rank, _ = factor_out.shape
    per_holder = page_store.shape[0]
    slots = cand_lists.shape[1]
    bf16 = jnp.bfloat16

    capacity = slots // holders
    home = page_home.reshape(-1, LANES)
    sources = [
        pltpu.with_memory_space_constraint(source, pltpu.HBM)
        for source in (query_grads, factor_in, factor_out, home, cand_lists)
    ]
    notes = max(LANES, holders // rows * capacity)
    packed, again, found = pl.pallas_call(
        functools.partial(condition_kernel, holders, capacity, per_holder),
        out_shape=[
            jax.ShapeDtypeStruct((rows, width + notes), bf16),
            jax.ShapeDtypeStruct((rows, width + notes), bf16),
            jax.ShapeDtypeStruct((8, slots), jnp.float32),
        ],
        in_specs=[HBM] * len(sources),
        out_specs=[VMEM] * 3,
        scratch_shapes=[pltpu.VMEM(source.shape, source.dtype) for source in sources]
        + [pltpu.SemaphoreType.DMA((len(sources),)), pltpu.VMEM((layers, rows * rank // 2, LANES), jnp.float32)],
        compiler_params=pltpu.CompilerParams(vmem_limit_bytes=10 * 2**20 + 24 * slots * slots),
    )(*sources)

    again, pages = pl.pallas_call(
        load_kernel,
        out_shape=[jax.ShapeDtypeStruct(again.shape, bf16), pltpu.VMEM((width, per_holder), bf16)],
        in_specs=[VMEM, HBM],
        out_specs=[VMEM] * 2,
        input_output_aliases={0: 0},
        scratch_shapes=[pltpu.VMEM(page_store.shape, bf16), pltpu.SemaphoreType.DMA((LOADS,))],
        compiler_params=pltpu.CompilerParams(vmem_limit_bytes=4 * 2**20 + 4 * per_holder * width),
        cost_estimate=pl.CostEstimate(flops=0, bytes_accessed=2 * page_store.size, transcendentals=0),
    )(again, pltpu.with_memory_space_constraint(page_store, pltpu.HBM))

    blocks = [None] * holders
    blocks[0] = packed
    for k in range(2, holders, 2):
        blocks[k] = swap(packed, "store", k)
    blocks[1] = swap(again, "store", 1)
    for k in range(2, holders, 2):
        blocks[k + 1] = swap(blocks[k], "store", 1)

    total = holders * rows
    bytes_in = 2 * holders * rows * (width + notes) + 2 * per_holder * width
    keep, send, used = pl.pallas_call(
        functools.partial(score_kernel, holders, capacity),
        out_shape=[
            jax.ShapeDtypeStruct((holders // 2, capacity // 2, 2 * total), jnp.float32),
            jax.ShapeDtypeStruct((holders // 2, capacity // 2, 2 * total), jnp.float32),
            jax.ShapeDtypeStruct(found.shape, jnp.float32),
        ],
        in_specs=[SMEM] + [VMEM] * (holders + 2),
        out_specs=[VMEM] * 3,
        scratch_shapes=[pltpu.VMEM((total, per_holder), jnp.float32), pltpu.VMEM((total, width), bf16)],
        compiler_params=pltpu.CompilerParams(vmem_limit_bytes=8 * 2**20 + 2 * bytes_in + 48 * total * slots),
    )(counts, found, *blocks[::-1], pltpu.with_memory_space_constraint(pages, pltpu.VMEM))

    handed = swap(send, "store", 1)
    landed = []
    for place, k in enumerate(kept_distances(holders)):
        pair = jnp.stack([keep[place], handed[place]])
        landed.append(swap(pair, "store", k) if k else pair)
    share = slots // groups
    terms = pl.pallas_call(
        functools.partial(spread_kernel, holders, groups),
        out_shape=[jax.ShapeDtypeStruct((share // 2, 2 * total), jnp.float32)] * groups,
        in_specs=[VMEM] * (1 + len(landed)),
        out_specs=[VMEM] * groups,
        compiler_params=pltpu.CompilerParams(vmem_limit_bytes=4 * 2**20 + 64 * total * slots),
    )(used, *landed)
    summed = terms[0]
    for step in range(1, groups):
        summed = summed + lax.ppermute(terms[step], "layer", [(g, (g + step) % groups) for g in range(groups)])
    return jnp.concatenate([summed[:, :total], summed[:, total:]], axis=0)[None]


def solution(mesh):
    placed = (
        P("store", "layer"),
        P("layer", None, None),
        P("layer", None, None),
        P("store", "layer"),
        P(),
        P("store", None),
        P("store"),
    )
    return jax.shard_map(
        on_device, mesh=mesh, in_specs=placed, out_specs=P("store", "layer", None), check_vma=False
    )
```

```python
import functools

import jax
import jax.numpy as jnp
from jax import lax
from jax.experimental import pallas as pl
from jax.experimental.pallas import tpu as pltpu
from jax.sharding import PartitionSpec as P

VMEM = pl.BlockSpec(memory_space=pltpu.VMEM)
SMEM = pl.BlockSpec(memory_space=pltpu.SMEM)
HBM = pl.BlockSpec(memory_space=pltpu.HBM)
LANES = 128
CHUNKS = 4
LOADS = 8


def iota(shape, dimension):
    return lax.broadcasted_iota(jnp.int32, shape, dimension)


def kept_distances(holders):
    return [0] + [k + 1 for k in range(2, holders, 2)]


def parts_of(value):
    parts = []
    for _ in range(3):
        part = value.astype(jnp.bfloat16)
        value = value - part.astype(jnp.float32)
        parts.append(part)
    return parts


def exact_product(value, chosen):
    rows = value.shape[0]
    product = jnp.dot(jnp.concatenate(parts_of(value), axis=0), chosen, preferred_element_type=jnp.float32)
    return product[2 * rows:] + product[rows:2 * rows] + product[:rows]


def exact_bf16(value):
    return value.astype(jnp.float32).astype(jnp.bfloat16)


def condition_kernel(holders, capacity, per_holder, *refs):
    sources, packed_ref, again_ref, found_ref, landing, arrived, turned_ref = refs[:5], *refs[5:8], refs[8:13], *refs[13:]
    copies = [
        pltpu.make_async_copy(source, target, arrived.at[i])
        for i, (source, target) in enumerate(zip(sources, landing))
    ]
    for copy in copies:
        copy.start()
    for copy in copies:
        copy.wait()
    query_ref, in_factor_ref, out_factor_ref, home_ref, cand_ref = landing
    rows, width = query_ref.shape
    layers, rank, _ = in_factor_ref.shape
    half = rank // 2
    query = query_ref[...].astype(jnp.float32)
    low = iota((half, LANES), 1) < rank
    zero = jnp.zeros((rank, rank), jnp.float32)
    terms = [(0, 0), (0, 1), (0, 2), (1, 0), (1, 1), (2, 0)]
    group = 2 * LANES
    source, place = iota((rank, 2 * group), 0), iota((rank, 2 * group), 1)
    inside = place % group
    column_found = (source == 2 * (inside % half) + place // group)
    chosen_part = sum((inside >= half * start).astype(jnp.int32) for start in (3, 5, 6))
    pickers = [exact_bf16(column_found & (chosen_part == i)) for i in range(3)]
    for layer in range(layers):
        first = layer * half
        packed = jnp.concatenate(
            [query[:, (first + t) * LANES:(first + t + 1) * LANES] for t in range(half)], axis=0
        ).astype(jnp.bfloat16)
        factor = in_factor_ref[layer]
        doubled = parts_of(
            jnp.concatenate(
                [jnp.concatenate([factor, zero], axis=1), jnp.concatenate([zero, factor], axis=1)], axis=0
            )
        )
        small = jnp.dot(
            jnp.concatenate([packed, packed], axis=1), jnp.concatenate(doubled[1:], axis=0),
            preferred_element_type=jnp.float32,
        )
        turned_ref[layer] = small + jnp.dot(packed, doubled[0], preferred_element_type=jnp.float32)
        wide = jnp.concatenate([turned_ref[layer, pl.ds(q, half, stride=rows), :] for q in range(rows)], axis=1)
        wide = parts_of(wide)
        stacked = jnp.concatenate([wide[j] for _, j in terms], axis=0)
        by_row = jnp.concatenate(
            [out_factor_ref[layer, pl.ds(parity, half, stride=2), :] for parity in range(2)], axis=0
        )
        sorted_columns = sum(
            jnp.dot(part, picker, preferred_element_type=jnp.float32) for part, picker in zip(parts_of(by_row), pickers)
        )
        quarters = jnp.concatenate(
            [
                sorted_columns[r * half:(r + 1) * half, c * group:c * group + len(terms) * half]
                for r in range(2) for c in range(2)
            ],
            axis=0,
        ).astype(jnp.bfloat16)
        left = jnp.dot(quarters, stacked, preferred_element_type=jnp.float32)
        for q in range(rows):
            part = left[:, q * LANES:(q + 1) * LANES]
            ee, eo, oe, oo = (part[i * half:(i + 1) * half] for i in range(4))
            done = jnp.where(low, ee, oo) + pltpu.roll(jnp.where(low, oe, eo), rank, 1)
            turned_ref[layer, pl.ds(q, half, stride=rows), :] = done
        for t in range(half):
            tile = turned_ref[layer, t * rows:(t + 1) * rows, :].astype(jnp.bfloat16)
            for target_ref in (packed_ref, again_ref):
                target_ref[:, (first + t) * LANES:(first + t + 1) * LANES] = tile

    slots = cand_ref.shape[1]
    home_rows = home_ref.shape[0]
    wanted = cand_ref[...]
    onehot = (iota((LANES, slots), 0) == wanted % LANES).astype(jnp.float32).astype(jnp.bfloat16)
    home = home_ref[...]
    table = jnp.concatenate([home // per_holder, home % per_holder], axis=0).astype(jnp.float32).astype(jnp.bfloat16)
    found = jnp.dot(table, onehot, preferred_element_type=jnp.float32)
    mine = iota((home_rows, slots), 0) == wanted // LANES
    holder = jnp.sum(jnp.where(mine, found[:home_rows], 0.0), axis=0, keepdims=True)
    within = jnp.sum(jnp.where(mine, found[home_rows:], 0.0), axis=0, keepdims=True)
    at_holder = iota((holders, slots), 0).astype(jnp.float32) == holder
    earlier = exact_bf16(iota((slots, slots), 0) < iota((slots, slots), 1))
    before = jnp.dot(exact_bf16(at_holder), earlier, preferred_element_type=jnp.float32)
    rank_there = jnp.sum(jnp.where(at_holder, before, 0.0), axis=0, keepdims=True)
    ranked = exact_bf16(iota((capacity, slots), 0).astype(jnp.float32) == rank_there)
    asked = lax.dot_general(
        exact_bf16(jnp.where(at_holder, within + 1.0, 0.0)), ranked, (((1,), (1,)), ((), ())),
        preferred_element_type=jnp.float32,
    )
    blocks = [asked[h:h + rows] for h in range(0, holders, rows)]
    spare = packed_ref.shape[1] - width - capacity * len(blocks)
    if spare:
        blocks.append(jnp.zeros((rows, spare), jnp.float32))
    for target_ref in (packed_ref, again_ref):
        target_ref[:, width:] = jnp.concatenate(blocks, axis=1).astype(jnp.bfloat16)
    found_ref[...] = jnp.concatenate([holder, rank_there, jnp.zeros((6, slots), jnp.float32)], axis=0)


def load_kernel(holders, count_ref, found_ref, block_ref, source_ref, same_block_ref, target_ref, used_ref, landing, arrived):
    step = landing.shape[1] // LOADS
    copies = [
        pltpu.make_async_copy(
            source_ref.at[:, pl.ds(i * step, step)], landing.at[:, pl.ds(i * step, step)], arrived.at[i]
        )
        for i in range(LOADS)
    ]
    for copy in copies:
        copy.start()
    used_ref[...] = found_ref[...]
    slots = found_ref.shape[1]
    used_ref[0:1] = jnp.where(iota((1, slots), 1) < count_ref[0], found_ref[0:1], float(holders))
    for i, copy in enumerate(copies):
        copy.wait()
        target_ref[i * step:(i + 1) * step, :] = landing[:, i * step:(i + 1) * step].T


def pick(scores, wanted):
    chosen = exact_bf16(iota((scores.shape[1], wanted.shape[1]), 0).astype(jnp.float32) + 1.0 == wanted)
    picked = exact_product(scores, chosen)
    cut = wanted.shape[1] // 2
    return jnp.concatenate([picked[:, :cut], picked[:, cut:]], axis=0).T


def score_kernel(holders, capacity, *refs):
    packed_refs, pages_ref, send_ref, scores_ref, rest_ref, queries = refs[:holders][::-1], *refs[holders:]
    me = lax.axis_index("store")
    width, count = pages_ref.shape
    rows = packed_refs[0].shape[0]
    half = capacity // 2
    step = width // CHUNKS
    scores = jnp.zeros((holders * rows, count), jnp.float32)
    for i in range(CHUNKS):
        columns = slice(i * step, (i + 1) * step)
        for k in range(holders):
            queries[k * rows:(k + 1) * rows, columns] = packed_refs[k][:, columns]
        scores = scores + jnp.dot(queries[:, columns], pages_ref[columns], preferred_element_type=jnp.float32)
    for k in range(holders):
        start = pl.multiple_of((me ^ k) * rows, rows)
        scores_ref[pl.ds(start, rows), :] = scores[k * rows:(k + 1) * rows]
    asked = []
    for k in range(holders):
        notes = packed_refs[k][:, width:].astype(jnp.float32)
        notes = jnp.sum(jnp.where(iota(notes.shape, 0) == me % rows, notes, 0.0), axis=0, keepdims=True)
        mine = notes[:, :capacity]
        for block in range(1, holders // rows):
            mine = jnp.where(me // rows == block, notes[:, block * capacity:(block + 1) * capacity], mine)
        asked.append(mine)
    kept = kept_distances(holders)
    wanted = [
        jnp.concatenate([asked[k][:, side * half:(side + 1) * half] for side in range(2) for k in distances], axis=1)
        for distances in ([k ^ 1 for k in kept], kept)
    ]
    rest_ref[...] = wanted[1]
    picked = pick(scores_ref[...], wanted[0])
    for place in range(len(kept)):
        send_ref[place] = picked[place * half:(place + 1) * half]


def rest_kernel(scores_ref, rest_ref, keep_ref):
    picked = pick(scores_ref[...], rest_ref[...])
    half = keep_ref.shape[1]
    for place in range(keep_ref.shape[0]):
        keep_ref[place] = picked[place * half:(place + 1) * half]


def spread_kernel(holders, groups, found_ref, *refs):
    landed_refs, out_refs = refs[:holders // 2], refs[holders // 2:]
    half = landed_refs[0].shape[1]
    slots = found_ref.shape[1]
    total = landed_refs[0].shape[2] // 2
    at = lax.axis_index("layer")
    share = slots // groups
    distance = found_ref[0:1].astype(jnp.int32) ^ lax.axis_index("store")
    order = [k ^ core for k in kept_distances(holders) for core in range(2)]
    begins = sum(jnp.where(distance == k, place * half + 1, 0) for place, k in enumerate(order)).astype(jnp.float32) - 1.0
    rank_there = found_ref[1:2]
    place = iota((2 * holders * half, slots), 0).astype(jnp.float32)
    upper = rank_there >= half
    target = begins + rank_there + jnp.where(upper, float(holders * half - half), 0.0)
    chosen = exact_bf16(place == jnp.where(begins >= 0.0, target, -1.0))
    landed = jnp.concatenate([ref[core] for ref in landed_refs for core in range(2)], axis=0).T
    result = exact_product(jnp.concatenate([landed[:total], landed[total:]], axis=1), chosen)
    result = result.T
    blocks = []
    for g in range(groups):
        block = result[g * share:(g + 1) * share]
        blocks.append(jnp.concatenate([block[:share // 2], block[share // 2:]], axis=1))
    for step, out_ref in enumerate(out_refs):
        chosen = blocks[0]
        for g in range(1, groups):
            chosen = jnp.where((at + step) % groups == g, blocks[g], chosen)
        out_ref[...] = chosen


def swap(value, axis, distance):
    return lax.ppermute(value, axis, [(i, i ^ distance) for i in range(lax.axis_size(axis))])


def on_device(query_grads, factor_out, factor_in, page_store, page_home, cand_lists, counts):
    holders = lax.axis_size("store")
    groups = lax.axis_size("layer")
    rows, width = query_grads.shape
    layers, rank, _ = factor_out.shape
    per_holder = page_store.shape[0]
    slots = cand_lists.shape[1]
    bf16 = jnp.bfloat16

    capacity = slots // holders
    home = page_home.reshape(-1, LANES)
    sources = [
        pltpu.with_memory_space_constraint(source, pltpu.HBM)
        for source in (query_grads, factor_in, factor_out, home, cand_lists)
    ]
    notes = max(LANES, holders // rows * capacity)
    packed, again, found = pl.pallas_call(
        functools.partial(condition_kernel, holders, capacity, per_holder),
        out_shape=[
            jax.ShapeDtypeStruct((rows, width + notes), bf16),
            jax.ShapeDtypeStruct((rows, width + notes), bf16),
            jax.ShapeDtypeStruct((8, slots), jnp.float32),
        ],
        in_specs=[HBM] * len(sources),
        out_specs=[VMEM] * 3,
        scratch_shapes=[pltpu.VMEM(source.shape, source.dtype) for source in sources]
        + [pltpu.SemaphoreType.DMA((len(sources),)), pltpu.VMEM((layers, rows * rank // 2, LANES), jnp.float32)],
        compiler_params=pltpu.CompilerParams(vmem_limit_bytes=10 * 2**20 + 24 * slots * slots),
    )(*sources)

    again, pages, used = pl.pallas_call(
        functools.partial(load_kernel, holders),
        out_shape=[
            jax.ShapeDtypeStruct(again.shape, bf16),
            pltpu.VMEM((width, per_holder), bf16),
            jax.ShapeDtypeStruct(found.shape, jnp.float32),
        ],
        in_specs=[SMEM, VMEM, VMEM, HBM],
        out_specs=[VMEM] * 3,
        input_output_aliases={2: 0},
        scratch_shapes=[pltpu.VMEM(page_store.shape, bf16), pltpu.SemaphoreType.DMA((LOADS,))],
        compiler_params=pltpu.CompilerParams(vmem_limit_bytes=4 * 2**20 + 4 * per_holder * width),
        cost_estimate=pl.CostEstimate(flops=0, bytes_accessed=2 * page_store.size, transcendentals=0),
    )(counts, found, again, pltpu.with_memory_space_constraint(page_store, pltpu.HBM))

    blocks = [None] * holders
    blocks[0] = packed
    for k in range(2, holders, 2):
        blocks[k] = swap(packed, "store", k)
    blocks[1] = swap(again, "store", 1)
    for k in range(2, holders, 2):
        blocks[k + 1] = swap(blocks[k], "store", 1)

    total = holders * rows
    bytes_in = 2 * holders * rows * (width + notes) + 2 * per_holder * width
    picked_shape = jax.ShapeDtypeStruct((holders // 2, capacity // 2, 2 * total), jnp.float32)
    send, scores, rest = pl.pallas_call(
        functools.partial(score_kernel, holders, capacity),
        out_shape=[
            picked_shape,
            jax.ShapeDtypeStruct((total, per_holder), jnp.float32),
            jax.ShapeDtypeStruct((1, slots // 2), jnp.float32),
        ],
        in_specs=[VMEM] * (holders + 1),
        out_specs=[VMEM] * 3,
        scratch_shapes=[pltpu.VMEM((total, width), bf16)],
        compiler_params=pltpu.CompilerParams(vmem_limit_bytes=8 * 2**20 + 2 * bytes_in + 48 * total * slots),
    )(*blocks[::-1], pltpu.with_memory_space_constraint(pages, pltpu.VMEM))

    handed = swap(send, "store", 1)
    keep = pl.pallas_call(
        rest_kernel,
        out_shape=picked_shape,
        in_specs=[VMEM] * 2,
        out_specs=VMEM,
        compiler_params=pltpu.CompilerParams(vmem_limit_bytes=4 * 2**20 + 24 * total * slots),
    )(scores, rest)
    landed = []
    for place, k in enumerate(kept_distances(holders)):
        pair = jnp.stack([keep[place], handed[place]])
        landed.append(swap(pair, "store", k) if k else pair)
    share = slots // groups
    terms = pl.pallas_call(
        functools.partial(spread_kernel, holders, groups),
        out_shape=[jax.ShapeDtypeStruct((share // 2, 2 * total), jnp.float32)] * groups,
        in_specs=[VMEM] * (1 + len(landed)),
        out_specs=[VMEM] * groups,
        compiler_params=pltpu.CompilerParams(vmem_limit_bytes=4 * 2**20 + 64 * total * slots),
    )(used, *landed)
    summed = terms[0]
    for step in range(1, groups):
        summed = summed + lax.ppermute(terms[step], "layer", [(g, (g + step) % groups) for g in range(groups)])
    return jnp.concatenate([summed[:, :total], summed[:, total:]], axis=0)[None]


def solution(mesh):
    placed = (
        P("store", "layer"),
        P("layer", None, None),
        P("layer", None, None),
        P("store", "layer"),
        P(),
        P("store", None),
        P("store"),
    )
    return jax.shard_map(
        on_device, mesh=mesh, in_specs=placed, out_specs=P("store", "layer", None), check_vma=False
    )
```

```python
import functools

import jax
import jax.numpy as jnp
from jax import lax
from jax.experimental import pallas as pl
from jax.experimental.pallas import tpu as pltpu
from jax.sharding import PartitionSpec as P

VMEM = pl.BlockSpec(memory_space=pltpu.VMEM)
SMEM = pl.BlockSpec(memory_space=pltpu.SMEM)
HBM = pl.BlockSpec(memory_space=pltpu.HBM)
LANES = 128
CHUNKS = 8
LOADS = 8


def iota(shape, dimension):
    return lax.broadcasted_iota(jnp.int32, shape, dimension)


def kept_distances(holders):
    return [0] + [k + 1 for k in range(2, holders, 2)]


def parts_of(value):
    parts = []
    for _ in range(3):
        part = value.astype(jnp.bfloat16)
        value = value - part.astype(jnp.float32)
        parts.append(part)
    return parts


def exact_product(value, chosen):
    rows = value.shape[0]
    product = jnp.dot(jnp.concatenate(parts_of(value), axis=0), chosen, preferred_element_type=jnp.float32)
    return product[2 * rows:] + product[rows:2 * rows] + product[:rows]


def exact_bf16(value):
    return value.astype(jnp.float32).astype(jnp.bfloat16)


def condition_kernel(holders, capacity, per_holder, *refs):
    sources, packed_ref, again_ref, found_ref, landing, arrived, turned_ref = refs[:5], *refs[5:8], refs[8:13], *refs[13:]
    copies = [
        pltpu.make_async_copy(source, target, arrived.at[i])
        for i, (source, target) in enumerate(zip(sources, landing))
    ]
    for copy in copies:
        copy.start()
    query_ref, in_factor_ref, out_factor_ref, home_ref, cand_ref = landing
    rows, width = query_ref.shape
    layers, rank, _ = in_factor_ref.shape
    half = rank // 2
    low = iota((half, LANES), 1) < rank
    zero = jnp.zeros((rank, rank), jnp.float32)
    terms = [(0, 0), (0, 1), (0, 2), (1, 0), (1, 1), (2, 0)]
    group = 2 * LANES
    source, place = iota((rank, 2 * group), 0), iota((rank, 2 * group), 1)
    inside = place % group
    column_found = (source == 2 * (inside % half) + place // group)
    chosen_part = sum((inside >= half * start).astype(jnp.int32) for start in (3, 5, 6))
    pickers = [exact_bf16(column_found & (chosen_part == i)) for i in range(3)]
    for copy in copies[1:]:
        copy.wait()
    doubled, quarters = [], []
    for layer in range(layers):
        factor = in_factor_ref[layer]
        doubled.append(
            parts_of(
                jnp.concatenate(
                    [jnp.concatenate([factor, zero], axis=1), jnp.concatenate([zero, factor], axis=1)], axis=0
                )
            )
        )
        by_row = jnp.concatenate(
            [out_factor_ref[layer, pl.ds(parity, half, stride=2), :] for parity in range(2)], axis=0
        )
        sorted_columns = sum(
            jnp.dot(part, picker, preferred_element_type=jnp.float32) for part, picker in zip(parts_of(by_row), pickers)
        )
        quarters.append(
            jnp.concatenate(
                [
                    sorted_columns[r * half:(r + 1) * half, c * group:c * group + len(terms) * half]
                    for r in range(2) for c in range(2)
                ],
                axis=0,
            ).astype(jnp.bfloat16)
        )

    slots = cand_ref.shape[1]
    home_rows = home_ref.shape[0]
    wanted = cand_ref[...]
    onehot = (iota((LANES, slots), 0) == wanted % LANES).astype(jnp.float32).astype(jnp.bfloat16)
    home = home_ref[...]
    table = jnp.concatenate([home // per_holder, home % per_holder], axis=0).astype(jnp.float32).astype(jnp.bfloat16)
    found = jnp.dot(table, onehot, preferred_element_type=jnp.float32)
    mine = iota((home_rows, slots), 0) == wanted // LANES
    holder = jnp.sum(jnp.where(mine, found[:home_rows], 0.0), axis=0, keepdims=True)
    within = jnp.sum(jnp.where(mine, found[home_rows:], 0.0), axis=0, keepdims=True)
    at_holder = iota((holders, slots), 0).astype(jnp.float32) == holder
    earlier = exact_bf16(iota((slots, slots), 0) < iota((slots, slots), 1))
    before = jnp.dot(exact_bf16(at_holder), earlier, preferred_element_type=jnp.float32)
    rank_there = jnp.sum(jnp.where(at_holder, before, 0.0), axis=0, keepdims=True)
    ranked = exact_bf16(iota((capacity, slots), 0).astype(jnp.float32) == rank_there)
    asked = lax.dot_general(
        exact_bf16(jnp.where(at_holder, within + 1.0, 0.0)), ranked, (((1,), (1,)), ((), ())),
        preferred_element_type=jnp.float32,
    )
    blocks = [asked[h:h + rows] for h in range(0, holders, rows)]
    spare = packed_ref.shape[1] - width - capacity * len(blocks)
    if spare:
        blocks.append(jnp.zeros((rows, spare), jnp.float32))
    for target_ref in (packed_ref, again_ref):
        target_ref[:, width:] = jnp.concatenate(blocks, axis=1).astype(jnp.bfloat16)
    found_ref[...] = jnp.concatenate([holder, rank_there, jnp.zeros((6, slots), jnp.float32)], axis=0)

    copies[0].wait()
    query = query_ref[...].astype(jnp.float32)
    for layer in range(layers):
        first = layer * half
        packed = jnp.concatenate(
            [query[:, (first + t) * LANES:(first + t + 1) * LANES] for t in range(half)], axis=0
        ).astype(jnp.bfloat16)
        small = jnp.dot(
            jnp.concatenate([packed, packed], axis=1), jnp.concatenate(doubled[layer][1:], axis=0),
            preferred_element_type=jnp.float32,
        )
        turned_ref[layer] = small + jnp.dot(packed, doubled[layer][0], preferred_element_type=jnp.float32)
        wide = jnp.concatenate([turned_ref[layer, pl.ds(q, half, stride=rows), :] for q in range(rows)], axis=1)
        wide = parts_of(wide)
        stacked = jnp.concatenate([wide[j] for _, j in terms], axis=0)
        left = jnp.dot(quarters[layer], stacked, preferred_element_type=jnp.float32)
        for q in range(rows):
            part = left[:, q * LANES:(q + 1) * LANES]
            ee, eo, oe, oo = (part[i * half:(i + 1) * half] for i in range(4))
            done = jnp.where(low, ee, oo) + pltpu.roll(jnp.where(low, oe, eo), rank, 1)
            turned_ref[layer, pl.ds(q, half, stride=rows), :] = done
        for t in range(half):
            tile = turned_ref[layer, t * rows:(t + 1) * rows, :].astype(jnp.bfloat16)
            for target_ref in (packed_ref, again_ref):
                target_ref[:, (first + t) * LANES:(first + t + 1) * LANES] = tile


def load_kernel(holders, count_ref, found_ref, block_ref, source_ref, same_block_ref, target_ref, used_ref, landing, arrived):
    step = landing.shape[1] // LOADS
    copies = [
        pltpu.make_async_copy(
            source_ref.at[:, pl.ds(i * step, step)], landing.at[:, pl.ds(i * step, step)], arrived.at[i]
        )
        for i in range(LOADS)
    ]
    for copy in copies:
        copy.start()
    used_ref[...] = found_ref[...]
    slots = found_ref.shape[1]
    used_ref[0:1] = jnp.where(iota((1, slots), 1) < count_ref[0], found_ref[0:1], float(holders))
    for i, copy in enumerate(copies):
        copy.wait()
        target_ref[i * step:(i + 1) * step, :] = landing[:, i * step:(i + 1) * step].T


def pick(scores, wanted):
    chosen = exact_bf16(iota((scores.shape[1], wanted.shape[1]), 0).astype(jnp.float32) + 1.0 == wanted)
    picked = exact_product(scores, chosen)
    cut = wanted.shape[1] // 2
    return jnp.concatenate([picked[:, :cut], picked[:, cut:]], axis=0).T


def score_kernel(holders, capacity, *refs):
    packed_refs, pages_ref, send_ref, scores_ref, rest_ref, queries = refs[:holders][::-1], *refs[holders:]
    me = lax.axis_index("store")
    width, count = pages_ref.shape
    rows = packed_refs[0].shape[0]
    half = capacity // 2
    step = width // CHUNKS
    scores = jnp.zeros((holders * rows, count), jnp.float32)
    for i in range(CHUNKS):
        columns = slice(i * step, (i + 1) * step)
        for k in range(holders):
            queries[k * rows:(k + 1) * rows, columns] = packed_refs[k][:, columns]
        scores = scores + jnp.dot(queries[:, columns], pages_ref[columns], preferred_element_type=jnp.float32)
    for k in range(holders):
        start = pl.multiple_of((me ^ k) * rows, rows)
        scores_ref[pl.ds(start, rows), :] = scores[k * rows:(k + 1) * rows]
    asked = []
    for k in range(holders):
        notes = packed_refs[k][:, width:].astype(jnp.float32)
        notes = jnp.sum(jnp.where(iota(notes.shape, 0) == me % rows, notes, 0.0), axis=0, keepdims=True)
        mine = notes[:, :capacity]
        for block in range(1, holders // rows):
            mine = jnp.where(me // rows == block, notes[:, block * capacity:(block + 1) * capacity], mine)
        asked.append(mine)
    kept = kept_distances(holders)
    wanted = [
        jnp.concatenate([asked[k][:, side * half:(side + 1) * half] for side in range(2) for k in distances], axis=1)
        for distances in ([k ^ 1 for k in kept], kept)
    ]
    rest_ref[...] = wanted[1]
    picked = pick(scores_ref[...], wanted[0])
    for place in range(len(kept)):
        send_ref[place] = picked[place * half:(place + 1) * half]


def rest_kernel(scores_ref, rest_ref, keep_ref):
    picked = pick(scores_ref[...], rest_ref[...])
    half = keep_ref.shape[1]
    for place in range(keep_ref.shape[0]):
        keep_ref[place] = picked[place * half:(place + 1) * half]


def spread_kernel(holders, groups, found_ref, *refs):
    landed_refs, out_refs = refs[:holders // 2], refs[holders // 2:]
    half = landed_refs[0].shape[1]
    slots = found_ref.shape[1]
    total = landed_refs[0].shape[2] // 2
    at = lax.axis_index("layer")
    share = slots // groups
    distance = found_ref[0:1].astype(jnp.int32) ^ lax.axis_index("store")
    order = [k ^ core for k in kept_distances(holders) for core in range(2)]
    begins = sum(jnp.where(distance == k, place * half + 1, 0) for place, k in enumerate(order)).astype(jnp.float32) - 1.0
    rank_there = found_ref[1:2]
    place = iota((2 * holders * half, slots), 0).astype(jnp.float32)
    upper = rank_there >= half
    target = begins + rank_there + jnp.where(upper, float(holders * half - half), 0.0)
    chosen = exact_bf16(place == jnp.where(begins >= 0.0, target, -1.0))
    landed = jnp.concatenate([ref[core] for ref in landed_refs for core in range(2)], axis=0).T
    result = exact_product(jnp.concatenate([landed[:total], landed[total:]], axis=1), chosen)
    result = result.T
    blocks = []
    for g in range(groups):
        block = result[g * share:(g + 1) * share]
        blocks.append(jnp.concatenate([block[:share // 2], block[share // 2:]], axis=1))
    for step, out_ref in enumerate(out_refs):
        chosen = blocks[0]
        for g in range(1, groups):
            chosen = jnp.where((at + step) % groups == g, blocks[g], chosen)
        out_ref[...] = chosen


def swap(value, axis, distance):
    return lax.ppermute(value, axis, [(i, i ^ distance) for i in range(lax.axis_size(axis))])


def on_device(query_grads, factor_out, factor_in, page_store, page_home, cand_lists, counts):
    holders = lax.axis_size("store")
    groups = lax.axis_size("layer")
    rows, width = query_grads.shape
    layers, rank, _ = factor_out.shape
    per_holder = page_store.shape[0]
    slots = cand_lists.shape[1]
    bf16 = jnp.bfloat16

    capacity = slots // holders
    home = page_home.reshape(-1, LANES)
    sources = [
        pltpu.with_memory_space_constraint(source, pltpu.HBM)
        for source in (query_grads, factor_in, factor_out, home, cand_lists)
    ]
    notes = max(LANES, holders // rows * capacity)
    packed, again, found = pl.pallas_call(
        functools.partial(condition_kernel, holders, capacity, per_holder),
        out_shape=[
            jax.ShapeDtypeStruct((rows, width + notes), bf16),
            jax.ShapeDtypeStruct((rows, width + notes), bf16),
            jax.ShapeDtypeStruct((8, slots), jnp.float32),
        ],
        in_specs=[HBM] * len(sources),
        out_specs=[VMEM] * 3,
        scratch_shapes=[pltpu.VMEM(source.shape, source.dtype) for source in sources]
        + [pltpu.SemaphoreType.DMA((len(sources),)), pltpu.VMEM((layers, rows * rank // 2, LANES), jnp.float32)],
        compiler_params=pltpu.CompilerParams(vmem_limit_bytes=10 * 2**20 + 24 * slots * slots),
    )(*sources)

    again, pages, used = pl.pallas_call(
        functools.partial(load_kernel, holders),
        out_shape=[
            jax.ShapeDtypeStruct(again.shape, bf16),
            pltpu.VMEM((width, per_holder), bf16),
            jax.ShapeDtypeStruct(found.shape, jnp.float32),
        ],
        in_specs=[SMEM, VMEM, VMEM, HBM],
        out_specs=[VMEM] * 3,
        input_output_aliases={2: 0},
        scratch_shapes=[pltpu.VMEM(page_store.shape, bf16), pltpu.SemaphoreType.DMA((LOADS,))],
        compiler_params=pltpu.CompilerParams(vmem_limit_bytes=4 * 2**20 + 4 * per_holder * width),
        cost_estimate=pl.CostEstimate(flops=0, bytes_accessed=2 * page_store.size, transcendentals=0),
    )(counts, found, again, pltpu.with_memory_space_constraint(page_store, pltpu.HBM))

    blocks = [None] * holders
    blocks[0] = packed
    for k in range(2, holders, 2):
        blocks[k] = swap(packed, "store", k)
    blocks[1] = swap(again, "store", 1)
    for k in range(2, holders, 2):
        blocks[k + 1] = swap(blocks[k], "store", 1)

    total = holders * rows
    bytes_in = 2 * holders * rows * (width + notes) + 2 * per_holder * width
    picked_shape = jax.ShapeDtypeStruct((holders // 2, capacity // 2, 2 * total), jnp.float32)
    send, scores, rest = pl.pallas_call(
        functools.partial(score_kernel, holders, capacity),
        out_shape=[
            picked_shape,
            jax.ShapeDtypeStruct((total, per_holder), jnp.float32),
            jax.ShapeDtypeStruct((1, slots // 2), jnp.float32),
        ],
        in_specs=[VMEM] * (holders + 1),
        out_specs=[VMEM] * 3,
        scratch_shapes=[pltpu.VMEM((total, width), bf16)],
        compiler_params=pltpu.CompilerParams(vmem_limit_bytes=8 * 2**20 + 2 * bytes_in + 48 * total * slots),
    )(*blocks[::-1], pltpu.with_memory_space_constraint(pages, pltpu.VMEM))

    handed = swap(send, "store", 1)
    keep = pl.pallas_call(
        rest_kernel,
        out_shape=picked_shape,
        in_specs=[VMEM] * 2,
        out_specs=VMEM,
        compiler_params=pltpu.CompilerParams(vmem_limit_bytes=4 * 2**20 + 24 * total * slots),
    )(scores, rest)
    landed = []
    for place, k in enumerate(kept_distances(holders)):
        pair = jnp.stack([keep[place], handed[place]])
        landed.append(swap(pair, "store", k) if k else pair)
    share = slots // groups
    terms = pl.pallas_call(
        functools.partial(spread_kernel, holders, groups),
        out_shape=[jax.ShapeDtypeStruct((share // 2, 2 * total), jnp.float32)] * groups,
        in_specs=[VMEM] * (1 + len(landed)),
        out_specs=[VMEM] * groups,
        compiler_params=pltpu.CompilerParams(vmem_limit_bytes=4 * 2**20 + 64 * total * slots),
    )(used, *landed)
    summed = terms[0]
    for step in range(1, groups):
        summed = summed + lax.ppermute(terms[step], "layer", [(g, (g + step) % groups) for g in range(groups)])
    return jnp.concatenate([summed[:, :total], summed[:, total:]], axis=0)[None]


def solution(mesh):
    placed = (
        P("store", "layer"),
        P("layer", None, None),
        P("layer", None, None),
        P("store", "layer"),
        P(),
        P("store", None),
        P("store"),
    )
    return jax.shard_map(
        on_device, mesh=mesh, in_specs=placed, out_specs=P("store", "layer", None), check_vma=False
    )
```

```python
import functools

import jax
import jax.numpy as jnp
from jax import lax
from jax.experimental import pallas as pl
from jax.experimental.pallas import tpu as pltpu
from jax.sharding import PartitionSpec as P

VMEM = pl.BlockSpec(memory_space=pltpu.VMEM)
SMEM = pl.BlockSpec(memory_space=pltpu.SMEM)
HBM = pl.BlockSpec(memory_space=pltpu.HBM)
LANES = 128
CHUNKS = 4
LOADS = 8


def iota(shape, dimension):
    return lax.broadcasted_iota(jnp.int32, shape, dimension)


def parts_of(value):
    parts = []
    for _ in range(3):
        part = value.astype(jnp.bfloat16)
        value = value - part.astype(jnp.float32)
        parts.append(part)
    return parts


def exact_product(value, chosen):
    rows = value.shape[0]
    product = jnp.dot(jnp.concatenate(parts_of(value), axis=0), chosen, preferred_element_type=jnp.float32)
    return product[2 * rows:] + product[rows:2 * rows] + product[:rows]


def exact_bf16(value):
    return value.astype(jnp.float32).astype(jnp.bfloat16)


def condition_kernel(holders, capacity, per_holder, *refs):
    sources, packed_ref, again_ref, found_ref, landing, arrived, turned_ref = refs[:5], *refs[5:8], refs[8:13], *refs[13:]
    copies = [
        pltpu.make_async_copy(source, target, arrived.at[i])
        for i, (source, target) in enumerate(zip(sources, landing))
    ]
    for copy in copies:
        copy.start()
    for copy in copies:
        copy.wait()
    query_ref, in_factor_ref, out_factor_ref, home_ref, cand_ref = landing
    rows, width = query_ref.shape
    layers, rank, _ = in_factor_ref.shape
    half = rank // 2
    query = query_ref[...].astype(jnp.float32)
    low = iota((half, LANES), 1) < rank
    zero = jnp.zeros((rank, rank), jnp.float32)
    terms = [(0, 0), (0, 1), (0, 2), (1, 0), (1, 1), (2, 0)]
    group = 2 * LANES
    source, place = iota((rank, 2 * group), 0), iota((rank, 2 * group), 1)
    inside = place % group
    column_found = (source == 2 * (inside % half) + place // group)
    chosen_part = sum((inside >= half * start).astype(jnp.int32) for start in (3, 5, 6))
    pickers = [exact_bf16(column_found & (chosen_part == i)) for i in range(3)]
    for layer in range(layers):
        first = layer * half
        packed = jnp.concatenate(
            [query[:, (first + t) * LANES:(first + t + 1) * LANES] for t in range(half)], axis=0
        ).astype(jnp.bfloat16)
        factor = in_factor_ref[layer]
        doubled = parts_of(
            jnp.concatenate(
                [jnp.concatenate([factor, zero], axis=1), jnp.concatenate([zero, factor], axis=1)], axis=0
            )
        )
        small = jnp.dot(
            jnp.concatenate([packed, packed], axis=1), jnp.concatenate(doubled[1:], axis=0),
            preferred_element_type=jnp.float32,
        )
        turned_ref[layer] = small + jnp.dot(packed, doubled[0], preferred_element_type=jnp.float32)
        wide = jnp.concatenate([turned_ref[layer, pl.ds(q, half, stride=rows), :] for q in range(rows)], axis=1)
        wide = parts_of(wide)
        stacked = jnp.concatenate([wide[j] for _, j in terms], axis=0)
        by_row = jnp.concatenate(
            [out_factor_ref[layer, pl.ds(parity, half, stride=2), :] for parity in range(2)], axis=0
        )
        sorted_columns = sum(
            jnp.dot(part, picker, preferred_element_type=jnp.float32) for part, picker in zip(parts_of(by_row), pickers)
        )
        quarters = jnp.concatenate(
            [
                sorted_columns[r * half:(r + 1) * half, c * group:c * group + len(terms) * half]
                for r in range(2) for c in range(2)
            ],
            axis=0,
        ).astype(jnp.bfloat16)
        left = jnp.dot(quarters, stacked, preferred_element_type=jnp.float32)
        for q in range(rows):
            part = left[:, q * LANES:(q + 1) * LANES]
            ee, eo, oe, oo = (part[i * half:(i + 1) * half] for i in range(4))
            done = jnp.where(low, ee, oo) + pltpu.roll(jnp.where(low, oe, eo), rank, 1)
            turned_ref[layer, pl.ds(q, half, stride=rows), :] = done
        for t in range(half):
            tile = turned_ref[layer, t * rows:(t + 1) * rows, :].astype(jnp.bfloat16)
            for target_ref in (packed_ref, again_ref):
                target_ref[:, (first + t) * LANES:(first + t + 1) * LANES] = tile

    slots = cand_ref.shape[1]
    home_rows = home_ref.shape[0]
    wanted = cand_ref[...]
    onehot = (iota((LANES, slots), 0) == wanted % LANES).astype(jnp.float32).astype(jnp.bfloat16)
    home = home_ref[...]
    table = jnp.concatenate([home // per_holder, home % per_holder], axis=0).astype(jnp.float32).astype(jnp.bfloat16)
    found = jnp.dot(table, onehot, preferred_element_type=jnp.float32)
    mine = iota((home_rows, slots), 0) == wanted // LANES
    holder = jnp.sum(jnp.where(mine, found[:home_rows], 0.0), axis=0, keepdims=True)
    within = jnp.sum(jnp.where(mine, found[home_rows:], 0.0), axis=0, keepdims=True)
    at_holder = iota((holders, slots), 0).astype(jnp.float32) == holder
    earlier = exact_bf16(iota((slots, slots), 0) < iota((slots, slots), 1))
    before = jnp.dot(exact_bf16(at_holder), earlier, preferred_element_type=jnp.float32)
    rank_there = jnp.sum(jnp.where(at_holder, before, 0.0), axis=0, keepdims=True)
    ranked = exact_bf16(iota((capacity, slots), 0).astype(jnp.float32) == rank_there)
    asked = lax.dot_general(
        exact_bf16(jnp.where(at_holder, within + 1.0, 0.0)), ranked, (((1,), (1,)), ((), ())),
        preferred_element_type=jnp.float32,
    )
    blocks = [asked[h:h + rows] for h in range(0, holders, rows)]
    spare = packed_ref.shape[1] - width - capacity * len(blocks)
    if spare:
        blocks.append(jnp.zeros((rows, spare), jnp.float32))
    for target_ref in (packed_ref, again_ref):
        target_ref[:, width:] = jnp.concatenate(blocks, axis=1).astype(jnp.bfloat16)
    found_ref[...] = jnp.concatenate([holder, rank_there, jnp.zeros((6, slots), jnp.float32)], axis=0)


def load_kernel(holders, count_ref, found_ref, block_ref, source_ref, same_block_ref, target_ref, used_ref, landing, arrived):
    step = landing.shape[1] // LOADS
    copies = [
        pltpu.make_async_copy(
            source_ref.at[:, pl.ds(i * step, step)], landing.at[:, pl.ds(i * step, step)], arrived.at[i]
        )
        for i in range(LOADS)
    ]
    for copy in copies:
        copy.start()
    used_ref[...] = found_ref[...]
    slots = found_ref.shape[1]
    used_ref[0:1] = jnp.where(iota((1, slots), 1) < count_ref[0], found_ref[0:1], float(holders))
    for i, copy in enumerate(copies):
        copy.wait()
        target_ref[i * step:(i + 1) * step, :] = landing[:, i * step:(i + 1) * step].T


def pick(scores, wanted):
    chosen = exact_bf16(iota((scores.shape[1], wanted.shape[1]), 0).astype(jnp.float32) + 1.0 == wanted)
    picked = exact_product(scores, chosen)
    cut = wanted.shape[1] // 2
    return jnp.concatenate([picked[:, :cut], picked[:, cut:]], axis=0).T


def score_kernel(holders, capacity, *refs):
    packed_refs, pages_ref, send_ref, scores_ref, rest_ref, queries = refs[:holders][::-1], *refs[holders:]
    me = lax.axis_index("store")
    width, count = pages_ref.shape
    rows = packed_refs[0].shape[0]
    half = capacity // 2
    step = width // CHUNKS
    scores = jnp.zeros((holders * rows, count), jnp.float32)
    for i in range(CHUNKS):
        columns = slice(i * step, (i + 1) * step)
        for k in range(holders):
            queries[k * rows:(k + 1) * rows, columns] = packed_refs[k][:, columns]
        scores = scores + jnp.dot(queries[:, columns], pages_ref[columns], preferred_element_type=jnp.float32)
    for k in range(holders):
        start = pl.multiple_of((me ^ k) * rows, rows)
        scores_ref[pl.ds(start, rows), :] = scores[k * rows:(k + 1) * rows]
    asked = []
    for k in range(holders):
        notes = packed_refs[k][:, width:].astype(jnp.float32)
        notes = jnp.sum(jnp.where(iota(notes.shape, 0) == me % rows, notes, 0.0), axis=0, keepdims=True)
        mine = notes[:, :capacity]
        for block in range(1, holders // rows):
            mine = jnp.where(me // rows == block, notes[:, block * capacity:(block + 1) * capacity], mine)
        asked.append(mine)
    chips = holders // 2
    chip = me // 2
    kept, handed = [asked[0]], [asked[1]]
    for step in range(1, chips):
        apart = chip ^ ((chip + step) % chips)
        for rows_of, core in ((kept, 1), (handed, 0)):
            chosen = asked[2 + core]
            for distance in range(2, chips):
                chosen = jnp.where(apart == distance, asked[2 * distance + core], chosen)
            rows_of.append(chosen)
    wanted = [
        jnp.concatenate([row[:, side * half:(side + 1) * half] for side in range(2) for row in rows_of], axis=1)
        for rows_of in (handed, kept)
    ]
    rest_ref[...] = wanted[1]
    picked = pick(scores_ref[...], wanted[0])
    for place in range(chips):
        send_ref[place] = picked[place * half:(place + 1) * half]


def rest_kernel(scores_ref, rest_ref, keep_ref):
    picked = pick(scores_ref[...], rest_ref[...])
    half = keep_ref.shape[1]
    for place in range(keep_ref.shape[0]):
        keep_ref[place] = picked[place * half:(place + 1) * half]


def spread_kernel(holders, groups, found_ref, *refs):
    landed_refs, out_refs = refs[:holders // 2][::-1], refs[holders // 2:]
    half = landed_refs[0].shape[1]
    slots = found_ref.shape[1]
    total = landed_refs[0].shape[2] // 2
    at = lax.axis_index("layer")
    share = slots // groups
    me = lax.axis_index("store")
    chips = holders // 2
    holder = found_ref[0:1].astype(jnp.int32)
    step = (me // 2 - holder // 2 + 2 * chips) % chips
    same_core = (holder % 2 == me % 2).astype(jnp.int32)
    place = 2 * step + jnp.where(step == 0, 1 - same_core, same_core)
    begins = jnp.where(holder < holders, place * half, -1).astype(jnp.float32)
    rank_there = found_ref[1:2]
    place = iota((2 * holders * half, slots), 0).astype(jnp.float32)
    upper = rank_there >= half
    target = begins + rank_there + jnp.where(upper, float(holders * half - half), 0.0)
    chosen = exact_bf16(place == jnp.where(begins >= 0.0, target, -1.0))
    landed = jnp.concatenate([ref[core] for ref in landed_refs for core in range(2)], axis=0).T
    result = exact_product(jnp.concatenate([landed[:total], landed[total:]], axis=1), chosen)
    result = result.T
    blocks = []
    for g in range(groups):
        block = result[g * share:(g + 1) * share]
        blocks.append(jnp.concatenate([block[:share // 2], block[share // 2:]], axis=1))
    for step, out_ref in enumerate(out_refs):
        chosen = blocks[0]
        for g in range(1, groups):
            chosen = jnp.where((at + step) % groups == g, blocks[g], chosen)
        out_ref[...] = chosen


def swap(value, axis, distance):
    return lax.ppermute(value, axis, [(i, i ^ distance) for i in range(lax.axis_size(axis))])


def on_device(query_grads, factor_out, factor_in, page_store, page_home, cand_lists, counts):
    holders = lax.axis_size("store")
    groups = lax.axis_size("layer")
    rows, width = query_grads.shape
    layers, rank, _ = factor_out.shape
    per_holder = page_store.shape[0]
    slots = cand_lists.shape[1]
    bf16 = jnp.bfloat16

    capacity = slots // holders
    home = page_home.reshape(-1, LANES)
    sources = [
        pltpu.with_memory_space_constraint(source, pltpu.HBM)
        for source in (query_grads, factor_in, factor_out, home, cand_lists)
    ]
    notes = max(LANES, holders // rows * capacity)
    packed, again, found = pl.pallas_call(
        functools.partial(condition_kernel, holders, capacity, per_holder),
        out_shape=[
            jax.ShapeDtypeStruct((rows, width + notes), bf16),
            jax.ShapeDtypeStruct((rows, width + notes), bf16),
            jax.ShapeDtypeStruct((8, slots), jnp.float32),
        ],
        in_specs=[HBM] * len(sources),
        out_specs=[VMEM] * 3,
        scratch_shapes=[pltpu.VMEM(source.shape, source.dtype) for source in sources]
        + [pltpu.SemaphoreType.DMA((len(sources),)), pltpu.VMEM((layers, rows * rank // 2, LANES), jnp.float32)],
        compiler_params=pltpu.CompilerParams(vmem_limit_bytes=10 * 2**20 + 24 * slots * slots),
    )(*sources)

    again, pages, used = pl.pallas_call(
        functools.partial(load_kernel, holders),
        out_shape=[
            jax.ShapeDtypeStruct(again.shape, bf16),
            pltpu.VMEM((width, per_holder), bf16),
            jax.ShapeDtypeStruct(found.shape, jnp.float32),
        ],
        in_specs=[SMEM, VMEM, VMEM, HBM],
        out_specs=[VMEM] * 3,
        input_output_aliases={2: 0},
        scratch_shapes=[pltpu.VMEM(page_store.shape, bf16), pltpu.SemaphoreType.DMA((LOADS,))],
        compiler_params=pltpu.CompilerParams(vmem_limit_bytes=4 * 2**20 + 4 * per_holder * width),
        cost_estimate=pl.CostEstimate(flops=0, bytes_accessed=2 * page_store.size, transcendentals=0),
    )(counts, found, again, pltpu.with_memory_space_constraint(page_store, pltpu.HBM))

    blocks = [None] * holders
    blocks[0] = packed
    for k in range(2, holders, 2):
        blocks[k] = swap(packed, "store", k)
    blocks[1] = swap(again, "store", 1)
    for k in range(2, holders, 2):
        blocks[k + 1] = swap(blocks[k], "store", 1)

    total = holders * rows
    bytes_in = 2 * holders * rows * (width + notes) + 2 * per_holder * width
    picked_shape = jax.ShapeDtypeStruct((holders // 2, capacity // 2, 2 * total), jnp.float32)
    send, scores, rest = pl.pallas_call(
        functools.partial(score_kernel, holders, capacity),
        out_shape=[
            picked_shape,
            jax.ShapeDtypeStruct((total, per_holder), jnp.float32),
            jax.ShapeDtypeStruct((1, slots // 2), jnp.float32),
        ],
        in_specs=[VMEM] * (holders + 1),
        out_specs=[VMEM] * 3,
        scratch_shapes=[pltpu.VMEM((total, width), bf16)],
        compiler_params=pltpu.CompilerParams(vmem_limit_bytes=8 * 2**20 + 2 * bytes_in + 48 * total * slots),
    )(*blocks[::-1], pltpu.with_memory_space_constraint(pages, pltpu.VMEM))

    handed = swap(send, "store", 1)
    keep = pl.pallas_call(
        rest_kernel,
        out_shape=picked_shape,
        in_specs=[VMEM] * 2,
        out_specs=VMEM,
        compiler_params=pltpu.CompilerParams(vmem_limit_bytes=4 * 2**20 + 24 * total * slots),
    )(scores, rest)
    chips = holders // 2
    landed = []
    for step in range(chips):
        pair = jnp.stack([keep[step], handed[step]])
        to = [(i, (i // 2 + step) % chips * 2 + 1 - i % 2) for i in range(holders)]
        landed.append(lax.ppermute(pair, "store", to) if step else pair)
    share = slots // groups
    terms = pl.pallas_call(
        functools.partial(spread_kernel, holders, groups),
        out_shape=[jax.ShapeDtypeStruct((share // 2, 2 * total), jnp.float32)] * groups,
        in_specs=[VMEM] * (1 + len(landed)),
        out_specs=[VMEM] * groups,
        compiler_params=pltpu.CompilerParams(vmem_limit_bytes=4 * 2**20 + 64 * total * slots),
    )(used, *landed[::-1])
    summed = terms[0]
    for step in range(1, groups):
        summed = summed + lax.ppermute(terms[step], "layer", [(g, (g + step) % groups) for g in range(groups)])
    return jnp.concatenate([summed[:, :total], summed[:, total:]], axis=0)[None]


def solution(mesh):
    placed = (
        P("store", "layer"),
        P("layer", None, None),
        P("layer", None, None),
        P("store", "layer"),
        P(),
        P("store", None),
        P("store"),
    )
    return jax.shard_map(
        on_device, mesh=mesh, in_specs=placed, out_specs=P("store", "layer", None), check_vma=False
    )
```

```python
import functools

import jax
import jax.numpy as jnp
from jax import lax
from jax.experimental import pallas as pl
from jax.experimental.pallas import tpu as pltpu
from jax.sharding import PartitionSpec as P

VMEM = pl.BlockSpec(memory_space=pltpu.VMEM)
SMEM = pl.BlockSpec(memory_space=pltpu.SMEM)
HBM = pl.BlockSpec(memory_space=pltpu.HBM)
LANES = 128
CHUNKS = 4
LOADS = 8


def iota(shape, dimension):
    return lax.broadcasted_iota(jnp.int32, shape, dimension)


def ring_place(chip, chips):
    return chip % 2 * 2 + chip // 2 if chips == 4 else chip


def parts_of(value):
    parts = []
    for _ in range(3):
        part = value.astype(jnp.bfloat16)
        value = value - part.astype(jnp.float32)
        parts.append(part)
    return parts


def exact_product(value, chosen):
    rows = value.shape[0]
    product = jnp.dot(jnp.concatenate(parts_of(value), axis=0), chosen, preferred_element_type=jnp.float32)
    return product[2 * rows:] + product[rows:2 * rows] + product[:rows]


def exact_bf16(value):
    return value.astype(jnp.float32).astype(jnp.bfloat16)


def condition_kernel(holders, capacity, per_holder, *refs):
    sources, packed_ref, again_ref, found_ref, landing, arrived, turned_ref = refs[:5], *refs[5:8], refs[8:13], *refs[13:]
    copies = [
        pltpu.make_async_copy(source, target, arrived.at[i])
        for i, (source, target) in enumerate(zip(sources, landing))
    ]
    for copy in copies:
        copy.start()
    for copy in copies:
        copy.wait()
    query_ref, in_factor_ref, out_factor_ref, home_ref, cand_ref = landing
    rows, width = query_ref.shape
    layers, rank, _ = in_factor_ref.shape
    half = rank // 2
    query = query_ref[...].astype(jnp.float32)
    low = iota((half, LANES), 1) < rank
    zero = jnp.zeros((rank, rank), jnp.float32)
    terms = [(0, 0), (0, 1), (0, 2), (1, 0), (1, 1), (2, 0)]
    group = 2 * LANES
    source, place = iota((rank, 2 * group), 0), iota((rank, 2 * group), 1)
    inside = place % group
    column_found = (source == 2 * (inside % half) + place // group)
    chosen_part = sum((inside >= half * start).astype(jnp.int32) for start in (3, 5, 6))
    pickers = [exact_bf16(column_found & (chosen_part == i)) for i in range(3)]
    for layer in range(layers):
        first = layer * half
        packed = jnp.concatenate(
            [query[:, (first + t) * LANES:(first + t + 1) * LANES] for t in range(half)], axis=0
        ).astype(jnp.bfloat16)
        factor = in_factor_ref[layer]
        doubled = parts_of(
            jnp.concatenate(
                [jnp.concatenate([factor, zero], axis=1), jnp.concatenate([zero, factor], axis=1)], axis=0
            )
        )
        small = jnp.dot(
            jnp.concatenate([packed, packed], axis=1), jnp.concatenate(doubled[1:], axis=0),
            preferred_element_type=jnp.float32,
        )
        turned_ref[layer] = small + jnp.dot(packed, doubled[0], preferred_element_type=jnp.float32)
        wide = jnp.concatenate([turned_ref[layer, pl.ds(q, half, stride=rows), :] for q in range(rows)], axis=1)
        wide = parts_of(wide)
        stacked = jnp.concatenate([wide[j] for _, j in terms], axis=0)
        by_row = jnp.concatenate(
            [out_factor_ref[layer, pl.ds(parity, half, stride=2), :] for parity in range(2)], axis=0
        )
        sorted_columns = sum(
            jnp.dot(part, picker, preferred_element_type=jnp.float32) for part, picker in zip(parts_of(by_row), pickers)
        )
        quarters = jnp.concatenate(
            [
                sorted_columns[r * half:(r + 1) * half, c * group:c * group + len(terms) * half]
                for r in range(2) for c in range(2)
            ],
            axis=0,
        ).astype(jnp.bfloat16)
        left = jnp.dot(quarters, stacked, preferred_element_type=jnp.float32)
        for q in range(rows):
            part = left[:, q * LANES:(q + 1) * LANES]
            ee, eo, oe, oo = (part[i * half:(i + 1) * half] for i in range(4))
            done = jnp.where(low, ee, oo) + pltpu.roll(jnp.where(low, oe, eo), rank, 1)
            turned_ref[layer, pl.ds(q, half, stride=rows), :] = done
        for t in range(half):
            tile = turned_ref[layer, t * rows:(t + 1) * rows, :].astype(jnp.bfloat16)
            for target_ref in (packed_ref, again_ref):
                target_ref[:, (first + t) * LANES:(first + t + 1) * LANES] = tile

    slots = cand_ref.shape[1]
    home_rows = home_ref.shape[0]
    wanted = cand_ref[...]
    onehot = (iota((LANES, slots), 0) == wanted % LANES).astype(jnp.float32).astype(jnp.bfloat16)
    home = home_ref[...]
    table = jnp.concatenate([home // per_holder, home % per_holder], axis=0).astype(jnp.float32).astype(jnp.bfloat16)
    found = jnp.dot(table, onehot, preferred_element_type=jnp.float32)
    mine = iota((home_rows, slots), 0) == wanted // LANES
    holder = jnp.sum(jnp.where(mine, found[:home_rows], 0.0), axis=0, keepdims=True)
    within = jnp.sum(jnp.where(mine, found[home_rows:], 0.0), axis=0, keepdims=True)
    at_holder = iota((holders, slots), 0).astype(jnp.float32) == holder
    earlier = exact_bf16(iota((slots, slots), 0) < iota((slots, slots), 1))
    before = jnp.dot(exact_bf16(at_holder), earlier, preferred_element_type=jnp.float32)
    rank_there = jnp.sum(jnp.where(at_holder, before, 0.0), axis=0, keepdims=True)
    ranked = exact_bf16(iota((capacity, slots), 0).astype(jnp.float32) == rank_there)
    asked = lax.dot_general(
        exact_bf16(jnp.where(at_holder, within + 1.0, 0.0)), ranked, (((1,), (1,)), ((), ())),
        preferred_element_type=jnp.float32,
    )
    blocks = [asked[h:h + rows] for h in range(0, holders, rows)]
    spare = packed_ref.shape[1] - width - capacity * len(blocks)
    if spare:
        blocks.append(jnp.zeros((rows, spare), jnp.float32))
    for target_ref in (packed_ref, again_ref):
        target_ref[:, width:] = jnp.concatenate(blocks, axis=1).astype(jnp.bfloat16)
    found_ref[...] = jnp.concatenate([holder, rank_there, jnp.zeros((6, slots), jnp.float32)], axis=0)


def load_kernel(holders, count_ref, found_ref, block_ref, source_ref, same_block_ref, target_ref, used_ref, landing, arrived):
    step = landing.shape[1] // LOADS
    copies = [
        pltpu.make_async_copy(
            source_ref.at[:, pl.ds(i * step, step)], landing.at[:, pl.ds(i * step, step)], arrived.at[i]
        )
        for i in range(LOADS)
    ]
    for copy in copies:
        copy.start()
    used_ref[...] = found_ref[...]
    slots = found_ref.shape[1]
    used_ref[0:1] = jnp.where(iota((1, slots), 1) < count_ref[0], found_ref[0:1], float(holders))
    for i, copy in enumerate(copies):
        copy.wait()
        target_ref[i * step:(i + 1) * step, :] = landing[:, i * step:(i + 1) * step].T


def pick(scores, wanted):
    chosen = exact_bf16(iota((scores.shape[1], wanted.shape[1]), 0).astype(jnp.float32) + 1.0 == wanted)
    picked = exact_product(scores, chosen)
    cut = wanted.shape[1] // 2
    return jnp.concatenate([picked[:, :cut], picked[:, cut:]], axis=0).T


def score_kernel(holders, capacity, *refs):
    packed_refs, pages_ref, send_ref, scores_ref, rest_ref, queries = refs[:holders][::-1], *refs[holders:]
    me = lax.axis_index("store")
    width, count = pages_ref.shape
    rows = packed_refs[0].shape[0]
    half = capacity // 2
    step = width // CHUNKS
    scores = jnp.zeros((holders * rows, count), jnp.float32)
    for i in range(CHUNKS):
        columns = slice(i * step, (i + 1) * step)
        for k in range(holders):
            queries[k * rows:(k + 1) * rows, columns] = packed_refs[k][:, columns]
        scores = scores + jnp.dot(queries[:, columns], pages_ref[columns], preferred_element_type=jnp.float32)
    for k in range(holders):
        start = pl.multiple_of((me ^ k) * rows, rows)
        scores_ref[pl.ds(start, rows), :] = scores[k * rows:(k + 1) * rows]
    asked = []
    for k in range(holders):
        notes = packed_refs[k][:, width:].astype(jnp.float32)
        notes = jnp.sum(jnp.where(iota(notes.shape, 0) == me % rows, notes, 0.0), axis=0, keepdims=True)
        mine = notes[:, :capacity]
        for block in range(1, holders // rows):
            mine = jnp.where(me // rows == block, notes[:, block * capacity:(block + 1) * capacity], mine)
        asked.append(mine)
    chips = holders // 2
    chip = me // 2
    kept, handed = [asked[0]], [asked[1]]
    for step in range(1, chips):
        apart = chip ^ ring_place((ring_place(chip, chips) + step) % chips, chips)
        for rows_of, core in ((kept, 1), (handed, 0)):
            chosen = asked[2 + core]
            for distance in range(2, chips):
                chosen = jnp.where(apart == distance, asked[2 * distance + core], chosen)
            rows_of.append(chosen)
    wanted = [
        jnp.concatenate([row[:, side * half:(side + 1) * half] for side in range(2) for row in rows_of], axis=1)
        for rows_of in (handed, kept)
    ]
    rest_ref[...] = wanted[1]
    picked = pick(scores_ref[...], wanted[0])
    for place in range(chips):
        send_ref[place] = picked[place * half:(place + 1) * half]


def rest_kernel(scores_ref, rest_ref, keep_ref):
    picked = pick(scores_ref[...], rest_ref[...])
    half = keep_ref.shape[1]
    for place in range(keep_ref.shape[0]):
        keep_ref[place] = picked[place * half:(place + 1) * half]


def spread_kernel(holders, groups, found_ref, *refs):
    landed_refs, out_refs = refs[:holders // 2][::-1], refs[holders // 2:]
    half = landed_refs[0].shape[1]
    slots = found_ref.shape[1]
    total = landed_refs[0].shape[2] // 2
    at = lax.axis_index("layer")
    share = slots // groups
    me = lax.axis_index("store")
    chips = holders // 2
    holder = found_ref[0:1].astype(jnp.int32)
    step = (ring_place(me // 2, chips) - ring_place(holder // 2, chips) + 2 * chips) % chips
    same_core = (holder % 2 == me % 2).astype(jnp.int32)
    place = 2 * step + jnp.where(step == 0, 1 - same_core, same_core)
    begins = jnp.where(holder < holders, place * half, -1).astype(jnp.float32)
    rank_there = found_ref[1:2]
    place = iota((2 * holders * half, slots), 0).astype(jnp.float32)
    upper = rank_there >= half
    target = begins + rank_there + jnp.where(upper, float(holders * half - half), 0.0)
    chosen = exact_bf16(place == jnp.where(begins >= 0.0, target, -1.0))
    landed = jnp.concatenate([ref[core] for ref in landed_refs for core in range(2)], axis=0).T
    result = exact_product(jnp.concatenate([landed[:total], landed[total:]], axis=1), chosen)
    result = result.T
    blocks = []
    for g in range(groups):
        block = result[g * share:(g + 1) * share]
        blocks.append(jnp.concatenate([block[:share // 2], block[share // 2:]], axis=1))
    for step, out_ref in enumerate(out_refs):
        chosen = blocks[0]
        for g in range(1, groups):
            chosen = jnp.where((at + step) % groups == g, blocks[g], chosen)
        out_ref[...] = chosen


def swap(value, axis, distance):
    return lax.ppermute(value, axis, [(i, i ^ distance) for i in range(lax.axis_size(axis))])


def on_device(query_grads, factor_out, factor_in, page_store, page_home, cand_lists, counts):
    holders = lax.axis_size("store")
    groups = lax.axis_size("layer")
    rows, width = query_grads.shape
    layers, rank, _ = factor_out.shape
    per_holder = page_store.shape[0]
    slots = cand_lists.shape[1]
    bf16 = jnp.bfloat16

    capacity = slots // holders
    home = page_home.reshape(-1, LANES)
    sources = [
        pltpu.with_memory_space_constraint(source, pltpu.HBM)
        for source in (query_grads, factor_in, factor_out, home, cand_lists)
    ]
    notes = max(LANES, holders // rows * capacity)
    packed, again, found = pl.pallas_call(
        functools.partial(condition_kernel, holders, capacity, per_holder),
        out_shape=[
            jax.ShapeDtypeStruct((rows, width + notes), bf16),
            jax.ShapeDtypeStruct((rows, width + notes), bf16),
            jax.ShapeDtypeStruct((8, slots), jnp.float32),
        ],
        in_specs=[HBM] * len(sources),
        out_specs=[VMEM] * 3,
        scratch_shapes=[pltpu.VMEM(source.shape, source.dtype) for source in sources]
        + [pltpu.SemaphoreType.DMA((len(sources),)), pltpu.VMEM((layers, rows * rank // 2, LANES), jnp.float32)],
        compiler_params=pltpu.CompilerParams(vmem_limit_bytes=10 * 2**20 + 24 * slots * slots),
    )(*sources)

    again, pages, used = pl.pallas_call(
        functools.partial(load_kernel, holders),
        out_shape=[
            jax.ShapeDtypeStruct(again.shape, bf16),
            pltpu.VMEM((width, per_holder), bf16),
            jax.ShapeDtypeStruct(found.shape, jnp.float32),
        ],
        in_specs=[SMEM, VMEM, VMEM, HBM],
        out_specs=[VMEM] * 3,
        input_output_aliases={2: 0},
        scratch_shapes=[pltpu.VMEM(page_store.shape, bf16), pltpu.SemaphoreType.DMA((LOADS,))],
        compiler_params=pltpu.CompilerParams(vmem_limit_bytes=4 * 2**20 + 4 * per_holder * width),
        cost_estimate=pl.CostEstimate(flops=0, bytes_accessed=2 * page_store.size, transcendentals=0),
    )(counts, found, again, pltpu.with_memory_space_constraint(page_store, pltpu.HBM))

    blocks = [None] * holders
    blocks[0] = packed
    for k in range(2, holders, 2):
        blocks[k] = swap(packed, "store", k)
    blocks[1] = swap(again, "store", 1)
    for k in range(2, holders, 2):
        blocks[k + 1] = swap(blocks[k], "store", 1)

    total = holders * rows
    bytes_in = 2 * holders * rows * (width + notes) + 2 * per_holder * width
    picked_shape = jax.ShapeDtypeStruct((holders // 2, capacity // 2, 2 * total), jnp.float32)
    send, scores, rest = pl.pallas_call(
        functools.partial(score_kernel, holders, capacity),
        out_shape=[
            picked_shape,
            jax.ShapeDtypeStruct((total, per_holder), jnp.float32),
            jax.ShapeDtypeStruct((1, slots // 2), jnp.float32),
        ],
        in_specs=[VMEM] * (holders + 1),
        out_specs=[VMEM] * 3,
        scratch_shapes=[pltpu.VMEM((total, width), bf16)],
        compiler_params=pltpu.CompilerParams(vmem_limit_bytes=8 * 2**20 + 2 * bytes_in + 48 * total * slots),
    )(*blocks[::-1], pltpu.with_memory_space_constraint(pages, pltpu.VMEM))

    handed = swap(send, "store", 1)
    keep = pl.pallas_call(
        rest_kernel,
        out_shape=picked_shape,
        in_specs=[VMEM] * 2,
        out_specs=VMEM,
        compiler_params=pltpu.CompilerParams(vmem_limit_bytes=4 * 2**20 + 24 * total * slots),
    )(scores, rest)
    chips = holders // 2
    landed = []
    for step in range(chips):
        pair = jnp.stack([keep[step], handed[step]])
        to = [
            (i, ring_place((ring_place(i // 2, chips) + step) % chips, chips) * 2 + 1 - i % 2) for i in range(holders)
        ]
        landed.append(lax.ppermute(pair, "store", to) if step else pair)
    share = slots // groups
    terms = pl.pallas_call(
        functools.partial(spread_kernel, holders, groups),
        out_shape=[jax.ShapeDtypeStruct((share // 2, 2 * total), jnp.float32)] * groups,
        in_specs=[VMEM] * (1 + len(landed)),
        out_specs=[VMEM] * groups,
        compiler_params=pltpu.CompilerParams(vmem_limit_bytes=4 * 2**20 + 64 * total * slots),
    )(used, *landed[::-1])
    summed = terms[0]
    for step in range(1, groups):
        summed = summed + lax.ppermute(terms[step], "layer", [(g, (g + step) % groups) for g in range(groups)])
    return jnp.concatenate([summed[:, :total], summed[:, total:]], axis=0)[None]


def solution(mesh):
    placed = (
        P("store", "layer"),
        P("layer", None, None),
        P("layer", None, None),
        P("store", "layer"),
        P(),
        P("store", None),
        P("store"),
    )
    return jax.shard_map(
        on_device, mesh=mesh, in_specs=placed, out_specs=P("store", "layer", None), check_vma=False
    )
```

```python
import functools

import jax
import jax.numpy as jnp
from jax import lax
from jax.experimental import pallas as pl
from jax.experimental.pallas import tpu as pltpu
from jax.sharding import PartitionSpec as P

VMEM = pl.BlockSpec(memory_space=pltpu.VMEM)
SMEM = pl.BlockSpec(memory_space=pltpu.SMEM)
HBM = pl.BlockSpec(memory_space=pltpu.HBM)
LANES = 128
CHUNKS = 4
LOADS = 8


def iota(shape, dimension):
    return lax.broadcasted_iota(jnp.int32, shape, dimension)


def parts_of(value):
    parts = []
    for _ in range(3):
        part = value.astype(jnp.bfloat16)
        value = value - part.astype(jnp.float32)
        parts.append(part)
    return parts


def exact_product(value, chosen):
    rows = value.shape[0]
    product = jnp.dot(jnp.concatenate(parts_of(value), axis=0), chosen, preferred_element_type=jnp.float32)
    return product[2 * rows:] + product[rows:2 * rows] + product[:rows]


def exact_bf16(value):
    return value.astype(jnp.float32).astype(jnp.bfloat16)


def condition(query_ref, in_factor_ref, out_factor_ref, turned_ref, target_refs):
    rows, width = query_ref.shape
    layers, rank, _ = in_factor_ref.shape
    half = rank // 2
    query = query_ref[...].astype(jnp.float32)
    low = iota((half, LANES), 1) < rank
    zero = jnp.zeros((rank, rank), jnp.float32)
    terms = [(0, 0), (0, 1), (0, 2), (1, 0), (1, 1), (2, 0)]
    group = 2 * LANES
    source, place = iota((rank, 2 * group), 0), iota((rank, 2 * group), 1)
    inside = place % group
    column_found = (source == 2 * (inside % half) + place // group)
    chosen_part = sum((inside >= half * start).astype(jnp.int32) for start in (3, 5, 6))
    pickers = [exact_bf16(column_found & (chosen_part == i)) for i in range(3)]
    for layer in range(layers):
        first = layer * half
        packed = jnp.concatenate(
            [query[:, (first + t) * LANES:(first + t + 1) * LANES] for t in range(half)], axis=0
        ).astype(jnp.bfloat16)
        factor = in_factor_ref[layer]
        doubled = parts_of(
            jnp.concatenate(
                [jnp.concatenate([factor, zero], axis=1), jnp.concatenate([zero, factor], axis=1)], axis=0
            )
        )
        small = jnp.dot(
            jnp.concatenate([packed, packed], axis=1), jnp.concatenate(doubled[1:], axis=0),
            preferred_element_type=jnp.float32,
        )
        turned_ref[layer] = small + jnp.dot(packed, doubled[0], preferred_element_type=jnp.float32)
        wide = jnp.concatenate([turned_ref[layer, pl.ds(q, half, stride=rows), :] for q in range(rows)], axis=1)
        wide = parts_of(wide)
        stacked = jnp.concatenate([wide[j] for _, j in terms], axis=0)
        by_row = jnp.concatenate(
            [out_factor_ref[layer, pl.ds(parity, half, stride=2), :] for parity in range(2)], axis=0
        )
        sorted_columns = sum(
            jnp.dot(part, picker, preferred_element_type=jnp.float32) for part, picker in zip(parts_of(by_row), pickers)
        )
        quarters = jnp.concatenate(
            [
                sorted_columns[r * half:(r + 1) * half, c * group:c * group + len(terms) * half]
                for r in range(2) for c in range(2)
            ],
            axis=0,
        ).astype(jnp.bfloat16)
        left = jnp.dot(quarters, stacked, preferred_element_type=jnp.float32)
        for q in range(rows):
            part = left[:, q * LANES:(q + 1) * LANES]
            ee, eo, oe, oo = (part[i * half:(i + 1) * half] for i in range(4))
            done = jnp.where(low, ee, oo) + pltpu.roll(jnp.where(low, oe, eo), rank, 1)
            turned_ref[layer, pl.ds(q, half, stride=rows), :] = done
        for t in range(half):
            tile = turned_ref[layer, t * rows:(t + 1) * rows, :].astype(jnp.bfloat16)
            for target_ref in target_refs:
                target_ref[:, (first + t) * LANES:(first + t + 1) * LANES] = tile


def condition_kernel(holders, capacity, per_holder, *refs):
    sources, packed_ref, again_ref, notes_ref, found_ref = refs[:6], *refs[6:10]
    in_factor_ref, out_factor_ref, pages_ref, query_ref, home_ref, cand_ref, arrived, turned_ref = refs[10:]
    copies = [
        pltpu.make_async_copy(source, target, arrived.at[i])
        for i, (source, target) in enumerate(
            zip(sources, (query_ref, in_factor_ref, out_factor_ref, home_ref, cand_ref, pages_ref))
        )
    ]
    for copy in copies:
        copy.start()
    for copy in copies[:-1]:
        copy.wait()
    rows, width = query_ref.shape
    condition(query_ref, in_factor_ref, out_factor_ref, turned_ref, (packed_ref, again_ref))
    slots = cand_ref.shape[1]
    home_rows = home_ref.shape[0]
    wanted = cand_ref[...]
    onehot = (iota((LANES, slots), 0) == wanted % LANES).astype(jnp.float32).astype(jnp.bfloat16)
    home = home_ref[...]
    table = jnp.concatenate([home // per_holder, home % per_holder], axis=0).astype(jnp.float32).astype(jnp.bfloat16)
    found = jnp.dot(table, onehot, preferred_element_type=jnp.float32)
    mine = iota((home_rows, slots), 0) == wanted // LANES
    holder = jnp.sum(jnp.where(mine, found[:home_rows], 0.0), axis=0, keepdims=True)
    within = jnp.sum(jnp.where(mine, found[home_rows:], 0.0), axis=0, keepdims=True)
    at_holder = iota((holders, slots), 0).astype(jnp.float32) == holder
    earlier = exact_bf16(iota((slots, slots), 0) < iota((slots, slots), 1))
    before = jnp.dot(exact_bf16(at_holder), earlier, preferred_element_type=jnp.float32)
    rank_there = jnp.sum(jnp.where(at_holder, before, 0.0), axis=0, keepdims=True)
    ranked = exact_bf16(iota((capacity, slots), 0).astype(jnp.float32) == rank_there)
    asked = lax.dot_general(
        exact_bf16(jnp.where(at_holder, within + 1.0, 0.0)), ranked, (((1,), (1,)), ((), ())),
        preferred_element_type=jnp.float32,
    )
    blocks = [asked[h:h + rows] for h in range(0, holders, rows)]
    spare = packed_ref.shape[1] - width - capacity * len(blocks)
    if spare:
        blocks.append(jnp.zeros((rows, spare), jnp.float32))
    notes = jnp.concatenate(blocks, axis=1).astype(jnp.bfloat16)
    notes_ref[...] = notes
    for target_ref in (packed_ref, again_ref):
        target_ref[:, width:] = notes
    found_ref[...] = jnp.concatenate([holder, rank_there, jnp.zeros((6, slots), jnp.float32)], axis=0)
    copies[-1].wait()


def late_kernel(query_ref, notes_ref, in_factor_ref, out_factor_ref, packed_ref, turned_ref):
    condition(query_ref, in_factor_ref, out_factor_ref, turned_ref, (packed_ref,))
    packed_ref[:, query_ref.shape[1]:] = notes_ref[...]


def load_kernel(holders, count_ref, found_ref, block_ref, source_ref, same_block_ref, target_ref, used_ref):
    used_ref[...] = found_ref[...]
    slots = found_ref.shape[1]
    used_ref[0:1] = jnp.where(iota((1, slots), 1) < count_ref[0], found_ref[0:1], float(holders))
    step = source_ref.shape[1] // LOADS
    for i in range(LOADS):
        target_ref[i * step:(i + 1) * step, :] = source_ref[:, i * step:(i + 1) * step].T


def pick(scores, wanted):
    chosen = exact_bf16(iota((scores.shape[1], wanted.shape[1]), 0).astype(jnp.float32) + 1.0 == wanted)
    picked = exact_product(scores, chosen)
    cut = wanted.shape[1] // 2
    return jnp.concatenate([picked[:, :cut], picked[:, cut:]], axis=0).T


def score_kernel(holders, capacity, *refs):
    packed_refs, pages_ref, send_ref, scores_ref, rest_ref, queries = refs[:holders][::-1], *refs[holders:]
    me = lax.axis_index("store")
    width, count = pages_ref.shape
    rows = packed_refs[0].shape[0]
    half = capacity // 2
    step = width // CHUNKS
    scores = jnp.zeros((holders * rows, count), jnp.float32)
    for i in range(CHUNKS):
        columns = slice(i * step, (i + 1) * step)
        for k in range(holders):
            queries[k * rows:(k + 1) * rows, columns] = packed_refs[k][:, columns]
        scores = scores + jnp.dot(queries[:, columns], pages_ref[columns], preferred_element_type=jnp.float32)
    for k in range(holders):
        start = pl.multiple_of((me ^ k) * rows, rows)
        scores_ref[pl.ds(start, rows), :] = scores[k * rows:(k + 1) * rows]
    asked = []
    for k in range(holders):
        notes = packed_refs[k][:, width:].astype(jnp.float32)
        notes = jnp.sum(jnp.where(iota(notes.shape, 0) == me % rows, notes, 0.0), axis=0, keepdims=True)
        mine = notes[:, :capacity]
        for block in range(1, holders // rows):
            mine = jnp.where(me // rows == block, notes[:, block * capacity:(block + 1) * capacity], mine)
        asked.append(mine)
    chips = holders // 2
    chip = me // 2
    kept, handed = [asked[0]], [asked[1]]
    for step in range(1, chips):
        apart = chip ^ ((chip + step) % chips)
        for rows_of, core in ((kept, 1), (handed, 0)):
            chosen = asked[2 + core]
            for distance in range(2, chips):
                chosen = jnp.where(apart == distance, asked[2 * distance + core], chosen)
            rows_of.append(chosen)
    wanted = [
        jnp.concatenate([row[:, side * half:(side + 1) * half] for side in range(2) for row in rows_of], axis=1)
        for rows_of in (handed, kept)
    ]
    rest_ref[...] = wanted[1]
    picked = pick(scores_ref[...], wanted[0])
    for place in range(chips):
        send_ref[place] = picked[place * half:(place + 1) * half]


def rest_kernel(scores_ref, rest_ref, keep_ref):
    picked = pick(scores_ref[...], rest_ref[...])
    half = keep_ref.shape[1]
    for place in range(keep_ref.shape[0]):
        keep_ref[place] = picked[place * half:(place + 1) * half]


def spread_kernel(holders, groups, found_ref, *refs):
    landed_refs, out_refs = refs[:holders // 2][::-1], refs[holders // 2:]
    half = landed_refs[0].shape[1]
    slots = found_ref.shape[1]
    total = landed_refs[0].shape[2] // 2
    at = lax.axis_index("layer")
    share = slots // groups
    me = lax.axis_index("store")
    chips = holders // 2
    holder = found_ref[0:1].astype(jnp.int32)
    step = (me // 2 - holder // 2 + 2 * chips) % chips
    same_core = (holder % 2 == me % 2).astype(jnp.int32)
    place = 2 * step + jnp.where(step == 0, 1 - same_core, same_core)
    begins = jnp.where(holder < holders, place * half, -1).astype(jnp.float32)
    rank_there = found_ref[1:2]
    place = iota((2 * holders * half, slots), 0).astype(jnp.float32)
    upper = rank_there >= half
    target = begins + rank_there + jnp.where(upper, float(holders * half - half), 0.0)
    chosen = exact_bf16(place == jnp.where(begins >= 0.0, target, -1.0))
    landed = jnp.concatenate([ref[core] for ref in landed_refs for core in range(2)], axis=0).T
    result = exact_product(jnp.concatenate([landed[:total], landed[total:]], axis=1), chosen)
    result = result.T
    blocks = []
    for g in range(groups):
        block = result[g * share:(g + 1) * share]
        blocks.append(jnp.concatenate([block[:share // 2], block[share // 2:]], axis=1))
    for step, out_ref in enumerate(out_refs):
        chosen = blocks[0]
        for g in range(1, groups):
            chosen = jnp.where((at + step) % groups == g, blocks[g], chosen)
        out_ref[...] = chosen


def swap(value, axis, distance):
    return lax.ppermute(value, axis, [(i, i ^ distance) for i in range(lax.axis_size(axis))])


def on_device(query_grads, factor_out, factor_in, page_store, page_home, cand_lists, counts):
    holders = lax.axis_size("store")
    groups = lax.axis_size("layer")
    rows, width = query_grads.shape
    layers, rank, _ = factor_out.shape
    per_holder = page_store.shape[0]
    slots = cand_lists.shape[1]
    bf16 = jnp.bfloat16

    capacity = slots // holders
    home = page_home.reshape(-1, LANES)
    sources = [
        pltpu.with_memory_space_constraint(source, pltpu.HBM)
        for source in (query_grads, factor_in, factor_out, home, cand_lists, page_store)
    ]
    notes = max(LANES, holders // rows * capacity)
    far = holders - 2
    raw = swap(query_grads, "store", far)
    turned = pltpu.VMEM((layers, rows * rank // 2, LANES), jnp.float32)
    packed, again, own_notes, found, in_factor, out_factor, pages = pl.pallas_call(
        functools.partial(condition_kernel, holders, capacity, per_holder),
        out_shape=[
            jax.ShapeDtypeStruct((rows, width + notes), bf16),
            jax.ShapeDtypeStruct((rows, width + notes), bf16),
            jax.ShapeDtypeStruct((rows, notes), bf16),
            jax.ShapeDtypeStruct((8, slots), jnp.float32),
            jax.ShapeDtypeStruct(factor_in.shape, jnp.float32),
            jax.ShapeDtypeStruct(factor_out.shape, jnp.float32),
            pltpu.VMEM(page_store.shape, bf16),
        ],
        in_specs=[HBM] * len(sources),
        out_specs=[VMEM] * 7,
        scratch_shapes=[pltpu.VMEM(sources[i].shape, sources[i].dtype) for i in (0, 3, 4)]
        + [pltpu.SemaphoreType.DMA((len(sources),)), turned],
        compiler_params=pltpu.CompilerParams(vmem_limit_bytes=14 * 2**20 + 24 * slots * slots),
    )(*sources)

    again, pages, used = pl.pallas_call(
        functools.partial(load_kernel, holders),
        out_shape=[
            jax.ShapeDtypeStruct(again.shape, bf16),
            pltpu.VMEM((width, per_holder), bf16),
            jax.ShapeDtypeStruct(found.shape, jnp.float32),
        ],
        in_specs=[SMEM, VMEM, VMEM, VMEM],
        out_specs=[VMEM] * 3,
        input_output_aliases={2: 0},
        compiler_params=pltpu.CompilerParams(vmem_limit_bytes=4 * 2**20 + 4 * per_holder * width),
        cost_estimate=pl.CostEstimate(flops=0, bytes_accessed=2 * page_store.size, transcendentals=0),
    )(counts, found, again, pltpu.with_memory_space_constraint(pages, pltpu.VMEM))

    blocks = [None] * holders
    blocks[0] = packed
    for k in range(2, holders - 2, 2):
        blocks[k] = swap(packed, "store", k)
    blocks[far] = pl.pallas_call(
        late_kernel,
        out_shape=jax.ShapeDtypeStruct(packed.shape, bf16),
        in_specs=[VMEM] * 4,
        out_specs=VMEM,
        scratch_shapes=[turned],
        compiler_params=pltpu.CompilerParams(vmem_limit_bytes=8 * 2**20),
        cost_estimate=pl.CostEstimate(flops=10**8, bytes_accessed=8 * packed.size, transcendentals=0),
    )(raw, swap(own_notes, "store", far), in_factor, out_factor)
    blocks[1] = swap(again, "store", 1)
    for k in range(2, holders, 2):
        blocks[k + 1] = swap(blocks[k], "store", 1)

    total = holders * rows
    bytes_in = 2 * holders * rows * (width + notes) + 2 * per_holder * width
    picked_shape = jax.ShapeDtypeStruct((holders // 2, capacity // 2, 2 * total), jnp.float32)
    send, scores, rest = pl.pallas_call(
        functools.partial(score_kernel, holders, capacity),
        out_shape=[
            picked_shape,
            jax.ShapeDtypeStruct((total, per_holder), jnp.float32),
            jax.ShapeDtypeStruct((1, slots // 2), jnp.float32),
        ],
        in_specs=[VMEM] * (holders + 1),
        out_specs=[VMEM] * 3,
        scratch_shapes=[pltpu.VMEM((total, width), bf16)],
        compiler_params=pltpu.CompilerParams(vmem_limit_bytes=8 * 2**20 + 2 * bytes_in + 48 * total * slots),
    )(*blocks[::-1], pltpu.with_memory_space_constraint(pages, pltpu.VMEM))

    handed = swap(send, "store", 1)
    keep = pl.pallas_call(
        rest_kernel,
        out_shape=picked_shape,
        in_specs=[VMEM] * 2,
        out_specs=VMEM,
        compiler_params=pltpu.CompilerParams(vmem_limit_bytes=4 * 2**20 + 24 * total * slots),
    )(scores, rest)
    chips = holders // 2
    landed = []
    for step in range(chips):
        pair = jnp.stack([keep[step], handed[step]])
        to = [(i, (i // 2 + step) % chips * 2 + 1 - i % 2) for i in range(holders)]
        landed.append(lax.ppermute(pair, "store", to) if step else pair)
    share = slots // groups
    terms = pl.pallas_call(
        functools.partial(spread_kernel, holders, groups),
        out_shape=[jax.ShapeDtypeStruct((share // 2, 2 * total), jnp.float32)] * groups,
        in_specs=[VMEM] * (1 + len(landed)),
        out_specs=[VMEM] * groups,
        compiler_params=pltpu.CompilerParams(vmem_limit_bytes=4 * 2**20 + 64 * total * slots),
    )(used, *landed[::-1])
    summed = terms[0]
    for step in range(1, groups):
        summed = summed + lax.ppermute(terms[step], "layer", [(g, (g + step) % groups) for g in range(groups)])
    return jnp.concatenate([summed[:, :total], summed[:, total:]], axis=0)[None]


def solution(mesh):
    placed = (
        P("store", "layer"),
        P("layer", None, None),
        P("layer", None, None),
        P("store", "layer"),
        P(),
        P("store", None),
        P("store"),
    )
    return jax.shard_map(
        on_device, mesh=mesh, in_specs=placed, out_specs=P("store", "layer", None), check_vma=False
    )
```

```python
import functools

import jax
import jax.numpy as jnp
from jax import lax
from jax.experimental import pallas as pl
from jax.experimental.pallas import tpu as pltpu
from jax.sharding import PartitionSpec as P

VMEM = pl.BlockSpec(memory_space=pltpu.VMEM)
SMEM = pl.BlockSpec(memory_space=pltpu.SMEM)
HBM = pl.BlockSpec(memory_space=pltpu.HBM)
LANES = 128
CHUNKS = 4
LATE_FLOPS = 5 * 10**9
LOADS = 8


def iota(shape, dimension):
    return lax.broadcasted_iota(jnp.int32, shape, dimension)


def parts_of(value):
    parts = []
    for _ in range(3):
        part = value.astype(jnp.bfloat16)
        value = value - part.astype(jnp.float32)
        parts.append(part)
    return parts


def exact_product(value, chosen):
    rows = value.shape[0]
    product = jnp.dot(jnp.concatenate(parts_of(value), axis=0), chosen, preferred_element_type=jnp.float32)
    return product[2 * rows:] + product[rows:2 * rows] + product[:rows]


def exact_bf16(value):
    return value.astype(jnp.float32).astype(jnp.bfloat16)


def condition(query_ref, in_factor_ref, out_factor_ref, turned_ref, target_refs):
    rows, width = query_ref.shape
    layers, rank, _ = in_factor_ref.shape
    half = rank // 2
    query = query_ref[...].astype(jnp.float32)
    low = iota((half, LANES), 1) < rank
    zero = jnp.zeros((rank, rank), jnp.float32)
    terms = [(0, 0), (0, 1), (0, 2), (1, 0), (1, 1), (2, 0)]
    group = 2 * LANES
    source, place = iota((rank, 2 * group), 0), iota((rank, 2 * group), 1)
    inside = place % group
    column_found = (source == 2 * (inside % half) + place // group)
    chosen_part = sum((inside >= half * start).astype(jnp.int32) for start in (3, 5, 6))
    pickers = [exact_bf16(column_found & (chosen_part == i)) for i in range(3)]
    for layer in range(layers):
        first = layer * half
        packed = jnp.concatenate(
            [query[:, (first + t) * LANES:(first + t + 1) * LANES] for t in range(half)], axis=0
        ).astype(jnp.bfloat16)
        factor = in_factor_ref[layer]
        doubled = parts_of(
            jnp.concatenate(
                [jnp.concatenate([factor, zero], axis=1), jnp.concatenate([zero, factor], axis=1)], axis=0
            )
        )
        small = jnp.dot(
            jnp.concatenate([packed, packed], axis=1), jnp.concatenate(doubled[1:], axis=0),
            preferred_element_type=jnp.float32,
        )
        turned_ref[layer] = small + jnp.dot(packed, doubled[0], preferred_element_type=jnp.float32)
        wide = jnp.concatenate([turned_ref[layer, pl.ds(q, half, stride=rows), :] for q in range(rows)], axis=1)
        wide = parts_of(wide)
        stacked = jnp.concatenate([wide[j] for _, j in terms], axis=0)
        by_row = jnp.concatenate(
            [out_factor_ref[layer, pl.ds(parity, half, stride=2), :] for parity in range(2)], axis=0
        )
        sorted_columns = sum(
            jnp.dot(part, picker, preferred_element_type=jnp.float32) for part, picker in zip(parts_of(by_row), pickers)
        )
        quarters = jnp.concatenate(
            [
                sorted_columns[r * half:(r + 1) * half, c * group:c * group + len(terms) * half]
                for r in range(2) for c in range(2)
            ],
            axis=0,
        ).astype(jnp.bfloat16)
        left = jnp.dot(quarters, stacked, preferred_element_type=jnp.float32)
        for q in range(rows):
            part = left[:, q * LANES:(q + 1) * LANES]
            ee, eo, oe, oo = (part[i * half:(i + 1) * half] for i in range(4))
            done = jnp.where(low, ee, oo) + pltpu.roll(jnp.where(low, oe, eo), rank, 1)
            turned_ref[layer, pl.ds(q, half, stride=rows), :] = done
        for t in range(half):
            tile = turned_ref[layer, t * rows:(t + 1) * rows, :].astype(jnp.bfloat16)
            for target_ref in target_refs:
                target_ref[:, (first + t) * LANES:(first + t + 1) * LANES] = tile


def look_up(holders, capacity, per_holder, rows, cand_ref, home_ref):
    slots = cand_ref.shape[1]
    home_rows = home_ref.shape[0]
    wanted = cand_ref[...]
    onehot = (iota((LANES, slots), 0) == wanted % LANES).astype(jnp.float32).astype(jnp.bfloat16)
    home = home_ref[...]
    table = jnp.concatenate([home // per_holder, home % per_holder], axis=0).astype(jnp.float32).astype(jnp.bfloat16)
    found = jnp.dot(table, onehot, preferred_element_type=jnp.float32)
    mine = iota((home_rows, slots), 0) == wanted // LANES
    holder = jnp.sum(jnp.where(mine, found[:home_rows], 0.0), axis=0, keepdims=True)
    within = jnp.sum(jnp.where(mine, found[home_rows:], 0.0), axis=0, keepdims=True)
    at_holder = iota((holders, slots), 0).astype(jnp.float32) == holder
    earlier = exact_bf16(iota((slots, slots), 0) < iota((slots, slots), 1))
    before = jnp.dot(exact_bf16(at_holder), earlier, preferred_element_type=jnp.float32)
    rank_there = jnp.sum(jnp.where(at_holder, before, 0.0), axis=0, keepdims=True)
    ranked = exact_bf16(iota((capacity, slots), 0).astype(jnp.float32) == rank_there)
    asked = lax.dot_general(
        exact_bf16(jnp.where(at_holder, within + 1.0, 0.0)), ranked, (((1,), (1,)), ((), ())),
        preferred_element_type=jnp.float32,
    )
    blocks = [asked[h:h + rows] for h in range(0, holders, rows)]
    spare = max(LANES, capacity * len(blocks)) - capacity * len(blocks)
    if spare:
        blocks.append(jnp.zeros((rows, spare), jnp.float32))
    notes = jnp.concatenate(blocks, axis=1).astype(jnp.bfloat16)
    return notes, holder, rank_there


def condition_kernel(holders, capacity, per_holder, *refs):
    sources, packed_ref, again_ref, found_ref = refs[:6], *refs[6:9]
    in_factor_ref, out_factor_ref, home_ref, pages_ref, query_ref, cand_ref, arrived, turned_ref = refs[9:]
    copies = [
        pltpu.make_async_copy(source, target, arrived.at[i])
        for i, (source, target) in enumerate(
            zip(sources, (query_ref, in_factor_ref, out_factor_ref, home_ref, cand_ref, pages_ref))
        )
    ]
    for copy in copies:
        copy.start()
    for copy in copies[:-1]:
        copy.wait()
    rows, width = query_ref.shape
    condition(query_ref, in_factor_ref, out_factor_ref, turned_ref, (packed_ref, again_ref))
    notes, holder, rank_there = look_up(holders, capacity, per_holder, rows, cand_ref, home_ref)
    slots = cand_ref.shape[1]
    for target_ref in (packed_ref, again_ref):
        target_ref[:, width:] = notes
    found_ref[...] = jnp.concatenate([holder, rank_there, jnp.zeros((6, slots), jnp.float32)], axis=0)
    copies[-1].wait()


def late_kernel(
    holders, capacity, per_holder, query_ref, cand_ref, in_factor_ref, out_factor_ref, home_ref, packed_ref, turned_ref
):
    rows, width = query_ref.shape
    condition(query_ref, in_factor_ref, out_factor_ref, turned_ref, (packed_ref,))
    packed_ref[:, width:] = look_up(holders, capacity, per_holder, rows, cand_ref, home_ref)[0]


def load_kernel(holders, count_ref, found_ref, block_ref, source_ref, same_block_ref, target_ref, used_ref):
    used_ref[...] = found_ref[...]
    slots = found_ref.shape[1]
    used_ref[0:1] = jnp.where(iota((1, slots), 1) < count_ref[0], found_ref[0:1], float(holders))
    step = source_ref.shape[1] // LOADS
    for i in range(LOADS):
        target_ref[i * step:(i + 1) * step, :] = source_ref[:, i * step:(i + 1) * step].T


def pick(scores, wanted):
    chosen = exact_bf16(iota((scores.shape[1], wanted.shape[1]), 0).astype(jnp.float32) + 1.0 == wanted)
    picked = exact_product(scores, chosen)
    cut = wanted.shape[1] // 2
    return jnp.concatenate([picked[:, :cut], picked[:, cut:]], axis=0).T


def score_kernel(holders, capacity, *refs):
    packed_refs, pages_ref, send_ref, scores_ref, rest_ref, queries = refs[:holders][::-1], *refs[holders:]
    me = lax.axis_index("store")
    width, count = pages_ref.shape
    rows = packed_refs[0].shape[0]
    half = capacity // 2
    step = width // CHUNKS
    scores = jnp.zeros((holders * rows, count), jnp.float32)
    for i in range(CHUNKS):
        columns = slice(i * step, (i + 1) * step)
        for k in range(holders):
            queries[k * rows:(k + 1) * rows, columns] = packed_refs[k][:, columns]
        scores = scores + jnp.dot(queries[:, columns], pages_ref[columns], preferred_element_type=jnp.float32)
    for k in range(holders):
        start = pl.multiple_of((me ^ k) * rows, rows)
        scores_ref[pl.ds(start, rows), :] = scores[k * rows:(k + 1) * rows]
    asked = []
    for k in range(holders):
        notes = packed_refs[k][:, width:].astype(jnp.float32)
        notes = jnp.sum(jnp.where(iota(notes.shape, 0) == me % rows, notes, 0.0), axis=0, keepdims=True)
        mine = notes[:, :capacity]
        for block in range(1, holders // rows):
            mine = jnp.where(me // rows == block, notes[:, block * capacity:(block + 1) * capacity], mine)
        asked.append(mine)
    chips = holders // 2
    chip = me // 2
    kept, handed = [asked[0]], [asked[1]]
    for step in range(1, chips):
        apart = chip ^ ((chip + step) % chips)
        for rows_of, core in ((kept, 1), (handed, 0)):
            chosen = asked[2 + core]
            for distance in range(2, chips):
                chosen = jnp.where(apart == distance, asked[2 * distance + core], chosen)
            rows_of.append(chosen)
    wanted = [
        jnp.concatenate([row[:, side * half:(side + 1) * half] for side in range(2) for row in rows_of], axis=1)
        for rows_of in (handed, kept)
    ]
    rest_ref[...] = wanted[1]
    picked = pick(scores_ref[...], wanted[0])
    for place in range(chips):
        send_ref[place] = picked[place * half:(place + 1) * half]


def rest_kernel(scores_ref, rest_ref, keep_ref):
    picked = pick(scores_ref[...], rest_ref[...])
    half = keep_ref.shape[1]
    for place in range(keep_ref.shape[0]):
        keep_ref[place] = picked[place * half:(place + 1) * half]


def spread_kernel(holders, groups, found_ref, *refs):
    landed_refs, out_refs = refs[:holders // 2][::-1], refs[holders // 2:]
    half = landed_refs[0].shape[1]
    slots = found_ref.shape[1]
    total = landed_refs[0].shape[2] // 2
    at = lax.axis_index("layer")
    share = slots // groups
    me = lax.axis_index("store")
    chips = holders // 2
    holder = found_ref[0:1].astype(jnp.int32)
    step = (me // 2 - holder // 2 + 2 * chips) % chips
    same_core = (holder % 2 == me % 2).astype(jnp.int32)
    place = 2 * step + jnp.where(step == 0, 1 - same_core, same_core)
    begins = jnp.where(holder < holders, place * half, -1).astype(jnp.float32)
    rank_there = found_ref[1:2]
    place = iota((2 * holders * half, slots), 0).astype(jnp.float32)
    upper = rank_there >= half
    target = begins + rank_there + jnp.where(upper, float(holders * half - half), 0.0)
    chosen = exact_bf16(place == jnp.where(begins >= 0.0, target, -1.0))
    landed = jnp.concatenate([ref[core] for ref in landed_refs for core in range(2)], axis=0).T
    result = exact_product(jnp.concatenate([landed[:total], landed[total:]], axis=1), chosen)
    result = result.T
    blocks = []
    for g in range(groups):
        block = result[g * share:(g + 1) * share]
        blocks.append(jnp.concatenate([block[:share // 2], block[share // 2:]], axis=1))
    for step, out_ref in enumerate(out_refs):
        chosen = blocks[0]
        for g in range(1, groups):
            chosen = jnp.where((at + step) % groups == g, blocks[g], chosen)
        out_ref[...] = chosen


def swap(value, axis, distance):
    return lax.ppermute(value, axis, [(i, i ^ distance) for i in range(lax.axis_size(axis))])


def on_device(query_grads, factor_out, factor_in, page_store, page_home, cand_lists, counts):
    holders = lax.axis_size("store")
    groups = lax.axis_size("layer")
    rows, width = query_grads.shape
    layers, rank, _ = factor_out.shape
    per_holder = page_store.shape[0]
    slots = cand_lists.shape[1]
    bf16 = jnp.bfloat16

    capacity = slots // holders
    home = page_home.reshape(-1, LANES)
    sources = [
        pltpu.with_memory_space_constraint(source, pltpu.HBM)
        for source in (query_grads, factor_in, factor_out, home, cand_lists, page_store)
    ]
    notes = max(LANES, holders // rows * capacity)
    far = holders - 2
    raw = swap(query_grads, "store", far)
    far_list = swap(cand_lists, "store", far)
    turned = pltpu.VMEM((layers, rows * rank // 2, LANES), jnp.float32)
    packed, again, found, in_factor, out_factor, home_here, pages = pl.pallas_call(
        functools.partial(condition_kernel, holders, capacity, per_holder),
        out_shape=[
            jax.ShapeDtypeStruct((rows, width + notes), bf16),
            jax.ShapeDtypeStruct((rows, width + notes), bf16),
            jax.ShapeDtypeStruct((8, slots), jnp.float32),
            jax.ShapeDtypeStruct(factor_in.shape, jnp.float32),
            jax.ShapeDtypeStruct(factor_out.shape, jnp.float32),
            jax.ShapeDtypeStruct(home.shape, jnp.int32),
            pltpu.VMEM(page_store.shape, bf16),
        ],
        in_specs=[HBM] * len(sources),
        out_specs=[VMEM] * 7,
        scratch_shapes=[pltpu.VMEM(sources[i].shape, sources[i].dtype) for i in (0, 4)]
        + [pltpu.SemaphoreType.DMA((len(sources),)), turned],
        compiler_params=pltpu.CompilerParams(vmem_limit_bytes=14 * 2**20 + 24 * slots * slots),
    )(*sources)

    again, pages, used = pl.pallas_call(
        functools.partial(load_kernel, holders),
        out_shape=[
            jax.ShapeDtypeStruct(again.shape, bf16),
            pltpu.VMEM((width, per_holder), bf16),
            jax.ShapeDtypeStruct(found.shape, jnp.float32),
        ],
        in_specs=[SMEM, VMEM, VMEM, VMEM],
        out_specs=[VMEM] * 3,
        input_output_aliases={2: 0},
        compiler_params=pltpu.CompilerParams(vmem_limit_bytes=4 * 2**20 + 4 * per_holder * width),
        cost_estimate=pl.CostEstimate(flops=0, bytes_accessed=2 * page_store.size, transcendentals=0),
    )(counts, found, again, pltpu.with_memory_space_constraint(pages, pltpu.VMEM))

    blocks = [None] * holders
    blocks[0] = packed
    for k in range(2, holders - 2, 2):
        blocks[k] = swap(packed, "store", k)
    blocks[far] = pl.pallas_call(
        functools.partial(late_kernel, holders, capacity, per_holder),
        out_shape=jax.ShapeDtypeStruct(packed.shape, bf16),
        in_specs=[VMEM] * 5,
        out_specs=VMEM,
        scratch_shapes=[turned],
        compiler_params=pltpu.CompilerParams(vmem_limit_bytes=10 * 2**20 + 24 * slots * slots),
        cost_estimate=pl.CostEstimate(flops=LATE_FLOPS, bytes_accessed=8 * packed.size, transcendentals=0),
    )(raw, far_list, in_factor, out_factor, home_here)
    blocks[1] = swap(again, "store", 1)
    for k in range(2, holders, 2):
        blocks[k + 1] = swap(blocks[k], "store", 1)

    total = holders * rows
    bytes_in = 2 * holders * rows * (width + notes) + 2 * per_holder * width
    picked_shape = jax.ShapeDtypeStruct((holders // 2, capacity // 2, 2 * total), jnp.float32)
    send, scores, rest = pl.pallas_call(
        functools.partial(score_kernel, holders, capacity),
        out_shape=[
            picked_shape,
            jax.ShapeDtypeStruct((total, per_holder), jnp.float32),
            jax.ShapeDtypeStruct((1, slots // 2), jnp.float32),
        ],
        in_specs=[VMEM] * (holders + 1),
        out_specs=[VMEM] * 3,
        scratch_shapes=[pltpu.VMEM((total, width), bf16)],
        compiler_params=pltpu.CompilerParams(vmem_limit_bytes=8 * 2**20 + 2 * bytes_in + 48 * total * slots),
    )(*blocks[::-1], pltpu.with_memory_space_constraint(pages, pltpu.VMEM))

    handed = swap(send, "store", 1)
    keep = pl.pallas_call(
        rest_kernel,
        out_shape=picked_shape,
        in_specs=[VMEM] * 2,
        out_specs=VMEM,
        compiler_params=pltpu.CompilerParams(vmem_limit_bytes=4 * 2**20 + 24 * total * slots),
    )(scores, rest)
    chips = holders // 2
    landed = []
    for step in range(chips):
        pair = jnp.stack([keep[step], handed[step]])
        to = [(i, (i // 2 + step) % chips * 2 + 1 - i % 2) for i in range(holders)]
        landed.append(lax.ppermute(pair, "store", to) if step else pair)
    share = slots // groups
    terms = pl.pallas_call(
        functools.partial(spread_kernel, holders, groups),
        out_shape=[jax.ShapeDtypeStruct((share // 2, 2 * total), jnp.float32)] * groups,
        in_specs=[VMEM] * (1 + len(landed)),
        out_specs=[VMEM] * groups,
        compiler_params=pltpu.CompilerParams(vmem_limit_bytes=4 * 2**20 + 64 * total * slots),
    )(used, *landed[::-1])
    summed = terms[0]
    for step in range(1, groups):
        summed = summed + lax.ppermute(terms[step], "layer", [(g, (g + step) % groups) for g in range(groups)])
    return jnp.concatenate([summed[:, :total], summed[:, total:]], axis=0)[None]


def solution(mesh):
    placed = (
        P("store", "layer"),
        P("layer", None, None),
        P("layer", None, None),
        P("store", "layer"),
        P(),
        P("store", None),
        P("store"),
    )
    return jax.shard_map(
        on_device, mesh=mesh, in_specs=placed, out_specs=P("store", "layer", None), check_vma=False
    )
```

```python
import functools

import jax
import jax.numpy as jnp
from jax import lax
from jax.experimental import pallas as pl
from jax.experimental.pallas import tpu as pltpu
from jax.sharding import PartitionSpec as P

VMEM = pl.BlockSpec(memory_space=pltpu.VMEM)
SMEM = pl.BlockSpec(memory_space=pltpu.SMEM)
HBM = pl.BlockSpec(memory_space=pltpu.HBM)
LANES = 128
CHUNKS = 4
LATE_FLOPS = 5 * 10**9
LOADS = 8


def iota(shape, dimension):
    return lax.broadcasted_iota(jnp.int32, shape, dimension)


def parts_of(value):
    parts = []
    for _ in range(3):
        part = value.astype(jnp.bfloat16)
        value = value - part.astype(jnp.float32)
        parts.append(part)
    return parts


def exact_product(value, chosen):
    rows = value.shape[0]
    product = jnp.dot(jnp.concatenate(parts_of(value), axis=0), chosen, preferred_element_type=jnp.float32)
    return product[2 * rows:] + product[rows:2 * rows] + product[:rows]


def exact_bf16(value):
    return value.astype(jnp.float32).astype(jnp.bfloat16)


def condition(query_ref, in_factor_ref, out_factor_ref, turned_ref, target_refs):
    rows, width = query_ref.shape
    layers, rank, _ = in_factor_ref.shape
    half = rank // 2
    query = query_ref[...].astype(jnp.float32)
    low = iota((half, LANES), 1) < rank
    zero = jnp.zeros((rank, rank), jnp.float32)
    terms = [(0, 0), (0, 1), (0, 2), (1, 0), (1, 1), (2, 0)]
    group = 2 * LANES
    source, place = iota((rank, 2 * group), 0), iota((rank, 2 * group), 1)
    inside = place % group
    column_found = (source == 2 * (inside % half) + place // group)
    chosen_part = sum((inside >= half * start).astype(jnp.int32) for start in (3, 5, 6))
    pickers = [exact_bf16(column_found & (chosen_part == i)) for i in range(3)]
    for layer in range(layers):
        first = layer * half
        packed = jnp.concatenate(
            [query[:, (first + t) * LANES:(first + t + 1) * LANES] for t in range(half)], axis=0
        ).astype(jnp.bfloat16)
        factor = in_factor_ref[layer]
        doubled = parts_of(
            jnp.concatenate(
                [jnp.concatenate([factor, zero], axis=1), jnp.concatenate([zero, factor], axis=1)], axis=0
            )
        )
        small = jnp.dot(
            jnp.concatenate([packed, packed], axis=1), jnp.concatenate(doubled[1:], axis=0),
            preferred_element_type=jnp.float32,
        )
        turned_ref[layer] = small + jnp.dot(packed, doubled[0], preferred_element_type=jnp.float32)
        wide = jnp.concatenate([turned_ref[layer, pl.ds(q, half, stride=rows), :] for q in range(rows)], axis=1)
        wide = parts_of(wide)
        stacked = jnp.concatenate([wide[j] for _, j in terms], axis=0)
        by_row = jnp.concatenate(
            [out_factor_ref[layer, pl.ds(parity, half, stride=2), :] for parity in range(2)], axis=0
        )
        sorted_columns = sum(
            jnp.dot(part, picker, preferred_element_type=jnp.float32) for part, picker in zip(parts_of(by_row), pickers)
        )
        quarters = jnp.concatenate(
            [
                sorted_columns[r * half:(r + 1) * half, c * group:c * group + len(terms) * half]
                for r in range(2) for c in range(2)
            ],
            axis=0,
        ).astype(jnp.bfloat16)
        left = jnp.dot(quarters, stacked, preferred_element_type=jnp.float32)
        for q in range(rows):
            part = left[:, q * LANES:(q + 1) * LANES]
            ee, eo, oe, oo = (part[i * half:(i + 1) * half] for i in range(4))
            done = jnp.where(low, ee, oo) + pltpu.roll(jnp.where(low, oe, eo), rank, 1)
            turned_ref[layer, pl.ds(q, half, stride=rows), :] = done
        for t in range(half):
            tile = turned_ref[layer, t * rows:(t + 1) * rows, :].astype(jnp.bfloat16)
            for target_ref in target_refs:
                target_ref[:, (first + t) * LANES:(first + t + 1) * LANES] = tile


def look_up(holders, capacity, per_holder, rows, cand_ref, home_ref):
    slots = cand_ref.shape[1]
    home_rows = home_ref.shape[0]
    wanted = cand_ref[...]
    onehot = (iota((LANES, slots), 0) == wanted % LANES).astype(jnp.float32).astype(jnp.bfloat16)
    home = home_ref[...]
    table = jnp.concatenate([home // per_holder, home % per_holder], axis=0).astype(jnp.float32).astype(jnp.bfloat16)
    found = jnp.dot(table, onehot, preferred_element_type=jnp.float32)
    mine = iota((home_rows, slots), 0) == wanted // LANES
    holder = jnp.sum(jnp.where(mine, found[:home_rows], 0.0), axis=0, keepdims=True)
    within = jnp.sum(jnp.where(mine, found[home_rows:], 0.0), axis=0, keepdims=True)
    at_holder = iota((holders, slots), 0).astype(jnp.float32) == holder
    earlier = exact_bf16(iota((slots, slots), 0) < iota((slots, slots), 1))
    before = jnp.dot(exact_bf16(at_holder), earlier, preferred_element_type=jnp.float32)
    rank_there = jnp.sum(jnp.where(at_holder, before, 0.0), axis=0, keepdims=True)
    ranked = exact_bf16(iota((capacity, slots), 0).astype(jnp.float32) == rank_there)
    asked = lax.dot_general(
        exact_bf16(jnp.where(at_holder, within + 1.0, 0.0)), ranked, (((1,), (1,)), ((), ())),
        preferred_element_type=jnp.float32,
    )
    blocks = [asked[h:h + rows] for h in range(0, holders, rows)]
    spare = max(LANES, capacity * len(blocks)) - capacity * len(blocks)
    if spare:
        blocks.append(jnp.zeros((rows, spare), jnp.float32))
    notes = jnp.concatenate(blocks, axis=1).astype(jnp.bfloat16)
    return notes, holder, rank_there


def condition_kernel(holders, capacity, per_holder, *refs):
    sources, packed_ref, again_ref, found_ref = refs[:6], *refs[6:9]
    in_factor_ref, out_factor_ref, home_ref, pages_ref, query_ref, cand_ref, arrived, turned_ref = refs[9:]
    copies = [
        pltpu.make_async_copy(source, target, arrived.at[i])
        for i, (source, target) in enumerate(
            zip(sources, (query_ref, in_factor_ref, out_factor_ref, home_ref, cand_ref, pages_ref))
        )
    ]
    for copy in copies:
        copy.start()
    for copy in copies[:-1]:
        copy.wait()
    rows, width = query_ref.shape
    condition(query_ref, in_factor_ref, out_factor_ref, turned_ref, (packed_ref, again_ref))
    notes, holder, rank_there = look_up(holders, capacity, per_holder, rows, cand_ref, home_ref)
    slots = cand_ref.shape[1]
    for target_ref in (packed_ref, again_ref):
        target_ref[:, width:] = notes
    found_ref[...] = jnp.concatenate([holder, rank_there, jnp.zeros((6, slots), jnp.float32)], axis=0)
    copies[-1].wait()


def late_kernel(
    holders, capacity, per_holder, query_ref, cand_ref, in_factor_ref, out_factor_ref, home_ref, packed_ref, turned_ref
):
    rows, width = query_ref.shape
    condition(query_ref, in_factor_ref, out_factor_ref, turned_ref, (packed_ref,))
    packed_ref[:, width:] = look_up(holders, capacity, per_holder, rows, cand_ref, home_ref)[0]


def load_kernel(block_ref, source_ref, same_block_ref, target_ref):
    step = source_ref.shape[1] // LOADS
    for i in range(LOADS):
        target_ref[i * step:(i + 1) * step, :] = source_ref[:, i * step:(i + 1) * step].T


def pick(scores, wanted):
    chosen = exact_bf16(iota((scores.shape[1], wanted.shape[1]), 0).astype(jnp.float32) + 1.0 == wanted)
    picked = exact_product(scores, chosen)
    cut = wanted.shape[1] // 2
    return jnp.concatenate([picked[:, :cut], picked[:, cut:]], axis=0).T


def score_kernel(holders, capacity, *refs):
    packed_refs, pages_ref, send_ref, scores_ref, rest_ref, queries = refs[:holders][::-1], *refs[holders:]
    me = lax.axis_index("store")
    width, count = pages_ref.shape
    rows = packed_refs[0].shape[0]
    half = capacity // 2
    step = width // CHUNKS
    scores = jnp.zeros((holders * rows, count), jnp.float32)
    for i in range(CHUNKS):
        columns = slice(i * step, (i + 1) * step)
        for k in range(holders):
            queries[k * rows:(k + 1) * rows, columns] = packed_refs[k][:, columns]
        scores = scores + jnp.dot(queries[:, columns], pages_ref[columns], preferred_element_type=jnp.float32)
    for k in range(holders):
        start = pl.multiple_of((me ^ k) * rows, rows)
        scores_ref[pl.ds(start, rows), :] = scores[k * rows:(k + 1) * rows]
    asked = []
    for k in range(holders):
        notes = packed_refs[k][:, width:].astype(jnp.float32)
        notes = jnp.sum(jnp.where(iota(notes.shape, 0) == me % rows, notes, 0.0), axis=0, keepdims=True)
        mine = notes[:, :capacity]
        for block in range(1, holders // rows):
            mine = jnp.where(me // rows == block, notes[:, block * capacity:(block + 1) * capacity], mine)
        asked.append(mine)
    chips = holders // 2
    chip = me // 2
    kept, handed = [asked[0]], [asked[1]]
    for step in range(1, chips):
        apart = chip ^ ((chip + step) % chips)
        for rows_of, core in ((kept, 1), (handed, 0)):
            chosen = asked[2 + core]
            for distance in range(2, chips):
                chosen = jnp.where(apart == distance, asked[2 * distance + core], chosen)
            rows_of.append(chosen)
    wanted = [
        jnp.concatenate([row[:, side * half:(side + 1) * half] for side in range(2) for row in rows_of], axis=1)
        for rows_of in (handed, kept)
    ]
    rest_ref[...] = wanted[1]
    picked = pick(scores_ref[...], wanted[0])
    for place in range(chips):
        send_ref[place] = picked[place * half:(place + 1) * half]


def rest_kernel(scores_ref, rest_ref, keep_ref):
    picked = pick(scores_ref[...], rest_ref[...])
    half = keep_ref.shape[1]
    for place in range(keep_ref.shape[0]):
        keep_ref[place] = picked[place * half:(place + 1) * half]


def spread_kernel(holders, groups, count_ref, found_ref, *refs):
    landed_refs, out_refs = refs[:holders // 2][::-1], refs[holders // 2:]
    half = landed_refs[0].shape[1]
    slots = found_ref.shape[1]
    total = landed_refs[0].shape[2] // 2
    at = lax.axis_index("layer")
    share = slots // groups
    me = lax.axis_index("store")
    chips = holders // 2
    holder = found_ref[0:1].astype(jnp.int32)
    step = (me // 2 - holder // 2 + 2 * chips) % chips
    same_core = (holder % 2 == me % 2).astype(jnp.int32)
    place = 2 * step + jnp.where(step == 0, 1 - same_core, same_core)
    used = iota((1, slots), 1) < count_ref[0]
    begins = jnp.where(used, place * half, -1).astype(jnp.float32)
    rank_there = found_ref[1:2]
    place = iota((2 * holders * half, slots), 0).astype(jnp.float32)
    upper = rank_there >= half
    target = begins + rank_there + jnp.where(upper, float(holders * half - half), 0.0)
    chosen = exact_bf16(place == jnp.where(begins >= 0.0, target, -1.0))
    landed = jnp.concatenate([ref[core] for ref in landed_refs for core in range(2)], axis=0).T
    result = exact_product(jnp.concatenate([landed[:total], landed[total:]], axis=1), chosen)
    result = result.T
    blocks = []
    for g in range(groups):
        block = result[g * share:(g + 1) * share]
        blocks.append(jnp.concatenate([block[:share // 2], block[share // 2:]], axis=1))
    for step, out_ref in enumerate(out_refs):
        chosen = blocks[0]
        for g in range(1, groups):
            chosen = jnp.where((at + step) % groups == g, blocks[g], chosen)
        out_ref[...] = chosen


def swap(value, axis, distance):
    return lax.ppermute(value, axis, [(i, i ^ distance) for i in range(lax.axis_size(axis))])


def on_device(query_grads, factor_out, factor_in, page_store, page_home, cand_lists, counts):
    holders = lax.axis_size("store")
    groups = lax.axis_size("layer")
    rows, width = query_grads.shape
    layers, rank, _ = factor_out.shape
    per_holder = page_store.shape[0]
    slots = cand_lists.shape[1]
    bf16 = jnp.bfloat16

    capacity = slots // holders
    home = page_home.reshape(-1, LANES)
    sources = [
        pltpu.with_memory_space_constraint(source, pltpu.HBM)
        for source in (query_grads, factor_in, factor_out, home, cand_lists, page_store)
    ]
    notes = max(LANES, holders // rows * capacity)
    far = holders - 2
    raw = swap(query_grads, "store", far)
    far_list = swap(cand_lists, "store", far)
    turned = pltpu.VMEM((layers, rows * rank // 2, LANES), jnp.float32)
    packed, again, found, in_factor, out_factor, home_here, pages = pl.pallas_call(
        functools.partial(condition_kernel, holders, capacity, per_holder),
        out_shape=[
            jax.ShapeDtypeStruct((rows, width + notes), bf16),
            jax.ShapeDtypeStruct((rows, width + notes), bf16),
            jax.ShapeDtypeStruct((8, slots), jnp.float32),
            jax.ShapeDtypeStruct(factor_in.shape, jnp.float32),
            jax.ShapeDtypeStruct(factor_out.shape, jnp.float32),
            jax.ShapeDtypeStruct(home.shape, jnp.int32),
            pltpu.VMEM(page_store.shape, bf16),
        ],
        in_specs=[HBM] * len(sources),
        out_specs=[VMEM] * 7,
        scratch_shapes=[pltpu.VMEM(sources[i].shape, sources[i].dtype) for i in (0, 4)]
        + [pltpu.SemaphoreType.DMA((len(sources),)), turned],
        compiler_params=pltpu.CompilerParams(vmem_limit_bytes=14 * 2**20 + 24 * slots * slots),
    )(*sources)

    again, pages = pl.pallas_call(
        load_kernel,
        out_shape=[jax.ShapeDtypeStruct(again.shape, bf16), pltpu.VMEM((width, per_holder), bf16)],
        in_specs=[VMEM] * 2,
        out_specs=[VMEM] * 2,
        input_output_aliases={0: 0},
        compiler_params=pltpu.CompilerParams(vmem_limit_bytes=4 * 2**20 + 4 * per_holder * width),
        cost_estimate=pl.CostEstimate(flops=0, bytes_accessed=2 * page_store.size, transcendentals=0),
    )(again, pltpu.with_memory_space_constraint(pages, pltpu.VMEM))

    blocks = [None] * holders
    blocks[0] = packed
    for k in range(2, holders - 2, 2):
        blocks[k] = swap(packed, "store", k)
    blocks[far] = pl.pallas_call(
        functools.partial(late_kernel, holders, capacity, per_holder),
        out_shape=jax.ShapeDtypeStruct(packed.shape, bf16),
        in_specs=[VMEM] * 5,
        out_specs=VMEM,
        scratch_shapes=[turned],
        compiler_params=pltpu.CompilerParams(vmem_limit_bytes=10 * 2**20 + 24 * slots * slots),
        cost_estimate=pl.CostEstimate(flops=LATE_FLOPS, bytes_accessed=8 * packed.size, transcendentals=0),
    )(raw, far_list, in_factor, out_factor, home_here)
    blocks[1] = swap(again, "store", 1)
    for k in range(2, holders, 2):
        blocks[k + 1] = swap(blocks[k], "store", 1)

    total = holders * rows
    bytes_in = 2 * holders * rows * (width + notes) + 2 * per_holder * width
    picked_shape = jax.ShapeDtypeStruct((holders // 2, capacity // 2, 2 * total), jnp.float32)
    send, scores, rest = pl.pallas_call(
        functools.partial(score_kernel, holders, capacity),
        out_shape=[
            picked_shape,
            jax.ShapeDtypeStruct((total, per_holder), jnp.float32),
            jax.ShapeDtypeStruct((1, slots // 2), jnp.float32),
        ],
        in_specs=[VMEM] * (holders + 1),
        out_specs=[VMEM] * 3,
        scratch_shapes=[pltpu.VMEM((total, width), bf16)],
        compiler_params=pltpu.CompilerParams(vmem_limit_bytes=8 * 2**20 + 2 * bytes_in + 48 * total * slots),
    )(*blocks[::-1], pltpu.with_memory_space_constraint(pages, pltpu.VMEM))

    handed = swap(send, "store", 1)
    keep = pl.pallas_call(
        rest_kernel,
        out_shape=picked_shape,
        in_specs=[VMEM] * 2,
        out_specs=VMEM,
        compiler_params=pltpu.CompilerParams(vmem_limit_bytes=4 * 2**20 + 24 * total * slots),
    )(scores, rest)
    chips = holders // 2
    landed = []
    for step in range(chips):
        pair = jnp.stack([keep[step], handed[step]])
        to = [(i, (i // 2 + step) % chips * 2 + 1 - i % 2) for i in range(holders)]
        landed.append(lax.ppermute(pair, "store", to) if step else pair)
    share = slots // groups
    terms = pl.pallas_call(
        functools.partial(spread_kernel, holders, groups),
        out_shape=[jax.ShapeDtypeStruct((share // 2, 2 * total), jnp.float32)] * groups,
        in_specs=[SMEM] + [VMEM] * (1 + len(landed)),
        out_specs=[VMEM] * groups,
        compiler_params=pltpu.CompilerParams(vmem_limit_bytes=4 * 2**20 + 64 * total * slots),
    )(counts, found, *landed[::-1])
    summed = terms[0]
    for step in range(1, groups):
        summed = summed + lax.ppermute(terms[step], "layer", [(g, (g + step) % groups) for g in range(groups)])
    return jnp.concatenate([summed[:, :total], summed[:, total:]], axis=0)[None]


def solution(mesh):
    placed = (
        P("store", "layer"),
        P("layer", None, None),
        P("layer", None, None),
        P("store", "layer"),
        P(),
        P("store", None),
        P("store"),
    )
    return jax.shard_map(
        on_device, mesh=mesh, in_specs=placed, out_specs=P("store", "layer", None), check_vma=False
    )
```

```python
import functools

import jax
import jax.numpy as jnp
from jax import lax
from jax.experimental import pallas as pl
from jax.experimental.pallas import tpu as pltpu
from jax.sharding import PartitionSpec as P

VMEM = pl.BlockSpec(memory_space=pltpu.VMEM)
SMEM = pl.BlockSpec(memory_space=pltpu.SMEM)
HBM = pl.BlockSpec(memory_space=pltpu.HBM)
LANES = 128
CHUNKS = 4
LATE_FLOPS = 5 * 10**9
LOADS = 8


def iota(shape, dimension):
    return lax.broadcasted_iota(jnp.int32, shape, dimension)


def block_owners(holders):
    if holders == 8:
        return [(0, 0), (1, 1), (2, 4), (5, 3), (4, 2), (3, 5), (6, 6), (7, 7)]
    return [(k, k) for k in range(holders)]


def parts_of(value):
    parts = []
    for _ in range(3):
        part = value.astype(jnp.bfloat16)
        value = value - part.astype(jnp.float32)
        parts.append(part)
    return parts


def exact_product(value, chosen):
    rows = value.shape[0]
    product = jnp.dot(jnp.concatenate(parts_of(value), axis=0), chosen, preferred_element_type=jnp.float32)
    return product[2 * rows:] + product[rows:2 * rows] + product[:rows]


def exact_bf16(value):
    return value.astype(jnp.float32).astype(jnp.bfloat16)


def condition(query_ref, in_factor_ref, out_factor_ref, turned_ref, target_refs):
    rows, width = query_ref.shape
    layers, rank, _ = in_factor_ref.shape
    half = rank // 2
    query = query_ref[...].astype(jnp.float32)
    low = iota((half, LANES), 1) < rank
    zero = jnp.zeros((rank, rank), jnp.float32)
    terms = [(0, 0), (0, 1), (0, 2), (1, 0), (1, 1), (2, 0)]
    group = 2 * LANES
    source, place = iota((rank, 2 * group), 0), iota((rank, 2 * group), 1)
    inside = place % group
    column_found = (source == 2 * (inside % half) + place // group)
    chosen_part = sum((inside >= half * start).astype(jnp.int32) for start in (3, 5, 6))
    pickers = [exact_bf16(column_found & (chosen_part == i)) for i in range(3)]
    for layer in range(layers):
        first = layer * half
        packed = jnp.concatenate(
            [query[:, (first + t) * LANES:(first + t + 1) * LANES] for t in range(half)], axis=0
        ).astype(jnp.bfloat16)
        factor = in_factor_ref[layer]
        doubled = parts_of(
            jnp.concatenate(
                [jnp.concatenate([factor, zero], axis=1), jnp.concatenate([zero, factor], axis=1)], axis=0
            )
        )
        small = jnp.dot(
            jnp.concatenate([packed, packed], axis=1), jnp.concatenate(doubled[1:], axis=0),
            preferred_element_type=jnp.float32,
        )
        turned_ref[layer] = small + jnp.dot(packed, doubled[0], preferred_element_type=jnp.float32)
        wide = jnp.concatenate([turned_ref[layer, pl.ds(q, half, stride=rows), :] for q in range(rows)], axis=1)
        wide = parts_of(wide)
        stacked = jnp.concatenate([wide[j] for _, j in terms], axis=0)
        by_row = jnp.concatenate(
            [out_factor_ref[layer, pl.ds(parity, half, stride=2), :] for parity in range(2)], axis=0
        )
        sorted_columns = sum(
            jnp.dot(part, picker, preferred_element_type=jnp.float32) for part, picker in zip(parts_of(by_row), pickers)
        )
        quarters = jnp.concatenate(
            [
                sorted_columns[r * half:(r + 1) * half, c * group:c * group + len(terms) * half]
                for r in range(2) for c in range(2)
            ],
            axis=0,
        ).astype(jnp.bfloat16)
        left = jnp.dot(quarters, stacked, preferred_element_type=jnp.float32)
        for q in range(rows):
            part = left[:, q * LANES:(q + 1) * LANES]
            ee, eo, oe, oo = (part[i * half:(i + 1) * half] for i in range(4))
            done = jnp.where(low, ee, oo) + pltpu.roll(jnp.where(low, oe, eo), rank, 1)
            turned_ref[layer, pl.ds(q, half, stride=rows), :] = done
        for t in range(half):
            tile = turned_ref[layer, t * rows:(t + 1) * rows, :].astype(jnp.bfloat16)
            for target_ref in target_refs:
                target_ref[:, (first + t) * LANES:(first + t + 1) * LANES] = tile


def look_up(holders, capacity, per_holder, rows, cand_ref, home_ref):
    slots = cand_ref.shape[1]
    home_rows = home_ref.shape[0]
    wanted = cand_ref[...]
    onehot = (iota((LANES, slots), 0) == wanted % LANES).astype(jnp.float32).astype(jnp.bfloat16)
    home = home_ref[...]
    table = jnp.concatenate([home // per_holder, home % per_holder], axis=0).astype(jnp.float32).astype(jnp.bfloat16)
    found = jnp.dot(table, onehot, preferred_element_type=jnp.float32)
    mine = iota((home_rows, slots), 0) == wanted // LANES
    holder = jnp.sum(jnp.where(mine, found[:home_rows], 0.0), axis=0, keepdims=True)
    within = jnp.sum(jnp.where(mine, found[home_rows:], 0.0), axis=0, keepdims=True)
    at_holder = iota((holders, slots), 0).astype(jnp.float32) == holder
    earlier = exact_bf16(iota((slots, slots), 0) < iota((slots, slots), 1))
    before = jnp.dot(exact_bf16(at_holder), earlier, preferred_element_type=jnp.float32)
    rank_there = jnp.sum(jnp.where(at_holder, before, 0.0), axis=0, keepdims=True)
    ranked = exact_bf16(iota((capacity, slots), 0).astype(jnp.float32) == rank_there)
    asked = lax.dot_general(
        exact_bf16(jnp.where(at_holder, within + 1.0, 0.0)), ranked, (((1,), (1,)), ((), ())),
        preferred_element_type=jnp.float32,
    )
    blocks = [asked[h:h + rows] for h in range(0, holders, rows)]
    spare = max(LANES, capacity * len(blocks)) - capacity * len(blocks)
    if spare:
        blocks.append(jnp.zeros((rows, spare), jnp.float32))
    notes = jnp.concatenate(blocks, axis=1).astype(jnp.bfloat16)
    return notes, holder, rank_there


def condition_kernel(holders, capacity, per_holder, *refs):
    sources, packed_ref, again_ref, found_ref = refs[:6], *refs[6:9]
    in_factor_ref, out_factor_ref, home_ref, pages_ref, query_ref, cand_ref, arrived, turned_ref = refs[9:]
    copies = [
        pltpu.make_async_copy(source, target, arrived.at[i])
        for i, (source, target) in enumerate(
            zip(sources, (query_ref, in_factor_ref, out_factor_ref, home_ref, cand_ref, pages_ref))
        )
    ]
    for copy in copies:
        copy.start()
    for copy in copies[:-1]:
        copy.wait()
    rows, width = query_ref.shape
    condition(query_ref, in_factor_ref, out_factor_ref, turned_ref, (packed_ref, again_ref))
    notes, holder, rank_there = look_up(holders, capacity, per_holder, rows, cand_ref, home_ref)
    slots = cand_ref.shape[1]
    for target_ref in (packed_ref, again_ref):
        target_ref[:, width:] = notes
    found_ref[...] = jnp.concatenate([holder, rank_there, jnp.zeros((6, slots), jnp.float32)], axis=0)
    copies[-1].wait()


def late_kernel(
    holders, capacity, per_holder, query_ref, cand_ref, in_factor_ref, out_factor_ref, home_ref, packed_ref, turned_ref
):
    rows, width = query_ref.shape
    condition(query_ref, in_factor_ref, out_factor_ref, turned_ref, (packed_ref,))
    packed_ref[:, width:] = look_up(holders, capacity, per_holder, rows, cand_ref, home_ref)[0]


def load_kernel(block_ref, source_ref, same_block_ref, target_ref):
    step = source_ref.shape[1] // LOADS
    for i in range(LOADS):
        target_ref[i * step:(i + 1) * step, :] = source_ref[:, i * step:(i + 1) * step].T


def pick(scores, wanted):
    chosen = exact_bf16(iota((scores.shape[1], wanted.shape[1]), 0).astype(jnp.float32) + 1.0 == wanted)
    picked = exact_product(scores, chosen)
    cut = wanted.shape[1] // 2
    return jnp.concatenate([picked[:, :cut], picked[:, cut:]], axis=0).T


def score_kernel(holders, capacity, *refs):
    packed_refs, pages_ref, send_ref, scores_ref, rest_ref, queries = refs[:holders][::-1], *refs[holders:]
    me = lax.axis_index("store")
    width, count = pages_ref.shape
    rows = packed_refs[0].shape[0]
    half = capacity // 2
    step = width // CHUNKS
    scores = jnp.zeros((holders * rows, count), jnp.float32)
    for i in range(CHUNKS):
        columns = slice(i * step, (i + 1) * step)
        for k in range(holders):
            queries[k * rows:(k + 1) * rows, columns] = packed_refs[k][:, columns]
        scores = scores + jnp.dot(queries[:, columns], pages_ref[columns], preferred_element_type=jnp.float32)
    second_core = me % 2 == 1
    owners = block_owners(holders)
    for k, (first, second) in enumerate(owners):
        start = pl.multiple_of((me ^ jnp.where(second_core, second, first)) * rows, rows)
        scores_ref[pl.ds(start, rows), :] = scores[k * rows:(k + 1) * rows]
    asked = []
    for k in range(holders):
        notes = packed_refs[k][:, width:].astype(jnp.float32)
        notes = jnp.sum(jnp.where(iota(notes.shape, 0) == me % rows, notes, 0.0), axis=0, keepdims=True)
        mine = notes[:, :capacity]
        for block in range(1, holders // rows):
            mine = jnp.where(me // rows == block, notes[:, block * capacity:(block + 1) * capacity], mine)
        asked.append(mine)
    places = [[pair[core] for pair in owners] for core in range(2)]
    asked = [
        jnp.where(second_core, asked[places[1].index(k)], asked[places[0].index(k)]) for k in range(holders)
    ]
    chips = holders // 2
    chip = me // 2
    kept, handed = [asked[0]], [asked[1]]
    for step in range(1, chips):
        apart = chip ^ ((chip + step) % chips)
        for rows_of, core in ((kept, 1), (handed, 0)):
            chosen = asked[2 + core]
            for distance in range(2, chips):
                chosen = jnp.where(apart == distance, asked[2 * distance + core], chosen)
            rows_of.append(chosen)
    wanted = [
        jnp.concatenate([row[:, side * half:(side + 1) * half] for side in range(2) for row in rows_of], axis=1)
        for rows_of in (handed, kept)
    ]
    rest_ref[...] = wanted[1]
    picked = pick(scores_ref[...], wanted[0])
    for place in range(chips):
        send_ref[place] = picked[place * half:(place + 1) * half]


def rest_kernel(scores_ref, rest_ref, keep_ref):
    picked = pick(scores_ref[...], rest_ref[...])
    half = keep_ref.shape[1]
    for place in range(keep_ref.shape[0]):
        keep_ref[place] = picked[place * half:(place + 1) * half]


def spread_kernel(holders, groups, count_ref, found_ref, *refs):
    landed_refs, out_refs = refs[:holders // 2][::-1], refs[holders // 2:]
    half = landed_refs[0].shape[1]
    slots = found_ref.shape[1]
    total = landed_refs[0].shape[2] // 2
    at = lax.axis_index("layer")
    share = slots // groups
    me = lax.axis_index("store")
    chips = holders // 2
    holder = found_ref[0:1].astype(jnp.int32)
    step = (me // 2 - holder // 2 + 2 * chips) % chips
    same_core = (holder % 2 == me % 2).astype(jnp.int32)
    place = 2 * step + jnp.where(step == 0, 1 - same_core, same_core)
    used = iota((1, slots), 1) < count_ref[0]
    begins = jnp.where(used, place * half, -1).astype(jnp.float32)
    rank_there = found_ref[1:2]
    place = iota((2 * holders * half, slots), 0).astype(jnp.float32)
    upper = rank_there >= half
    target = begins + rank_there + jnp.where(upper, float(holders * half - half), 0.0)
    chosen = exact_bf16(place == jnp.where(begins >= 0.0, target, -1.0))
    landed = jnp.concatenate([ref[core] for ref in landed_refs for core in range(2)], axis=0).T
    result = exact_product(jnp.concatenate([landed[:total], landed[total:]], axis=1), chosen)
    result = result.T
    blocks = []
    for g in range(groups):
        block = result[g * share:(g + 1) * share]
        blocks.append(jnp.concatenate([block[:share // 2], block[share // 2:]], axis=1))
    for step, out_ref in enumerate(out_refs):
        chosen = blocks[0]
        for g in range(1, groups):
            chosen = jnp.where((at + step) % groups == g, blocks[g], chosen)
        out_ref[...] = chosen


def swap(value, axis, distance):
    return lax.ppermute(value, axis, [(i, i ^ distance) for i in range(lax.axis_size(axis))])


def on_device(query_grads, factor_out, factor_in, page_store, page_home, cand_lists, counts):
    holders = lax.axis_size("store")
    groups = lax.axis_size("layer")
    rows, width = query_grads.shape
    layers, rank, _ = factor_out.shape
    per_holder = page_store.shape[0]
    slots = cand_lists.shape[1]
    bf16 = jnp.bfloat16

    capacity = slots // holders
    home = page_home.reshape(-1, LANES)
    sources = [
        pltpu.with_memory_space_constraint(source, pltpu.HBM)
        for source in (query_grads, factor_in, factor_out, home, cand_lists, page_store)
    ]
    notes = max(LANES, holders // rows * capacity)
    far = holders - 2
    raw = swap(query_grads, "store", far)
    far_list = swap(cand_lists, "store", far)
    turned = pltpu.VMEM((layers, rows * rank // 2, LANES), jnp.float32)
    packed, again, found, in_factor, out_factor, home_here, pages = pl.pallas_call(
        functools.partial(condition_kernel, holders, capacity, per_holder),
        out_shape=[
            jax.ShapeDtypeStruct((rows, width + notes), bf16),
            jax.ShapeDtypeStruct((rows, width + notes), bf16),
            jax.ShapeDtypeStruct((8, slots), jnp.float32),
            jax.ShapeDtypeStruct(factor_in.shape, jnp.float32),
            jax.ShapeDtypeStruct(factor_out.shape, jnp.float32),
            jax.ShapeDtypeStruct(home.shape, jnp.int32),
            pltpu.VMEM(page_store.shape, bf16),
        ],
        in_specs=[HBM] * len(sources),
        out_specs=[VMEM] * 7,
        scratch_shapes=[pltpu.VMEM(sources[i].shape, sources[i].dtype) for i in (0, 4)]
        + [pltpu.SemaphoreType.DMA((len(sources),)), turned],
        compiler_params=pltpu.CompilerParams(vmem_limit_bytes=14 * 2**20 + 24 * slots * slots),
    )(*sources)

    again, pages = pl.pallas_call(
        load_kernel,
        out_shape=[jax.ShapeDtypeStruct(again.shape, bf16), pltpu.VMEM((width, per_holder), bf16)],
        in_specs=[VMEM] * 2,
        out_specs=[VMEM] * 2,
        input_output_aliases={0: 0},
        compiler_params=pltpu.CompilerParams(vmem_limit_bytes=4 * 2**20 + 4 * per_holder * width),
        cost_estimate=pl.CostEstimate(flops=0, bytes_accessed=2 * page_store.size, transcendentals=0),
    )(again, pltpu.with_memory_space_constraint(pages, pltpu.VMEM))

    blocks = [None] * holders
    blocks[0] = packed
    for k in range(2, holders - 2, 2):
        pair = block_owners(holders)[k]
        blocks[k] = lax.ppermute(packed, "store", [(i, i ^ pair[i % 2]) for i in range(holders)])
    blocks[far] = pl.pallas_call(
        functools.partial(late_kernel, holders, capacity, per_holder),
        out_shape=jax.ShapeDtypeStruct(packed.shape, bf16),
        in_specs=[VMEM] * 5,
        out_specs=VMEM,
        scratch_shapes=[turned],
        compiler_params=pltpu.CompilerParams(vmem_limit_bytes=10 * 2**20 + 24 * slots * slots),
        cost_estimate=pl.CostEstimate(flops=LATE_FLOPS, bytes_accessed=8 * packed.size, transcendentals=0),
    )(raw, far_list, in_factor, out_factor, home_here)
    blocks[1] = swap(again, "store", 1)
    for k in range(2, holders, 2):
        blocks[k + 1] = swap(blocks[k], "store", 1)

    total = holders * rows
    bytes_in = 2 * holders * rows * (width + notes) + 2 * per_holder * width
    picked_shape = jax.ShapeDtypeStruct((holders // 2, capacity // 2, 2 * total), jnp.float32)
    send, scores, rest = pl.pallas_call(
        functools.partial(score_kernel, holders, capacity),
        out_shape=[
            picked_shape,
            jax.ShapeDtypeStruct((total, per_holder), jnp.float32),
            jax.ShapeDtypeStruct((1, slots // 2), jnp.float32),
        ],
        in_specs=[VMEM] * (holders + 1),
        out_specs=[VMEM] * 3,
        scratch_shapes=[pltpu.VMEM((total, width), bf16)],
        compiler_params=pltpu.CompilerParams(vmem_limit_bytes=8 * 2**20 + 2 * bytes_in + 48 * total * slots),
    )(*blocks[::-1], pltpu.with_memory_space_constraint(pages, pltpu.VMEM))

    handed = swap(send, "store", 1)
    keep = pl.pallas_call(
        rest_kernel,
        out_shape=picked_shape,
        in_specs=[VMEM] * 2,
        out_specs=VMEM,
        compiler_params=pltpu.CompilerParams(vmem_limit_bytes=4 * 2**20 + 24 * total * slots),
    )(scores, rest)
    chips = holders // 2
    landed = []
    for step in range(chips):
        pair = jnp.stack([keep[step], handed[step]])
        to = [(i, (i // 2 + step) % chips * 2 + 1 - i % 2) for i in range(holders)]
        landed.append(lax.ppermute(pair, "store", to) if step else pair)
    share = slots // groups
    terms = pl.pallas_call(
        functools.partial(spread_kernel, holders, groups),
        out_shape=[jax.ShapeDtypeStruct((share // 2, 2 * total), jnp.float32)] * groups,
        in_specs=[SMEM] + [VMEM] * (1 + len(landed)),
        out_specs=[VMEM] * groups,
        compiler_params=pltpu.CompilerParams(vmem_limit_bytes=4 * 2**20 + 64 * total * slots),
    )(counts, found, *landed[::-1])
    summed = terms[0]
    for step in range(1, groups):
        summed = summed + lax.ppermute(terms[step], "layer", [(g, (g + step) % groups) for g in range(groups)])
    return jnp.concatenate([summed[:, :total], summed[:, total:]], axis=0)[None]


def solution(mesh):
    placed = (
        P("store", "layer"),
        P("layer", None, None),
        P("layer", None, None),
        P("store", "layer"),
        P(),
        P("store", None),
        P("store"),
    )
    return jax.shard_map(
        on_device, mesh=mesh, in_specs=placed, out_specs=P("store", "layer", None), check_vma=False
    )
```

```python
import functools

import jax
import jax.numpy as jnp
from jax import lax
from jax.experimental import pallas as pl
from jax.experimental.pallas import tpu as pltpu
from jax.sharding import PartitionSpec as P

VMEM = pl.BlockSpec(memory_space=pltpu.VMEM)
SMEM = pl.BlockSpec(memory_space=pltpu.SMEM)
HBM = pl.BlockSpec(memory_space=pltpu.HBM)
LANES = 128
CHUNKS = 4
LATE_FLOPS = 5 * 10**9
LOADS = 8


def iota(shape, dimension):
    return lax.broadcasted_iota(jnp.int32, shape, dimension)


def parts_of(value):
    parts = []
    for _ in range(3):
        part = value.astype(jnp.bfloat16)
        value = value - part.astype(jnp.float32)
        parts.append(part)
    return parts


def exact_product(value, chosen):
    rows = value.shape[0]
    product = jnp.dot(jnp.concatenate(parts_of(value), axis=0), chosen, preferred_element_type=jnp.float32)
    return product[2 * rows:] + product[rows:2 * rows] + product[:rows]


def exact_bf16(value):
    return value.astype(jnp.float32).astype(jnp.bfloat16)


def condition(query_ref, in_factor_ref, out_factor_ref, turned_ref, target_refs):
    rows, width = query_ref.shape
    layers, rank, _ = in_factor_ref.shape
    half = rank // 2
    query = query_ref[...].astype(jnp.float32)
    low = iota((half, LANES), 1) < rank
    zero = jnp.zeros((rank, rank), jnp.float32)
    terms = [(0, 0), (0, 1), (0, 2), (1, 0), (1, 1), (2, 0)]
    group = 2 * LANES
    source, place = iota((rank, 2 * group), 0), iota((rank, 2 * group), 1)
    inside = place % group
    column_found = (source == 2 * (inside % half) + place // group)
    chosen_part = sum((inside >= half * start).astype(jnp.int32) for start in (3, 5, 6))
    pickers = [exact_bf16(column_found & (chosen_part == i)) for i in range(3)]
    for layer in range(layers):
        first = layer * half
        packed = jnp.concatenate(
            [query[:, (first + t) * LANES:(first + t + 1) * LANES] for t in range(half)], axis=0
        ).astype(jnp.bfloat16)
        factor = in_factor_ref[layer]
        doubled = parts_of(
            jnp.concatenate(
                [jnp.concatenate([factor, zero], axis=1), jnp.concatenate([zero, factor], axis=1)], axis=0
            )
        )
        small = jnp.dot(
            jnp.concatenate([packed, packed], axis=1), jnp.concatenate(doubled[1:], axis=0),
            preferred_element_type=jnp.float32,
        )
        turned_ref[layer] = small + jnp.dot(packed, doubled[0], preferred_element_type=jnp.float32)
        wide = jnp.concatenate([turned_ref[layer, pl.ds(q, half, stride=rows), :] for q in range(rows)], axis=1)
        wide = parts_of(wide)
        stacked = jnp.concatenate([wide[j] for _, j in terms], axis=0)
        by_row = jnp.concatenate(
            [out_factor_ref[layer, pl.ds(parity, half, stride=2), :] for parity in range(2)], axis=0
        )
        sorted_columns = sum(
            jnp.dot(part, picker, preferred_element_type=jnp.float32) for part, picker in zip(parts_of(by_row), pickers)
        )
        quarters = jnp.concatenate(
            [
                sorted_columns[r * half:(r + 1) * half, c * group:c * group + len(terms) * half]
                for r in range(2) for c in range(2)
            ],
            axis=0,
        ).astype(jnp.bfloat16)
        left = jnp.dot(quarters, stacked, preferred_element_type=jnp.float32)
        for q in range(rows):
            part = left[:, q * LANES:(q + 1) * LANES]
            ee, eo, oe, oo = (part[i * half:(i + 1) * half] for i in range(4))
            done = jnp.where(low, ee, oo) + pltpu.roll(jnp.where(low, oe, eo), rank, 1)
            turned_ref[layer, pl.ds(q, half, stride=rows), :] = done
        for t in range(half):
            tile = turned_ref[layer, t * rows:(t + 1) * rows, :].astype(jnp.bfloat16)
            for target_ref in target_refs:
                target_ref[:, (first + t) * LANES:(first + t + 1) * LANES] = tile


def look_up(holders, capacity, per_holder, rows, cand_ref, home_ref):
    slots = cand_ref.shape[1]
    home_rows = home_ref.shape[0]
    wanted = cand_ref[...]
    onehot = (iota((LANES, slots), 0) == wanted % LANES).astype(jnp.float32).astype(jnp.bfloat16)
    home = home_ref[...]
    table = jnp.concatenate([home // per_holder, home % per_holder], axis=0).astype(jnp.float32).astype(jnp.bfloat16)
    found = jnp.dot(table, onehot, preferred_element_type=jnp.float32)
    mine = iota((home_rows, slots), 0) == wanted // LANES
    holder = jnp.sum(jnp.where(mine, found[:home_rows], 0.0), axis=0, keepdims=True)
    within = jnp.sum(jnp.where(mine, found[home_rows:], 0.0), axis=0, keepdims=True)
    at_holder = iota((holders, slots), 0).astype(jnp.float32) == holder
    earlier = exact_bf16(iota((slots, slots), 0) < iota((slots, slots), 1))
    before = jnp.dot(exact_bf16(at_holder), earlier, preferred_element_type=jnp.float32)
    rank_there = jnp.sum(jnp.where(at_holder, before, 0.0), axis=0, keepdims=True)
    ranked = exact_bf16(iota((capacity, slots), 0).astype(jnp.float32) == rank_there)
    asked = lax.dot_general(
        exact_bf16(jnp.where(at_holder, within + 1.0, 0.0)), ranked, (((1,), (1,)), ((), ())),
        preferred_element_type=jnp.float32,
    )
    blocks = [asked[h:h + rows] for h in range(0, holders, rows)]
    spare = max(LANES, capacity * len(blocks)) - capacity * len(blocks)
    if spare:
        blocks.append(jnp.zeros((rows, spare), jnp.float32))
    notes = jnp.concatenate(blocks, axis=1).astype(jnp.bfloat16)
    return notes, holder, rank_there


def condition_kernel(holders, capacity, per_holder, *refs):
    sources, packed_ref, again_ref, found_ref = refs[:6], *refs[6:9]
    in_factor_ref, out_factor_ref, home_ref, pages_ref, query_ref, cand_ref, arrived, turned_ref = refs[9:]
    copies = [
        pltpu.make_async_copy(source, target, arrived.at[i])
        for i, (source, target) in enumerate(
            zip(sources, (query_ref, in_factor_ref, out_factor_ref, home_ref, cand_ref, pages_ref))
        )
    ]
    for copy in copies:
        copy.start()
    for copy in copies[:-1]:
        copy.wait()
    rows, width = query_ref.shape
    condition(query_ref, in_factor_ref, out_factor_ref, turned_ref, (packed_ref, again_ref))
    notes, holder, rank_there = look_up(holders, capacity, per_holder, rows, cand_ref, home_ref)
    slots = cand_ref.shape[1]
    for target_ref in (packed_ref, again_ref):
        target_ref[:, width:] = notes
    found_ref[...] = jnp.concatenate([holder, rank_there, jnp.zeros((6, slots), jnp.float32)], axis=0)
    copies[-1].wait()


def late_kernel(query_ref, in_factor_ref, out_factor_ref, target_ref, turned_ref):
    condition(query_ref, in_factor_ref, out_factor_ref, turned_ref, (target_ref,))


def list_kernel(holders, capacity, per_holder, rows, cand_ref, home_ref, notes_ref):
    notes_ref[...] = look_up(holders, capacity, per_holder, rows, cand_ref, home_ref)[0]


def load_kernel(holders, count_ref, found_ref, block_ref, source_ref, same_block_ref, target_ref, used_ref):
    used_ref[...] = found_ref[...]
    slots = found_ref.shape[1]
    used_ref[0:1] = jnp.where(iota((1, slots), 1) < count_ref[0], found_ref[0:1], float(holders))
    step = source_ref.shape[1] // LOADS
    for i in range(LOADS):
        target_ref[i * step:(i + 1) * step, :] = source_ref[:, i * step:(i + 1) * step].T


def pick(scores, wanted):
    chosen = exact_bf16(iota((scores.shape[1], wanted.shape[1]), 0).astype(jnp.float32) + 1.0 == wanted)
    picked = exact_product(scores, chosen)
    cut = wanted.shape[1] // 2
    return jnp.concatenate([picked[:, :cut], picked[:, cut:]], axis=0).T


def score_kernel(holders, capacity, *refs):
    packed_refs, far_refs = refs[:holders][::-1], refs[holders:holders + 2]
    pages_ref, send_ref, scores_ref, rest_ref, queries = refs[holders + 2:]
    me = lax.axis_index("store")
    width, count = pages_ref.shape
    rows = packed_refs[0].shape[0]
    half = capacity // 2
    step = width // CHUNKS
    scores = jnp.zeros((holders * rows, count), jnp.float32)
    for i in range(CHUNKS):
        columns = slice(i * step, (i + 1) * step)
        for k in range(holders):
            queries[k * rows:(k + 1) * rows, columns] = packed_refs[k][:, columns]
        scores = scores + jnp.dot(queries[:, columns], pages_ref[columns], preferred_element_type=jnp.float32)
    for k in range(holders):
        start = pl.multiple_of((me ^ k) * rows, rows)
        scores_ref[pl.ds(start, rows), :] = scores[k * rows:(k + 1) * rows]
    asked = []
    for k in range(holders):
        notes = packed_refs[k][:, width:] if k < holders - 2 else far_refs[k - holders + 2][...]
        notes = notes.astype(jnp.float32)
        notes = jnp.sum(jnp.where(iota(notes.shape, 0) == me % rows, notes, 0.0), axis=0, keepdims=True)
        mine = notes[:, :capacity]
        for block in range(1, holders // rows):
            mine = jnp.where(me // rows == block, notes[:, block * capacity:(block + 1) * capacity], mine)
        asked.append(mine)
    chips = holders // 2
    chip = me // 2
    kept, handed = [asked[0]], [asked[1]]
    for step in range(1, chips):
        apart = chip ^ ((chip + step) % chips)
        for rows_of, core in ((kept, 1), (handed, 0)):
            chosen = asked[2 + core]
            for distance in range(2, chips):
                chosen = jnp.where(apart == distance, asked[2 * distance + core], chosen)
            rows_of.append(chosen)
    wanted = [
        jnp.concatenate([row[:, side * half:(side + 1) * half] for side in range(2) for row in rows_of], axis=1)
        for rows_of in (handed, kept)
    ]
    rest_ref[...] = wanted[1]
    picked = pick(scores_ref[...], wanted[0])
    for place in range(chips):
        send_ref[place] = picked[place * half:(place + 1) * half]


def rest_kernel(scores_ref, rest_ref, keep_ref):
    picked = pick(scores_ref[...], rest_ref[...])
    half = keep_ref.shape[1]
    for place in range(keep_ref.shape[0]):
        keep_ref[place] = picked[place * half:(place + 1) * half]


def spread_kernel(holders, groups, found_ref, *refs):
    landed_refs, out_refs = refs[:holders // 2][::-1], refs[holders // 2:]
    half = landed_refs[0].shape[1]
    slots = found_ref.shape[1]
    total = landed_refs[0].shape[2] // 2
    at = lax.axis_index("layer")
    share = slots // groups
    me = lax.axis_index("store")
    chips = holders // 2
    holder = found_ref[0:1].astype(jnp.int32)
    step = (me // 2 - holder // 2 + 2 * chips) % chips
    same_core = (holder % 2 == me % 2).astype(jnp.int32)
    place = 2 * step + jnp.where(step == 0, 1 - same_core, same_core)
    begins = jnp.where(holder < holders, place * half, -1).astype(jnp.float32)
    rank_there = found_ref[1:2]
    place = iota((2 * holders * half, slots), 0).astype(jnp.float32)
    upper = rank_there >= half
    target = begins + rank_there + jnp.where(upper, float(holders * half - half), 0.0)
    chosen = exact_bf16(place == jnp.where(begins >= 0.0, target, -1.0))
    landed = jnp.concatenate([ref[core] for ref in landed_refs for core in range(2)], axis=0).T
    result = exact_product(jnp.concatenate([landed[:total], landed[total:]], axis=1), chosen)
    result = result.T
    blocks = []
    for g in range(groups):
        block = result[g * share:(g + 1) * share]
        blocks.append(jnp.concatenate([block[:share // 2], block[share // 2:]], axis=1))
    for step, out_ref in enumerate(out_refs):
        chosen = blocks[0]
        for g in range(1, groups):
            chosen = jnp.where((at + step) % groups == g, blocks[g], chosen)
        out_ref[...] = chosen


def swap(value, axis, distance):
    return lax.ppermute(value, axis, [(i, i ^ distance) for i in range(lax.axis_size(axis))])


def on_device(query_grads, factor_out, factor_in, page_store, page_home, cand_lists, counts):
    holders = lax.axis_size("store")
    groups = lax.axis_size("layer")
    rows, width = query_grads.shape
    layers, rank, _ = factor_out.shape
    per_holder = page_store.shape[0]
    slots = cand_lists.shape[1]
    bf16 = jnp.bfloat16

    capacity = slots // holders
    home = page_home.reshape(-1, LANES)
    sources = [
        pltpu.with_memory_space_constraint(source, pltpu.HBM)
        for source in (query_grads, factor_in, factor_out, home, cand_lists, page_store)
    ]
    notes = max(LANES, holders // rows * capacity)
    far = holders - 2
    raw = swap(query_grads, "store", far)
    far_list = swap(cand_lists, "store", far)
    turned = pltpu.VMEM((layers, rows * rank // 2, LANES), jnp.float32)
    packed, again, found, in_factor, out_factor, home_here, pages = pl.pallas_call(
        functools.partial(condition_kernel, holders, capacity, per_holder),
        out_shape=[
            jax.ShapeDtypeStruct((rows, width + notes), bf16),
            jax.ShapeDtypeStruct((rows, width + notes), bf16),
            jax.ShapeDtypeStruct((8, slots), jnp.float32),
            jax.ShapeDtypeStruct(factor_in.shape, jnp.float32),
            jax.ShapeDtypeStruct(factor_out.shape, jnp.float32),
            jax.ShapeDtypeStruct(home.shape, jnp.int32),
            pltpu.VMEM(page_store.shape, bf16),
        ],
        in_specs=[HBM] * len(sources),
        out_specs=[VMEM] * 7,
        scratch_shapes=[pltpu.VMEM(sources[i].shape, sources[i].dtype) for i in (0, 4)]
        + [pltpu.SemaphoreType.DMA((len(sources),)), turned],
        compiler_params=pltpu.CompilerParams(vmem_limit_bytes=14 * 2**20 + 24 * slots * slots),
    )(*sources)

    again, pages, used = pl.pallas_call(
        functools.partial(load_kernel, holders),
        out_shape=[
            jax.ShapeDtypeStruct(again.shape, bf16),
            pltpu.VMEM((width, per_holder), bf16),
            jax.ShapeDtypeStruct(found.shape, jnp.float32),
        ],
        in_specs=[SMEM, VMEM, VMEM, VMEM],
        out_specs=[VMEM] * 3,
        input_output_aliases={2: 0},
        compiler_params=pltpu.CompilerParams(vmem_limit_bytes=4 * 2**20 + 4 * per_holder * width),
        cost_estimate=pl.CostEstimate(flops=0, bytes_accessed=2 * page_store.size, transcendentals=0),
    )(counts, found, again, pltpu.with_memory_space_constraint(pages, pltpu.VMEM))

    blocks = [None] * holders
    blocks[0] = packed
    for k in range(2, holders - 2, 2):
        blocks[k] = swap(packed, "store", k)
    blocks[far] = pl.pallas_call(
        late_kernel,
        out_shape=jax.ShapeDtypeStruct((rows, width), bf16),
        in_specs=[VMEM] * 3,
        out_specs=VMEM,
        scratch_shapes=[turned],
        compiler_params=pltpu.CompilerParams(vmem_limit_bytes=10 * 2**20 + 24 * slots * slots),
        cost_estimate=pl.CostEstimate(flops=LATE_FLOPS, bytes_accessed=8 * packed.size, transcendentals=0),
    )(raw, in_factor, out_factor)
    far_notes = pl.pallas_call(
        functools.partial(list_kernel, holders, capacity, per_holder, rows),
        out_shape=jax.ShapeDtypeStruct((rows, notes), bf16),
        in_specs=[VMEM] * 2,
        out_specs=VMEM,
        compiler_params=pltpu.CompilerParams(vmem_limit_bytes=4 * 2**20 + 24 * slots * slots),
        cost_estimate=pl.CostEstimate(flops=LATE_FLOPS, bytes_accessed=4 * home.size, transcendentals=0),
    )(far_list, home_here)
    far_notes = [far_notes, swap(far_notes, "store", 1)]
    blocks[1] = swap(again, "store", 1)
    for k in range(2, holders, 2):
        blocks[k + 1] = swap(blocks[k], "store", 1)

    total = holders * rows
    bytes_in = 2 * holders * rows * (width + notes) + 2 * per_holder * width
    picked_shape = jax.ShapeDtypeStruct((holders // 2, capacity // 2, 2 * total), jnp.float32)
    send, scores, rest = pl.pallas_call(
        functools.partial(score_kernel, holders, capacity),
        out_shape=[
            picked_shape,
            jax.ShapeDtypeStruct((total, per_holder), jnp.float32),
            jax.ShapeDtypeStruct((1, slots // 2), jnp.float32),
        ],
        in_specs=[VMEM] * (holders + 3),
        out_specs=[VMEM] * 3,
        scratch_shapes=[pltpu.VMEM((total, width), bf16)],
        compiler_params=pltpu.CompilerParams(vmem_limit_bytes=8 * 2**20 + 2 * bytes_in + 48 * total * slots),
    )(*blocks[::-1], *far_notes, pltpu.with_memory_space_constraint(pages, pltpu.VMEM))

    handed = swap(send, "store", 1)
    keep = pl.pallas_call(
        rest_kernel,
        out_shape=picked_shape,
        in_specs=[VMEM] * 2,
        out_specs=VMEM,
        compiler_params=pltpu.CompilerParams(vmem_limit_bytes=4 * 2**20 + 24 * total * slots),
    )(scores, rest)
    chips = holders // 2
    landed = []
    for step in range(chips):
        pair = jnp.stack([keep[step], handed[step]])
        to = [(i, (i // 2 + step) % chips * 2 + 1 - i % 2) for i in range(holders)]
        landed.append(lax.ppermute(pair, "store", to) if step else pair)
    share = slots // groups
    terms = pl.pallas_call(
        functools.partial(spread_kernel, holders, groups),
        out_shape=[jax.ShapeDtypeStruct((share // 2, 2 * total), jnp.float32)] * groups,
        in_specs=[VMEM] * (1 + len(landed)),
        out_specs=[VMEM] * groups,
        compiler_params=pltpu.CompilerParams(vmem_limit_bytes=4 * 2**20 + 64 * total * slots),
    )(used, *landed[::-1])
    summed = terms[0]
    for step in range(1, groups):
        summed = summed + lax.ppermute(terms[step], "layer", [(g, (g + step) % groups) for g in range(groups)])
    return jnp.concatenate([summed[:, :total], summed[:, total:]], axis=0)[None]


def solution(mesh):
    placed = (
        P("store", "layer"),
        P("layer", None, None),
        P("layer", None, None),
        P("store", "layer"),
        P(),
        P("store", None),
        P("store"),
    )
    return jax.shard_map(
        on_device, mesh=mesh, in_specs=placed, out_specs=P("store", "layer", None), check_vma=False
    )
```

```python
import functools

import jax
import jax.numpy as jnp
from jax import lax
from jax.experimental import pallas as pl
from jax.experimental.pallas import tpu as pltpu
from jax.sharding import PartitionSpec as P

VMEM = pl.BlockSpec(memory_space=pltpu.VMEM)
SMEM = pl.BlockSpec(memory_space=pltpu.SMEM)
HBM = pl.BlockSpec(memory_space=pltpu.HBM)
LANES = 128
CHUNKS = 4
LATE_FLOPS = 5 * 10**9
LOADS = 8


def iota(shape, dimension):
    return lax.broadcasted_iota(jnp.int32, shape, dimension)


def parts_of(value):
    parts = []
    for _ in range(3):
        part = value.astype(jnp.bfloat16)
        value = value - part.astype(jnp.float32)
        parts.append(part)
    return parts


def exact_product(value, chosen):
    rows = value.shape[0]
    product = jnp.dot(jnp.concatenate(parts_of(value), axis=0), chosen, preferred_element_type=jnp.float32)
    return product[2 * rows:] + product[rows:2 * rows] + product[:rows]


def exact_bf16(value):
    return value.astype(jnp.float32).astype(jnp.bfloat16)


def condition(query_ref, in_factor_ref, out_factor_ref, turned_ref, target_refs):
    rows, width = query_ref.shape
    layers, rank, _ = in_factor_ref.shape
    half = rank // 2
    query = query_ref[...].astype(jnp.float32)
    low = iota((half, LANES), 1) < rank
    zero = jnp.zeros((rank, rank), jnp.float32)
    terms = [(0, 0), (0, 1), (0, 2), (1, 0), (1, 1), (2, 0)]
    group = 2 * LANES
    source, place = iota((rank, 2 * group), 0), iota((rank, 2 * group), 1)
    inside = place % group
    column_found = (source == 2 * (inside % half) + place // group)
    chosen_part = sum((inside >= half * start).astype(jnp.int32) for start in (3, 5, 6))
    pickers = [exact_bf16(column_found & (chosen_part == i)) for i in range(3)]
    for layer in range(layers):
        first = layer * half
        packed = jnp.concatenate(
            [query[:, (first + t) * LANES:(first + t + 1) * LANES] for t in range(half)], axis=0
        ).astype(jnp.bfloat16)
        factor = in_factor_ref[layer]
        doubled = parts_of(
            jnp.concatenate(
                [jnp.concatenate([factor, zero], axis=1), jnp.concatenate([zero, factor], axis=1)], axis=0
            )
        )
        small = jnp.dot(
            jnp.concatenate([packed, packed], axis=1), jnp.concatenate(doubled[1:], axis=0),
            preferred_element_type=jnp.float32,
        )
        turned_ref[layer] = small + jnp.dot(packed, doubled[0], preferred_element_type=jnp.float32)
        wide = jnp.concatenate([turned_ref[layer, pl.ds(q, half, stride=rows), :] for q in range(rows)], axis=1)
        wide = parts_of(wide)
        stacked = jnp.concatenate([wide[j] for _, j in terms], axis=0)
        by_row = jnp.concatenate(
            [out_factor_ref[layer, pl.ds(parity, half, stride=2), :] for parity in range(2)], axis=0
        )
        sorted_columns = sum(
            jnp.dot(part, picker, preferred_element_type=jnp.float32) for part, picker in zip(parts_of(by_row), pickers)
        )
        quarters = jnp.concatenate(
            [
                sorted_columns[r * half:(r + 1) * half, c * group:c * group + len(terms) * half]
                for r in range(2) for c in range(2)
            ],
            axis=0,
        ).astype(jnp.bfloat16)
        left = jnp.dot(quarters, stacked, preferred_element_type=jnp.float32)
        for q in range(rows):
            part = left[:, q * LANES:(q + 1) * LANES]
            ee, eo, oe, oo = (part[i * half:(i + 1) * half] for i in range(4))
            done = jnp.where(low, ee, oo) + pltpu.roll(jnp.where(low, oe, eo), rank, 1)
            turned_ref[layer, pl.ds(q, half, stride=rows), :] = done
        for t in range(half):
            tile = turned_ref[layer, t * rows:(t + 1) * rows, :].astype(jnp.bfloat16)
            for target_ref in target_refs:
                target_ref[:, (first + t) * LANES:(first + t + 1) * LANES] = tile


def look_up(holders, capacity, per_holder, rows, cand_ref, home_ref):
    slots = cand_ref.shape[1]
    home_rows = home_ref.shape[0]
    wanted = cand_ref[...]
    onehot = (iota((LANES, slots), 0) == wanted % LANES).astype(jnp.float32).astype(jnp.bfloat16)
    home = home_ref[...]
    table = jnp.concatenate([home // per_holder, home % per_holder], axis=0).astype(jnp.float32).astype(jnp.bfloat16)
    found = jnp.dot(table, onehot, preferred_element_type=jnp.float32)
    mine = iota((home_rows, slots), 0) == wanted // LANES
    holder = jnp.sum(jnp.where(mine, found[:home_rows], 0.0), axis=0, keepdims=True)
    within = jnp.sum(jnp.where(mine, found[home_rows:], 0.0), axis=0, keepdims=True)
    at_holder = iota((holders, slots), 0).astype(jnp.float32) == holder
    earlier = exact_bf16(iota((slots, slots), 0) < iota((slots, slots), 1))
    before = jnp.dot(exact_bf16(at_holder), earlier, preferred_element_type=jnp.float32)
    rank_there = jnp.sum(jnp.where(at_holder, before, 0.0), axis=0, keepdims=True)
    ranked = exact_bf16(iota((capacity, slots), 0).astype(jnp.float32) == rank_there)
    asked = lax.dot_general(
        exact_bf16(jnp.where(at_holder, within + 1.0, 0.0)), ranked, (((1,), (1,)), ((), ())),
        preferred_element_type=jnp.float32,
    )
    blocks = [asked[h:h + rows] for h in range(0, holders, rows)]
    spare = max(LANES, capacity * len(blocks)) - capacity * len(blocks)
    if spare:
        blocks.append(jnp.zeros((rows, spare), jnp.float32))
    notes = jnp.concatenate(blocks, axis=1).astype(jnp.bfloat16)
    return notes, holder, rank_there


def condition_kernel(holders, capacity, per_holder, *refs):
    sources, packed_ref, again_ref, found_ref = refs[:6], *refs[6:9]
    in_factor_ref, out_factor_ref, home_ref, pages_ref, query_ref, cand_ref, arrived, turned_ref = refs[9:]
    copies = [
        pltpu.make_async_copy(source, target, arrived.at[i])
        for i, (source, target) in enumerate(
            zip(sources, (query_ref, in_factor_ref, out_factor_ref, home_ref, cand_ref, pages_ref))
        )
    ]
    for copy in copies:
        copy.start()
    for copy in copies[:-1]:
        copy.wait()
    rows, width = query_ref.shape
    condition(query_ref, in_factor_ref, out_factor_ref, turned_ref, (packed_ref, again_ref))
    notes, holder, rank_there = look_up(holders, capacity, per_holder, rows, cand_ref, home_ref)
    slots = cand_ref.shape[1]
    for target_ref in (packed_ref, again_ref):
        target_ref[:, width:] = notes
    found_ref[...] = jnp.concatenate([holder, rank_there, jnp.zeros((6, slots), jnp.float32)], axis=0)
    copies[-1].wait()


def late_kernel(query_ref, in_factor_ref, out_factor_ref, target_ref, turned_ref):
    condition(query_ref, in_factor_ref, out_factor_ref, turned_ref, (target_ref,))


def list_kernel(holders, capacity, per_holder, rows, cand_ref, home_ref, notes_ref):
    notes_ref[...] = look_up(holders, capacity, per_holder, rows, cand_ref, home_ref)[0]


def load_kernel(block_ref, source_ref, same_block_ref, target_ref):
    step = source_ref.shape[1] // LOADS
    for i in range(LOADS):
        target_ref[i * step:(i + 1) * step, :] = source_ref[:, i * step:(i + 1) * step].T


def pick(scores, wanted):
    chosen = exact_bf16(iota((scores.shape[1], wanted.shape[1]), 0).astype(jnp.float32) + 1.0 == wanted)
    picked = exact_product(scores, chosen)
    cut = wanted.shape[1] // 2
    return jnp.concatenate([picked[:, :cut], picked[:, cut:]], axis=0).T


def score_kernel(holders, capacity, *refs):
    packed_refs, far_refs = refs[:holders][::-1], refs[holders:holders + 2]
    pages_ref, send_ref, scores_ref, rest_ref, queries = refs[holders + 2:]
    me = lax.axis_index("store")
    width, count = pages_ref.shape
    rows = packed_refs[0].shape[0]
    half = capacity // 2
    step = width // CHUNKS
    scores = jnp.zeros((holders * rows, count), jnp.float32)
    for i in range(CHUNKS):
        columns = slice(i * step, (i + 1) * step)
        for k in range(holders):
            queries[k * rows:(k + 1) * rows, columns] = packed_refs[k][:, columns]
        scores = scores + jnp.dot(queries[:, columns], pages_ref[columns], preferred_element_type=jnp.float32)
    for k in range(holders):
        start = pl.multiple_of((me ^ k) * rows, rows)
        scores_ref[pl.ds(start, rows), :] = scores[k * rows:(k + 1) * rows]
    asked = []
    for k in range(holders):
        notes = packed_refs[k][:, width:] if k < holders - 2 else far_refs[k - holders + 2][...]
        notes = notes.astype(jnp.float32)
        notes = jnp.sum(jnp.where(iota(notes.shape, 0) == me % rows, notes, 0.0), axis=0, keepdims=True)
        mine = notes[:, :capacity]
        for block in range(1, holders // rows):
            mine = jnp.where(me // rows == block, notes[:, block * capacity:(block + 1) * capacity], mine)
        asked.append(mine)
    chips = holders // 2
    chip = me // 2
    kept, handed = [asked[0]], [asked[1]]
    for step in range(1, chips):
        apart = chip ^ ((chip + step) % chips)
        for rows_of, core in ((kept, 1), (handed, 0)):
            chosen = asked[2 + core]
            for distance in range(2, chips):
                chosen = jnp.where(apart == distance, asked[2 * distance + core], chosen)
            rows_of.append(chosen)
    wanted = [
        jnp.concatenate([row[:, side * half:(side + 1) * half] for side in range(2) for row in rows_of], axis=1)
        for rows_of in (handed, kept)
    ]
    rest_ref[...] = wanted[1]
    picked = pick(scores_ref[...], wanted[0])
    for place in range(chips):
        send_ref[place] = picked[place * half:(place + 1) * half]


def rest_kernel(scores_ref, rest_ref, keep_ref):
    picked = pick(scores_ref[...], rest_ref[...])
    half = keep_ref.shape[1]
    for place in range(keep_ref.shape[0]):
        keep_ref[place] = picked[place * half:(place + 1) * half]


def spread_kernel(holders, groups, count_ref, found_ref, *refs):
    landed_refs, out_refs = refs[:holders // 2][::-1], refs[holders // 2:]
    half = landed_refs[0].shape[1]
    slots = found_ref.shape[1]
    total = landed_refs[0].shape[2] // 2
    at = lax.axis_index("layer")
    share = slots // groups
    me = lax.axis_index("store")
    chips = holders // 2
    holder = found_ref[0:1].astype(jnp.int32)
    step = (me // 2 - holder // 2 + 2 * chips) % chips
    same_core = (holder % 2 == me % 2).astype(jnp.int32)
    place = 2 * step + jnp.where(step == 0, 1 - same_core, same_core)
    used = iota((1, slots), 1) < count_ref[0]
    begins = jnp.where(used, place * half, -1).astype(jnp.float32)
    rank_there = found_ref[1:2]
    place = iota((2 * holders * half, slots), 0).astype(jnp.float32)
    upper = rank_there >= half
    target = begins + rank_there + jnp.where(upper, float(holders * half - half), 0.0)
    chosen = exact_bf16(place == jnp.where(begins >= 0.0, target, -1.0))
    landed = jnp.concatenate([ref[core] for ref in landed_refs for core in range(2)], axis=0).T
    result = exact_product(jnp.concatenate([landed[:total], landed[total:]], axis=1), chosen)
    result = result.T
    blocks = []
    for g in range(groups):
        block = result[g * share:(g + 1) * share]
        blocks.append(jnp.concatenate([block[:share // 2], block[share // 2:]], axis=1))
    for step, out_ref in enumerate(out_refs):
        chosen = blocks[0]
        for g in range(1, groups):
            chosen = jnp.where((at + step) % groups == g, blocks[g], chosen)
        out_ref[...] = chosen


def swap(value, axis, distance):
    return lax.ppermute(value, axis, [(i, i ^ distance) for i in range(lax.axis_size(axis))])


def on_device(query_grads, factor_out, factor_in, page_store, page_home, cand_lists, counts):
    holders = lax.axis_size("store")
    groups = lax.axis_size("layer")
    rows, width = query_grads.shape
    layers, rank, _ = factor_out.shape
    per_holder = page_store.shape[0]
    slots = cand_lists.shape[1]
    bf16 = jnp.bfloat16

    capacity = slots // holders
    home = page_home.reshape(-1, LANES)
    sources = [
        pltpu.with_memory_space_constraint(source, pltpu.HBM)
        for source in (query_grads, factor_in, factor_out, home, cand_lists, page_store)
    ]
    notes = max(LANES, holders // rows * capacity)
    far = holders - 2
    raw = swap(query_grads, "store", far)
    far_list = swap(cand_lists, "store", far)
    turned = pltpu.VMEM((layers, rows * rank // 2, LANES), jnp.float32)
    packed, again, found, in_factor, out_factor, home_here, pages = pl.pallas_call(
        functools.partial(condition_kernel, holders, capacity, per_holder),
        out_shape=[
            jax.ShapeDtypeStruct((rows, width + notes), bf16),
            jax.ShapeDtypeStruct((rows, width + notes), bf16),
            jax.ShapeDtypeStruct((8, slots), jnp.float32),
            jax.ShapeDtypeStruct(factor_in.shape, jnp.float32),
            jax.ShapeDtypeStruct(factor_out.shape, jnp.float32),
            jax.ShapeDtypeStruct(home.shape, jnp.int32),
            pltpu.VMEM(page_store.shape, bf16),
        ],
        in_specs=[HBM] * len(sources),
        out_specs=[VMEM] * 7,
        scratch_shapes=[pltpu.VMEM(sources[i].shape, sources[i].dtype) for i in (0, 4)]
        + [pltpu.SemaphoreType.DMA((len(sources),)), turned],
        compiler_params=pltpu.CompilerParams(vmem_limit_bytes=14 * 2**20 + 24 * slots * slots),
    )(*sources)

    again, pages = pl.pallas_call(
        load_kernel,
        out_shape=[jax.ShapeDtypeStruct(again.shape, bf16), pltpu.VMEM((width, per_holder), bf16)],
        in_specs=[VMEM] * 2,
        out_specs=[VMEM] * 2,
        input_output_aliases={0: 0},
        compiler_params=pltpu.CompilerParams(vmem_limit_bytes=4 * 2**20 + 4 * per_holder * width),
        cost_estimate=pl.CostEstimate(flops=0, bytes_accessed=2 * page_store.size, transcendentals=0),
    )(again, pltpu.with_memory_space_constraint(pages, pltpu.VMEM))

    blocks = [None] * holders
    blocks[0] = packed
    for k in range(2, holders - 2, 2):
        blocks[k] = swap(packed, "store", k)
    blocks[far] = pl.pallas_call(
        late_kernel,
        out_shape=jax.ShapeDtypeStruct((rows, width), bf16),
        in_specs=[VMEM] * 3,
        out_specs=VMEM,
        scratch_shapes=[turned],
        compiler_params=pltpu.CompilerParams(vmem_limit_bytes=10 * 2**20 + 24 * slots * slots),
        cost_estimate=pl.CostEstimate(flops=LATE_FLOPS, bytes_accessed=8 * packed.size, transcendentals=0),
    )(raw, in_factor, out_factor)
    far_notes = pl.pallas_call(
        functools.partial(list_kernel, holders, capacity, per_holder, rows),
        out_shape=jax.ShapeDtypeStruct((rows, notes), bf16),
        in_specs=[VMEM] * 2,
        out_specs=VMEM,
        compiler_params=pltpu.CompilerParams(vmem_limit_bytes=4 * 2**20 + 24 * slots * slots),
        cost_estimate=pl.CostEstimate(flops=LATE_FLOPS, bytes_accessed=4 * home.size, transcendentals=0),
    )(far_list, home_here)
    far_notes = [far_notes, swap(far_notes, "store", 1)]
    blocks[1] = swap(again, "store", 1)
    for k in range(2, holders, 2):
        blocks[k + 1] = swap(blocks[k], "store", 1)

    total = holders * rows
    bytes_in = 2 * holders * rows * (width + notes) + 2 * per_holder * width
    picked_shape = jax.ShapeDtypeStruct((holders // 2, capacity // 2, 2 * total), jnp.float32)
    send, scores, rest = pl.pallas_call(
        functools.partial(score_kernel, holders, capacity),
        out_shape=[
            picked_shape,
            jax.ShapeDtypeStruct((total, per_holder), jnp.float32),
            jax.ShapeDtypeStruct((1, slots // 2), jnp.float32),
        ],
        in_specs=[VMEM] * (holders + 3),
        out_specs=[VMEM] * 3,
        scratch_shapes=[pltpu.VMEM((total, width), bf16)],
        compiler_params=pltpu.CompilerParams(vmem_limit_bytes=8 * 2**20 + 2 * bytes_in + 48 * total * slots),
    )(*blocks[::-1], *far_notes, pltpu.with_memory_space_constraint(pages, pltpu.VMEM))

    handed = swap(send, "store", 1)
    keep = pl.pallas_call(
        rest_kernel,
        out_shape=picked_shape,
        in_specs=[VMEM] * 2,
        out_specs=VMEM,
        compiler_params=pltpu.CompilerParams(vmem_limit_bytes=4 * 2**20 + 24 * total * slots),
    )(scores, rest)
    chips = holders // 2
    landed = []
    for step in range(chips):
        pair = jnp.stack([keep[step], handed[step]])
        to = [(i, (i // 2 + step) % chips * 2 + 1 - i % 2) for i in range(holders)]
        landed.append(lax.ppermute(pair, "store", to) if step else pair)
    share = slots // groups
    terms = pl.pallas_call(
        functools.partial(spread_kernel, holders, groups),
        out_shape=[jax.ShapeDtypeStruct((share // 2, 2 * total), jnp.float32)] * groups,
        in_specs=[SMEM] + [VMEM] * (1 + len(landed)),
        out_specs=[VMEM] * groups,
        compiler_params=pltpu.CompilerParams(vmem_limit_bytes=4 * 2**20 + 64 * total * slots),
    )(counts, found, *landed[::-1])
    summed = terms[0]
    for step in range(1, groups):
        summed = summed + lax.ppermute(terms[step], "layer", [(g, (g + step) % groups) for g in range(groups)])
    return jnp.concatenate([summed[:, :total], summed[:, total:]], axis=0)[None]


def solution(mesh):
    placed = (
        P("store", "layer"),
        P("layer", None, None),
        P("layer", None, None),
        P("store", "layer"),
        P(),
        P("store", None),
        P("store"),
    )
    return jax.shard_map(
        on_device, mesh=mesh, in_specs=placed, out_specs=P("store", "layer", None), check_vma=False
    )
```
